32 devices in a mesh: dp: 8 (over z, x), mp: 4 (over y, core).
Axes of the slice: x: 2, y: 2, z: 4, core: 2. Of those that a mesh axis runs over, the one named last changes fastest.
Arguments:
- pieces: bfloat16 [2048, 8, 512], P(('dp', 'mp')), may hold values from -6 to 6
- counts: int32 [2048], P('dp'), may hold values from 1 to 8
- entry_ids: int32 [8192], P('dp'), may hold values from 0 to 2047
- segment_ids: int32 [8, 1024], P('dp'), may hold values from 0 to 256, as said below
- norm1_gain: float32 [512], replicated, may hold values from 0.5 to 1.5
- norm1_shift: float32 [512], replicated, may hold values from -3 to 3
- query_weight: bfloat16 [512, 512], P(None, 'mp'), may hold values from -0.25 to 0.25
- key_weight: bfloat16 [512, 512], P(None, 'mp'), may hold values from -0.25 to 0.25
- value_weight: bfloat16 [512, 512], P(None, 'mp'), may hold values from -0.25 to 0.25
- out_weight: bfloat16 [512, 512], P(None, 'mp'), may hold values from -0.5 to 0.5
- norm2_gain: float32 [512], replicated, may hold values from 0.5 to 1.5
- norm2_shift: float32 [512], replicated, may hold values from -3 to 3
- up_weight: bfloat16 [512, 2048], P(None, 'mp'), may hold values from -0.25 to 0.25
- down_weight: bfloat16 [512, 2048], P(None, 'mp'), may hold values from -0.125 to 0.125
- proj_weight: bfloat16 [512, 2048], P(None, 'mp'), may hold values from -0.25 to 0.25
- proj_bias: float32 [2048], P('mp'), may hold values from -3 to 3
- text_norm1_gain: float32 [2048], replicated, may hold values from 0.25 to 1.75
- text_query: bfloat16 [2048, 2048], P(None, 'mp'), may hold values from -0.125 to 0.125
- text_key: bfloat16 [2048, 256], replicated, may hold values from -0.125 to 0.125
- text_value: bfloat16 [2048, 256], replicated, may hold values from -0.125 to 0.125
- text_out_proj: bfloat16 [2048, 2048], P(None, 'mp'), may hold values from -0.5 to 0.5
- text_norm2_gain: float32 [2048], replicated, may hold values from 0.25 to 1.75
- text_gate: bfloat16 [2048, 5632], P(None, 'mp'), may hold values from -0.125 to 0.125
- text_up: bfloat16 [2048, 5632], P(None, 'mp'), may hold values from -0.125 to 0.125
- text_down: bfloat16 [2048, 5632], P(None, 'mp'), may hold values from -0.15625 to 0.15625
- token_grad: bfloat16 [8192, 2048], P(('dp', 'mp')), may hold values from -6 to 6
Outputs:
- text_out: float32 [8192, 2048], P(('dp', 'mp'))
- pieces_grad: float32 [2048, 8, 512], P(('dp', 'mp'))
- norm1_gain_grad: float32 [512], replicated
- norm1_shift_grad: float32 [512], replicated
- query_grad: float32 [512, 512], P(None, 'mp')
- key_grad: float32 [512, 512], P(None, 'mp')
- value_grad: float32 [512, 512], P(None, 'mp')
- out_grad: float32 [512, 512], P(None, 'mp')
- norm2_gain_grad: float32 [512], replicated
- norm2_shift_grad: float32 [512], replicated
- up_grad: float32 [512, 2048], P(None, 'mp')
- down_grad: float32 [512, 2048], P(None, 'mp')
- proj_grad: float32 [512, 2048], P(None, 'mp')
- proj_bias_grad: float32 [2048], P('mp')
The draws below stay inside these ranges and needn't reach their ends.
Inputs may be any that keep to these rules, and one draw needn't show every extreme that they name: `counts`: slots at or past an entry's count are padding. `entry_ids`: any token may name any entry of the whole set. `segment_ids`: segment numbers start at 0 in every row and never fall along it; the last segment of every row has number 1024 // 4; in every row one segment covers positions 127 through 1024 - 1024 // 8.
All inputs are finite; a program needn't handle non-finite values.
Results may differ from the reference program's by a relative error of at most 0.029.
Values may be sent and summed in bfloat16 or wider, within the bound.
A program may use at most 256 MiB of HBM per device.

```python
import math
import jax
import jax.numpy as jnp
from jax import lax

W = 512
HEADS = 8
HD = 64
FF = 2048
OUT = 2048
QHEADS = 32
KVHEADS = 4
FHD = 64
FFT = 5632
SLOTS = 8
LENGTH = 1024
ENTRIES = 2048
ROWS = 8
TOKENS = 8192


def draw_segment_ids(key, part):
    key = jax.random.fold_in(key, 11)
    first_key, last_key, break_key = jax.random.split(key, 3)
    edge_width = LENGTH // 8
    first_spot = jax.random.randint(first_key, (ROWS, 1), 0, edge_width)
    last_spot = jax.random.randint(last_key, (ROWS, 1), LENGTH - edge_width + 1, LENGTH + 1)
    positions = jnp.arange(LENGTH, dtype=jnp.int32)[None, :]
    breaks = jax.random.randint(break_key, (ROWS, LENGTH), 0, 24) == 0
    outside = (positions < first_spot) | (positions >= last_spot)
    starts = breaks & outside | (positions == first_spot) | (positions == last_spot)
    starts = starts & (positions > 0)
    numbers = jnp.cumsum(starts.astype(jnp.int32), axis=1).astype(jnp.int32)
    final_number = numbers[:, -1:]
    top_number = jnp.zeros_like(numbers) + LENGTH // 4
    return jnp.where(numbers == final_number, top_number, numbers).astype(jnp.int32)


def place_ends(result, stream_key, smallest, high):
    longest = result.shape.index(max(result.shape))
    spots = []
    for shift in (0, 1):
        where = [jax.random.randint(jax.random.fold_in(stream_key, axis), (), 0, length) for axis, length in enumerate(result.shape)]
        where[longest] = (where[longest] + shift) % result.shape[longest]
        spots.append(tuple(where))
    return result.at[spots[0]].set(smallest).at[spots[1]].set(high)


def block_levels(key, shape, shards, least, top_value):
    def one(position, blocks):
        draws = jax.random.uniform(jax.random.fold_in(jax.random.fold_in(key, 6), position), (blocks,), jnp.float32, least / len(shards), top_value / len(shards))
        return jnp.repeat(jnp.exp(draws), shape[position] // blocks).reshape((-1,) + (1,) * (len(shape) - position - 1))

    gain = one(*shards[0])
    for cut in shards[1:]:
        gain = gain * one(*cut)
    return gain


def noise(own_key, dims, deviation, reach, shards=(), kind=jnp.bfloat16):
    entries = jax.random.normal(own_key, dims, jnp.float32) * deviation
    if len(shards) > 0:
        entries = block_levels(own_key, dims, shards, -0.22, 0.18) * entries
    return jnp.clip(entries, min=-reach, max=reach).astype(kind)


def setup_inputs(seed: int = 0) -> dict:
    keys = jax.random.split(jax.random.key(seed), 27)
    pieces = noise(keys[0], (ENTRIES, SLOTS, W), 1.0, 6.0, ((0, 32),))
    counts = place_ends(jax.random.randint(keys[1], (ENTRIES,), 1, SLOTS + 1), jax.random.fold_in(keys[1], 1), 1, SLOTS).astype(jnp.int32)
    entry_ids = place_ends(jax.random.randint(keys[2], (TOKENS,), 0, ENTRIES), jax.random.fold_in(keys[2], 1), 0, ENTRIES - 1).astype(jnp.int32)
    segment_ids = draw_segment_ids(jax.random.fold_in(keys[26], 71), 0)
    norm1_gain = jnp.clip(1.0 + 0.1 * jax.random.normal(keys[4], (W,), jnp.float32), 0.5, 1.5)
    norm1_shift = noise(keys[5], (W,), 0.5, 3.0, (), jnp.float32)
    query_weight = noise(keys[6], (W, HEADS * HD), W ** -0.5, 0.25, ((1, 4),))
    key_weight = noise(keys[7], (W, HEADS * HD), W ** -0.5, 0.25, ((1, 4),))
    value_weight = noise(keys[8], (W, HEADS * HD), W ** -0.5, 0.25, ((1, 4),))
    out_weight = noise(keys[9], (W, HEADS * HD), (HEADS * HD // 4) ** -0.5, 0.5, ((1, 4),))
    norm2_gain = jnp.clip(1.0 + 0.1 * jax.random.normal(keys[10], (W,), jnp.float32), 0.5, 1.5)
    norm2_shift = noise(keys[11], (W,), 0.5, 3.0, (), jnp.float32)
    up_weight = noise(keys[12], (W, FF), W ** -0.5, 0.25, ((1, 4),))
    down_weight = noise(keys[13], (W, FF), FF ** -0.5, 0.125, ((1, 4),))
    proj_weight = noise(keys[14], (W, OUT), W ** -0.5, 0.25, ((1, 4),))
    proj_bias = noise(keys[15], (OUT,), 0.5, 3.0, ((0, 4),), jnp.float32)
    text_norm1_gain = jnp.clip(1.0 + 0.15 * jax.random.normal(keys[16], (OUT,), jnp.float32), 0.25, 1.75)
    text_query = noise(keys[17], (OUT, QHEADS * FHD), OUT ** -0.5, 0.125, ((1, 4),))
    text_key = noise(keys[18], (OUT, KVHEADS * FHD), OUT ** -0.5, 0.125)
    text_value = noise(keys[19], (OUT, KVHEADS * FHD), OUT ** -0.5, 0.125)
    text_out_proj = noise(keys[20], (OUT, QHEADS * FHD), (QHEADS * FHD // 16) ** -0.5, 0.5, ((1, 4),))
    text_norm2_gain = jnp.clip(1.0 + 0.15 * jax.random.normal(keys[21], (OUT,), jnp.float32), 0.25, 1.75)
    text_gate = noise(keys[22], (OUT, FFT), OUT ** -0.5, 0.125, ((1, 4),))
    text_up = noise(keys[23], (OUT, FFT), OUT ** -0.5, 0.125, ((1, 4),))
    text_down = noise(keys[24], (OUT, FFT), (FFT // 4) ** -0.5, 0.15625, ((1, 4),))
    token_grad = noise(keys[25], (TOKENS, OUT), 1.0, 6.0, ((0, 32),))
    return {"pieces": pieces, "counts": counts, "entry_ids": entry_ids, "segment_ids": segment_ids, "norm1_gain": norm1_gain, "norm1_shift": norm1_shift, "query_weight": query_weight, "key_weight": key_weight, "value_weight": value_weight, "out_weight": out_weight, "norm2_gain": norm2_gain, "norm2_shift": norm2_shift, "up_weight": up_weight, "down_weight": down_weight, "proj_weight": proj_weight, "proj_bias": proj_bias, "text_norm1_gain": text_norm1_gain, "text_query": text_query, "text_key": text_key, "text_value": text_value, "text_out_proj": text_out_proj, "text_norm2_gain": text_norm2_gain, "text_gate": text_gate, "text_up": text_up, "text_down": text_down, "token_grad": token_grad}


@jax.custom_vjp
def low(v):
    return lax.optimization_barrier(v.astype(jnp.bfloat16)).astype(jnp.float32)

@jax.custom_vjp
def low_back(v):
    return v

def low_keep(v):
    return (low(v), None)

def low_pass(kept, grad):
    return (grad,)

def back_keep(v):
    return (v, None)

def back_low(kept, grad):
    return (low(grad),)
low.defvjp(low_keep, low_pass)
low_back.defvjp(back_keep, back_low)
exact_mode = lax.Precision.HIGHEST

def round_both(values):
    return low(low_back(values))

def layer_norm(values, norm_gain, norm_shift):
    average = lax.optimization_barrier(jnp.mean(values, axis=-1, keepdims=True))
    centred = values - average
    variance = lax.optimization_barrier(jnp.mean(centred * centred, axis=-1, keepdims=True))
    return centred * lax.rsqrt(variance + 1e-05) * norm_gain + norm_shift

def rms_norm(values, norm_gain):
    return values * lax.rsqrt(lax.optimization_barrier(jnp.mean(values * values, axis=-1, keepdims=True)) + 1e-05) * norm_gain

def rope_tables(length, head_size):
    positions = jnp.arange(length, dtype=jnp.float32)
    inverse_rates = jnp.exp(jnp.arange(head_size // 2, dtype=jnp.float32) * (-2.0 * math.log(10000.0) / head_size))
    angles = positions[:, None] * inverse_rates[None, :]
    angles = jnp.concatenate([angles, angles], axis=-1)
    return (jnp.cos(angles)[:, None, :], jnp.sin(angles)[:, None, :])

def rotate(values, cosine_table, sine_table):
    half_size = values.shape[-1] // 2
    turned = jnp.concatenate([-values[..., half_size:], values[..., :half_size]], axis=-1)
    return values * cosine_table + turned * sine_table

def hyper_block(entry_rows, row_counts, params):
    gain_one, shift_one, w_query, w_key, w_value, w_out, gain_two, shift_two, w_up, w_down = params
    entry_total = entry_rows.shape[0]
    attn_in = low(layer_norm(entry_rows, gain_one, shift_one))

    def heads_of(weight):
        projected = jnp.einsum('esw,wf->esf', attn_in, weight, precision=exact_mode)
        return round_both(projected).reshape(entry_total, SLOTS, HEADS, HD)
    queries = heads_of(w_query)
    key_rows = heads_of(w_key)
    value_rows = heads_of(w_value)
    key_mask = jnp.arange(SLOTS)[None, :] < row_counts[:, None]
    scores = jnp.einsum('eshd,ethd->ehst', queries, key_rows, precision=exact_mode) * HD ** (-0.5)
    scores = low_back(jnp.where(key_mask[:, None, None, :], scores, -1e+30))
    softmax_low = low(jax.nn.softmax(scores, axis=-1))
    attended = jnp.einsum('ehst,ethd->eshd', softmax_low, value_rows, precision=exact_mode)
    attended = round_both(attended.reshape(entry_total, SLOTS, HEADS * HD))
    residual = entry_rows + low_back(jnp.einsum('esf,wf->esw', attended, w_out, precision=exact_mode))
    ffn_in = low(layer_norm(residual, gain_two, shift_two))
    hidden_pre = low_back(jnp.einsum('esw,wf->esf', ffn_in, w_up, precision=exact_mode))
    hidden_low = low(jax.nn.gelu(hidden_pre))
    block_out = residual + low_back(jnp.einsum('esf,wf->esw', hidden_low, w_down, precision=exact_mode))
    valid_mask = key_mask.astype(jnp.float32)
    pooled = lax.optimization_barrier(jnp.sum(block_out * valid_mask[:, :, None], axis=1))
    return pooled / row_counts.astype(jnp.float32)[:, None]

def text_row(row_inputs, row_segments, frozen):
    gain_one, w_query, w_key, w_value, w_out, gain_two, w_gate, w_up, w_down = frozen
    length = row_inputs.shape[0]
    cosine_table, sine_table = rope_tables(length, FHD)
    repeat_count = QHEADS // KVHEADS
    normed = low(rms_norm(row_inputs, gain_one))
    query_pre = low_back(jnp.dot(normed, w_query, precision=exact_mode)).reshape(length, QHEADS, FHD)
    queries = low(rotate(query_pre, cosine_table, sine_table))
    key_pre = jnp.dot(normed, w_key, precision=exact_mode).reshape(length, KVHEADS, FHD)
    key_rows = low(rotate(low_back(jnp.repeat(key_pre, repeat_count, axis=1)), cosine_table, sine_table))
    value_pre = low(jnp.dot(normed, w_value, precision=exact_mode)).reshape(length, KVHEADS, FHD)
    value_rows = low_back(jnp.repeat(value_pre, repeat_count, axis=1))
    positions = jnp.arange(length)
    allowed = (positions[None, :] <= positions[:, None]) & (row_segments[None, :] == row_segments[:, None])
    scores = jnp.einsum('qhd,khd->hqk', queries, key_rows, precision=exact_mode) * FHD ** (-0.5)
    scores = low_back(jnp.where(allowed[None], scores, -1e+30))
    weights = low(jax.nn.softmax(scores, axis=-1))
    attended = jnp.einsum('hqk,khd->qhd', weights, value_rows, precision=exact_mode)
    attended = round_both(attended.reshape(length, QHEADS * FHD))
    residual = row_inputs + low_back(jnp.dot(attended, w_out.T, precision=exact_mode))
    mlp_in = low(rms_norm(residual, gain_two))
    gate_pre = low_back(jnp.dot(mlp_in, w_gate, precision=exact_mode))
    up_pre = low_back(jnp.dot(mlp_in, w_up, precision=exact_mode))
    mixed_act = low(jax.nn.silu(gate_pre) * up_pre)
    return residual + low_back(jnp.dot(mixed_act, w_down.T, precision=exact_mode))

def reference(pieces, counts, entry_ids, segment_ids, norm1_gain, norm1_shift, query_weight, key_weight, value_weight, out_weight, norm2_gain, norm2_shift, up_weight, down_weight, proj_weight, proj_bias, text_norm1_gain, text_query, text_key, text_value, text_out_proj, text_norm2_gain, text_gate, text_up, text_down, token_grad):
    block_size = math.gcd(ENTRIES, 1024)
    block_count = ENTRIES // block_size
    frozen = (text_norm1_gain.astype(jnp.float32), text_query.astype(jnp.float32), text_key.astype(jnp.float32), text_value.astype(jnp.float32), text_out_proj.astype(jnp.float32), text_norm2_gain.astype(jnp.float32), text_gate.astype(jnp.float32), text_up.astype(jnp.float32), text_down.astype(jnp.float32))

    def forward(pieces_f, gain_one, shift_one, w_query, w_key, w_value, w_out, gain_two, shift_two, w_up, w_down, w_proj, bias_proj):
        params = (gain_one, shift_one, w_query, w_key, w_value, w_out, gain_two, shift_two, w_up, w_down)

        def run_block(entry_block):
            return hyper_block(entry_block[0], entry_block[1], params)
        pooled = lax.map(jax.checkpoint(run_block), (pieces_f.reshape(block_count, block_size, SLOTS, W), counts.reshape(block_count, block_size)))
        pooled_low = low(pooled.reshape(ENTRIES, W))
        predicted = round_both(jnp.dot(pooled_low, w_proj, precision=exact_mode) + bias_proj)
        embeds = jnp.take(predicted, entry_ids, axis=0).reshape(ROWS, LENGTH, OUT)

        def run_row(row_parts):
            return text_row(row_parts[0], row_parts[1], frozen)
        outputs = lax.map(jax.checkpoint(run_row), (embeds, segment_ids))
        return outputs.reshape(TOKENS, OUT)
    outputs, pullback = jax.vjp(forward, pieces.astype(jnp.float32), norm1_gain.astype(jnp.float32), norm1_shift.astype(jnp.float32), query_weight.astype(jnp.float32), key_weight.astype(jnp.float32), value_weight.astype(jnp.float32), out_weight.astype(jnp.float32), norm2_gain.astype(jnp.float32), norm2_shift.astype(jnp.float32), up_weight.astype(jnp.float32), down_weight.astype(jnp.float32), proj_weight.astype(jnp.float32), proj_bias.astype(jnp.float32))
    gradients = pullback(token_grad.astype(jnp.float32))
    return (outputs, gradients[0], gradients[1], gradients[2], gradients[3], gradients[4], gradients[5], gradients[6], gradients[7], gradients[8], gradients[9], gradients[10], gradients[11], gradients[12])
```

```python
from functools import partial
import math

import jax
import jax.numpy as jnp
from jax import lax
from jax.sharding import PartitionSpec as P

HD = 64
QHEADS = 32
KVHEADS = 4
FHD = 64


def layer_norm(values, norm_gain, norm_shift):
    average = jnp.mean(values, axis=-1, keepdims=True)
    centred = values - average
    variance = jnp.mean(centred * centred, axis=-1, keepdims=True)
    return centred * lax.rsqrt(variance + 1e-05) * norm_gain + norm_shift


def rms_norm(values, norm_gain):
    return values * lax.rsqrt(jnp.mean(values * values, axis=-1, keepdims=True) + 1e-05) * norm_gain


def swiglu(gate_pre, up_pre):
    return jax.nn.silu(gate_pre) * up_pre


def rope_tables(length, head_size):
    positions = jnp.arange(length, dtype=jnp.float32)
    inverse_rates = jnp.exp(
        jnp.arange(head_size // 2, dtype=jnp.float32) * (-2.0 * math.log(10000.0) / head_size)
    )
    angles = positions[:, None] * inverse_rates[None, :]
    angles = jnp.concatenate([angles, angles], axis=-1)
    return (jnp.cos(angles)[:, None, :], jnp.sin(angles)[:, None, :])


def rotate(values, cosine_table, sine_table):
    half_size = values.shape[-1] // 2
    turned = jnp.concatenate([-values[..., half_size:], values[..., :half_size]], axis=-1)
    return values * cosine_table + turned * sine_table


def pool_rows(values, valid_mask, row_counts):
    return (
        jnp.sum(values * valid_mask[:, :, None], axis=1) / row_counts.astype(jnp.float32)[:, None]
    )


def place_rows(block_rows, first_row, total_rows):
    zero_rows = jnp.zeros((total_rows, block_rows.shape[1]), jnp.float32)
    return lax.dynamic_update_slice(zero_rows, block_rows, (first_row, first_row * 0))


def hyper_rows(values):
    return lax.all_gather(values, "mp", axis=0, tiled=True)


def hyper_sums(values):
    return lax.psum_scatter(
        values.astype(jnp.bfloat16), "mp", scatter_dimension=0, tiled=True
    ).astype(jnp.float32)


def text_rows(values):
    return lax.all_gather(values, "mp", axis=0, tiled=True)


def text_sums(values):
    return lax.psum_scatter(
        values.astype(jnp.bfloat16), "mp", scatter_dimension=0, tiled=True
    ).astype(jnp.float32)


def group_total(values):
    return lax.psum(values.astype(jnp.bfloat16), "mp").astype(jnp.float32)


def masked_scores(query_block, key_row, query_segments, key_segments, query_first, score_scale):
    raw_scores = (
        jnp.einsum("qhd,kd->hqk", query_block, key_row, preferred_element_type=jnp.float32)
        * score_scale
    )
    query_spots = query_first + jnp.arange(query_block.shape[0])
    key_spots = jnp.arange(key_row.shape[0])
    allowed = (key_spots[None, :] <= query_spots[:, None]) & (
        key_segments[None, :] == query_segments[:, None]
    )
    return jnp.where(allowed[None], raw_scores, -1e30)


def attend_forward(
    query_block, key_row, value_row, query_segments, key_segments, query_first, score_scale
):
    scores = masked_scores(
        query_block, key_row, query_segments, key_segments, query_first, score_scale
    )
    top_score = jnp.max(scores, axis=-1, keepdims=True)
    log_total = top_score + jnp.log(jnp.sum(jnp.exp(scores - top_score), axis=-1, keepdims=True))
    weights = jnp.exp(scores - log_total).astype(jnp.bfloat16)
    attended = jnp.einsum("hqk,kd->qhd", weights, value_row, preferred_element_type=jnp.float32)
    return (attended.astype(jnp.bfloat16), log_total)


def on_device(
    pieces,
    counts,
    entry_ids,
    segment_ids,
    norm1_gain,
    norm1_shift,
    query_weight,
    key_weight,
    value_weight,
    out_weight,
    norm2_gain,
    norm2_shift,
    up_weight,
    down_weight,
    proj_weight,
    proj_bias,
    text_norm1_gain,
    text_query,
    text_key,
    text_value,
    text_out_proj,
    text_norm2_gain,
    text_gate,
    text_up,
    text_down,
    token_grad,
):
    local_count, slot_count, feature_count = pieces.shape
    group_count = counts.shape[0]
    score_scale = HD ** (-0.5)
    own_start = lax.axis_index("mp") * local_count
    own_counts = lax.dynamic_slice_in_dim(counts, own_start, local_count)
    slot_index = jnp.arange(slot_count)
    own_mask = (slot_index[None, :] < own_counts[:, None]).astype(jnp.float32)
    rows_mask = (slot_index[None, :] < counts[:, None]).astype(jnp.float32)
    pieces_f = pieces.astype(jnp.float32)
    normed_one, norm_one_back = jax.vjp(layer_norm, pieces_f, norm1_gain, norm1_shift)
    attn_in = hyper_rows(normed_one.astype(jnp.bfloat16))
    row_total = attn_in.shape[0]
    head_count = query_weight.shape[1] // HD

    def heads_of(weight):
        projected = jnp.einsum("esw,wf->esf", attn_in, weight, preferred_element_type=jnp.float32)
        return projected.astype(jnp.bfloat16).reshape(row_total, slot_count, head_count, HD)

    def merge_heads(head_rows):
        return head_rows.reshape(row_total, slot_count, head_count * HD)

    queries = heads_of(query_weight)
    key_rows = heads_of(key_weight)
    value_rows = heads_of(value_weight)

    def scores_of():
        raw_scores = (
            jnp.einsum("eshd,ethd->ehst", queries, key_rows, preferred_element_type=jnp.float32)
            * score_scale
        )
        return jnp.where(rows_mask[:, None, None, :] > 0.5, raw_scores, -1e30)

    scores = scores_of()
    top_score = jnp.max(scores, axis=-1, keepdims=True)
    log_total = top_score + jnp.log(jnp.sum(jnp.exp(scores - top_score), axis=-1, keepdims=True))
    softmax_low = jnp.exp(scores - log_total).astype(jnp.bfloat16)
    attended = jnp.einsum(
        "ehst,ethd->eshd", softmax_low, value_rows, preferred_element_type=jnp.float32
    )
    attended = merge_heads(attended.astype(jnp.bfloat16))
    attn_part = jnp.einsum("esf,wf->esw", attended, out_weight, preferred_element_type=jnp.float32)
    residual = pieces_f + hyper_sums(attn_part)
    normed_two, norm_two_back = jax.vjp(layer_norm, residual, norm2_gain, norm2_shift)
    ffn_in = hyper_rows(normed_two.astype(jnp.bfloat16))
    hidden_pre = jnp.einsum("esw,wf->esf", ffn_in, up_weight, preferred_element_type=jnp.float32)
    hidden_act, gelu_back = jax.vjp(jax.nn.gelu, hidden_pre)
    hidden_low = hidden_act.astype(jnp.bfloat16)
    ffn_part = jnp.einsum(
        "esf,wf->esw", hidden_low, down_weight, preferred_element_type=jnp.float32
    )
    pooled_terms = pool_rows(ffn_part, rows_mask, counts)
    pooled_terms = pooled_terms + place_rows(
        pool_rows(residual, own_mask, own_counts), own_start, group_count
    )
    pooled = group_total(pooled_terms)
    pooled_low = pooled.astype(jnp.bfloat16)
    entries_low = lax.all_gather(pooled_low, "dp", axis=0, tiled=True)
    proj_full = lax.all_gather(proj_weight, "mp", axis=1, tiled=True)
    bias_full = lax.all_gather(proj_bias, "mp", axis=0, tiled=True)
    entry_total = entries_low.shape[0]
    chosen = (entry_ids[:, None] == jnp.arange(entry_total)[None, :]).astype(jnp.bfloat16)
    token_pooled = jnp.dot(chosen, entries_low, preferred_element_type=jnp.float32).astype(
        jnp.bfloat16
    )
    text_full = (
        jnp.dot(token_pooled, proj_full, preferred_element_type=jnp.float32) + bias_full
    ).astype(jnp.bfloat16)
    tok_count = text_full.shape[0]
    row_share = tok_count // lax.axis_size("mp")
    text_start = lax.axis_index("mp") * row_share
    pack_count = segment_ids.shape[0]
    length = segment_ids.shape[1]
    query_rows = min(512, length)
    block_count = length // query_rows
    local_heads = text_query.shape[1] // FHD
    text_scale = FHD ** (-0.5)
    kv_index = lax.axis_index("mp") * local_heads // (QHEADS // KVHEADS)
    key_local = lax.dynamic_slice_in_dim(text_key, kv_index * FHD, FHD, 1)
    value_local = lax.dynamic_slice_in_dim(text_value, kv_index * FHD, FHD, 1)
    cosine_table, sine_table = rope_tables(length, FHD)
    block_starts = jnp.arange(block_count) * query_rows
    inputs_f = text_full.astype(jnp.float32)
    own_inputs = lax.dynamic_slice_in_dim(inputs_f, text_start, row_share)
    text_normed = rms_norm(inputs_f, text_norm1_gain).astype(jnp.bfloat16)
    query_pre = jnp.dot(text_normed, text_query, preferred_element_type=jnp.float32).reshape(
        pack_count, length, local_heads, FHD
    )
    text_queries = rotate(query_pre, cosine_table, sine_table).astype(jnp.bfloat16)
    key_pre = jnp.dot(text_normed, key_local, preferred_element_type=jnp.float32).reshape(
        pack_count, length, 1, FHD
    )
    text_keys = rotate(key_pre, cosine_table, sine_table)[:, :, 0, :].astype(jnp.bfloat16)
    text_values = (
        jnp.dot(text_normed, value_local, preferred_element_type=jnp.float32)
        .astype(jnp.bfloat16)
        .reshape(pack_count, length, FHD)
    )

    def forward_row(row_parts):
        query_row, key_row, value_row, segment_row = row_parts

        def forward_block(block_parts):
            query_block, block_segments, block_first = block_parts
            return attend_forward(
                query_block,
                key_row,
                value_row,
                block_segments,
                segment_row,
                block_first,
                text_scale,
            )

        return lax.map(
            forward_block,
            (
                query_row.reshape(block_count, query_rows, local_heads, FHD),
                segment_row.reshape(block_count, query_rows),
                block_starts,
            ),
        )

    text_attended, text_logs = lax.map(
        forward_row, (text_queries, text_keys, text_values, segment_ids)
    )
    attended_flat = text_attended.reshape(tok_count, local_heads * FHD)
    attn_rows = text_sums(
        jnp.einsum("tf,wf->tw", attended_flat, text_out_proj, preferred_element_type=jnp.float32)
    )
    text_residual = own_inputs + attn_rows
    mlp_normed, rms_two_back = jax.vjp(partial(rms_norm, norm_gain=text_norm2_gain), text_residual)
    mlp_in = text_rows(mlp_normed.astype(jnp.bfloat16))
    gate_pre = jnp.dot(mlp_in, text_gate, preferred_element_type=jnp.float32)
    up_pre = jnp.dot(mlp_in, text_up, preferred_element_type=jnp.float32)
    mixed_act, swiglu_back = jax.vjp(swiglu, gate_pre, up_pre)
    mixed_low = mixed_act.astype(jnp.bfloat16)
    text_out = text_residual + text_sums(
        jnp.einsum("tf,wf->tw", mixed_low, text_down, preferred_element_type=jnp.float32)
    )
    mlp_grad = text_rows(token_grad)
    act_grad_text = jnp.dot(mlp_grad, text_down, preferred_element_type=jnp.float32)
    gate_grad, up_grad_text = swiglu_back(act_grad_text)
    mlp_in_part = jnp.einsum(
        "tf,wf->tw", gate_grad.astype(jnp.bfloat16), text_gate, preferred_element_type=jnp.float32
    )
    mlp_in_part = mlp_in_part + jnp.einsum(
        "tf,wf->tw", up_grad_text.astype(jnp.bfloat16), text_up, preferred_element_type=jnp.float32
    )
    text_residual_grad = token_grad.astype(jnp.float32) + rms_two_back(text_sums(mlp_in_part))[0]
    attn_back_rows = text_rows(text_residual_grad.astype(jnp.bfloat16))
    attended_grad_text = jnp.dot(attn_back_rows, text_out_proj, preferred_element_type=jnp.float32)
    attended_grad_text = attended_grad_text.astype(jnp.bfloat16).reshape(
        pack_count, length, local_heads, FHD
    )

    def backward_row(row_parts):
        query_row, key_row, value_row, grad_row, segment_row, log_row = row_parts

        def backward_block(totals, block_parts):
            key_total, value_total = totals
            query_block, grad_block, block_segments, block_log, block_first = block_parts
            scores_again = masked_scores(
                query_block, key_row, block_segments, segment_row, block_first, text_scale
            )
            prob_full = jnp.exp(scores_again - block_log)
            prob_low = prob_full.astype(jnp.bfloat16)
            prob_grad = jnp.einsum(
                "qhd,kd->hqk", grad_block, value_row, preferred_element_type=jnp.float32
            )
            value_total = value_total + jnp.einsum(
                "hqk,qhd->khd", prob_low, grad_block, preferred_element_type=jnp.float32
            )
            score_grad_text = prob_full * (
                prob_grad - jnp.sum(prob_full * prob_grad, axis=-1, keepdims=True)
            )
            score_grad_text = score_grad_text.astype(jnp.bfloat16)
            query_grad_block = (
                jnp.einsum(
                    "hqk,kd->qhd", score_grad_text, key_row, preferred_element_type=jnp.float32
                )
                * text_scale
            )
            key_total = (
                key_total
                + jnp.einsum(
                    "hqk,qhd->khd", score_grad_text, query_block, preferred_element_type=jnp.float32
                )
                * text_scale
            )
            return ((key_total, value_total), query_grad_block)

        zero_rows = jnp.zeros((length, local_heads, FHD), jnp.float32)
        block_parts = (
            query_row.reshape(block_count, query_rows, local_heads, FHD),
            grad_row.reshape(block_count, query_rows, local_heads, FHD),
            segment_row.reshape(block_count, query_rows),
            log_row,
            block_starts,
        )
        totals, query_grads_row = lax.scan(backward_block, (zero_rows, zero_rows), block_parts)
        return (query_grads_row.reshape(length, local_heads, FHD), totals[0], totals[1])

    query_grads, key_grads, value_grads = lax.map(
        backward_row,
        (text_queries, text_keys, text_values, attended_grad_text, segment_ids, text_logs),
    )
    query_low = (
        rotate(query_grads, cosine_table, -sine_table)
        .astype(jnp.bfloat16)
        .reshape(tok_count, local_heads * FHD)
    )
    key_low = (
        rotate(key_grads, cosine_table, -sine_table)
        .astype(jnp.bfloat16)
        .reshape(tok_count, local_heads * FHD)
    )
    value_low = value_grads.astype(jnp.bfloat16).reshape(tok_count, local_heads * FHD)
    normed_part = jnp.einsum("tf,wf->tw", query_low, text_query, preferred_element_type=jnp.float32)
    normed_part = normed_part + jnp.einsum(
        "tf,wf->tw",
        key_low,
        jnp.tile(key_local, (1, local_heads)),
        preferred_element_type=jnp.float32,
    )
    normed_part = normed_part + jnp.einsum(
        "tf,wf->tw",
        value_low,
        jnp.tile(value_local, (1, local_heads)),
        preferred_element_type=jnp.float32,
    )
    normed_sum = text_sums(normed_part)
    rms_one_back = jax.vjp(partial(rms_norm, norm_gain=text_norm1_gain), own_inputs)[1]
    embed_rows = text_residual_grad + rms_one_back(normed_sum)[0]
    embed_low = embed_rows.astype(jnp.bfloat16)
    pooled_tokens = text_rows(
        jnp.einsum("to,wo->tw", embed_low, proj_full, preferred_element_type=jnp.float32).astype(
            jnp.bfloat16
        )
    )
    share = pooled_tokens.shape[1] // lax.axis_size("mp")
    pooled_share = lax.dynamic_slice_in_dim(
        pooled_tokens, lax.axis_index("mp") * share, share, 1
    )
    entry_part = jnp.einsum(
        "te,tw->ew", chosen, pooled_share, preferred_element_type=jnp.float32
    ).astype(jnp.bfloat16)
    pooled_own = lax.psum_scatter(entry_part, "dp", scatter_dimension=0, tiled=True)
    pooled_grad = lax.all_gather(pooled_own, "mp", axis=1, tiled=True).astype(jnp.float32)
    embed_grad = lax.all_to_all(embed_low, "mp", split_axis=1, concat_axis=0, tiled=True)
    proj_bias_grad = jnp.sum(embed_grad.astype(jnp.float32), axis=0)
    proj_grad = jnp.einsum(
        "tw,to->wo", token_pooled, embed_grad, preferred_element_type=jnp.float32
    )
    rows_share = pooled_grad / counts.astype(jnp.float32)[:, None]
    out_grad_rows = (rows_mask[:, :, None] * rows_share[:, None, :]).astype(jnp.bfloat16)
    down_grad = jnp.einsum(
        "esw,esf->wf", out_grad_rows, hidden_low, preferred_element_type=jnp.float32
    )
    act_grad = jnp.einsum(
        "esw,wf->esf", out_grad_rows, down_weight, preferred_element_type=jnp.float32
    )
    pre_grad = gelu_back(act_grad)[0].astype(jnp.bfloat16)
    up_grad = jnp.einsum("esw,esf->wf", ffn_in, pre_grad, preferred_element_type=jnp.float32)
    normed_two_grad = hyper_sums(
        jnp.einsum("esf,wf->esw", pre_grad, up_weight, preferred_element_type=jnp.float32)
    )
    residual_norm, gain_two, shift_two = norm_two_back(normed_two_grad)
    own_share = (
        lax.dynamic_slice_in_dim(pooled_grad, own_start, local_count)
        / own_counts.astype(jnp.float32)[:, None]
    )
    residual_grad = own_mask[:, :, None] * own_share[:, None, :] + residual_norm
    attn_grad = hyper_rows(residual_grad.astype(jnp.bfloat16))
    out_grad = jnp.einsum("esw,esf->wf", attn_grad, attended, preferred_element_type=jnp.float32)
    attended_grad = jnp.einsum(
        "esw,wf->esf", attn_grad, out_weight, preferred_element_type=jnp.float32
    )
    attended_grad = attended_grad.astype(jnp.bfloat16).reshape(
        row_total, slot_count, head_count, HD
    )
    softmax_f = jnp.exp(scores_of() - log_total)
    softmax_again = softmax_f.astype(jnp.bfloat16)
    prob_grad = jnp.einsum(
        "eshd,ethd->ehst", attended_grad, value_rows, preferred_element_type=jnp.float32
    )
    value_grad_rows = jnp.einsum(
        "ehst,eshd->ethd", softmax_again, attended_grad, preferred_element_type=jnp.float32
    ).astype(jnp.bfloat16)
    score_grad = softmax_f * (prob_grad - jnp.sum(softmax_f * prob_grad, axis=-1, keepdims=True))
    score_grad = score_grad.astype(jnp.bfloat16)
    query_grad_rows = (
        jnp.einsum("ehst,ethd->eshd", score_grad, key_rows, preferred_element_type=jnp.float32)
        * score_scale
    ).astype(jnp.bfloat16)
    key_grad_rows = (
        jnp.einsum("ehst,eshd->ethd", score_grad, queries, preferred_element_type=jnp.float32)
        * score_scale
    ).astype(jnp.bfloat16)
    query_flat = merge_heads(query_grad_rows)
    key_flat = merge_heads(key_grad_rows)
    value_flat = merge_heads(value_grad_rows)
    query_grad = jnp.einsum("esw,esf->wf", attn_in, query_flat, preferred_element_type=jnp.float32)
    key_grad = jnp.einsum("esw,esf->wf", attn_in, key_flat, preferred_element_type=jnp.float32)
    value_grad = jnp.einsum("esw,esf->wf", attn_in, value_flat, preferred_element_type=jnp.float32)
    normed_one_part = jnp.einsum(
        "esf,wf->esw", query_flat, query_weight, preferred_element_type=jnp.float32
    )
    normed_one_part = normed_one_part + jnp.einsum(
        "esf,wf->esw", key_flat, key_weight, preferred_element_type=jnp.float32
    )
    normed_one_part = normed_one_part + jnp.einsum(
        "esf,wf->esw", value_flat, value_weight, preferred_element_type=jnp.float32
    )
    normed_one_grad = hyper_sums(normed_one_part)
    pieces_norm, gain_one, shift_one = norm_one_back(normed_one_grad)
    pieces_grad = residual_grad + pieces_norm
    summed = (
        lax.psum(query_grad.astype(jnp.bfloat16), "dp").astype(jnp.float32),
        lax.psum(key_grad.astype(jnp.bfloat16), "dp").astype(jnp.float32),
        lax.psum(value_grad.astype(jnp.bfloat16), "dp").astype(jnp.float32),
        lax.psum(out_grad.astype(jnp.bfloat16), "dp").astype(jnp.float32),
        lax.psum(up_grad.astype(jnp.bfloat16), "dp").astype(jnp.float32),
        lax.psum(down_grad.astype(jnp.bfloat16), "dp").astype(jnp.float32),
        lax.psum(proj_grad.astype(jnp.bfloat16), "dp").astype(jnp.float32),
        lax.psum(proj_bias_grad.astype(jnp.bfloat16), "dp").astype(jnp.float32),
    )
    norm_sums = lax.psum((gain_one, shift_one, gain_two, shift_two), ("dp", "mp"))
    return (
        text_out,
        pieces_grad,
        norm_sums[0],
        norm_sums[1],
        summed[0],
        summed[1],
        summed[2],
        summed[3],
        norm_sums[2],
        norm_sums[3],
        summed[4],
        summed[5],
        summed[6],
        summed[7],
    )


def solution(mesh):
    return jax.shard_map(
        on_device,
        mesh=mesh,
        in_specs=(
            P(("dp", "mp"), None, None),
            P("dp"),
            P("dp"),
            P("dp", None),
            P(),
            P(),
            P(None, "mp"),
            P(None, "mp"),
            P(None, "mp"),
            P(None, "mp"),
            P(),
            P(),
            P(None, "mp"),
            P(None, "mp"),
            P(None, "mp"),
            P("mp"),
            P(),
            P(None, "mp"),
            P(),
            P(),
            P(None, "mp"),
            P(),
            P(None, "mp"),
            P(None, "mp"),
            P(None, "mp"),
            P(("dp", "mp"), None),
        ),
        out_specs=(
            P(("dp", "mp"), None),
            P(("dp", "mp"), None, None),
            P(),
            P(),
            P(None, "mp"),
            P(None, "mp"),
            P(None, "mp"),
            P(None, "mp"),
            P(),
            P(),
            P(None, "mp"),
            P(None, "mp"),
            P(None, "mp"),
            P("mp"),
        ),
        check_vma=False,
    )
```

```python
from functools import partial
import math

import jax
import jax.numpy as jnp
from jax import lax
from jax.experimental import pallas as pl
from jax.experimental.pallas import tpu as pltpu
from jax.sharding import PartitionSpec as P

HD = 64
QHEADS = 32
KVHEADS = 4
FHD = 64


def layer_norm(values, norm_gain, norm_shift):
    average = jnp.mean(values, axis=-1, keepdims=True)
    centred = values - average
    variance = jnp.mean(centred * centred, axis=-1, keepdims=True)
    return centred * lax.rsqrt(variance + 1e-05) * norm_gain + norm_shift


def rms_norm(values, norm_gain):
    return values * lax.rsqrt(jnp.mean(values * values, axis=-1, keepdims=True) + 1e-05) * norm_gain


def swiglu(gate_pre, up_pre):
    return jax.nn.silu(gate_pre) * up_pre


def rope_tables(length, head_size):
    positions = jnp.arange(length, dtype=jnp.float32)
    inverse_rates = jnp.exp(
        jnp.arange(head_size // 2, dtype=jnp.float32) * (-2.0 * math.log(10000.0) / head_size)
    )
    angles = positions[:, None] * inverse_rates[None, :]
    angles = jnp.concatenate([angles, angles], axis=-1)
    return (jnp.cos(angles)[:, None, :], jnp.sin(angles)[:, None, :])


def rotate(values, cosine_table, sine_table):
    half_size = values.shape[-1] // 2
    turned = jnp.concatenate([-values[..., half_size:], values[..., :half_size]], axis=-1)
    return values * cosine_table + turned * sine_table


def pool_rows(values, valid_mask, row_counts):
    return (
        jnp.sum(values * valid_mask[:, :, None], axis=1) / row_counts.astype(jnp.float32)[:, None]
    )


def place_rows(block_rows, first_row, total_rows):
    zero_rows = jnp.zeros((total_rows, block_rows.shape[1]), jnp.float32)
    return lax.dynamic_update_slice(zero_rows, block_rows, (first_row, first_row * 0))


def hyper_rows(values):
    return lax.all_gather(values, "mp", axis=0, tiled=True)


def hyper_sums(values):
    return lax.psum_scatter(
        values.astype(jnp.bfloat16), "mp", scatter_dimension=0, tiled=True
    ).astype(jnp.float32)


def text_rows(values):
    return lax.all_gather(values, "mp", axis=0, tiled=True)


def text_sums(values):
    return lax.psum_scatter(
        values.astype(jnp.bfloat16), "mp", scatter_dimension=0, tiled=True
    ).astype(jnp.float32)


def group_total(values):
    return lax.psum(values.astype(jnp.bfloat16), "mp").astype(jnp.float32)


def masked_scores(query_block, key_row, query_segments, key_segments, query_first, score_scale):
    raw_scores = (
        jnp.einsum("qhd,kd->hqk", query_block, key_row, preferred_element_type=jnp.float32)
        * score_scale
    )
    query_spots = query_first + jnp.arange(query_block.shape[0])
    key_spots = jnp.arange(key_row.shape[0])
    allowed = (key_spots[None, :] <= query_spots[:, None]) & (
        key_segments[None, :] == query_segments[:, None]
    )
    return jnp.where(allowed[None], raw_scores, -1e30)


def attend_forward(
    query_block, key_row, value_row, query_segments, key_segments, query_first, score_scale
):
    scores = masked_scores(
        query_block, key_row, query_segments, key_segments, query_first, score_scale
    )
    top_score = jnp.max(scores, axis=-1, keepdims=True)
    log_total = top_score + jnp.log(jnp.sum(jnp.exp(scores - top_score), axis=-1, keepdims=True))
    weights = jnp.exp(scores - log_total).astype(jnp.bfloat16)
    attended = jnp.einsum("hqk,kd->qhd", weights, value_row, preferred_element_type=jnp.float32)
    return (attended.astype(jnp.bfloat16), log_total)


MESH = pl.DeviceIdType.MESH
F32 = jnp.float32
BF16 = jnp.bfloat16
CHUNKS = 4
FAR = -1e30


def dot_nn(a, b):
    return lax.dot_general(a, b, (((1,), (0,)), ((), ())), preferred_element_type=F32)


def dot_nt(a, b):
    return lax.dot_general(a, b, (((1,), (1,)), ((), ())), preferred_element_type=F32)


def column_tiles(total, width, body):
    full = total // width
    if full > 0:

        @pl.loop(0, full)
        def _(t):
            body(pl.ds(pl.multiple_of(t * width, width), width))

    if total % width:
        body(pl.ds(full * width, total % width))


def rms_scale(values):
    return lax.rsqrt(jnp.mean(values * values, axis=-1, keepdims=True) + 1e-05)


def rms_back(values, grad, gain):
    scale = rms_scale(values)
    scaled = grad * gain
    return scale * (
        scaled - values * (scale * scale) * jnp.mean(scaled * values, axis=-1, keepdims=True)
    )


class Exchange:
    def __init__(self, chips, chip, core, group_axis):
        self.chips, self.chip, self.core = chips, chip, core
        self.axis = group_axis

    def sibling(self):
        return {self.axis: self.chip * 2 + 1 - self.core}

    def peer(self, other):
        return {self.axis: other * 2 + self.core}

    def others(self):
        return [lax.rem(self.chip + step, self.chips) for step in range(1, self.chips)]

    def barrier(self):
        flag = pltpu.get_barrier_semaphore()
        pl.semaphore_signal(flag, inc=1, device_id=self.sibling(), device_id_type=MESH)
        for other in self.others():
            pl.semaphore_signal(flag, inc=1, device_id=self.peer(other), device_id_type=MESH)
        pl.semaphore_wait(flag, self.chips)

    def to_sibling(self, source, target, send, recv):
        return pltpu.make_async_remote_copy(
            src_ref=source,
            dst_ref=target,
            send_sem=send,
            recv_sem=recv,
            device_id=self.sibling(),
            device_id_type=MESH,
        )

    def to_peer(self, other, source, target, send, recv):
        return pltpu.make_async_remote_copy(
            src_ref=source,
            dst_ref=target,
            send_sem=send,
            recv_sem=recv,
            device_id=self.peer(other),
            device_id_type=MESH,
        )


class Scatter:
    def __init__(self, net, part, near, far, sems):
        self.net, self.part, self.near, self.far = net, part, near, far
        self.near_send, self.near_recv, self.far_send, self.far_recv = sems

    def near_copy(self, i):
        net = self.net
        return net.to_sibling(
            self.part.at[i, 1 - net.core],
            self.near.at[i],
            self.near_send.at[i],
            self.near_recv.at[i],
        )

    def far_copy(self, i, other):
        net = self.net
        return net.to_peer(
            other,
            self.part.at[i, net.core, other],
            self.far.at[i, net.chip],
            self.far_send.at[i, other],
            self.far_recv.at[i, net.chip],
        )

    def far_landing(self, i, other):
        net = self.net
        return net.to_peer(
            other,
            self.part.at[i, net.core, other],
            self.far.at[i, other],
            self.far_send.at[i, other],
            self.far_recv.at[i, other],
        )

    def start(self, i):
        self.near_copy(i).start()

    def middle(self, i):
        net = self.net
        self.near_copy(i).wait_recv()
        for other in net.others():
            total = self.part[i, net.core, other].astype(F32) + self.near[i, other].astype(F32)
            self.part[i, net.core, other] = total.astype(BF16)
            self.far_copy(i, other).start()

    def finish(self, i):
        net = self.net
        total = self.part[i, net.core, net.chip].astype(F32) + self.near[i, net.chip].astype(F32)
        for other in net.others():
            self.far_landing(i, other).wait_recv()
            total = total + self.far[i, other].astype(F32)
        return total

    def sent(self, i):
        self.near_copy(i).wait_send()
        for other in self.net.others():
            self.far_copy(i, other).wait_send()


class Gather:
    def __init__(self, net, full, sems):
        self.net, self.full = net, full
        self.far_send, self.far_recv, self.near_send, self.near_recv = sems

    def far_copy(self, i, other):
        net = self.net
        block = self.full.at[i, net.core, net.chip]
        return net.to_peer(
            other, block, block, self.far_send.at[i, other], self.far_recv.at[i, net.chip]
        )

    def far_landing(self, i, other):
        net = self.net
        block = self.full.at[i, net.core, other]
        return net.to_peer(
            other, block, block, self.far_send.at[i, other], self.far_recv.at[i, other]
        )

    def near_copy(self, i):
        block = self.full.at[i, self.net.core]
        return self.net.to_sibling(block, block, self.near_send.at[i], self.near_recv.at[i])

    def near_landing(self, i):
        block = self.full.at[i, 1 - self.net.core]
        return self.net.to_sibling(block, block, self.near_send.at[i], self.near_recv.at[i])

    def start(self, i):
        for other in self.net.others():
            self.far_copy(i, other).start()

    def middle(self, i):
        for other in self.net.others():
            self.far_landing(i, other).wait_recv()
        self.near_copy(i).start()

    def finish(self, i):
        self.near_landing(i).wait_recv()

    def sent(self, i):
        for other in self.net.others():
            self.far_copy(i, other).wait_send()
        self.near_copy(i).wait_send()


def text_body(
    chips,
    head_count,
    embeds_own,
    grad_own,
    grad_full,
    q_t,
    q_n,
    k_n,
    v_n,
    k_t,
    v_t,
    seg_q,
    seg_k,
    cos_t,
    sin_t,
    gain_one,
    gain_two,
    w_kv,
    w_query_hbm,
    w_out_hbm,
    w_gate_hbm,
    w_up_hbm,
    w_down_hbm,
    out_part,
    embed_grad,
    w_query,
    w_out,
    w_gate,
    w_up,
    w_down,
    part_a,
    near_a,
    far_a,
    part_b,
    near_b,
    far_b,
    full,
    out_t,
    logs,
    bias,
    residual,
    residual_grad,
    grad_chunk,
    mixed,
    gate_grad,
    up_grad,
    out_tile,
    out_stage,
    d_out_t,
    d_out_n,
    d_query_t,
    value_even,
    value_odd,
    key_even,
    key_odd,
    weight_sem,
    grad_sem,
    stage_sem,
    scatter_near,
    scatter_far_send,
    scatter_far_recv,
    gather_near,
    gather_far_send,
    gather_far_recv,
):
    me = lax.axis_index("mp")
    chip, core = me // 2, lax.rem(me, 2)
    net = Exchange(chips, chip, core, "mp")
    chunk_rows = q_n.shape[1]
    width = embeds_own.shape[2]
    units = w_gate.shape[1]
    head_width = FHD * head_count
    own_rows = embeds_own.shape[1]
    first_own = (core * chips + chip) * own_rows

    def scatter_of(kind, part, near, far):
        return Scatter(
            net,
            part,
            near,
            far,
            (
                scatter_near.at[kind, 0],
                scatter_near.at[kind, 1],
                scatter_far_send.at[kind],
                scatter_far_recv.at[kind],
            ),
        )

    def gather_of(kind):
        return Gather(
            net,
            full,
            (
                gather_far_send.at[kind],
                gather_far_recv.at[kind],
                gather_near.at[kind, 0],
                gather_near.at[kind, 1],
            ),
        )

    attn_sum = scatter_of(0, part_a, near_a, far_a)
    mlp_sum = scatter_of(1, part_b, near_b, far_b)
    normed_sum = scatter_of(2, part_a, near_a, far_a)
    mlp_rows = gather_of(0)
    back_rows = gather_of(1)

    weights = [
        pltpu.make_async_copy(source, target, weight_sem.at[k])
        for k, (source, target) in enumerate(
            (
                (w_out_hbm, w_out),
                (w_gate_hbm, w_gate),
                (w_up_hbm, w_up),
                (w_down_hbm, w_down),
                (w_query_hbm, w_query),
            )
        )
    ]
    for copy in weights:
        copy.start()

    def grad_copy(i):
        return pltpu.make_async_copy(grad_full.at[i], grad_chunk, grad_sem)

    def stage_copy(i):
        return pltpu.make_async_copy(out_stage, out_part.at[i], stage_sem)

    grad_copy(CHUNKS - 1).start()
    net.barrier()
    for ref in (value_even, value_odd, key_even, key_odd):
        ref[...] = jnp.zeros_like(ref)

    def put_rows(part, i, columns, values):
        half = chunk_rows // 2
        for k in range(2):
            for j in range(chips):
                first = k * half + j * own_rows
                part[i, k, j, :, columns] = values[first : first + own_rows].astype(BF16)

    def rows_of(ref, i):
        return ref[i].reshape(chunk_rows, width)

    def make_bias(i):
        query_spots = i * chunk_rows + lax.broadcasted_iota(jnp.int32, (chunk_rows, chunk_rows), 1)
        query_segments = seg_q[i]

        for kb in range(CHUNKS):

            @pl.when(kb <= i)
            def _():
                key_spots = kb * chunk_rows + lax.broadcasted_iota(
                    jnp.int32, (chunk_rows, chunk_rows), 0
                )
                allowed = (key_spots <= query_spots) & (seg_k[kb] == query_segments)
                bias[kb] = jnp.where(allowed, 0.0, FAR)

    def head_span(h):
        return pl.ds(pl.multiple_of(h * FHD, FHD), FHD)

    def attend(i, key_blocks):
        @pl.loop(0, head_count)
        def _(h):
            query = q_t[i, head_span(h), :]
            scores = [dot_nn(k_n[kb], query) + bias[kb] for kb in range(key_blocks)]
            top = jnp.max(scores[0], axis=0, keepdims=True)
            for block in scores[1:]:
                top = jnp.maximum(top, jnp.max(block, axis=0, keepdims=True))
            total = jnp.zeros_like(top)
            attended = jnp.zeros((FHD, chunk_rows), F32)
            for kb in range(key_blocks):
                weights_block = jnp.exp(scores[kb] - top)
                total = total + jnp.sum(weights_block, axis=0, keepdims=True)
                attended = attended + dot_nn(v_t[kb], weights_block.astype(BF16))
            logs[i, h] = top + jnp.log(total)
            out_t[i, head_span(h), :] = (attended / total).astype(BF16)

    def attend_back(i, key_blocks):
        cosine, sine = cos_t[i], sin_t[i]

        @pl.loop(0, head_count // 2)
        def _(pair):
            pair_span = pl.ds(pl.multiple_of(pair * 2 * FHD, 2 * FHD), 2 * FHD)
            query_pair = q_n[i, :, pair_span]
            grad_pair = d_out_n[:, pair_span]
            for odd in range(2):
                h = pair * 2 + odd
                query = q_t[i, head_span(h), :]
                grad = d_out_t[head_span(h), :]
                log_row = logs[i, h]
                grad_f = grad.astype(F32)
                centre = jnp.sum(
                    grad_f * out_t[i, head_span(h), :].astype(F32), axis=0, keepdims=True
                )
                value_total = value_odd if odd else value_even
                key_total = key_odd if odd else key_even
                query_grad = jnp.zeros((FHD, chunk_rows), F32)
                for kb in range(key_blocks):
                    probs = jnp.exp(dot_nn(k_n[kb], query) + bias[kb] - log_row)
                    value_total[kb] += dot_nn(probs.astype(BF16), grad_pair)
                    score_grad = (probs * (dot_nn(v_n[kb], grad) - centre)).astype(BF16)
                    key_total[kb] += dot_nn(score_grad, query_pair)
                    query_grad = query_grad + dot_nn(k_t[kb], score_grad)
                query_grad = query_grad * (FHD**-0.5)
                low_half, high_half = query_grad[: FHD // 2], query_grad[FHD // 2 :]
                d_query_t[head_span(h), :] = jnp.concatenate(
                    [low_half * cosine + high_half * sine, high_half * cosine - low_half * sine],
                    axis=0,
                ).astype(BF16)

    def each_length(i, body):
        for blocks in range(1, CHUNKS + 1):

            @pl.when(i == blocks - 1)
            def _():
                body(i, blocks)

    def stage_attend(i, first):
        make_bias(i)
        each_length(i, attend)

        @pl.when(first)
        def _():
            weights[0].wait()

        attended = out_t[i].T

        def tile(columns):
            put_rows(part_a, i, columns, dot_nt(attended, w_out[columns, :]))

        column_tiles(width, 512, tile)
        attn_sum.start(i)

    def stage_norm(i):
        values = embeds_own[i].astype(F32) + attn_sum.finish(i)
        residual[i] = values
        full[i, core, chip] = (values * rms_scale(values) * gain_two[...]).astype(BF16)
        mlp_rows.start(i)

    def stage_mlp(i, first, last):
        @pl.when(first)
        def _():
            for k in (1, 2, 3):
                weights[k].wait()

        mlp_rows.finish(i)
        grad_copy(i).wait()

        def unit_tile(columns):
            rows = rows_of(full, i)
            gate_pre = dot_nn(rows, w_gate[:, columns])
            up_pre = dot_nn(rows, w_up[:, columns])
            act_grad = dot_nn(grad_chunk[...], w_down[:, columns])
            inverse = 1.0 / (1.0 + jnp.exp(-gate_pre))
            silu = gate_pre * inverse
            mixed[:, columns] = (silu * up_pre).astype(BF16)
            up_grad[:, columns] = (act_grad * silu).astype(BF16)
            slope = inverse * (1.0 + gate_pre * (1.0 - inverse))
            gate_grad[:, columns] = (act_grad * up_pre * slope).astype(BF16)

        column_tiles(units, 256, unit_tile)

        def grad_tile(columns):
            put_rows(
                part_b,
                i,
                columns,
                dot_nt(gate_grad[...], w_gate[columns, :])
                + dot_nt(up_grad[...], w_up[columns, :]),
            )

        column_tiles(width, 512, grad_tile)
        mlp_rows.sent(i)
        mlp_sum.start(i)

        @pl.when(jnp.logical_not(last))
        def _():
            grad_copy(i - 1).start()

        @pl.when(jnp.logical_not(first))
        def _():
            stage_copy(i + 1).wait()

        def out_columns(columns):
            out_tile[...] = dot_nt(mixed[...], w_down[columns, :])
            own = pl.ds(pl.multiple_of(first_own, own_rows), own_rows)
            out_tile[own, :] += residual[i, :, columns]
            out_stage[:, columns] = out_tile[...].astype(BF16)

        column_tiles(width, 512, out_columns)
        stage_copy(i).start()

    def stage_residual_grad(i):
        grad = mlp_sum.finish(i)
        values = grad_own[i].astype(F32) + rms_back(residual[i], grad, gain_two[...])
        residual_grad[i] = values
        full[i, core, chip] = values.astype(BF16)
        back_rows.start(i)

    def stage_attend_back(i, first):
        back_rows.finish(i)
        attended_grad = dot_nn(rows_of(full, i), w_out[...]).astype(BF16)
        d_out_n[...] = attended_grad
        d_out_t[...] = attended_grad.T
        make_bias(i)
        each_length(i, attend_back)

        @pl.when(first)
        def _():
            weights[4].wait()

        attn_sum.sent(i)
        key_grad = (key_even[i][:, :FHD] + key_odd[i][:, FHD:]).T
        cosine, sine = cos_t[i], sin_t[i]
        low_half, high_half = key_grad[: FHD // 2], key_grad[FHD // 2 :]
        value_grad = (value_even[i][:, :FHD] + value_odd[i][:, FHD:]).T
        both = jnp.concatenate(
            [low_half * cosine + high_half * sine, high_half * cosine - low_half * sine, value_grad],
            axis=0,
        )
        both_rows = both.T.astype(BF16)
        query_rows = d_query_t[...].T

        def tile(columns):
            put_rows(
                part_a,
                i,
                columns,
                dot_nt(query_rows, w_query[columns, :]) + dot_nt(both_rows, w_kv[columns, :]),
            )

        column_tiles(width, 512, tile)
        normed_sum.start(i)

    def stage_embed_grad(i):
        grad = normed_sum.finish(i)
        values = residual_grad[i] + rms_back(embeds_own[i].astype(F32), grad, gain_one[...])
        embed_grad[i] = values.astype(BF16)

    def at(step, offset, body):
        turn = step - offset

        @pl.when((turn >= 0) & (turn < CHUNKS))
        def _():
            body(CHUNKS - 1 - turn)

    @pl.loop(0, CHUNKS + 3)
    def _(step):
        last = CHUNKS - 1
        at(step, 1, stage_norm)
        at(step, 0, lambda i: stage_attend(i, i == last))
        at(step, 2, mlp_sum.middle)
        at(step, 3, lambda i: stage_attend_back(i, i == last))
        at(step, 1, mlp_rows.middle)
        at(step, 0, attn_sum.middle)
        at(step, 2, stage_residual_grad)
        at(step, 3, normed_sum.middle)
        at(step, 1, lambda i: stage_mlp(i, i == last, i == 0))
        at(step, 2, back_rows.middle)

    @pl.loop(0, CHUNKS)
    def _(turn):
        i = CHUNKS - 1 - turn
        stage_embed_grad(i)
        normed_sum.sent(i)
        mlp_sum.sent(i)
        back_rows.sent(i)

    stage_copy(0).wait()


def text_layer(
    group,
    embeds_own,
    grad_own,
    grad_full,
    q_t,
    q_n,
    k_n,
    v_n,
    k_t,
    v_t,
    seg_q,
    seg_k,
    cos_t,
    sin_t,
    gain_one,
    gain_two,
    w_kv,
    w_query,
    w_out,
    w_gate,
    w_up,
    w_down,
):
    chips = group // 2
    chunks, chunk_rows, head_width = q_n.shape
    own_rows, width = embeds_own.shape[1:]
    head_count = head_width // FHD
    units = w_gate.shape[1]
    vmem = pl.BlockSpec(memory_space=pltpu.VMEM)
    hbm = pl.BlockSpec(memory_space=pl.ANY)
    blocks = (chunks, 2, chips, own_rows, width)
    landing = (chunks, chips, own_rows, width)
    return pl.pallas_call(
        partial(text_body, chips, head_count),
        out_shape=(
            jax.ShapeDtypeStruct((chunks, chunk_rows, width), BF16),
            jax.ShapeDtypeStruct((chunks, own_rows, width), BF16),
        ),
        in_specs=[vmem, vmem, hbm] + [vmem] * 13 + [hbm] * 5,
        out_specs=(hbm, vmem),
        scratch_shapes=[
            pltpu.VMEM(w_query.shape, BF16),
            pltpu.VMEM(w_out.shape, BF16),
            pltpu.VMEM(w_gate.shape, BF16),
            pltpu.VMEM(w_up.shape, BF16),
            pltpu.VMEM(w_down.shape, BF16),
            pltpu.VMEM(blocks, BF16),
            pltpu.VMEM(landing, BF16),
            pltpu.VMEM(landing, BF16),
            pltpu.VMEM(blocks, BF16),
            pltpu.VMEM(landing, BF16),
            pltpu.VMEM(landing, BF16),
            pltpu.VMEM(blocks, BF16),
            pltpu.VMEM((chunks, head_width, chunk_rows), BF16),
            pltpu.VMEM((chunks, head_count, 1, chunk_rows), F32),
            pltpu.VMEM((chunks, chunk_rows, chunk_rows), F32),
            pltpu.VMEM((chunks, own_rows, width), F32),
            pltpu.VMEM((chunks, own_rows, width), F32),
            pltpu.VMEM((chunk_rows, width), BF16),
            pltpu.VMEM((chunk_rows, units), BF16),
            pltpu.VMEM((chunk_rows, units), BF16),
            pltpu.VMEM((chunk_rows, units), BF16),
            pltpu.VMEM((chunk_rows, 512), F32),
            pltpu.VMEM((chunk_rows, width), BF16),
            pltpu.VMEM((head_width, chunk_rows), BF16),
            pltpu.VMEM((chunk_rows, head_width), BF16),
            pltpu.VMEM((head_width, chunk_rows), BF16),
        ]
        + [pltpu.VMEM((chunks, chunk_rows, 2 * FHD), F32)] * 4
        + [
            pltpu.SemaphoreType.DMA((5,)),
            pltpu.SemaphoreType.DMA,
            pltpu.SemaphoreType.DMA,
            pltpu.SemaphoreType.DMA((3, 2, chunks)),
            pltpu.SemaphoreType.DMA((3, chunks, chips)),
            pltpu.SemaphoreType.DMA((3, chunks, chips)),
            pltpu.SemaphoreType.DMA((2, 2, chunks)),
            pltpu.SemaphoreType.DMA((2, chunks, chips)),
            pltpu.SemaphoreType.DMA((2, chunks, chips)),
        ],
        compiler_params=pltpu.CompilerParams(
            collective_id=0, has_side_effects=True, vmem_limit_bytes=63 * 1024 * 1024
        ),
        cost_estimate=pl.CostEstimate(
            flops=80 * 10**9, bytes_accessed=40 * 10**6, transcendentals=20 * 10**6
        ),
    )(
        embeds_own,
        grad_own,
        grad_full,
        q_t,
        q_n,
        k_n,
        v_n,
        k_t,
        v_t,
        seg_q,
        seg_k,
        cos_t,
        sin_t,
        gain_one,
        gain_two,
        w_kv,
        w_query,
        w_out,
        w_gate,
        w_up,
        w_down,
    )


def on_device(
    pieces,
    counts,
    entry_ids,
    segment_ids,
    norm1_gain,
    norm1_shift,
    query_weight,
    key_weight,
    value_weight,
    out_weight,
    norm2_gain,
    norm2_shift,
    up_weight,
    down_weight,
    proj_weight,
    proj_bias,
    text_norm1_gain,
    text_query,
    text_key,
    text_value,
    text_out_proj,
    text_norm2_gain,
    text_gate,
    text_up,
    text_down,
    token_grad,
):
    local_count, slot_count, feature_count = pieces.shape
    group_count = counts.shape[0]
    score_scale = HD ** (-0.5)
    own_start = lax.axis_index("mp") * local_count
    own_counts = lax.dynamic_slice_in_dim(counts, own_start, local_count)
    slot_index = jnp.arange(slot_count)
    own_mask = (slot_index[None, :] < own_counts[:, None]).astype(jnp.float32)
    rows_mask = (slot_index[None, :] < counts[:, None]).astype(jnp.float32)
    pieces_f = pieces.astype(jnp.float32)
    normed_one, norm_one_back = jax.vjp(layer_norm, pieces_f, norm1_gain, norm1_shift)
    attn_in = hyper_rows(normed_one.astype(jnp.bfloat16))
    row_total = attn_in.shape[0]
    head_count = query_weight.shape[1] // HD

    def heads_of(weight):
        projected = jnp.einsum("esw,wf->esf", attn_in, weight, preferred_element_type=jnp.float32)
        return projected.astype(jnp.bfloat16).reshape(row_total, slot_count, head_count, HD)

    def merge_heads(head_rows):
        return head_rows.reshape(row_total, slot_count, head_count * HD)

    queries = heads_of(query_weight)
    key_rows = heads_of(key_weight)
    value_rows = heads_of(value_weight)

    def scores_of():
        raw_scores = (
            jnp.einsum("eshd,ethd->ehst", queries, key_rows, preferred_element_type=jnp.float32)
            * score_scale
        )
        return jnp.where(rows_mask[:, None, None, :] > 0.5, raw_scores, -1e30)

    scores = scores_of()
    top_score = jnp.max(scores, axis=-1, keepdims=True)
    log_total = top_score + jnp.log(jnp.sum(jnp.exp(scores - top_score), axis=-1, keepdims=True))
    softmax_low = jnp.exp(scores - log_total).astype(jnp.bfloat16)
    attended = jnp.einsum(
        "ehst,ethd->eshd", softmax_low, value_rows, preferred_element_type=jnp.float32
    )
    attended = merge_heads(attended.astype(jnp.bfloat16))
    attn_part = jnp.einsum("esf,wf->esw", attended, out_weight, preferred_element_type=jnp.float32)
    residual = pieces_f + hyper_sums(attn_part)
    normed_two, norm_two_back = jax.vjp(layer_norm, residual, norm2_gain, norm2_shift)
    ffn_in = hyper_rows(normed_two.astype(jnp.bfloat16))
    hidden_pre = jnp.einsum("esw,wf->esf", ffn_in, up_weight, preferred_element_type=jnp.float32)
    hidden_act, gelu_back = jax.vjp(jax.nn.gelu, hidden_pre)
    hidden_low = hidden_act.astype(jnp.bfloat16)
    ffn_part = jnp.einsum(
        "esf,wf->esw", hidden_low, down_weight, preferred_element_type=jnp.float32
    )
    pooled_terms = pool_rows(ffn_part, rows_mask, counts)
    pooled_terms = pooled_terms + place_rows(
        pool_rows(residual, own_mask, own_counts), own_start, group_count
    )
    pooled = group_total(pooled_terms)
    pooled_low = pooled.astype(jnp.bfloat16)
    entries_low = lax.all_gather(pooled_low, "dp", axis=0, tiled=True)
    proj_full = lax.all_gather(proj_weight, "mp", axis=1, tiled=True)
    bias_full = lax.all_gather(proj_bias, "mp", axis=0, tiled=True)
    entry_total = entries_low.shape[0]
    chosen = (entry_ids[:, None] == jnp.arange(entry_total)[None, :]).astype(jnp.bfloat16)
    token_pooled = jnp.dot(chosen, entries_low, preferred_element_type=jnp.float32).astype(
        jnp.bfloat16
    )
    text_full = (
        jnp.dot(token_pooled, proj_full, preferred_element_type=jnp.float32) + bias_full
    ).astype(jnp.bfloat16)
    group = lax.axis_size("mp")
    length, text_width = text_full.shape
    chunk_rows = length // CHUNKS
    own_rows = chunk_rows // group
    me = lax.axis_index("mp")
    own_block = lax.rem(me, 2) * (group // 2) + me // 2

    def own_of(values):
        split = values.reshape(CHUNKS, group, own_rows, text_width)
        return lax.dynamic_index_in_dim(split, own_block, 1, keepdims=False)

    head_width = text_query.shape[1]
    local_heads = head_width // FHD
    kv_index = me * local_heads // (QHEADS // KVHEADS)
    key_local = lax.dynamic_slice_in_dim(text_key, kv_index * FHD, FHD, 1)
    value_local = lax.dynamic_slice_in_dim(text_value, kv_index * FHD, FHD, 1)
    inputs_f = text_full.astype(jnp.float32)
    text_normed = rms_norm(inputs_f, text_norm1_gain).astype(jnp.bfloat16)
    positions = jnp.arange(length, dtype=jnp.float32)
    inverse_rates = jnp.exp(
        jnp.arange(FHD // 2, dtype=jnp.float32) * (-2.0 * math.log(10000.0) / FHD)
    )
    angles = inverse_rates[:, None] * positions[None, :]
    cosine, sine = jnp.cos(angles), jnp.sin(angles)

    def projected_t(weight):
        return lax.dot_general(
            weight, text_normed, (((0,), (1,)), ((), ())), preferred_element_type=jnp.float32
        )

    def turned(values):
        split = values.reshape(-1, 2, FHD // 2, length)
        low_half, high_half = split[:, 0], split[:, 1]
        both = jnp.stack(
            [low_half * cosine - high_half * sine, high_half * cosine + low_half * sine], axis=1
        )
        return both.reshape(values.shape)

    def columns_of(values):
        return values.reshape(values.shape[0], CHUNKS, chunk_rows).transpose(1, 0, 2)

    def rows_of(values):
        return values.reshape(values.shape[0], CHUNKS, chunk_rows).transpose(1, 2, 0)

    query_t = (turned(projected_t(text_query)).astype(jnp.bfloat16) * FHD**-0.5).astype(
        jnp.bfloat16
    )
    key_t = turned(projected_t(key_local)).astype(jnp.bfloat16)
    value_t = projected_t(value_local).astype(jnp.bfloat16)
    token_grads = text_rows(token_grad).reshape(CHUNKS, chunk_rows, text_width)
    segments = segment_ids[0]
    out_part, embed_rows = text_layer(
        group,
        own_of(text_full),
        own_of(token_grads),
        token_grads,
        columns_of(query_t),
        rows_of(query_t),
        rows_of(key_t),
        rows_of(value_t),
        columns_of(key_t),
        columns_of(value_t),
        segments.reshape(CHUNKS, 1, chunk_rows),
        segments.reshape(CHUNKS, chunk_rows, 1),
        columns_of(cosine),
        columns_of(sine),
        text_norm1_gain[None, :],
        text_norm2_gain[None, :],
        jnp.concatenate([key_local, value_local], axis=1),
        text_query,
        text_out_proj,
        text_gate,
        text_up,
        text_down,
    )
    text_out = text_sums(out_part.reshape(length, text_width))
    embed_rows = embed_rows.reshape(CHUNKS * own_rows, text_width)
    embed_low = embed_rows.astype(jnp.bfloat16)
    pooled_tokens = text_rows(
        jnp.einsum("to,wo->tw", embed_low, proj_full, preferred_element_type=jnp.float32).astype(
            jnp.bfloat16
        )
    )
    share = pooled_tokens.shape[1] // lax.axis_size("mp")
    def by_owner(values):
        split = values.reshape((CHUNKS, 2, group // 2, own_rows) + values.shape[1:])
        return jnp.transpose(split, (2, 1, 0, 3) + tuple(range(4, split.ndim))).reshape(
            values.shape
        )

    owner_entries = by_owner(entry_ids)
    owner_chosen = (owner_entries[:, None] == jnp.arange(entry_total)[None, :]).astype(
        jnp.bfloat16
    )
    owner_pooled = by_owner(token_pooled)
    pooled_share = lax.dynamic_slice_in_dim(
        pooled_tokens, lax.axis_index("mp") * share, share, 1
    )
    entry_part = jnp.einsum(
        "te,tw->ew", owner_chosen, pooled_share, preferred_element_type=jnp.float32
    ).astype(jnp.bfloat16)
    pooled_own = lax.psum_scatter(entry_part, "dp", scatter_dimension=0, tiled=True)
    pooled_grad = lax.all_gather(pooled_own, "mp", axis=1, tiled=True).astype(jnp.float32)
    embed_grad = lax.all_to_all(embed_low, "mp", split_axis=1, concat_axis=0, tiled=True)
    proj_bias_grad = jnp.sum(embed_grad.astype(jnp.float32), axis=0)
    proj_grad = jnp.einsum(
        "tw,to->wo", owner_pooled, embed_grad, preferred_element_type=jnp.float32
    )
    rows_share = pooled_grad / counts.astype(jnp.float32)[:, None]
    out_grad_rows = (rows_mask[:, :, None] * rows_share[:, None, :]).astype(jnp.bfloat16)
    down_grad = jnp.einsum(
        "esw,esf->wf", out_grad_rows, hidden_low, preferred_element_type=jnp.float32
    )
    act_grad = jnp.einsum(
        "esw,wf->esf", out_grad_rows, down_weight, preferred_element_type=jnp.float32
    )
    pre_grad = gelu_back(act_grad)[0].astype(jnp.bfloat16)
    up_grad = jnp.einsum("esw,esf->wf", ffn_in, pre_grad, preferred_element_type=jnp.float32)
    normed_two_grad = hyper_sums(
        jnp.einsum("esf,wf->esw", pre_grad, up_weight, preferred_element_type=jnp.float32)
    )
    residual_norm, gain_two, shift_two = norm_two_back(normed_two_grad)
    own_share = (
        lax.dynamic_slice_in_dim(pooled_grad, own_start, local_count)
        / own_counts.astype(jnp.float32)[:, None]
    )
    residual_grad = own_mask[:, :, None] * own_share[:, None, :] + residual_norm
    attn_grad = hyper_rows(residual_grad.astype(jnp.bfloat16))
    out_grad = jnp.einsum("esw,esf->wf", attn_grad, attended, preferred_element_type=jnp.float32)
    attended_grad = jnp.einsum(
        "esw,wf->esf", attn_grad, out_weight, preferred_element_type=jnp.float32
    )
    attended_grad = attended_grad.astype(jnp.bfloat16).reshape(
        row_total, slot_count, head_count, HD
    )
    softmax_f = jnp.exp(scores_of() - log_total)
    softmax_again = softmax_f.astype(jnp.bfloat16)
    prob_grad = jnp.einsum(
        "eshd,ethd->ehst", attended_grad, value_rows, preferred_element_type=jnp.float32
    )
    value_grad_rows = jnp.einsum(
        "ehst,eshd->ethd", softmax_again, attended_grad, preferred_element_type=jnp.float32
    ).astype(jnp.bfloat16)
    score_grad = softmax_f * (prob_grad - jnp.sum(softmax_f * prob_grad, axis=-1, keepdims=True))
    score_grad = score_grad.astype(jnp.bfloat16)
    query_grad_rows = (
        jnp.einsum("ehst,ethd->eshd", score_grad, key_rows, preferred_element_type=jnp.float32)
        * score_scale
    ).astype(jnp.bfloat16)
    key_grad_rows = (
        jnp.einsum("ehst,eshd->ethd", score_grad, queries, preferred_element_type=jnp.float32)
        * score_scale
    ).astype(jnp.bfloat16)
    query_flat = merge_heads(query_grad_rows)
    key_flat = merge_heads(key_grad_rows)
    value_flat = merge_heads(value_grad_rows)
    query_grad = jnp.einsum("esw,esf->wf", attn_in, query_flat, preferred_element_type=jnp.float32)
    key_grad = jnp.einsum("esw,esf->wf", attn_in, key_flat, preferred_element_type=jnp.float32)
    value_grad = jnp.einsum("esw,esf->wf", attn_in, value_flat, preferred_element_type=jnp.float32)
    normed_one_part = jnp.einsum(
        "esf,wf->esw", query_flat, query_weight, preferred_element_type=jnp.float32
    )
    normed_one_part = normed_one_part + jnp.einsum(
        "esf,wf->esw", key_flat, key_weight, preferred_element_type=jnp.float32
    )
    normed_one_part = normed_one_part + jnp.einsum(
        "esf,wf->esw", value_flat, value_weight, preferred_element_type=jnp.float32
    )
    normed_one_grad = hyper_sums(normed_one_part)
    pieces_norm, gain_one, shift_one = norm_one_back(normed_one_grad)
    pieces_grad = residual_grad + pieces_norm
    summed = (
        lax.psum(query_grad.astype(jnp.bfloat16), "dp").astype(jnp.float32),
        lax.psum(key_grad.astype(jnp.bfloat16), "dp").astype(jnp.float32),
        lax.psum(value_grad.astype(jnp.bfloat16), "dp").astype(jnp.float32),
        lax.psum(out_grad.astype(jnp.bfloat16), "dp").astype(jnp.float32),
        lax.psum(up_grad.astype(jnp.bfloat16), "dp").astype(jnp.float32),
        lax.psum(down_grad.astype(jnp.bfloat16), "dp").astype(jnp.float32),
        lax.psum(proj_grad.astype(jnp.bfloat16), "dp").astype(jnp.float32),
        lax.psum(proj_bias_grad.astype(jnp.bfloat16), "dp").astype(jnp.float32),
    )
    norm_sums = lax.psum((gain_one, shift_one, gain_two, shift_two), ("dp", "mp"))
    return (
        text_out,
        pieces_grad,
        norm_sums[0],
        norm_sums[1],
        summed[0],
        summed[1],
        summed[2],
        summed[3],
        norm_sums[2],
        norm_sums[3],
        summed[4],
        summed[5],
        summed[6],
        summed[7],
    )


def solution(mesh):
    return jax.shard_map(
        on_device,
        mesh=mesh,
        in_specs=(
            P(("dp", "mp"), None, None),
            P("dp"),
            P("dp"),
            P("dp", None),
            P(),
            P(),
            P(None, "mp"),
            P(None, "mp"),
            P(None, "mp"),
            P(None, "mp"),
            P(),
            P(),
            P(None, "mp"),
            P(None, "mp"),
            P(None, "mp"),
            P("mp"),
            P(),
            P(None, "mp"),
            P(),
            P(),
            P(None, "mp"),
            P(),
            P(None, "mp"),
            P(None, "mp"),
            P(None, "mp"),
            P(("dp", "mp"), None),
        ),
        out_specs=(
            P(("dp", "mp"), None),
            P(("dp", "mp"), None, None),
            P(),
            P(),
            P(None, "mp"),
            P(None, "mp"),
            P(None, "mp"),
            P(None, "mp"),
            P(),
            P(),
            P(None, "mp"),
            P(None, "mp"),
            P(None, "mp"),
            P("mp"),
        ),
        check_vma=False,
    )
```

```python
from functools import partial
import math

import jax
import jax.numpy as jnp
import numpy as np
from jax import lax
from jax.experimental import pallas as pl
from jax.experimental.pallas import tpu as pltpu
from jax.sharding import PartitionSpec as P

HD = 64
QHEADS = 32
KVHEADS = 4
FHD = 64


def rope_tables(length):
    positions = np.arange(length, dtype=np.float32)
    rates = np.exp(
        np.arange(FHD // 2, dtype=np.float32) * np.float32(-2.0 * math.log(10000.0) / FHD)
    ).astype(np.float32)
    angles = (positions[None, :] * rates[:, None]).reshape(FHD // 2, CHUNKS, length // CHUNKS)
    angles = angles.transpose(1, 0, 2)
    return jnp.asarray(np.cos(angles)), jnp.asarray(np.sin(angles))


MESH = pl.DeviceIdType.MESH
F32 = jnp.float32
BF16 = jnp.bfloat16
CHUNKS = 4
FAR = -1e30


def dot_nn(a, b):
    return lax.dot_general(a, b, (((1,), (0,)), ((), ())), preferred_element_type=F32)


def dot_nt(a, b):
    return lax.dot_general(a, b, (((1,), (1,)), ((), ())), preferred_element_type=F32)


def column_tiles(total, width, body):
    full = total // width
    if full > 0:

        @pl.loop(0, full)
        def _(t):
            body(pl.ds(pl.multiple_of(t * width, width), width))

    if total % width:
        body(pl.ds(full * width, total % width))


def rms_scale(values):
    return lax.rsqrt(jnp.mean(values * values, axis=-1, keepdims=True) + 1e-05)


def rms_back(values, grad, gain):
    scale = rms_scale(values)
    scaled = grad * gain
    return scale * (
        scaled - values * (scale * scale) * jnp.mean(scaled * values, axis=-1, keepdims=True)
    )


class Exchange:
    def __init__(self, chips, chip, core, group_axis):
        self.chips, self.chip, self.core = chips, chip, core
        self.axis = group_axis

    def sibling(self):
        return {self.axis: self.chip * 2 + 1 - self.core}

    def peer(self, other):
        return {self.axis: other * 2 + self.core}

    def others(self):
        return [lax.rem(self.chip + step, self.chips) for step in range(1, self.chips)]

    def barrier(self):
        flag = pltpu.get_barrier_semaphore()
        pl.semaphore_signal(flag, inc=1, device_id=self.sibling(), device_id_type=MESH)
        for other in self.others():
            pl.semaphore_signal(flag, inc=1, device_id=self.peer(other), device_id_type=MESH)
        pl.semaphore_wait(flag, self.chips)

    def to_sibling(self, source, target, send, recv):
        return pltpu.make_async_remote_copy(
            src_ref=source,
            dst_ref=target,
            send_sem=send,
            recv_sem=recv,
            device_id=self.sibling(),
            device_id_type=MESH,
        )

    def to_peer(self, other, source, target, send, recv):
        return pltpu.make_async_remote_copy(
            src_ref=source,
            dst_ref=target,
            send_sem=send,
            recv_sem=recv,
            device_id=self.peer(other),
            device_id_type=MESH,
        )


class Scatter:
    def __init__(self, net, part, near, far, sems):
        self.net, self.part, self.near, self.far = net, part, near, far
        self.near_send, self.near_recv, self.far_send, self.far_recv = sems

    def near_copy(self, i):
        net = self.net
        return net.to_sibling(
            self.part.at[i, 1 - net.core],
            self.near.at[i],
            self.near_send.at[i],
            self.near_recv.at[i],
        )

    def far_copy(self, i, other):
        net = self.net
        return net.to_peer(
            other,
            self.part.at[i, net.core, other],
            self.far.at[i, net.chip],
            self.far_send.at[i, other],
            self.far_recv.at[i, net.chip],
        )

    def far_landing(self, i, other):
        net = self.net
        return net.to_peer(
            other,
            self.part.at[i, net.core, other],
            self.far.at[i, other],
            self.far_send.at[i, other],
            self.far_recv.at[i, other],
        )

    def start(self, i):
        self.near_copy(i).start()

    def middle(self, i):
        net = self.net
        self.near_copy(i).wait_recv()
        for other in net.others():
            total = self.part[i, net.core, other].astype(F32) + self.near[i, other].astype(F32)
            self.part[i, net.core, other] = total.astype(BF16)
            self.far_copy(i, other).start()

    def finish(self, i):
        net = self.net
        total = self.part[i, net.core, net.chip].astype(F32) + self.near[i, net.chip].astype(F32)
        for other in net.others():
            self.far_landing(i, other).wait_recv()
            total = total + self.far[i, other].astype(F32)
        return total

    def sent(self, i):
        self.near_copy(i).wait_send()
        for other in self.net.others():
            self.far_copy(i, other).wait_send()


class Gather:
    def __init__(self, net, full, sems):
        self.net, self.full = net, full
        self.far_send, self.far_recv, self.near_send, self.near_recv = sems

    def far_copy(self, i, other):
        net = self.net
        block = self.full.at[i, net.core, net.chip]
        return net.to_peer(
            other, block, block, self.far_send.at[i, other], self.far_recv.at[i, net.chip]
        )

    def far_landing(self, i, other):
        net = self.net
        block = self.full.at[i, net.core, other]
        return net.to_peer(
            other, block, block, self.far_send.at[i, other], self.far_recv.at[i, other]
        )

    def near_copy(self, i):
        block = self.full.at[i, self.net.core]
        return self.net.to_sibling(block, block, self.near_send.at[i], self.near_recv.at[i])

    def near_landing(self, i):
        block = self.full.at[i, 1 - self.net.core]
        return self.net.to_sibling(block, block, self.near_send.at[i], self.near_recv.at[i])

    def start(self, i):
        for other in self.net.others():
            self.far_copy(i, other).start()

    def middle(self, i):
        for other in self.net.others():
            self.far_landing(i, other).wait_recv()
        self.near_copy(i).start()

    def finish(self, i):
        self.near_landing(i).wait_recv()

    def sent(self, i):
        for other in self.net.others():
            self.far_copy(i, other).wait_send()
        self.near_copy(i).wait_send()


def text_body(
    chips,
    head_count,
    embeds_own,
    grad_full,
    q_t,
    q_n,
    k_n,
    v_n,
    k_t,
    v_t,
    seg_q,
    seg_k,
    cos_t,
    sin_t,
    gain_one,
    gain_two,
    w_kv,
    w_query_hbm,
    w_out_hbm,
    w_gate_hbm,
    w_up_hbm,
    w_down_hbm,
    out_part,
    embed_grad,
    w_query,
    w_out,
    w_gate,
    w_up,
    w_down,
    part_a,
    near_a,
    far_a,
    part_b,
    near_b,
    far_b,
    full,
    out_t,
    logs,
    bias,
    residual,
    residual_grad,
    grad_own,
    grad_chunk,
    mixed,
    gate_grad,
    up_grad,
    out_tile,
    out_stage,
    d_out_t,
    d_out_n,
    d_query_t,
    value_even,
    value_odd,
    key_even,
    key_odd,
    weight_sem,
    own_sem,
    grad_sem,
    stage_sem,
    scatter_near,
    scatter_far_send,
    scatter_far_recv,
    gather_near,
    gather_far_send,
    gather_far_recv,
):
    me = lax.axis_index("mp")
    chip, core = me // 2, lax.rem(me, 2)
    net = Exchange(chips, chip, core, "mp")
    chunk_rows = q_n.shape[1]
    width = embeds_own.shape[2]
    units = w_gate.shape[1]
    head_width = FHD * head_count
    own_rows = embeds_own.shape[1]
    first_own = (core * chips + chip) * own_rows

    def scatter_of(kind, part, near, far):
        return Scatter(
            net,
            part,
            near,
            far,
            (
                scatter_near.at[kind, 0],
                scatter_near.at[kind, 1],
                scatter_far_send.at[kind],
                scatter_far_recv.at[kind],
            ),
        )

    def gather_of(kind):
        return Gather(
            net,
            full,
            (
                gather_far_send.at[kind],
                gather_far_recv.at[kind],
                gather_near.at[kind, 0],
                gather_near.at[kind, 1],
            ),
        )

    attn_sum = scatter_of(0, part_a, near_a, far_a)
    mlp_sum = scatter_of(1, part_b, near_b, far_b)
    normed_sum = scatter_of(2, part_a, near_a, far_a)
    mlp_rows = gather_of(0)
    back_rows = gather_of(1)

    weights = [
        pltpu.make_async_copy(source, target, weight_sem.at[k])
        for k, (source, target) in enumerate(
            (
                (w_out_hbm, w_out),
                (w_gate_hbm, w_gate),
                (w_up_hbm, w_up),
                (w_down_hbm, w_down),
                (w_query_hbm, w_query),
            )
        )
    ]
    for copy in weights:
        copy.start()

    def grad_copy(i):
        return pltpu.make_async_copy(grad_full.at[i], grad_chunk, grad_sem)

    def stage_copy(i):
        return pltpu.make_async_copy(out_stage, out_part.at[i], stage_sem)

    def own_copy(i):
        return pltpu.make_async_copy(
            grad_full.at[i, pl.ds(pl.multiple_of(first_own, own_rows), own_rows)],
            grad_own.at[i],
            own_sem.at[i],
        )

    grad_copy(CHUNKS - 1).start()
    for i in range(CHUNKS):
        own_copy(i).start()
    net.barrier()
    for ref in (value_even, value_odd, key_even, key_odd):
        ref[...] = jnp.zeros_like(ref)

    def put_rows(part, i, columns, values):
        half = chunk_rows // 2
        for k in range(2):
            for j in range(chips):
                first = k * half + j * own_rows
                part[i, k, j, :, columns] = values[first : first + own_rows].astype(BF16)

    def rows_of(ref, i):
        return ref[i].reshape(chunk_rows, width)

    def make_bias(i):
        query_spots = i * chunk_rows + lax.broadcasted_iota(jnp.int32, (chunk_rows, chunk_rows), 1)
        query_segments = seg_q[i]

        for kb in range(CHUNKS):

            @pl.when(kb <= i)
            def _():
                key_spots = kb * chunk_rows + lax.broadcasted_iota(
                    jnp.int32, (chunk_rows, chunk_rows), 0
                )
                allowed = (key_spots <= query_spots) & (seg_k[kb] == query_segments)
                bias[kb] = jnp.where(allowed, 0.0, FAR)

    def head_span(h):
        return pl.ds(pl.multiple_of(h * FHD, FHD), FHD)

    def attend(i, key_blocks):
        @pl.loop(0, head_count)
        def _(h):
            query = q_t[i, head_span(h), :]
            scores = [dot_nn(k_n[kb], query) + bias[kb] for kb in range(key_blocks)]
            top = jnp.max(scores[0], axis=0, keepdims=True)
            for block in scores[1:]:
                top = jnp.maximum(top, jnp.max(block, axis=0, keepdims=True))
            total = jnp.zeros_like(top)
            attended = jnp.zeros((FHD, chunk_rows), F32)
            for kb in range(key_blocks):
                weights_block = jnp.exp(scores[kb] - top)
                total = total + jnp.sum(weights_block, axis=0, keepdims=True)
                attended = attended + dot_nn(v_t[kb], weights_block.astype(BF16))
            logs[i, h] = top + jnp.log(total)
            out_t[i, head_span(h), :] = (attended / total).astype(BF16)

    def attend_back(i, key_blocks):
        cosine, sine = cos_t[i], sin_t[i]

        @pl.loop(0, head_count // 2)
        def _(pair):
            pair_span = pl.ds(pl.multiple_of(pair * 2 * FHD, 2 * FHD), 2 * FHD)
            query_pair = q_n[i, :, pair_span]
            grad_pair = d_out_n[:, pair_span]
            for odd in range(2):
                h = pair * 2 + odd
                query = q_t[i, head_span(h), :]
                grad = d_out_t[head_span(h), :]
                log_row = logs[i, h]
                grad_f = grad.astype(F32)
                centre = jnp.sum(
                    grad_f * out_t[i, head_span(h), :].astype(F32), axis=0, keepdims=True
                )
                value_total = value_odd if odd else value_even
                key_total = key_odd if odd else key_even
                query_grad = jnp.zeros((FHD, chunk_rows), F32)
                for kb in range(key_blocks):
                    probs = jnp.exp(dot_nn(k_n[kb], query) + bias[kb] - log_row)
                    value_total[kb] += dot_nn(probs.astype(BF16), grad_pair)
                    score_grad = (probs * (dot_nn(v_n[kb], grad) - centre)).astype(BF16)
                    key_total[kb] += dot_nn(score_grad, query_pair)
                    query_grad = query_grad + dot_nn(k_t[kb], score_grad)
                query_grad = query_grad * (FHD**-0.5)
                low_half, high_half = query_grad[: FHD // 2], query_grad[FHD // 2 :]
                d_query_t[head_span(h), :] = jnp.concatenate(
                    [low_half * cosine + high_half * sine, high_half * cosine - low_half * sine],
                    axis=0,
                ).astype(BF16)

    def each_length(i, body):
        for blocks in range(1, CHUNKS + 1):

            @pl.when(i == blocks - 1)
            def _():
                body(i, blocks)

    def stage_attend(i, first):
        make_bias(i)
        each_length(i, attend)

        @pl.when(first)
        def _():
            weights[0].wait()

        attended = out_t[i].T

        def tile(columns):
            put_rows(part_a, i, columns, dot_nt(attended, w_out[columns, :]))

        column_tiles(width, 512, tile)
        attn_sum.start(i)

    def stage_norm(i):
        values = embeds_own[i].astype(F32) + attn_sum.finish(i)
        residual[i] = values
        full[i, core, chip] = (values * rms_scale(values) * gain_two[...]).astype(BF16)
        mlp_rows.start(i)

    def stage_mlp(i, first, last):
        @pl.when(first)
        def _():
            for k in (1, 2, 3):
                weights[k].wait()

        mlp_rows.finish(i)
        grad_copy(i).wait()

        def unit_tile(columns):
            rows = rows_of(full, i)
            gate_pre = dot_nn(rows, w_gate[:, columns])
            up_pre = dot_nn(rows, w_up[:, columns])
            act_grad = dot_nn(grad_chunk[...], w_down[:, columns])
            inverse = 1.0 / (1.0 + jnp.exp(-gate_pre))
            silu = gate_pre * inverse
            mixed[:, columns] = (silu * up_pre).astype(BF16)
            up_grad[:, columns] = (act_grad * silu).astype(BF16)
            slope = inverse * (1.0 + gate_pre * (1.0 - inverse))
            gate_grad[:, columns] = (act_grad * up_pre * slope).astype(BF16)

        column_tiles(units, 256, unit_tile)

        def grad_tile(columns):
            put_rows(
                part_b,
                i,
                columns,
                dot_nt(gate_grad[...], w_gate[columns, :])
                + dot_nt(up_grad[...], w_up[columns, :]),
            )

        column_tiles(width, 512, grad_tile)
        mlp_rows.sent(i)
        mlp_sum.start(i)

        @pl.when(jnp.logical_not(last))
        def _():
            grad_copy(i - 1).start()

        @pl.when(jnp.logical_not(first))
        def _():
            stage_copy(i + 1).wait()

        def out_columns(columns):
            out_tile[...] = dot_nt(mixed[...], w_down[columns, :])
            own = pl.ds(pl.multiple_of(first_own, own_rows), own_rows)
            out_tile[own, :] += residual[i, :, columns]
            out_stage[:, columns] = out_tile[...].astype(BF16)

        column_tiles(width, 512, out_columns)
        stage_copy(i).start()

    def stage_residual_grad(i):
        grad = mlp_sum.finish(i)
        own_copy(i).wait()
        values = grad_own[i].astype(F32) + rms_back(residual[i], grad, gain_two[...])
        residual_grad[i] = values
        full[i, core, chip] = values.astype(BF16)
        back_rows.start(i)

    def stage_attend_back(i, first):
        back_rows.finish(i)
        attended_grad = dot_nn(rows_of(full, i), w_out[...]).astype(BF16)
        d_out_n[...] = attended_grad
        d_out_t[...] = attended_grad.T
        make_bias(i)
        each_length(i, attend_back)

        @pl.when(first)
        def _():
            weights[4].wait()

        attn_sum.sent(i)
        key_grad = (key_even[i][:, :FHD] + key_odd[i][:, FHD:]).T
        cosine, sine = cos_t[i], sin_t[i]
        low_half, high_half = key_grad[: FHD // 2], key_grad[FHD // 2 :]
        value_grad = (value_even[i][:, :FHD] + value_odd[i][:, FHD:]).T
        both = jnp.concatenate(
            [low_half * cosine + high_half * sine, high_half * cosine - low_half * sine, value_grad],
            axis=0,
        )
        both_rows = both.T.astype(BF16)
        query_rows = d_query_t[...].T

        def tile(columns):
            put_rows(
                part_a,
                i,
                columns,
                dot_nt(query_rows, w_query[columns, :]) + dot_nt(both_rows, w_kv[columns, :]),
            )

        column_tiles(width, 512, tile)
        normed_sum.start(i)

    def stage_embed_grad(i):
        grad = normed_sum.finish(i)
        values = residual_grad[i] + rms_back(embeds_own[i].astype(F32), grad, gain_one[...])
        embed_grad[i] = values.astype(BF16)

    def at(step, offset, body):
        turn = step - offset

        @pl.when((turn >= 0) & (turn < CHUNKS))
        def _():
            body(CHUNKS - 1 - turn)

    @pl.loop(0, CHUNKS + 3)
    def _(step):
        last = CHUNKS - 1
        at(step, 1, stage_norm)
        at(step, 0, lambda i: stage_attend(i, i == last))
        at(step, 2, mlp_sum.middle)
        at(step, 3, lambda i: stage_attend_back(i, i == last))
        at(step, 1, mlp_rows.middle)
        at(step, 0, attn_sum.middle)
        at(step, 2, stage_residual_grad)
        at(step, 3, normed_sum.middle)
        at(step, 1, lambda i: stage_mlp(i, i == last, i == 0))
        at(step, 2, back_rows.middle)

    @pl.loop(0, CHUNKS)
    def _(turn):
        i = CHUNKS - 1 - turn
        stage_embed_grad(i)
        normed_sum.sent(i)
        mlp_sum.sent(i)
        back_rows.sent(i)

    stage_copy(0).wait()


def text_layer(
    group,
    embeds_own,
    grad_full,
    q_t,
    q_n,
    k_n,
    v_n,
    k_t,
    v_t,
    seg_q,
    seg_k,
    cos_t,
    sin_t,
    gain_one,
    gain_two,
    w_kv,
    w_query,
    w_out,
    w_gate,
    w_up,
    w_down,
):
    chips = group // 2
    chunks, chunk_rows, head_width = q_n.shape
    own_rows, width = embeds_own.shape[1:]
    head_count = head_width // FHD
    units = w_gate.shape[1]
    vmem = pl.BlockSpec(memory_space=pltpu.VMEM)
    hbm = pl.BlockSpec(memory_space=pl.ANY)
    blocks = (chunks, 2, chips, own_rows, width)
    landing = (chunks, chips, own_rows, width)
    return pl.pallas_call(
        partial(text_body, chips, head_count),
        out_shape=(
            jax.ShapeDtypeStruct((chunks, chunk_rows, width), BF16),
            jax.ShapeDtypeStruct((chunks, own_rows, width), BF16),
        ),
        in_specs=[vmem, hbm] + [vmem] * 13 + [hbm] * 5,
        out_specs=(hbm, vmem),
        scratch_shapes=[
            pltpu.VMEM(w_query.shape, BF16),
            pltpu.VMEM(w_out.shape, BF16),
            pltpu.VMEM(w_gate.shape, BF16),
            pltpu.VMEM(w_up.shape, BF16),
            pltpu.VMEM(w_down.shape, BF16),
            pltpu.VMEM(blocks, BF16),
            pltpu.VMEM(landing, BF16),
            pltpu.VMEM(landing, BF16),
            pltpu.VMEM(blocks, BF16),
            pltpu.VMEM(landing, BF16),
            pltpu.VMEM(landing, BF16),
            pltpu.VMEM(blocks, BF16),
            pltpu.VMEM((chunks, head_width, chunk_rows), BF16),
            pltpu.VMEM((chunks, head_count, 1, chunk_rows), F32),
            pltpu.VMEM((chunks, chunk_rows, chunk_rows), F32),
            pltpu.VMEM((chunks, own_rows, width), F32),
            pltpu.VMEM((chunks, own_rows, width), F32),
            pltpu.VMEM((chunks, own_rows, width), BF16),
            pltpu.VMEM((chunk_rows, width), BF16),
            pltpu.VMEM((chunk_rows, units), BF16),
            pltpu.VMEM((chunk_rows, units), BF16),
            pltpu.VMEM((chunk_rows, units), BF16),
            pltpu.VMEM((chunk_rows, 512), F32),
            pltpu.VMEM((chunk_rows, width), BF16),
            pltpu.VMEM((head_width, chunk_rows), BF16),
            pltpu.VMEM((chunk_rows, head_width), BF16),
            pltpu.VMEM((head_width, chunk_rows), BF16),
        ]
        + [pltpu.VMEM((chunks, chunk_rows, 2 * FHD), F32)] * 4
        + [
            pltpu.SemaphoreType.DMA((5,)),
            pltpu.SemaphoreType.DMA((chunks,)),
            pltpu.SemaphoreType.DMA,
            pltpu.SemaphoreType.DMA,
            pltpu.SemaphoreType.DMA((3, 2, chunks)),
            pltpu.SemaphoreType.DMA((3, chunks, chips)),
            pltpu.SemaphoreType.DMA((3, chunks, chips)),
            pltpu.SemaphoreType.DMA((2, 2, chunks)),
            pltpu.SemaphoreType.DMA((2, chunks, chips)),
            pltpu.SemaphoreType.DMA((2, chunks, chips)),
        ],
        compiler_params=pltpu.CompilerParams(
            collective_id=0, has_side_effects=True, vmem_limit_bytes=63 * 1024 * 1024
        ),
        cost_estimate=pl.CostEstimate(
            flops=80 * 10**9, bytes_accessed=40 * 10**6, transcendentals=20 * 10**6
        ),
    )(
        embeds_own,
        grad_full,
        q_t,
        q_n,
        k_n,
        v_n,
        k_t,
        v_t,
        seg_q,
        seg_k,
        cos_t,
        sin_t,
        gain_one,
        gain_two,
        w_kv,
        w_query,
        w_out,
        w_gate,
        w_up,
        w_down,
    )


def norm_parts(values):
    average = jnp.mean(values, axis=-1, keepdims=True)
    centred = values - average
    scale = lax.rsqrt(jnp.mean(centred * centred, axis=-1, keepdims=True) + 1e-05)
    return centred * scale, scale


def norm_back(values, grad, gain):
    unit, scale = norm_parts(values)
    scaled = grad * gain
    back = scale * (
        scaled
        - jnp.mean(scaled, axis=-1, keepdims=True)
        - unit * jnp.mean(scaled * unit, axis=-1, keepdims=True)
    )
    return (
        back,
        jnp.sum(grad * unit, axis=0, keepdims=True),
        jnp.sum(grad, axis=0, keepdims=True),
    )


def gelu_parts(values):
    root = math.sqrt(2.0 / math.pi)
    squared = values * values
    bent = jnp.tanh(root * values * (1.0 + 0.044715 * squared))
    half = 0.5 * (1.0 + bent)
    slope = half + 0.5 * values * (1.0 - bent * bent) * root * (1.0 + 3 * 0.044715 * squared)
    return values * half, slope


def pool_matrix(counts_col, entries, rows):
    entry = lax.broadcasted_iota(jnp.int32, (entries, rows), 0)
    row = lax.broadcasted_iota(jnp.int32, (entries, rows), 1)
    slots = rows // entries
    inside = (row // slots == entry) & (lax.rem(row, slots) < counts_col)
    return jnp.where(inside, 1.0, 0.0)


def spread_matrix(counts_row, entries, rows):
    row = lax.broadcasted_iota(jnp.int32, (rows, entries), 0)
    entry = lax.broadcasted_iota(jnp.int32, (rows, entries), 1)
    slots = rows // entries
    inside = (row // slots == entry) & (lax.rem(row, slots) < counts_row)
    return jnp.where(inside, 1.0, 0.0)


def slot_bias(valid_col, slots):
    rows = valid_col.shape[0]
    key = lax.broadcasted_iota(jnp.int32, (rows, rows), 0)
    query = lax.broadcasted_iota(jnp.int32, (rows, rows), 1)
    return jnp.where((key // slots == query // slots) & (valid_col > 0.5), 0.0, FAR)


ROW_BLOCK = 256


def shards_of(chips):
    return [(y * 2 + c, c, y) for y in range(chips) for c in range(2)]


def each_shard(chips, columns, body):
    @pl.loop(0, 2)
    def _(c):
        @pl.loop(0, chips)
        def _(y):
            first = pl.multiple_of((y * 2 + c) * columns, columns)
            body(c, y, pl.ds(first, columns))


def hyper_body(
    chips,
    dp_count,
    pieces,
    counts_col,
    counts_row,
    gain_one,
    shift_one,
    gain_two,
    shift_two,
    shards,
    entries,
    weights_out,
    attn_in,
    q_n,
    k_n,
    v_n,
    attended,
    logs,
    residual,
    ffn_in,
    full,
    q_t,
    v_t,
    out_t,
    bias,
    hidden,
    local_sem,
    store_sem,
    far_send,
    far_recv,
    x_send,
    x_recv,
    near_send,
    near_recv,
    dp_send,
    dp_recv,
    y_send,
    y_recv,
    last_send,
    last_recv,
):
    me = lax.axis_index("mp")
    dp = lax.axis_index("dp")
    chip, core = me // 2, lax.rem(me, 2)
    net = Exchange(chips, chip, core, "mp")
    side = lax.rem(dp, 2)
    mate = dp + 1 - 2 * side
    kinds, width, columns = shards.shape
    rows = pieces.shape[0]
    entry_count = counts_col.shape[0]
    slots = rows // entry_count
    head_columns = columns // 4
    half = width // 2
    heads = width // HD

    flag = pltpu.get_barrier_semaphore()
    pl.semaphore_signal(flag, inc=1, device_id=net.sibling(), device_id_type=MESH)
    for other in net.others():
        pl.semaphore_signal(flag, inc=1, device_id=net.peer(other), device_id_type=MESH)

    @pl.loop(1, dp_count)
    def _(j):
        pl.semaphore_signal(
            flag, inc=1, device_id={"dp": lax.rem(dp + j, dp_count)}, device_id_type=MESH
        )

    local = [
        pltpu.make_async_copy(shards.at[k], full.at[k, core, chip], local_sem.at[k])
        for k in range(kinds)
    ]
    for copy in local:
        copy.start()
    pl.semaphore_wait(flag, chips + dp_count - 1)

    def rows_half(which):
        return pl.ds(pl.multiple_of(which * half, half), half)

    def far_copy(k, other):
        return net.to_peer(
            other,
            shards.at[k, rows_half(side)],
            full.at[k, core, chip, rows_half(side)],
            far_send.at[k, other],
            far_recv.at[k, chip],
        )

    def far_landing(k, other):
        block = full.at[k, core, other, rows_half(side)]
        return net.to_peer(other, block, block, far_send.at[k, other], far_recv.at[k, other])

    def x_copy(k, other, which):
        block = full.at[k, core, other, rows_half(which)]
        return pltpu.make_async_remote_copy(
            src_ref=block,
            dst_ref=block,
            send_sem=x_send.at[k, other],
            recv_sem=x_recv.at[k, other],
            device_id={"dp": mate},
            device_id_type=MESH,
        )

    def near_copy(k, which):
        block = full.at[k, which]
        return net.to_sibling(block, block, near_send.at[k], near_recv.at[k])

    def far_middle(k):
        for other in net.others():
            far_landing(k, other).wait_recv()
            x_copy(k, other, side).start()

    def x_middle(k):
        for other in net.others():
            x_copy(k, other, 1 - side).wait_recv()
        local[k].wait()
        near_copy(k, core).start()

    def store(k):
        return pltpu.make_async_copy(full.at[k], weights_out.at[k], store_sem.at[k])

    def near_finish(k):
        near_copy(k, 1 - core).wait_recv()
        store(k).start()

    for k in range(kinds):
        for other in net.others():
            far_copy(k, other).start()

    values = pieces[...].astype(F32)
    attn_in[...] = (norm_parts(values)[0] * gain_one[...] + shift_one[...]).astype(BF16)
    blocks = rows // ROW_BLOCK
    valid = jnp.sum(spread_matrix(counts_row[...], entry_count, rows), axis=1, keepdims=True)
    for b in range(blocks):
        bias[b] = slot_bias(valid[b * ROW_BLOCK : (b + 1) * ROW_BLOCK], slots)

    far_middle(0)
    far_middle(1)
    x_middle(0)
    far_middle(2)
    near_finish(0)
    for m, c, y in shards_of(chips):
        span = slice(m * head_columns, (m + 1) * head_columns)
        projected = dot_nn(attn_in[...], full[0, c, y, :, : 3 * head_columns])
        q_n[:, span] = (projected[:, :head_columns].astype(BF16).astype(F32) * HD**-0.5).astype(
            BF16
        )
        k_n[:, span] = projected[:, head_columns : 2 * head_columns].astype(BF16)
        v_n[:, span] = projected[:, 2 * head_columns :].astype(BF16)
    x_middle(1)
    far_middle(3)
    for b in range(blocks):
        block_rows = slice(b * ROW_BLOCK, (b + 1) * ROW_BLOCK)
        q_t[b] = q_n[block_rows, :].T
        v_t[b] = v_n[block_rows, :].T

    @pl.loop(0, heads // 2)
    def _(pair):
        pair_span = pl.ds(pl.multiple_of(pair * 2 * HD, 2 * HD), 2 * HD)
        for b in range(blocks):
            key_pair = k_n[b * ROW_BLOCK : (b + 1) * ROW_BLOCK, pair_span]
            for odd in range(2):
                h = pair * 2 + odd
                span = pl.ds(pl.multiple_of(h * HD, HD), HD)
                scores = dot_nn(key_pair[:, odd * HD : (odd + 1) * HD], q_t[b, span, :]) + bias[b]
                top = jnp.max(scores, axis=0, keepdims=True)
                weights = jnp.exp(scores - top)
                total = jnp.sum(weights, axis=0, keepdims=True)
                logs[b, h] = top + jnp.log(total)
                out_t[b, span, :] = (dot_nn(v_t[b, span, :], weights.astype(BF16)) / total).astype(
                    BF16
                )

    x_middle(2)
    for b in range(blocks):
        attended[b * ROW_BLOCK : (b + 1) * ROW_BLOCK, :] = out_t[b].T
    total = values
    for m, c, y in shards_of(chips):
        span = slice(m * head_columns, (m + 1) * head_columns)
        total = total + dot_nt(attended[:, span], full[0, c, y, :, 3 * head_columns :])
    residual[...] = total
    ffn_in[...] = (norm_parts(total)[0] * gain_two[...] + shift_two[...]).astype(BF16)
    near_finish(1)
    x_middle(3)
    pool = pool_matrix(counts_col[...], entry_count, rows).astype(BF16)

    def up_shard(c, y, span):
        act = gelu_parts(dot_nn(ffn_in[...], full[1, c, y]))[0]
        hidden[:, span] = dot_nn(pool, act.astype(BF16)).astype(BF16)

    each_shard(chips, columns, up_shard)
    near_finish(2)
    pooled = jnp.sum(
        (residual[...] * valid).reshape(entry_count, slots, width), axis=1
    )
    for m, c, y in shards_of(chips):
        pooled = pooled + dot_nt(hidden[:, m * columns : (m + 1) * columns], full[2, c, y])
    entries[core, chip, dp] = (pooled / counts_col[...].astype(F32)).astype(BF16)

    def dp_copy(block, target, slot):
        piece = entries.at[core, chip, block]
        return pltpu.make_async_remote_copy(
            src_ref=piece,
            dst_ref=piece,
            send_sem=dp_send.at[slot],
            recv_sem=dp_recv.at[block],
            device_id={"dp": target},
            device_id_type=MESH,
        )

    def y_copy(other, owner, block):
        piece = entries.at[core, owner, block]
        return net.to_peer(
            other, piece, piece, y_send.at[other, block], y_recv.at[owner, block]
        )

    @pl.loop(1, dp_count)
    def _(j):
        target = lax.rem(dp + j, dp_count)
        dp_copy(dp, target, target).start()

    for other in net.others():
        y_copy(other, chip, dp).start()
    near_finish(3)

    @pl.loop(1, dp_count)
    def _(j):
        source = lax.rem(dp + dp_count - j, dp_count)
        dp_copy(source, source, source).wait_recv()
        for other in net.others():
            y_copy(other, chip, source).start()

    def last_copy(part, c, owner):
        piece = entries.at[c, owner]
        return net.to_sibling(piece, piece, last_send.at[part], last_recv.at[owner])

    last_copy(chip, core, chip).start()
    for other in net.others():

        @pl.loop(0, dp_count)
        def _(block):
            y_copy(other, other, block).wait_recv()

        last_copy(other, core, other).start()
    last_copy(chip, 1 - core, chip).wait_recv()
    for other in net.others():
        last_copy(other, 1 - core, other).wait_recv()

    for k in range(kinds):
        store(k).wait()
        near_copy(k, core).wait_send()
        for other in net.others():
            far_copy(k, other).wait_send()
            x_copy(k, other, side).wait_send()

    @pl.loop(1, dp_count)
    def _(j):
        target = lax.rem(dp + j, dp_count)
        dp_copy(dp, target, target).wait_send()

    last_copy(chip, core, chip).wait_send()
    for other in net.others():
        last_copy(other, core, other).wait_send()

        @pl.loop(0, dp_count)
        def _(block):
            y_copy(other, chip, block).wait_send()


def hyper_forward(
    group, dp_count, pieces, counts_col, counts_row, gain_one, shift_one, gain_two, shift_two, shards
):
    chips = group // 2
    rows, width = pieces.shape
    kinds, _, columns = shards.shape
    entry_count = counts_col.shape[0]
    heads = width // HD
    blocks = rows // ROW_BLOCK
    vmem = pl.BlockSpec(memory_space=pltpu.VMEM)
    hbm = pl.BlockSpec(memory_space=pl.ANY)
    row_shape = jax.ShapeDtypeStruct((rows, width), BF16)
    dma = pltpu.SemaphoreType.DMA
    return pl.pallas_call(
        partial(hyper_body, chips, dp_count),
        out_shape=(
            jax.ShapeDtypeStruct((2, chips, dp_count, entry_count, width), BF16),
            jax.ShapeDtypeStruct((kinds, 2, chips, width, columns), BF16),
            row_shape,
            row_shape,
            row_shape,
            row_shape,
            row_shape,
            jax.ShapeDtypeStruct((blocks, heads, 1, ROW_BLOCK), F32),
            jax.ShapeDtypeStruct((rows, width), F32),
            row_shape,
        ),
        in_specs=[vmem] * 7 + [hbm],
        out_specs=(vmem, hbm) + (vmem,) * 8,
        scratch_shapes=[
            pltpu.VMEM((kinds, 2, chips, width, columns), BF16),
            pltpu.VMEM((blocks, width, ROW_BLOCK), BF16),
            pltpu.VMEM((blocks, width, ROW_BLOCK), BF16),
            pltpu.VMEM((blocks, width, ROW_BLOCK), BF16),
            pltpu.VMEM((blocks, ROW_BLOCK, ROW_BLOCK), F32),
            pltpu.VMEM((entry_count, columns * group), BF16),
            dma((kinds,)),
            dma((kinds,)),
            dma((kinds, chips)),
            dma((kinds, chips)),
            dma((kinds, chips)),
            dma((kinds, chips)),
            dma((kinds,)),
            dma((kinds,)),
            dma((dp_count,)),
            dma((dp_count,)),
            dma((chips, dp_count)),
            dma((chips, dp_count)),
            dma((chips,)),
            dma((chips,)),
        ],
        compiler_params=pltpu.CompilerParams(
            collective_id=1, has_side_effects=True, vmem_limit_bytes=60 * 1024 * 1024
        ),
        cost_estimate=pl.CostEstimate(
            flops=60 * 10**9, bytes_accessed=20 * 10**6, transcendentals=5 * 10**6
        ),
    )(pieces, counts_col, counts_row, gain_one, shift_one, gain_two, shift_two, shards)


def embed_body(
    group,
    spots,
    entries,
    proj,
    bias,
    gain,
    w_query,
    w_kv,
    cos_t,
    sin_t,
    embeds_own,
    pooled_own,
    q_t,
    q_n,
    k_n,
    v_n,
    k_t,
    v_t,
    embeds,
    pooled,
):
    me = lax.axis_index("mp")
    chips = group // 2
    chunk_rows, width = embeds.shape
    own_rows = chunk_rows // group
    own = pl.ds(pl.multiple_of((lax.rem(me, 2) * chips + me // 2) * own_rows, own_rows), own_rows)
    entry_total = entries.shape[0]
    columns = proj.shape[3]
    numbers = lax.broadcasted_iota(jnp.int32, (chunk_rows, entry_total), 1)
    chosen = jnp.where(numbers == spots[0], 1.0, 0.0).astype(BF16)
    pooled[...] = dot_nn(chosen, entries[...]).astype(BF16)
    pooled_own[0] = pooled[own, :]
    for m, c, y in shards_of(chips):
        span = slice(m * columns, (m + 1) * columns)
        embeds[:, span] = (dot_nn(pooled[...], proj[c, y]) + bias[:, span]).astype(BF16)
    embeds_own[0] = embeds[own, :]
    values = embeds[...].astype(F32)
    normed = (values * rms_scale(values) * gain[...]).astype(BF16)
    cosine, sine = cos_t[0], sin_t[0]

    def turned(block):
        low_half, high_half = block[: FHD // 2], block[FHD // 2 :]
        return jnp.concatenate(
            [low_half * cosine - high_half * sine, high_half * cosine + low_half * sine], axis=0
        )

    queries = dot_nn(normed, w_query[...]).T
    for h in range(queries.shape[0] // FHD):
        span = slice(h * FHD, (h + 1) * FHD)
        q_t[0, span, :] = (turned(queries[span]).astype(BF16).astype(F32) * FHD**-0.5).astype(BF16)
    q_n[0] = q_t[0].T
    both = dot_nn(normed, w_kv[...])
    keys_t = turned(both.T[:FHD]).astype(BF16)
    k_t[0] = keys_t
    k_n[0] = keys_t.T
    v_n[0] = both[:, FHD:].astype(BF16)
    v_t[0] = both.T[FHD:].astype(BF16)


def embed_tokens(group, spots, entries, proj, bias, gain, w_query, w_kv, cos_t, sin_t):
    chunks, chunk_rows, _ = spots.shape
    own_rows = chunk_rows // group
    entry_width = entries.shape[1]
    width = bias.shape[1]
    head_width = w_query.shape[1]

    def whole(values):
        return pl.BlockSpec(values.shape, lambda i: (0,) * values.ndim)

    def chunked(*shape):
        return pl.BlockSpec((1,) + shape, lambda i: (i,) + (0,) * len(shape))

    shapes = (
        (own_rows, width),
        (own_rows, entry_width),
        (head_width, chunk_rows),
        (chunk_rows, head_width),
        (chunk_rows, FHD),
        (chunk_rows, FHD),
        (FHD, chunk_rows),
        (FHD, chunk_rows),
    )
    return pl.pallas_call(
        partial(embed_body, group),
        grid=(chunks,),
        out_shape=tuple(jax.ShapeDtypeStruct((chunks,) + shape, BF16) for shape in shapes),
        in_specs=[
            chunked(chunk_rows, 1),
            whole(entries),
            whole(proj),
            whole(bias),
            whole(gain),
            whole(w_query),
            whole(w_kv),
            chunked(FHD // 2, chunk_rows),
            chunked(FHD // 2, chunk_rows),
        ],
        out_specs=tuple(chunked(*shape) for shape in shapes),
        scratch_shapes=[
            pltpu.VMEM((chunk_rows, width), BF16),
            pltpu.VMEM((chunk_rows, entry_width), BF16),
        ],
        compiler_params=pltpu.CompilerParams(vmem_limit_bytes=60 * 1024 * 1024),
        cost_estimate=pl.CostEstimate(
            flops=9 * 10**9, bytes_accessed=12 * 10**6, transcendentals=10**4
        ),
    )(spots, entries, proj, bias, gain, w_query, w_kv, cos_t, sin_t)


class Total:
    def __init__(self, net, dp, dp_count, scatter, mine, x_land, z_land, final, sems):
        self.net, self.scatter, self.mine = net, scatter, mine
        self.x_land, self.z_land, self.final = x_land, z_land, final
        self.x_send, self.x_recv, self.z_send, self.z_recv = sems[:4]
        self.g_send, self.g_recv, self.l_send, self.l_recv = sems[4:]
        self.side = lax.rem(dp, 2)
        self.spot = dp // 2
        self.mate = dp + 1 - 2 * self.side
        self.spots = dp_count // 2

    def remote(self, source, target, send, recv, device):
        return pltpu.make_async_remote_copy(
            src_ref=source,
            dst_ref=target,
            send_sem=send,
            recv_sem=recv,
            device_id={"dp": device},
            device_id_type=MESH,
        )

    def x_copy(self, k):
        return self.remote(
            self.mine.at[k, 1 - self.side],
            self.x_land.at[k],
            self.x_send.at[k],
            self.x_recv.at[k],
            self.mate,
        )

    def z_copy(self, k, spot, slot):
        return self.remote(
            self.mine.at[k, self.side, spot],
            self.z_land.at[k, slot],
            self.z_send.at[k, spot],
            self.z_recv.at[k, slot],
            spot * 2 + self.side,
        )

    def g_copy(self, k, spot, owner):
        block = self.final.at[k, self.side, owner]
        return self.remote(
            block, block, self.g_send.at[k, spot], self.g_recv.at[k, owner], spot * 2 + self.side
        )

    def l_copy(self, k, side):
        block = self.final.at[k, side]
        return self.remote(block, block, self.l_send.at[k], self.l_recv.at[k], self.mate)

    def each_spot(self, body):
        if self.spots > 1:

            @pl.loop(1, self.spots)
            def _(j):
                body(lax.rem(self.spot + j, self.spots))

    def start(self, k):
        self.scatter.start(k)

    def near_middle(self, k):
        self.scatter.middle(k)

    def far_middle(self, k):
        total = self.scatter.finish(k)
        self.mine[k] = total.astype(BF16).reshape(self.mine.shape[1:])
        self.x_copy(k).start()

    def x_middle(self, k):
        self.x_copy(k).wait_recv()
        block = self.mine[k, self.side].astype(F32) + self.x_land[k].astype(F32)
        self.mine[k, self.side] = block.astype(BF16)
        self.each_spot(lambda spot: self.z_copy(k, spot, self.spot).start())

    def z_middle(self, k):
        def add(spot):
            self.z_copy(k, spot, spot).wait_recv()

        self.each_spot(add)
        total = self.mine[k, self.side, self.spot].astype(F32)
        for j in range(1, self.spots):
            spot = lax.rem(self.spot + j, self.spots)
            total = total + self.z_land[k, spot].astype(F32)
        self.final[k, self.side, self.spot] = total.astype(BF16)
        self.each_spot(lambda spot: self.g_copy(k, spot, self.spot).start())

    def g_middle(self, k):
        self.each_spot(lambda spot: self.g_copy(k, spot, spot).wait_recv())
        self.l_copy(k, self.side).start()

    def finish(self, k):
        self.l_copy(k, 1 - self.side).wait_recv()

    def sent(self, k):
        self.scatter.sent(k)
        self.x_copy(k).wait_send()
        self.each_spot(lambda spot: self.z_copy(k, spot, self.spot).wait_send())
        self.each_spot(lambda spot: self.g_copy(k, spot, self.spot).wait_send())
        self.l_copy(k, self.side).wait_send()


PARTS = 8


def back_body(
    chips,
    dp_count,
    embed_rows,
    pooled_own,
    token_row,
    pieces,
    counts_col,
    counts_row,
    gain_one,
    gain_two,
    attn_in,
    q_n,
    k_n,
    v_n,
    attended,
    logs,
    residual,
    ffn_in,
    weights_hbm,
    pieces_grad,
    final,
    small_total,
    weights,
    part,
    near,
    far,
    mine,
    x_land,
    z_land,
    token_full,
    entry_part,
    entry_land,
    hidden,
    hidden_pre,
    ffn_t,
    row_total,
    d_out_n,
    d_query,
    d_key,
    d_value,
    q_t,
    out_t,
    d_out_t,
    k_t,
    d_query_t,
    bias,
    small_near,
    small_far,
    small_dp,
    small_part,
    weight_sem,
    gather_near,
    gather_far_send,
    gather_far_recv,
    entry_send,
    entry_recv,
    scatter_near,
    scatter_far_send,
    scatter_far_recv,
    x_sem,
    z_send,
    z_recv,
    g_send,
    g_recv,
    l_sem,
    small_sem,
    small_far_send,
    small_far_recv,
    small_dp_send,
    small_dp_recv,
):
    me = lax.axis_index("mp")
    dp = lax.axis_index("dp")
    group = chips * 2
    chip, core = me // 2, lax.rem(me, 2)
    net = Exchange(chips, chip, core, "mp")
    rows, width = pieces.shape
    entry_count = counts_col.shape[0]
    slots = rows // entry_count
    columns = weights.shape[4]
    half_columns = columns // 2
    head_columns = columns // 4
    heads = width // HD
    blocks = rows // ROW_BLOCK
    total_sum = Total(
        net,
        dp,
        dp_count,
        Scatter(
            net,
            part,
            near,
            far,
            (scatter_near.at[0], scatter_near.at[1], scatter_far_send, scatter_far_recv),
        ),
        mine,
        x_land,
        z_land,
        final,
        (x_sem.at[0], x_sem.at[1], z_send, z_recv, g_send, g_recv, l_sem.at[0], l_sem.at[1]),
    )
    stages = (
        total_sum.near_middle,
        total_sum.far_middle,
        total_sum.x_middle,
        total_sum.z_middle,
        total_sum.g_middle,
        total_sum.finish,
    )

    def run(step):
        for offset, stage in enumerate(stages):
            if 0 <= step - offset < PARTS:
                stage(step - offset)

    token_rows = Gather(
        net, token_full, (gather_far_send, gather_far_recv, gather_near.at[0], gather_near.at[1])
    )

    flag = pltpu.get_barrier_semaphore()
    pl.semaphore_signal(flag, inc=1, device_id=net.sibling(), device_id_type=MESH)
    for other in net.others():
        pl.semaphore_signal(flag, inc=1, device_id=net.peer(other), device_id_type=MESH)

    def each_dp(body):
        @pl.loop(1, dp_count)
        def _(j):
            body(lax.rem(dp + j, dp_count))

    each_dp(
        lambda target: pl.semaphore_signal(
            flag, inc=1, device_id={"dp": target}, device_id_type=MESH
        )
    )
    loads = [
        pltpu.make_async_copy(weights_hbm.at[k], weights.at[k], weight_sem.at[k])
        for k in (3, 1, 2, 0)
    ]
    for copy in loads:
        copy.start()
    pl.semaphore_wait(flag, chips + dp_count - 1)

    def put(k, c, y, values):
        part[k, c, y] = values[:, :half_columns].astype(BF16)
        part[k + 1, c, y] = values[:, half_columns:].astype(BF16)

    loads[0].wait()
    token_grad = jnp.zeros((embed_rows.shape[0], width), F32)
    for m, c, y in shards_of(chips):
        token_grad = token_grad + dot_nt(
            embed_rows[:, m * columns : (m + 1) * columns], weights[3, c, y]
        )
    token_full[0, core, chip] = token_grad.astype(BF16)
    token_rows.start(0)
    pooled_t = pooled_own[...].T

    def proj_shard(c, y, span):
        put(0, c, y, dot_nn(pooled_t, embed_rows[:, span]))

    each_shard(chips, columns, proj_shard)
    total_sum.start(0)
    total_sum.start(1)
    bias_sums = jnp.sum(embed_rows[...].astype(F32), axis=0, keepdims=True)
    for j in range(4):
        small_part[4 + j : 5 + j, :] = bias_sums[:, j * width : (j + 1) * width]
    token_rows.middle(0)
    loads[1].wait()

    pool = pool_matrix(counts_col[...], entry_count, rows).astype(BF16)
    spread = spread_matrix(counts_row[...], entry_count, rows)
    valid = jnp.sum(spread, axis=1, keepdims=True)
    spread = spread.astype(BF16)
    for b in range(blocks):
        bias[b] = slot_bias(valid[b * ROW_BLOCK : (b + 1) * ROW_BLOCK], slots)
    ffn_t[...] = ffn_in[...].T

    token_rows.finish(0)
    token_total = token_full.shape[1] * token_full.shape[2] * token_full.shape[3]
    all_tokens = token_full[0].reshape(token_total, width)
    dp_step = max(1, ROW_BLOCK // entry_count)

    @pl.loop(0, dp_count // dp_step)
    def _(block):
        row = lax.broadcasted_iota(jnp.int32, (dp_step * entry_count, token_total), 0)
        owner = block * dp_step + row // entry_count
        number = (owner * group + me) * entry_count + lax.rem(row, entry_count)
        chosen = jnp.where(number == token_row[...], 1.0, 0.0).astype(BF16)
        sums = dot_nn(chosen, all_tokens).astype(BF16)
        for j in range(dp_step):
            entry_part[block * dp_step + j] = sums[j * entry_count : (j + 1) * entry_count]

    def entry_copy(target, slot):
        return pltpu.make_async_remote_copy(
            src_ref=entry_part.at[target],
            dst_ref=entry_land.at[slot],
            send_sem=entry_send.at[target],
            recv_sem=entry_recv.at[slot],
            device_id={"dp": target},
            device_id_type=MESH,
        )

    each_dp(lambda target: entry_copy(target, dp).start())
    run(0)

    def hidden_shard(c, y, span):
        before = dot_nn(ffn_in[...], weights[1, c, y])
        hidden_pre[:, span] = before
        hidden[:, span] = dot_nn(pool, gelu_parts(before)[0].astype(BF16)).astype(BF16)

    each_shard(chips, columns, hidden_shard)
    run(1)
    each_dp(lambda source: entry_copy(source, source).wait_recv())
    pooled_grad = entry_part[dp].astype(F32)
    for j in range(1, dp_count):
        pooled_grad = pooled_grad + entry_land[lax.rem(dp + j, dp_count)].astype(F32)
    entry_low = (pooled_grad / counts_col[...].astype(F32)).astype(BF16)
    out_rows = dot_nn(spread, entry_low)
    entry_t = entry_low.T
    loads[2].wait()
    out_low = out_rows.astype(BF16)
    row_total[...] = jnp.zeros_like(row_total)

    def unit_shard(c, y, span):
        put(2, c, y, dot_nn(entry_t, hidden[:, span]))
        act_grad = dot_nn(out_low, weights[2, c, y])
        pre_grad = (act_grad * gelu_parts(hidden_pre[:, span])[1]).astype(BF16)
        put(4, c, y, dot_nn(ffn_t[...], pre_grad))
        row_total[...] += dot_nt(pre_grad, weights[1, c, y])

    each_shard(chips, columns, unit_shard)
    for k in (2, 3, 4, 5):
        total_sum.start(k)
    run(2)
    back, gain_grad, shift_grad = norm_back(residual[...], row_total[...], gain_two[...])
    small_part[2:3, :] = gain_grad
    small_part[3:4, :] = shift_grad
    residual_grad = out_rows + back
    pieces_grad[...] = residual_grad
    attn_grad = residual_grad.astype(BF16)
    loads[3].wait()
    for m, c, y in shards_of(chips):
        span = slice(m * head_columns, (m + 1) * head_columns)
        d_out_n[:, span] = dot_nn(attn_grad, weights[0, c, y, :, 3 * head_columns :]).astype(BF16)
    out_grad = dot_nn(attn_grad.T, attended[...])
    for m, c, y in shards_of(chips):
        span = slice(m * head_columns, (m + 1) * head_columns)
        part[7, c, y, :, head_columns:] = out_grad[:, span].astype(BF16)
    for b in range(blocks):
        block_rows = slice(b * ROW_BLOCK, (b + 1) * ROW_BLOCK)
        q_t[b] = q_n[block_rows, :].T
        k_t[b] = k_n[block_rows, :].T
        out_t[b] = attended[block_rows, :].T
        d_out_t[b] = d_out_n[block_rows, :].T
    run(3)

    @pl.loop(0, heads // 2)
    def _(pair):
        pair_span = pl.ds(pl.multiple_of(pair * 2 * HD, 2 * HD), 2 * HD)
        for b in range(blocks):
            block_rows = slice(b * ROW_BLOCK, (b + 1) * ROW_BLOCK)
            key_pair = k_n[block_rows, pair_span]
            value_pair = v_n[block_rows, pair_span]
            query_pair = q_n[block_rows, pair_span]
            grad_pair = d_out_n[block_rows, pair_span]
            key_sums, value_sums = [], []
            for odd in range(2):
                h = pair * 2 + odd
                span = pl.ds(pl.multiple_of(h * HD, HD), HD)
                lanes = slice(odd * HD, (odd + 1) * HD)
                scores = dot_nn(key_pair[:, lanes], q_t[b, span, :]) + bias[b]
                probs = jnp.exp(scores - logs[b, h])
                grad_t = d_out_t[b, span, :]
                centre = jnp.sum(
                    grad_t.astype(F32) * out_t[b, span, :].astype(F32), axis=0, keepdims=True
                )
                value_sums.append(dot_nn(probs.astype(BF16), grad_pair[:, lanes]))
                score_grad = (probs * (dot_nn(value_pair[:, lanes], grad_t) - centre)).astype(BF16)
                key_sums.append(dot_nn(score_grad, query_pair[:, lanes]))
                d_query_t[b, span, :] = (
                    dot_nn(k_t[b, span, :], score_grad) * (HD**-0.5)
                ).astype(BF16)
            d_key[block_rows, pair_span] = jnp.concatenate(key_sums, axis=1).astype(BF16)
            d_value[block_rows, pair_span] = jnp.concatenate(value_sums, axis=1).astype(BF16)

    for b in range(blocks):
        d_query[b * ROW_BLOCK : (b + 1) * ROW_BLOCK, :] = d_query_t[b].T
    run(4)
    rows_t = attn_in[...].T
    for place, (k, lanes, source) in enumerate(
        ((6, 0, d_query), (6, 1, d_key), (7, 0, d_value))
    ):
        grads = dot_nn(rows_t, source[...])
        for m, c, y in shards_of(chips):
            span = slice(m * head_columns, (m + 1) * head_columns)
            part[k, c, y, :, lanes * head_columns : (lanes + 1) * head_columns] = grads[
                :, span
            ].astype(BF16)
    total_sum.start(6)
    total_sum.start(7)
    normed = jnp.zeros((rows, width), F32)
    for m, c, y in shards_of(chips):
        span = slice(m * head_columns, (m + 1) * head_columns)
        for j, source in enumerate((d_query, d_key, d_value)):
            normed = normed + dot_nt(
                source[:, span], weights[0, c, y, :, j * head_columns : (j + 1) * head_columns]
            )
    back, gain_grad, shift_grad = norm_back(pieces[...].astype(F32), normed, gain_one[...])
    small_part[0:1, :] = gain_grad
    small_part[1:2, :] = shift_grad
    pieces_grad[...] += back

    small_copy = net.to_sibling(small_part, small_near, small_sem.at[0], small_sem.at[1])
    small_copy.start()

    def small_far_copy(other, owner):
        return net.to_peer(
            other,
            small_far.at[owner],
            small_far.at[owner],
            small_far_send.at[other],
            small_far_recv.at[owner],
        )

    def small_dp_copy(other, owner):
        return pltpu.make_async_remote_copy(
            src_ref=small_dp.at[owner],
            dst_ref=small_dp.at[owner],
            send_sem=small_dp_send.at[other],
            recv_sem=small_dp_recv.at[owner],
            device_id={"dp": other},
            device_id_type=MESH,
        )

    def small_near_done():
        small_copy.wait_recv()
        small_far[chip] = small_part[...] + small_near[...]
        for other in net.others():
            small_far_copy(other, chip).start()

    def small_far_done():
        for other in net.others():
            small_far_copy(other, other).wait_recv()
        total = small_far[0]
        for j in range(1, chips):
            total = total + small_far[j]
        small_dp[dp] = total
        each_dp(lambda other: small_dp_copy(other, dp).start())

    @pl.loop(5, PARTS + 5)
    def _(step):
        for offset, stage in enumerate(stages):
            k = step - offset

            @pl.when((k >= 0) & (k < PARTS))
            def _():
                stage(k)

        pl.when(step == 5)(small_near_done)
        pl.when(step == 7)(small_far_done)

    each_dp(lambda other: small_dp_copy(other, other).wait_recv())
    total = small_dp[0]
    for j in range(1, dp_count):
        total = total + small_dp[j]
    small_total[...] = total

    small_copy.wait_send()
    for other in net.others():
        small_far_copy(other, chip).wait_send()
    each_dp(lambda other: small_dp_copy(other, dp).wait_send())
    each_dp(lambda other: entry_copy(other, dp).wait_send())
    token_rows.sent(0)

    @pl.loop(0, PARTS)
    def _(k):
        total_sum.sent(k)


def hyper_backward(
    group,
    dp_count,
    embed_rows,
    pooled_own,
    token_row,
    pieces,
    counts_col,
    counts_row,
    gain_one,
    gain_two,
    saved,
    weights,
):
    chips = group // 2
    rows, width = pieces.shape
    entry_count = counts_col.shape[0]
    tokens = embed_rows.shape[0]
    kinds, columns = weights.shape[0], weights.shape[4]
    half_columns = columns // 2
    heads = width // HD
    blocks = rows // ROW_BLOCK
    spots = dp_count // 2
    vmem = pl.BlockSpec(memory_space=pltpu.VMEM)
    hbm = pl.BlockSpec(memory_space=pl.ANY)
    dma = pltpu.SemaphoreType.DMA
    final = (PARTS, 2, spots, width // (2 * spots), half_columns)
    units = columns * group

    def low(*shape):
        return pltpu.VMEM(shape, BF16)

    def wide(*shape):
        return pltpu.VMEM(shape, F32)

    return pl.pallas_call(
        partial(back_body, chips, dp_count),
        out_shape=(
            jax.ShapeDtypeStruct((rows, width), F32),
            jax.ShapeDtypeStruct(final, BF16),
            jax.ShapeDtypeStruct((8, width), F32),
        ),
        in_specs=[vmem] * 16 + [hbm],
        out_specs=(vmem, vmem, vmem),
        scratch_shapes=[
            low(kinds, 2, chips, width, columns),
            low(PARTS, 2, chips, width, half_columns),
            low(PARTS, chips, width, half_columns),
            low(PARTS, chips, width, half_columns),
            low(*final),
            low(PARTS, spots, width // (2 * spots), half_columns),
            low(PARTS, spots, width // (2 * spots), half_columns),
            low(1, 2, chips, tokens, width),
            low(dp_count, entry_count, width),
            low(dp_count, entry_count, width),
            low(entry_count, units),
            wide(rows, units),
            low(width, rows),
            wide(rows, width),
            low(rows, width),
            low(rows, width),
            low(rows, width),
            low(rows, width),
        ]
        + [low(blocks, width, ROW_BLOCK)] * 5
        + [
            wide(blocks, ROW_BLOCK, ROW_BLOCK),
            wide(8, width),
            wide(chips, 8, width),
            wide(dp_count, 8, width),
            wide(8, width),
            dma((kinds,)),
            dma((2, 1)),
            dma((1, chips)),
            dma((1, chips)),
            dma((dp_count,)),
            dma((dp_count,)),
            dma((2, PARTS)),
            dma((PARTS, chips)),
            dma((PARTS, chips)),
            dma((2, PARTS)),
            dma((PARTS, spots)),
            dma((PARTS, spots)),
            dma((PARTS, spots)),
            dma((PARTS, spots)),
            dma((2, PARTS)),
            dma((2,)),
            dma((chips,)),
            dma((chips,)),
            dma((dp_count,)),
            dma((dp_count,)),
        ],
        compiler_params=pltpu.CompilerParams(
            collective_id=2, has_side_effects=True, vmem_limit_bytes=62 * 1024 * 1024
        ),
        cost_estimate=pl.CostEstimate(
            flops=60 * 10**9, bytes_accessed=20 * 10**6, transcendentals=5 * 10**6
        ),
    )(
        embed_rows,
        pooled_own,
        token_row,
        pieces,
        counts_col,
        counts_row,
        gain_one,
        gain_two,
        *saved,
        weights,
    )


def spread_body(sums, query, key, value, out, up, down, proj):
    half_columns = sums.shape[2]
    head_columns = query.shape[1]
    for first, target in ((0, proj), (2, down), (4, up)):
        target[:, :half_columns] = sums[first].astype(F32)
        target[:, half_columns:] = sums[first + 1].astype(F32)
    for k, lanes, target in ((6, 0, query), (6, 1, key), (7, 0, value), (7, 1, out)):
        target[...] = sums[k, :, lanes * head_columns : (lanes + 1) * head_columns].astype(F32)


def spread_sums(sums):
    _, width, half_columns = sums.shape
    small = jax.ShapeDtypeStruct((width, half_columns // 2), F32)
    large = jax.ShapeDtypeStruct((width, half_columns * 2), F32)
    vmem = pl.BlockSpec(memory_space=pltpu.VMEM)
    return pl.pallas_call(
        spread_body,
        out_shape=(small,) * 4 + (large,) * 3,
        in_specs=[vmem],
        out_specs=(vmem,) * 7,
        compiler_params=pltpu.CompilerParams(vmem_limit_bytes=40 * 1024 * 1024),
    )(sums)


def on_device(
    pieces,
    counts,
    entry_ids,
    segment_ids,
    norm1_gain,
    norm1_shift,
    query_weight,
    key_weight,
    value_weight,
    out_weight,
    norm2_gain,
    norm2_shift,
    up_weight,
    down_weight,
    proj_weight,
    proj_bias,
    text_norm1_gain,
    text_query,
    text_key,
    text_value,
    text_out_proj,
    text_norm2_gain,
    text_gate,
    text_up,
    text_down,
    token_grad,
):
    group, dp_count = lax.axis_size("mp"), lax.axis_size("dp")
    chips = group // 2
    me = lax.axis_index("mp")
    entry_count, slot_count, width = pieces.shape
    text_width = token_grad.shape[1]
    length = segment_ids.shape[1]
    chunk_rows = length // CHUNKS
    own_rows = chunk_rows // group
    token_grads = lax.all_gather(token_grad, "mp", axis=0, tiled=True)
    bias_full = lax.all_gather(proj_bias, "mp", axis=0, tiled=True)
    own_counts = lax.dynamic_slice_in_dim(counts, me * entry_count, entry_count)
    counts_col, counts_row = own_counts[:, None], own_counts[None, :]
    pieces_rows = pieces.reshape(entry_count * slot_count, width)
    shards = jnp.stack(
        [
            jnp.concatenate([query_weight, key_weight, value_weight, out_weight], axis=1),
            up_weight,
            down_weight,
            proj_weight,
        ]
    )
    entries, weights, *saved = hyper_forward(
        group,
        dp_count,
        pieces_rows,
        counts_col,
        counts_row,
        norm1_gain[None, :],
        norm1_shift[None, :],
        norm2_gain[None, :],
        norm2_shift[None, :],
        shards,
    )
    owner = entry_ids // entry_count
    owner_mp, owner_dp = owner % group, owner // group
    spots = (
        ((owner_mp % 2) * chips + owner_mp // 2) * dp_count + owner_dp
    ) * entry_count + entry_ids % entry_count
    head_width = text_query.shape[1]
    kv_index = me * (head_width // FHD) // (QHEADS // KVHEADS)
    key_local = lax.dynamic_slice_in_dim(text_key, kv_index * FHD, FHD, 1)
    value_local = lax.dynamic_slice_in_dim(text_value, kv_index * FHD, FHD, 1)
    key_value = jnp.concatenate([key_local, value_local], axis=1)
    cos_t, sin_t = rope_tables(length)
    embeds_own, pooled_own, *heads = embed_tokens(
        group,
        spots.reshape(CHUNKS, chunk_rows, 1),
        entries.reshape(-1, width),
        weights[3],
        bias_full[None, :],
        text_norm1_gain[None, :],
        text_query,
        key_value,
        cos_t,
        sin_t,
    )
    segments = segment_ids[0]
    out_part, embed_rows = text_layer(
        group,
        embeds_own,
        token_grads.reshape(CHUNKS, chunk_rows, text_width),
        *heads,
        segments.reshape(CHUNKS, 1, chunk_rows),
        segments.reshape(CHUNKS, chunk_rows, 1),
        cos_t,
        sin_t,
        text_norm1_gain[None, :],
        text_norm2_gain[None, :],
        key_value,
        text_query,
        text_out_proj,
        text_gate,
        text_up,
        text_down,
    )
    text_out = lax.psum_scatter(
        out_part.reshape(length, text_width), "mp", scatter_dimension=0, tiled=True
    ).astype(jnp.float32)
    token_row = (
        entry_ids.reshape(CHUNKS, 2, chips, own_rows).transpose(1, 2, 0, 3).reshape(1, length)
    )
    pieces_grad, final, small = hyper_backward(
        group,
        dp_count,
        embed_rows.reshape(CHUNKS * own_rows, text_width),
        pooled_own.reshape(CHUNKS * own_rows, width),
        token_row,
        pieces_rows,
        counts_col,
        counts_row,
        norm1_gain[None, :],
        norm2_gain[None, :],
        saved,
        weights,
    )
    query_grad, key_grad, value_grad, out_grad, up_grad, down_grad, proj_grad = spread_sums(
        final.reshape(PARTS, width, -1)
    )
    bias_share = proj_bias.shape[0]
    proj_bias_grad = lax.dynamic_slice_in_dim(
        small[4:].reshape(-1), me * bias_share, bias_share
    )
    return (
        text_out,
        pieces_grad.reshape(pieces.shape),
        small[0],
        small[1],
        query_grad,
        key_grad,
        value_grad,
        out_grad,
        small[2],
        small[3],
        up_grad,
        down_grad,
        proj_grad,
        proj_bias_grad,
    )


def solution(mesh):
    return jax.shard_map(
        on_device,
        mesh=mesh,
        in_specs=(
            P(("dp", "mp"), None, None),
            P("dp"),
            P("dp"),
            P("dp", None),
            P(),
            P(),
            P(None, "mp"),
            P(None, "mp"),
            P(None, "mp"),
            P(None, "mp"),
            P(),
            P(),
            P(None, "mp"),
            P(None, "mp"),
            P(None, "mp"),
            P("mp"),
            P(),
            P(None, "mp"),
            P(),
            P(),
            P(None, "mp"),
            P(),
            P(None, "mp"),
            P(None, "mp"),
            P(None, "mp"),
            P(("dp", "mp"), None),
        ),
        out_specs=(
            P(("dp", "mp"), None),
            P(("dp", "mp"), None, None),
            P(),
            P(),
            P(None, "mp"),
            P(None, "mp"),
            P(None, "mp"),
            P(None, "mp"),
            P(),
            P(),
            P(None, "mp"),
            P(None, "mp"),
            P(None, "mp"),
            P("mp"),
        ),
        check_vma=False,
    )
```

```python
from functools import partial
import math

import jax
import jax.numpy as jnp
import numpy as np
from jax import lax
from jax.experimental import pallas as pl
from jax.experimental.pallas import tpu as pltpu
from jax.sharding import PartitionSpec as P

HD = 64
QHEADS = 32
KVHEADS = 4
FHD = 64


def rope_tables(length):
    positions = np.arange(length, dtype=np.float32)
    rates = np.exp(
        np.arange(FHD // 2, dtype=np.float32) * np.float32(-2.0 * math.log(10000.0) / FHD)
    ).astype(np.float32)
    angles = (positions[None, :] * rates[:, None]).reshape(FHD // 2, CHUNKS, length // CHUNKS)
    angles = angles.transpose(1, 0, 2)
    return jnp.asarray(np.cos(angles)), jnp.asarray(np.sin(angles))


MESH = pl.DeviceIdType.MESH
F32 = jnp.float32
BF16 = jnp.bfloat16
CHUNKS = 4
FAR = -1e30


def dot_nn(a, b):
    return lax.dot_general(a, b, (((1,), (0,)), ((), ())), preferred_element_type=F32)


def dot_nt(a, b):
    return lax.dot_general(a, b, (((1,), (1,)), ((), ())), preferred_element_type=F32)


def column_tiles(total, width, body):
    full = total // width
    if full > 0:

        @pl.loop(0, full)
        def _(t):
            body(pl.ds(pl.multiple_of(t * width, width), width))

    if total % width:
        body(pl.ds(full * width, total % width))


def rms_scale(values):
    return lax.rsqrt(jnp.mean(values * values, axis=-1, keepdims=True) + 1e-05)


def rms_back(values, grad, gain):
    scale = rms_scale(values)
    scaled = grad * gain
    return scale * (
        scaled - values * (scale * scale) * jnp.mean(scaled * values, axis=-1, keepdims=True)
    )


class Exchange:
    def __init__(self, chips, chip, core, group_axis):
        self.chips, self.chip, self.core = chips, chip, core
        self.axis = group_axis

    def sibling(self):
        return {self.axis: self.chip * 2 + 1 - self.core}

    def peer(self, other):
        return {self.axis: other * 2 + self.core}

    def others(self):
        return [lax.rem(self.chip + step, self.chips) for step in range(1, self.chips)]

    def barrier(self):
        flag = pltpu.get_barrier_semaphore()
        pl.semaphore_signal(flag, inc=1, device_id=self.sibling(), device_id_type=MESH)
        for other in self.others():
            pl.semaphore_signal(flag, inc=1, device_id=self.peer(other), device_id_type=MESH)
        pl.semaphore_wait(flag, self.chips)

    def to_sibling(self, source, target, send, recv):
        return pltpu.make_async_remote_copy(
            src_ref=source,
            dst_ref=target,
            send_sem=send,
            recv_sem=recv,
            device_id=self.sibling(),
            device_id_type=MESH,
        )

    def to_peer(self, other, source, target, send, recv):
        return pltpu.make_async_remote_copy(
            src_ref=source,
            dst_ref=target,
            send_sem=send,
            recv_sem=recv,
            device_id=self.peer(other),
            device_id_type=MESH,
        )


class Scatter:
    def __init__(self, net, part, near, far, sems):
        self.net, self.part, self.near, self.far = net, part, near, far
        self.slots = None if part.shape[0] == near.shape[0] else part.shape[0]
        self.near_send, self.near_recv, self.far_send, self.far_recv = sems

    def slot(self, i):
        return i if self.slots is None else i % self.slots

    def landing(self, source, target):
        return lax.rem(source - target + self.net.chips - 1, self.net.chips)

    def near_copy(self, i):
        net = self.net
        return net.to_sibling(
            self.part.at[self.slot(i), 1 - net.core],
            self.near.at[i],
            self.near_send.at[i],
            self.near_recv.at[i],
        )

    def far_copy(self, i, other):
        net = self.net
        return net.to_peer(
            other,
            self.part.at[self.slot(i), net.core, other],
            self.far.at[i, self.landing(net.chip, other)],
            self.far_send.at[i, other],
            self.far_recv.at[i, net.chip],
        )

    def far_landing(self, i, other):
        net = self.net
        return net.to_peer(
            other,
            self.part.at[self.slot(i), net.core, other],
            self.far.at[i, self.landing(other, net.chip)],
            self.far_send.at[i, other],
            self.far_recv.at[i, other],
        )

    def start(self, i):
        self.near_copy(i).start()

    def middle(self, i):
        net = self.net
        self.near_copy(i).wait_recv()
        slot = self.slot(i)
        for other in net.others():
            total = self.part[slot, net.core, other].astype(F32) + self.near[
                i, other
            ].astype(F32)
            self.part[slot, net.core, other] = total.astype(BF16)
            self.far_copy(i, other).start()

    def finish(self, i):
        net = self.net
        slot = self.slot(i)
        total = self.part[slot, net.core, net.chip].astype(F32) + self.near[
            i, net.chip
        ].astype(F32)
        for other in net.others():
            self.far_landing(i, other).wait_recv()
            total = total + self.far[i, self.landing(other, net.chip)].astype(F32)
        return total

    def sent(self, i):
        self.near_copy(i).wait_send()
        for other in self.net.others():
            self.far_copy(i, other).wait_send()


class Gather:
    def __init__(self, net, full, sems, single=False):
        self.net, self.full, self.single = net, full, single
        self.far_send, self.far_recv, self.near_send, self.near_recv = sems

    def block(self, i, *place):
        return self.full.at[place] if self.single else self.full.at[(i, *place)]

    def far_copy(self, i, other):
        net = self.net
        block = self.block(i, net.core, net.chip)
        return net.to_peer(
            other, block, block, self.far_send.at[i, other], self.far_recv.at[i, net.chip]
        )

    def far_landing(self, i, other):
        net = self.net
        block = self.block(i, net.core, other)
        return net.to_peer(
            other, block, block, self.far_send.at[i, other], self.far_recv.at[i, other]
        )

    def near_copy(self, i):
        block = self.block(i, self.net.core)
        return self.net.to_sibling(block, block, self.near_send.at[i], self.near_recv.at[i])

    def near_landing(self, i):
        block = self.block(i, 1 - self.net.core)
        return self.net.to_sibling(block, block, self.near_send.at[i], self.near_recv.at[i])

    def start(self, i):
        for other in self.net.others():
            self.far_copy(i, other).start()

    def middle(self, i):
        for other in self.net.others():
            self.far_landing(i, other).wait_recv()
        self.near_copy(i).start()

    def finish(self, i):
        self.near_landing(i).wait_recv()

    def sent(self, i):
        for other in self.net.others():
            self.far_copy(i, other).wait_send()
        self.near_copy(i).wait_send()


STEPS = (
    ("attend", 0),
    ("attn_part", 0),
    ("attend", 2),
    ("attn_far", 0),
    ("attend", 1),
    ("attn_part", 1),
    ("norm", 0),
    ("attn_part", 2),
    ("attn_far", 1),
    ("attend", 3),
    ("rows_near", 0),
    ("attn_part", 3),
    ("attn_far", 2),
    ("units_low", 0),
    ("norm", 1),
    ("units_high", 0),
    ("unit_grads", 0),
    ("attn_far", 3),
    ("outputs", 0),
    ("rows_near", 1),
    ("norm", 2),
    ("units_far", 0),
    ("units_low", 1),
    ("units_high", 1),
    ("outputs", 1),
    ("norm", 3),
    ("rows_near", 2),
    ("unit_grads", 1),
    ("units_low", 2),
    ("residual", 0),
    ("units_high", 2),
    ("outputs", 2),
    ("rows_near", 3),
    ("units_far", 1),
    ("unit_grads", 2),
    ("units_low", 3),
    ("back_near", 0),
    ("units_far", 2),
    ("residual", 1),
    ("units_high", 3),
    ("unit_grads", 3),
    ("units_far", 3),
    ("residual", 2),
    ("attend_back", 0),
    ("back_near", 1),
    ("normed_part", 0),
    ("back_near", 2),
    ("attend_back", 1),
    ("residual", 3),
    ("normed_part", 1),
    ("normed_far", 0),
    ("outputs", 3),
    ("normed_far", 1),
    ("attend_back", 2),
    ("back_near", 3),
    ("embed_grad", 0),
    ("normed_part", 2),
    ("attend_back", 3),
    ("normed_far", 2),
    ("normed_part", 3),
    ("token_near", 0),
    ("embed_grad", 1),
    ("normed_far", 3),
    ("embed_grad", 2),
    ("token_near", 1),
    ("token_near", 2),
    ("embed_grad", 3),
    ("token_near", 3),
)


def column_of(row):
    return jnp.broadcast_to(row, (8, row.shape[1])).T[:, :1]


def text_body(
    chips,
    dp_count,
    entry_count,
    head_count,
    entry_ids,
    segments,
    cos_t,
    sin_t,
    bias_full,
    gain_one,
    gain_two,
    w_kv,
    entries_hbm,
    weights_hbm,
    token_grad,
    w_query_hbm,
    w_out_hbm,
    w_gate_hbm,
    w_up_hbm,
    w_down_hbm,
    out_part,
    embed_grad,
    pooled_own,
    token_full,
    proj,
    w_query,
    w_out,
    w_gate,
    w_up,
    w_down,
    part_a,
    near_a,
    far_a,
    part_b,
    near_b,
    far_b,
    full,
    grad_full,
    embeds_own,
    q_t,
    q_n,
    k_n,
    v_n,
    k_t,
    v_t,
    seg_k,
    out_t,
    logs,
    bias,
    residual,
    weight_sem,
    local_sem,
    stage_sem,
    scatter_near,
    scatter_far_send,
    scatter_far_recv,
    gather_near,
    gather_far_send,
    gather_far_recv,
    grad_near,
    grad_far_send,
    grad_far_recv,
):
    me = lax.axis_index("mp")
    chip, core = me // 2, lax.rem(me, 2)
    net = Exchange(chips, chip, core, "mp")
    group = chips * 2
    chunk_rows = q_n.shape[1]
    width = embeds_own.shape[2]
    units = w_gate.shape[1]
    own_rows = embeds_own.shape[1]
    head_width = FHD * head_count
    columns = proj.shape[3]
    entry_total, entry_width = entries_hbm.shape
    owned = token_grad.shape[0]
    first_own = pl.multiple_of((core * chips + chip) * own_rows, own_rows)
    owners = group // CHUNKS if group > CHUNKS else 1

    def scatter_of(kind, part, near, far):
        return Scatter(
            net,
            part,
            near,
            far,
            (
                scatter_near.at[kind, 0],
                scatter_near.at[kind, 1],
                scatter_far_send.at[kind],
                scatter_far_recv.at[kind],
            ),
        )

    def gather_of(kind, ref):
        return Gather(
            net,
            ref,
            (
                gather_far_send.at[kind],
                gather_far_recv.at[kind],
                gather_near.at[kind, 0],
                gather_near.at[kind, 1],
            ),
        )

    attn_sum = scatter_of(0, part_a, near_a, far_a)
    mlp_sum = scatter_of(1, part_b, near_b, far_b)
    normed_sum = scatter_of(2, part_a, near_a, far_a)
    mlp_rows = gather_of(0, full)
    back_rows = gather_of(1, full)
    token_rows = gather_of(2, token_full)

    def load(k, source, target):
        return pltpu.make_async_copy(source, target, weight_sem.at[k])

    load_proj = load(1, weights_hbm.at[3], proj)
    load_query = load(2, w_query_hbm, w_query)
    load_out = load(3, w_out_hbm, w_out)
    load_units = [
        load(4, w_gate_hbm, w_gate),
        load(5, w_up_hbm, w_up),
        load(6, w_down_hbm, w_down),
    ]

    def grad_far(owner_chip, other):
        return net.to_peer(
            other,
            token_grad,
            grad_full.at[owner_chip * 2 + core],
            grad_far_send.at[other],
            grad_far_recv.at[owner_chip],
        )

    def grad_near_copy(owner_chip, owner_core):
        block = grad_full.at[owner_chip * 2 + owner_core]
        return net.to_sibling(
            block, block, grad_near.at[0, owner_chip], grad_near.at[1, owner_chip]
        )

    grad_local = pltpu.make_async_copy(token_grad, grad_full.at[me], local_sem)

    def grad_start():
        for other in net.others():
            grad_far(chip, other).start()

    def grad_middle():
        grad_local.wait()
        grad_near_copy(chip, core).start()
        for other in net.others():
            grad_far(other, other).wait_recv()
            grad_near_copy(other, core).start()

    def grad_chunk(i):
        return grad_full[i * owners : (i + 1) * owners].reshape(chunk_rows, width)

    def grad_finish(i):
        for owner in range(i * owners, (i + 1) * owners):

            @pl.when(core != owner % 2)
            def _():
                grad_near_copy(owner // 2, owner % 2).wait_recv()

    def embed(entries, pooled, embeds):
        load_entries = load(0, entries_hbm, entries)
        load_entries.start()
        for copy in (load_proj, load_query, load_out, *load_units):
            copy.start()
        grad_local.start()
        net.barrier()
        pl.when(core == 1)(grad_start)
        load_entries.wait()
        load_proj.wait()
        load_query.wait()

        @pl.loop(0, CHUNKS)
        def _(i):
            seg_k[i] = column_of(segments[i].astype(F32)).astype(jnp.int32)
            ids = entry_ids[i]
            owner = ids // entry_count
            owner_mp, owner_dp = lax.rem(owner, group), owner // group
            place = (lax.rem(owner_mp, 2) * chips + owner_mp // 2) * dp_count + owner_dp
            spots = column_of(
                (place * entry_count + lax.rem(ids, entry_count)).astype(F32)
            ).astype(jnp.int32)
            numbers = lax.broadcasted_iota(jnp.int32, (chunk_rows, entry_total), 1)
            chosen = jnp.where(numbers == spots, 1.0, 0.0).astype(BF16)
            pooled[...] = dot_nn(chosen, entries[...]).astype(BF16)
            pooled_own[i] = pooled[pl.ds(first_own, own_rows), :]
            for m, c, y in shards_of(chips):
                span = slice(m * columns, (m + 1) * columns)
                embeds[:, span] = (dot_nn(pooled[...], proj[c, y]) + bias_full[c, y]).astype(BF16)
            embeds_own[i] = embeds[pl.ds(first_own, own_rows), :]
            values = embeds[...].astype(F32)
            embeds[...] = (values * rms_scale(values) * gain_one[...]).astype(BF16)
            cosine, sine = cos_t[i], sin_t[i]

            def turned(block):
                low_half, high_half = block[: FHD // 2], block[FHD // 2 :]
                return jnp.concatenate(
                    [low_half * cosine - high_half * sine, high_half * cosine + low_half * sine],
                    axis=0,
                )

            queries = dot_nn(embeds[...], w_query[...]).T
            for h in range(head_count):
                span = slice(h * FHD, (h + 1) * FHD)
                q_t[i, span, :] = (
                    turned(queries[span]).astype(BF16).astype(F32) * FHD**-0.5
                ).astype(BF16)
            q_n[i] = q_t[i].T
            both = dot_nn(embeds[...], w_kv[...])
            keys_t = turned(both.T[:FHD]).astype(BF16)
            k_t[i] = keys_t
            k_n[i] = keys_t.T
            v_n[i] = both[:, FHD:].astype(BF16)
            v_t[i] = both.T[FHD:].astype(BF16)

        pl.when(core == 0)(grad_start)
        pl.when(core == 1)(grad_middle)

    pl.run_scoped(
        embed,
        pltpu.VMEM((entry_total, entry_width), BF16),
        pltpu.VMEM((chunk_rows, entry_width), BF16),
        pltpu.VMEM((chunk_rows, width), BF16),
    )

    def put_rows(part, slot, columns, values):
        half = chunk_rows // 2
        for k in range(2):
            for j in range(chips):
                first = k * half + j * own_rows
                part[slot, k, j, :, columns] = values[first : first + own_rows].astype(BF16)

    def rows_of(ref, i):
        return ref[i].reshape(chunk_rows, width)

    def make_bias(i):
        query_spots = i * chunk_rows + lax.broadcasted_iota(jnp.int32, (chunk_rows, chunk_rows), 1)
        query_segments = segments[i]
        for kb in range(i + 1):
            allowed = seg_k[kb] == query_segments
            if kb == i:
                key_spots = kb * chunk_rows + lax.broadcasted_iota(
                    jnp.int32, (chunk_rows, chunk_rows), 0
                )
                allowed = allowed & (key_spots <= query_spots)
            bias[kb] = jnp.where(allowed, 0.0, FAR)

    def head_span(h):
        return pl.ds(pl.multiple_of(h * FHD, FHD), FHD)

    def layer(
        mixed,
        gate_grad,
        up_grad,
        out_tile,
        out_stage,
        d_out_t,
        d_out_n,
        d_query_t,
        value_even,
        value_odd,
        key_even,
        key_odd,
    ):
        for ref in (value_even, value_odd, key_even, key_odd):
            ref[...] = jnp.zeros_like(ref)

        def stage_copy(i):
            return pltpu.make_async_copy(out_stage, out_part.at[i], stage_sem)

        def attend(i):
            make_bias(i)

            @pl.loop(0, head_count)
            def _(h):
                query = q_t[i, head_span(h), :]
                scores = [dot_nn(k_n[kb], query) + bias[kb] for kb in range(i + 1)]
                top = jnp.max(scores[0], axis=0, keepdims=True)
                for block in scores[1:]:
                    top = jnp.maximum(top, jnp.max(block, axis=0, keepdims=True))
                total = jnp.zeros_like(top)
                attended = jnp.zeros((FHD, chunk_rows), F32)
                for kb in range(i + 1):
                    weights_block = jnp.exp(scores[kb] - top)
                    total = total + jnp.sum(weights_block, axis=0, keepdims=True)
                    attended = attended + dot_nn(v_t[kb], weights_block.astype(BF16))
                logs[i, h] = top + jnp.log(total)
                out_t[i, head_span(h), :] = (attended / total).astype(BF16)

        def attn_part(i):
            if i == CHUNKS - 1:
                load_out.wait()
            attended = out_t[i].T

            def tile(columns):
                put_rows(part_a, i, columns, dot_nt(attended, w_out[columns, :]))

            column_tiles(width, 512, tile)
            attn_sum.start(i)

        def norm(i):
            values = embeds_own[i].astype(F32) + attn_sum.finish(i)
            residual[i] = values
            full[i, core, chip] = (values * rms_scale(values) * gain_two[...]).astype(BF16)
            mlp_rows.start(i)

        def unit_tile(i, columns):
            rows = rows_of(full, i)
            gate_pre = dot_nn(rows, w_gate[:, columns])
            up_pre = dot_nn(rows, w_up[:, columns])
            act_grad = dot_nn(grad_chunk(i), w_down[:, columns])
            inverse = 1.0 / (1.0 + jnp.exp(-gate_pre))
            silu = gate_pre * inverse
            mixed[:, columns] = (silu * up_pre).astype(BF16)
            up_grad[:, columns] = (act_grad * silu).astype(BF16)
            slope = inverse * (1.0 + gate_pre * (1.0 - inverse))
            gate_grad[:, columns] = (act_grad * up_pre * slope).astype(BF16)

        tiles = units // 256
        middle_tile = (tiles + 1) // 2

        def unit_tiles(i, first, last):
            @pl.loop(first, last)
            def _(t):
                unit_tile(i, pl.ds(pl.multiple_of(t * 256, 256), 256))

        def units_low(i):
            if i == CHUNKS - 1:
                pl.when(core == 0)(grad_middle)
                for copy in load_units:
                    copy.wait()
            grad_finish(i)
            mlp_rows.finish(i)
            unit_tiles(i, 0, middle_tile)

        def units_high(i):
            unit_tiles(i, middle_tile, tiles)
            if units % 256:
                unit_tile(i, pl.ds(tiles * 256, units % 256))
            mlp_rows.sent(i)

        def unit_grads(i):
            if i + 2 < CHUNKS:
                mlp_sum.sent(i + 2)

            def tile(columns):
                put_rows(
                    part_b,
                    i % 2,
                    columns,
                    dot_nt(gate_grad[...], w_gate[columns, :])
                    + dot_nt(up_grad[...], w_up[columns, :]),
                )

            column_tiles(width, 512, tile)
            mlp_sum.start(i)

        def outputs(i):
            if i < CHUNKS - 1:
                stage_copy(i + 1).wait()

            def tile(columns):
                out_tile[...] = dot_nt(mixed[...], w_down[columns, :])
                out_tile[pl.ds(first_own, own_rows), :] += residual[i, :, columns]
                out_stage[:, columns] = out_tile[...].astype(BF16)

            column_tiles(width, 512, tile)
            stage_copy(i).start()

        def residual_back(i):
            grad = mlp_sum.finish(i)
            block = i * owners + first_own // owned
            start = pl.multiple_of(lax.rem(first_own, owned), own_rows)
            own_grad = grad_full[block, pl.ds(start, own_rows), :].astype(F32)
            values = own_grad + rms_back(residual[i], grad, gain_two[...])
            full[i, core, chip] = values.astype(BF16)
            back_rows.start(i)

        def attend_back(i):
            back_rows.finish(i)
            attended_grad = dot_nn(rows_of(full, i), w_out[...]).astype(BF16)
            d_out_n[...] = attended_grad
            d_out_t[...] = attended_grad.T
            make_bias(i)
            cosine, sine = cos_t[i], sin_t[i]

            @pl.loop(0, head_count // 2)
            def _(pair):
                pair_span = pl.ds(pl.multiple_of(pair * 2 * FHD, 2 * FHD), 2 * FHD)
                query_pair = q_n[i, :, pair_span]
                grad_pair = d_out_n[:, pair_span]
                for odd in range(2):
                    h = pair * 2 + odd
                    query = q_t[i, head_span(h), :]
                    grad = d_out_t[head_span(h), :]
                    log_row = logs[i, h]
                    centre = jnp.sum(
                        grad.astype(F32) * out_t[i, head_span(h), :].astype(F32),
                        axis=0,
                        keepdims=True,
                    )
                    value_total = value_odd if odd else value_even
                    key_total = key_odd if odd else key_even
                    query_grad = jnp.zeros((FHD, chunk_rows), F32)
                    for kb in range(i + 1):
                        probs = jnp.exp(dot_nn(k_n[kb], query) + bias[kb] - log_row)
                        value_total[kb] += dot_nn(probs.astype(BF16), grad_pair)
                        score_grad = (probs * (dot_nn(v_n[kb], grad) - centre)).astype(BF16)
                        key_total[kb] += dot_nn(score_grad, query_pair)
                        query_grad = query_grad + dot_nn(k_t[kb], score_grad)
                    query_grad = query_grad * (FHD**-0.5)
                    low_half, high_half = query_grad[: FHD // 2], query_grad[FHD // 2 :]
                    d_query_t[head_span(h), :] = jnp.concatenate(
                        [
                            low_half * cosine + high_half * sine,
                            high_half * cosine - low_half * sine,
                        ],
                        axis=0,
                    ).astype(BF16)

        def normed_part(i):
            attn_sum.sent(i)
            key_grad = (key_even[i][:, :FHD] + key_odd[i][:, FHD:]).T
            cosine, sine = cos_t[i], sin_t[i]
            low_half, high_half = key_grad[: FHD // 2], key_grad[FHD // 2 :]
            value_grad = (value_even[i][:, :FHD] + value_odd[i][:, FHD:]).T
            both = jnp.concatenate(
                [
                    low_half * cosine + high_half * sine,
                    high_half * cosine - low_half * sine,
                    value_grad,
                ],
                axis=0,
            )
            both_rows = both.T.astype(BF16)
            query_rows = d_query_t[...].T

            def tile(columns):
                put_rows(
                    part_a,
                    i,
                    columns,
                    dot_nt(query_rows, w_query[columns, :]) + dot_nt(both_rows, w_kv[columns, :]),
                )

            column_tiles(width, 512, tile)
            normed_sum.start(i)

        def embed_back(i):
            grad = normed_sum.finish(i)
            kept = full[i, core, chip].astype(F32)
            values = kept + rms_back(embeds_own[i].astype(F32), grad, gain_one[...])
            embed_grad[i] = values.astype(BF16)
            total = jnp.zeros((own_rows, entry_width), F32)
            for m, c, y in shards_of(chips):
                total = total + dot_nt(
                    embed_grad[i, :, m * columns : (m + 1) * columns], proj[c, y]
                )
            token_full[i, core, chip] = total.astype(BF16)
            token_rows.start(i)

        stages = {
            "attend": attend,
            "attn_part": attn_part,
            "attn_far": attn_sum.middle,
            "norm": norm,
            "rows_near": mlp_rows.middle,
            "units_low": units_low,
            "units_high": units_high,
            "unit_grads": unit_grads,
            "outputs": outputs,
            "units_far": mlp_sum.middle,
            "residual": residual_back,
            "back_near": back_rows.middle,
            "attend_back": attend_back,
            "normed_part": normed_part,
            "normed_far": normed_sum.middle,
            "embed_grad": embed_back,
            "token_near": token_rows.middle,
        }
        for name, turn in STEPS:
            stages[name](CHUNKS - 1 - turn)

        stage_copy(0).wait()

    lines = (chunk_rows, units)
    keys = (CHUNKS, chunk_rows, 2 * FHD)
    pl.run_scoped(
        layer,
        pltpu.VMEM(lines, BF16),
        pltpu.VMEM(lines, BF16),
        pltpu.VMEM(lines, BF16),
        pltpu.VMEM((chunk_rows, 512), F32),
        pltpu.VMEM((chunk_rows, width), BF16),
        pltpu.VMEM((head_width, chunk_rows), BF16),
        pltpu.VMEM((chunk_rows, head_width), BF16),
        pltpu.VMEM((head_width, chunk_rows), BF16),
        pltpu.VMEM(keys, F32),
        pltpu.VMEM(keys, F32),
        pltpu.VMEM(keys, F32),
        pltpu.VMEM(keys, F32),
    )

    @pl.loop(0, CHUNKS)
    def _(i):
        token_rows.finish(i)
        token_rows.sent(i)
        normed_sum.sent(i)
        back_rows.sent(i)

    for i in range(2):
        mlp_sum.sent(i)
    for other in net.others():
        grad_far(chip, other).wait_send()
    for owner_chip in range(chips):
        grad_near_copy(owner_chip, core).wait_send()


def text_layer(
    group,
    dp_count,
    entry_count,
    entry_ids,
    segments,
    cos_t,
    sin_t,
    bias_full,
    gain_one,
    gain_two,
    w_kv,
    entries,
    weights,
    token_grad,
    w_query,
    w_out,
    w_gate,
    w_up,
    w_down,
):
    chips = group // 2
    chunks, _, chunk_rows = entry_ids.shape
    own_rows = chunk_rows // group
    owned, width = token_grad.shape
    head_width = w_query.shape[1]
    head_count = head_width // FHD
    entry_width = entries.shape[1]
    vmem = pl.BlockSpec(memory_space=pltpu.VMEM)
    hbm = pl.BlockSpec(memory_space=pl.ANY)
    dma = pltpu.SemaphoreType.DMA

    def low(*shape):
        return pltpu.VMEM(shape, BF16)

    return pl.pallas_call(
        partial(text_body, chips, dp_count, entry_count, head_count),
        out_shape=(
            jax.ShapeDtypeStruct((chunks, chunk_rows, width), BF16),
            jax.ShapeDtypeStruct((chunks, own_rows, width), BF16),
            jax.ShapeDtypeStruct((chunks, own_rows, entry_width), BF16),
            jax.ShapeDtypeStruct((chunks, 2, chips, own_rows, entry_width), BF16),
        ),
        in_specs=[vmem] * 8 + [hbm] * 8,
        out_specs=(hbm, vmem, vmem, vmem),
        scratch_shapes=[
            low(*weights.shape[1:]),
            low(*w_query.shape),
            low(*w_out.shape),
            low(*w_gate.shape),
            low(*w_up.shape),
            low(*w_down.shape),
            low(chunks, 2, chips, own_rows, width),
            low(chunks, chips, own_rows, width),
            low(chunks, chips - 1, own_rows, width),
            low(2, 2, chips, own_rows, width),
            low(chunks, chips, own_rows, width),
            low(chunks, chips - 1, own_rows, width),
            low(chunks, 2, chips, own_rows, width),
            low(group, owned, width),
            low(chunks, own_rows, width),
            low(chunks, head_width, chunk_rows),
            low(chunks, chunk_rows, head_width),
            low(chunks, chunk_rows, FHD),
            low(chunks, chunk_rows, FHD),
            low(chunks, FHD, chunk_rows),
            low(chunks, FHD, chunk_rows),
            pltpu.VMEM((chunks, chunk_rows, 1), jnp.int32),
            low(chunks, head_width, chunk_rows),
            pltpu.VMEM((chunks, head_count, 1, chunk_rows), F32),
            pltpu.VMEM((chunks, chunk_rows, chunk_rows), F32),
            pltpu.VMEM((chunks, own_rows, width), F32),
            dma((7,)),
            dma,
            dma,
            dma((3, 2, chunks)),
            dma((3, chunks, chips)),
            dma((3, chunks, chips)),
            dma((3, 2, chunks)),
            dma((3, chunks, chips)),
            dma((3, chunks, chips)),
            dma((2, chips)),
            dma((chips,)),
            dma((chips,)),
        ],
        compiler_params=pltpu.CompilerParams(
            collective_id=0, has_side_effects=True, vmem_limit_bytes=63 * 1024 * 1024
        ),
        cost_estimate=pl.CostEstimate(
            flops=90 * 10**9, bytes_accessed=40 * 10**6, transcendentals=20 * 10**6
        ),
    )(
        entry_ids,
        segments,
        cos_t,
        sin_t,
        bias_full,
        gain_one,
        gain_two,
        w_kv,
        entries,
        weights,
        token_grad,
        w_query,
        w_out,
        w_gate,
        w_up,
        w_down,
    )


def norm_parts(values):
    average = jnp.mean(values, axis=-1, keepdims=True)
    centred = values - average
    scale = lax.rsqrt(jnp.mean(centred * centred, axis=-1, keepdims=True) + 1e-05)
    return centred * scale, scale


def norm_back(values, grad, gain):
    unit, scale = norm_parts(values)
    scaled = grad * gain
    back = scale * (
        scaled
        - jnp.mean(scaled, axis=-1, keepdims=True)
        - unit * jnp.mean(scaled * unit, axis=-1, keepdims=True)
    )
    return (
        back,
        jnp.sum(grad * unit, axis=0, keepdims=True),
        jnp.sum(grad, axis=0, keepdims=True),
    )


def gelu_parts(values):
    root = math.sqrt(2.0 / math.pi)
    squared = values * values
    bent = jnp.tanh(root * values * (1.0 + 0.044715 * squared))
    half = 0.5 * (1.0 + bent)
    slope = half + 0.5 * values * (1.0 - bent * bent) * root * (1.0 + 3 * 0.044715 * squared)
    return values * half, slope


def pool_matrix(counts_col, entries, rows):
    entry = lax.broadcasted_iota(jnp.int32, (entries, rows), 0)
    row = lax.broadcasted_iota(jnp.int32, (entries, rows), 1)
    slots = rows // entries
    inside = (row // slots == entry) & (lax.rem(row, slots).astype(F32) < counts_col)
    return jnp.where(inside, 1.0, 0.0)


def spread_matrix(counts_row, entries, rows):
    row = lax.broadcasted_iota(jnp.int32, (rows, entries), 0)
    entry = lax.broadcasted_iota(jnp.int32, (rows, entries), 1)
    slots = rows // entries
    inside = (row // slots == entry) & (lax.rem(row, slots).astype(F32) < counts_row)
    return jnp.where(inside, 1.0, 0.0)


def slot_bias(valid_col, slots):
    rows = valid_col.shape[0]
    key = lax.broadcasted_iota(jnp.int32, (rows, rows), 0)
    query = lax.broadcasted_iota(jnp.int32, (rows, rows), 1)
    return jnp.where((key // slots == query // slots) & (valid_col > 0.5), 0.0, FAR)


ROW_BLOCK = 256


def shards_of(chips):
    return [(y * 2 + c, c, y) for y in range(chips) for c in range(2)]


def each_shard(chips, columns, body):
    @pl.loop(0, 2)
    def _(c):
        @pl.loop(0, chips)
        def _(y):
            first = pl.multiple_of((y * 2 + c) * columns, columns)
            body(c, y, pl.ds(first, columns))


def hyper_body(
    chips,
    dp_count,
    pieces,
    counts_all,
    gain_one,
    shift_one,
    gain_two,
    shift_two,
    w_query,
    w_key,
    w_value,
    w_out,
    bias_own,
    w_up_hbm,
    w_down_hbm,
    w_proj_hbm,
    entries,
    weights_out,
    attn_in,
    q_n,
    k_n,
    v_n,
    attended,
    logs,
    residual,
    ffn_in,
    counts_col,
    counts_row,
    bias_full,
    full,
    q_t,
    v_t,
    out_t,
    bias,
    hidden,
    counts_scratch,
    local_sem,
    store_sem,
    far_send,
    far_recv,
    x_send,
    x_recv,
    near_send,
    near_recv,
    dp_send,
    dp_recv,
    y_send,
    y_recv,
    last_send,
    last_recv,
    bias_far_send,
    bias_far_recv,
    bias_near,
):
    me = lax.axis_index("mp")
    dp = lax.axis_index("dp")
    chip, core = me // 2, lax.rem(me, 2)
    net = Exchange(chips, chip, core, "mp")
    side = lax.rem(dp, 2)
    mate = dp + 1 - 2 * side
    kinds, _, _, width, columns = full.shape
    sources = (None, w_up_hbm, w_down_hbm, w_proj_hbm)
    rows = pieces.shape[0]
    entry_count = counts_col.shape[0]
    slots = rows // entry_count
    head_columns = columns // 4
    half = width // 2
    heads = width // HD

    flag = pltpu.get_barrier_semaphore()
    pl.semaphore_signal(flag, inc=1, device_id=net.sibling(), device_id_type=MESH)
    for other in net.others():
        pl.semaphore_signal(flag, inc=1, device_id=net.peer(other), device_id_type=MESH)

    @pl.loop(1, dp_count)
    def _(j):
        pl.semaphore_signal(
            flag, inc=1, device_id={"dp": lax.rem(dp + j, dp_count)}, device_id_type=MESH
        )

    local = [
        pltpu.make_async_copy(sources[k], full.at[k, core, chip], local_sem.at[k - 1])
        for k in range(1, kinds)
    ]
    for copy in local:
        copy.start()
    for j, source in enumerate((w_query, w_key, w_value, w_out)):
        full[0, core, chip, :, j * head_columns : (j + 1) * head_columns] = source[...]
    bias_full[core, chip] = bias_own[...]
    pl.semaphore_wait(flag, chips + dp_count - 1)

    def rows_half(which):
        return pl.ds(pl.multiple_of(which * half, half), half)

    def far_copy(k, other):
        return net.to_peer(
            other,
            sources[k].at[rows_half(side)] if k else full.at[0, core, chip, rows_half(side)],
            full.at[k, core, chip, rows_half(side)],
            far_send.at[k, other],
            far_recv.at[k, chip],
        )

    def far_landing(k, other):
        block = full.at[k, core, other, rows_half(side)]
        return net.to_peer(other, block, block, far_send.at[k, other], far_recv.at[k, other])

    def x_copy(k, other, which):
        block = full.at[k, core, other, rows_half(which)]
        return pltpu.make_async_remote_copy(
            src_ref=block,
            dst_ref=block,
            send_sem=x_send.at[k, other],
            recv_sem=x_recv.at[k, other],
            device_id={"dp": mate},
            device_id_type=MESH,
        )

    def near_copy(k, which):
        block = full.at[k, which]
        return net.to_sibling(block, block, near_send.at[k], near_recv.at[k])

    def far_middle(k):
        for other in net.others():
            far_landing(k, other).wait_recv()
            x_copy(k, other, side).start()

    def x_middle(k):
        for other in net.others():
            x_copy(k, other, 1 - side).wait_recv()
        if k:
            local[k - 1].wait()
        near_copy(k, core).start()

    def store(k):
        return pltpu.make_async_copy(full.at[k], weights_out.at[k], store_sem.at[k])

    def near_finish(k):
        near_copy(k, 1 - core).wait_recv()
        store(k).start()

    bias_rows = Gather(
        net, bias_full, (bias_far_send, bias_far_recv, bias_near.at[0], bias_near.at[1]), True
    )
    for k in range(kinds):
        for other in net.others():
            far_copy(k, other).start()
    bias_rows.start(0)
    counts_scratch[...] = column_of(counts_all[...].astype(F32))
    own_counts = counts_scratch[pl.ds(pl.multiple_of(me * entry_count, entry_count), entry_count)]
    counts_col[...] = own_counts
    counts_row[...] = jnp.broadcast_to(own_counts, (entry_count, 128)).T[:1]

    values = pieces[...].astype(F32)
    attn_in[...] = (norm_parts(values)[0] * gain_one[...] + shift_one[...]).astype(BF16)
    blocks = rows // ROW_BLOCK
    valid = jnp.sum(spread_matrix(counts_row[...], entry_count, rows), axis=1, keepdims=True)
    for b in range(blocks):
        bias[b] = slot_bias(valid[b * ROW_BLOCK : (b + 1) * ROW_BLOCK], slots)

    far_middle(0)
    far_middle(1)
    bias_rows.middle(0)
    x_middle(0)
    far_middle(2)
    near_finish(0)
    for m, c, y in shards_of(chips):
        span = slice(m * head_columns, (m + 1) * head_columns)
        projected = dot_nn(attn_in[...], full[0, c, y, :, : 3 * head_columns])
        q_n[:, span] = (projected[:, :head_columns].astype(BF16).astype(F32) * HD**-0.5).astype(
            BF16
        )
        k_n[:, span] = projected[:, head_columns : 2 * head_columns].astype(BF16)
        v_n[:, span] = projected[:, 2 * head_columns :].astype(BF16)
    x_middle(1)
    far_middle(3)
    for b in range(blocks):
        block_rows = slice(b * ROW_BLOCK, (b + 1) * ROW_BLOCK)
        q_t[b] = q_n[block_rows, :].T
        v_t[b] = v_n[block_rows, :].T

    @pl.loop(0, heads // 2)
    def _(pair):
        pair_span = pl.ds(pl.multiple_of(pair * 2 * HD, 2 * HD), 2 * HD)
        for b in range(blocks):
            key_pair = k_n[b * ROW_BLOCK : (b + 1) * ROW_BLOCK, pair_span]
            for odd in range(2):
                h = pair * 2 + odd
                span = pl.ds(pl.multiple_of(h * HD, HD), HD)
                scores = dot_nn(key_pair[:, odd * HD : (odd + 1) * HD], q_t[b, span, :]) + bias[b]
                top = jnp.max(scores, axis=0, keepdims=True)
                weights = jnp.exp(scores - top)
                total = jnp.sum(weights, axis=0, keepdims=True)
                logs[b, h] = top + jnp.log(total)
                out_t[b, span, :] = (dot_nn(v_t[b, span, :], weights.astype(BF16)) / total).astype(
                    BF16
                )

    x_middle(2)
    for b in range(blocks):
        attended[b * ROW_BLOCK : (b + 1) * ROW_BLOCK, :] = out_t[b].T
    total = values
    for m, c, y in shards_of(chips):
        span = slice(m * head_columns, (m + 1) * head_columns)
        total = total + dot_nt(attended[:, span], full[0, c, y, :, 3 * head_columns :])
    residual[...] = total
    ffn_in[...] = (norm_parts(total)[0] * gain_two[...] + shift_two[...]).astype(BF16)
    near_finish(1)
    x_middle(3)
    pool = pool_matrix(counts_col[...], entry_count, rows).astype(BF16)

    def up_shard(c, y, span):
        act = gelu_parts(dot_nn(ffn_in[...], full[1, c, y]))[0]
        hidden[:, span] = dot_nn(pool, act.astype(BF16)).astype(BF16)

    each_shard(chips, columns, up_shard)
    near_finish(2)
    pooled = jnp.sum(
        (residual[...] * valid).reshape(entry_count, slots, width), axis=1
    )
    for m, c, y in shards_of(chips):
        pooled = pooled + dot_nt(hidden[:, m * columns : (m + 1) * columns], full[2, c, y])
    entries[core, chip, dp] = (pooled / counts_col[...]).astype(BF16)

    def dp_copy(block, target, slot):
        piece = entries.at[core, chip, block]
        return pltpu.make_async_remote_copy(
            src_ref=piece,
            dst_ref=piece,
            send_sem=dp_send.at[slot],
            recv_sem=dp_recv.at[block],
            device_id={"dp": target},
            device_id_type=MESH,
        )

    def y_copy(other, owner, block):
        piece = entries.at[core, owner, block]
        return net.to_peer(
            other, piece, piece, y_send.at[other, block], y_recv.at[owner, block]
        )

    @pl.loop(1, dp_count)
    def _(j):
        target = lax.rem(dp + j, dp_count)
        dp_copy(dp, target, target).start()

    for other in net.others():
        y_copy(other, chip, dp).start()
    near_finish(3)
    bias_rows.finish(0)

    @pl.loop(1, dp_count)
    def _(j):
        source = lax.rem(dp + dp_count - j, dp_count)
        dp_copy(source, source, source).wait_recv()
        for other in net.others():
            y_copy(other, chip, source).start()

    def last_copy(part, c, owner):
        piece = entries.at[c, owner]
        return net.to_sibling(piece, piece, last_send.at[part], last_recv.at[owner])

    last_copy(chip, core, chip).start()
    for other in net.others():

        @pl.loop(0, dp_count)
        def _(block):
            y_copy(other, other, block).wait_recv()

        last_copy(other, core, other).start()
    last_copy(chip, 1 - core, chip).wait_recv()
    for other in net.others():
        last_copy(other, 1 - core, other).wait_recv()

    bias_rows.sent(0)
    for k in range(kinds):
        store(k).wait()
        near_copy(k, core).wait_send()
        for other in net.others():
            far_copy(k, other).wait_send()
            x_copy(k, other, side).wait_send()

    @pl.loop(1, dp_count)
    def _(j):
        target = lax.rem(dp + j, dp_count)
        dp_copy(dp, target, target).wait_send()

    last_copy(chip, core, chip).wait_send()
    for other in net.others():
        last_copy(other, core, other).wait_send()

        @pl.loop(0, dp_count)
        def _(block):
            y_copy(other, chip, block).wait_send()


def hyper_forward(
    group,
    dp_count,
    pieces,
    counts,
    gain_one,
    shift_one,
    gain_two,
    shift_two,
    head_weights,
    bias_own,
    unit_weights,
):
    chips = group // 2
    rows, width = pieces.shape
    columns = unit_weights[0].shape[1]
    kinds = 4
    entry_count = counts.shape[1] // group
    heads = width // HD
    blocks = rows // ROW_BLOCK
    vmem = pl.BlockSpec(memory_space=pltpu.VMEM)
    hbm = pl.BlockSpec(memory_space=pl.ANY)
    row_shape = jax.ShapeDtypeStruct((rows, width), BF16)
    dma = pltpu.SemaphoreType.DMA
    return pl.pallas_call(
        partial(hyper_body, chips, dp_count),
        out_shape=(
            jax.ShapeDtypeStruct((2, chips, dp_count, entry_count, width), BF16),
            jax.ShapeDtypeStruct((kinds, 2, chips, width, columns), BF16),
            row_shape,
            row_shape,
            row_shape,
            row_shape,
            row_shape,
            jax.ShapeDtypeStruct((blocks, heads, 1, ROW_BLOCK), F32),
            jax.ShapeDtypeStruct((rows, width), F32),
            row_shape,
            jax.ShapeDtypeStruct((entry_count, 1), F32),
            jax.ShapeDtypeStruct((1, entry_count), F32),
            jax.ShapeDtypeStruct((2, chips, 1, columns), F32),
        ),
        in_specs=[vmem] * 11 + [hbm] * 3,
        out_specs=(vmem, hbm) + (vmem,) * 11,
        scratch_shapes=[
            pltpu.VMEM((kinds, 2, chips, width, columns), BF16),
            pltpu.VMEM((blocks, width, ROW_BLOCK), BF16),
            pltpu.VMEM((blocks, width, ROW_BLOCK), BF16),
            pltpu.VMEM((blocks, width, ROW_BLOCK), BF16),
            pltpu.VMEM((blocks, ROW_BLOCK, ROW_BLOCK), F32),
            pltpu.VMEM((entry_count, columns * group), BF16),
            pltpu.VMEM((counts.shape[1], 1), F32),
            dma((kinds - 1,)),
            dma((kinds,)),
            dma((kinds, chips)),
            dma((kinds, chips)),
            dma((kinds, chips)),
            dma((kinds, chips)),
            dma((kinds,)),
            dma((kinds,)),
            dma((dp_count,)),
            dma((dp_count,)),
            dma((chips, dp_count)),
            dma((chips, dp_count)),
            dma((chips,)),
            dma((chips,)),
            dma((1, chips)),
            dma((1, chips)),
            dma((2, 1)),
        ],
        compiler_params=pltpu.CompilerParams(
            collective_id=1, has_side_effects=True, vmem_limit_bytes=60 * 1024 * 1024
        ),
        cost_estimate=pl.CostEstimate(
            flops=60 * 10**9, bytes_accessed=20 * 10**6, transcendentals=5 * 10**6
        ),
    )(
        pieces,
        counts,
        gain_one,
        shift_one,
        gain_two,
        shift_two,
        *head_weights,
        bias_own,
        *unit_weights,
    )


class Total:
    def __init__(self, net, dp, dp_count, scatter, mine, x_land, z_land, final, sems):
        self.net, self.scatter, self.mine = net, scatter, mine
        self.x_land, self.z_land, self.final = x_land, z_land, final
        self.x_send, self.x_recv, self.z_send, self.z_recv = sems[:4]
        self.g_send, self.g_recv, self.l_send, self.l_recv = sems[4:]
        self.side = lax.rem(dp, 2)
        self.spot = dp // 2
        self.mate = dp + 1 - 2 * self.side
        self.spots = dp_count // 2

    def remote(self, source, target, send, recv, device):
        return pltpu.make_async_remote_copy(
            src_ref=source,
            dst_ref=target,
            send_sem=send,
            recv_sem=recv,
            device_id={"dp": device},
            device_id_type=MESH,
        )

    def x_copy(self, k):
        return self.remote(
            self.mine.at[k, 1 - self.side],
            self.x_land.at[k],
            self.x_send.at[k],
            self.x_recv.at[k],
            self.mate,
        )

    def z_copy(self, k, spot, slot):
        return self.remote(
            self.mine.at[k, self.side, spot],
            self.z_land.at[k, slot],
            self.z_send.at[k, spot],
            self.z_recv.at[k, slot],
            spot * 2 + self.side,
        )

    def g_copy(self, k, spot, owner):
        block = self.final.at[k, self.side, owner]
        return self.remote(
            block, block, self.g_send.at[k, spot], self.g_recv.at[k, owner], spot * 2 + self.side
        )

    def l_copy(self, k, side):
        block = self.final.at[k, side]
        return self.remote(block, block, self.l_send.at[k], self.l_recv.at[k], self.mate)

    def each_spot(self, body):
        if self.spots > 1:

            @pl.loop(1, self.spots)
            def _(j):
                body(lax.rem(self.spot + j, self.spots))

    def start(self, k):
        self.scatter.start(k)

    def near_middle(self, k):
        self.scatter.middle(k)

    def far_middle(self, k):
        total = self.scatter.finish(k)
        self.mine[k] = total.astype(BF16).reshape(self.mine.shape[1:])
        self.x_copy(k).start()

    def x_middle(self, k):
        self.x_copy(k).wait_recv()
        block = self.mine[k, self.side].astype(F32) + self.x_land[k].astype(F32)
        self.mine[k, self.side] = block.astype(BF16)
        self.each_spot(lambda spot: self.z_copy(k, spot, self.spot).start())

    def z_middle(self, k):
        def add(spot):
            self.z_copy(k, spot, spot).wait_recv()

        self.each_spot(add)
        total = self.mine[k, self.side, self.spot].astype(F32)
        for j in range(1, self.spots):
            spot = lax.rem(self.spot + j, self.spots)
            total = total + self.z_land[k, spot].astype(F32)
        self.final[k, self.side, self.spot] = total.astype(BF16)
        self.each_spot(lambda spot: self.g_copy(k, spot, self.spot).start())

    def g_middle(self, k):
        self.each_spot(lambda spot: self.g_copy(k, spot, spot).wait_recv())
        self.l_copy(k, self.side).start()

    def finish(self, k):
        self.l_copy(k, 1 - self.side).wait_recv()

    def sent(self, k):
        self.scatter.sent(k)
        self.x_copy(k).wait_send()
        self.each_spot(lambda spot: self.z_copy(k, spot, self.spot).wait_send())
        self.each_spot(lambda spot: self.g_copy(k, spot, self.spot).wait_send())
        self.l_copy(k, self.side).wait_send()


PARTS = 8


def back_body(
    chips,
    dp_count,
    embed_rows,
    pooled_own,
    token_rows,
    token_row,
    pieces,
    counts_col,
    counts_row,
    gain_one,
    gain_two,
    attn_in,
    q_n,
    k_n,
    v_n,
    attended,
    logs,
    residual,
    ffn_in,
    weights_hbm,
    pieces_grad,
    final,
    small_total,
    weights,
    part,
    near,
    far,
    mine,
    x_land,
    z_land,
    entry_part,
    entry_land,
    hidden,
    hidden_pre,
    ffn_t,
    row_total,
    d_out_n,
    d_query,
    d_key,
    d_value,
    q_t,
    out_t,
    d_out_t,
    k_t,
    d_query_t,
    bias,
    small_near,
    small_far,
    small_dp,
    small_part,
    weight_sem,
    entry_send,
    entry_recv,
    scatter_near,
    scatter_far_send,
    scatter_far_recv,
    x_sem,
    z_send,
    z_recv,
    g_send,
    g_recv,
    l_sem,
    small_sem,
    small_far_send,
    small_far_recv,
    small_dp_send,
    small_dp_recv,
):
    me = lax.axis_index("mp")
    dp = lax.axis_index("dp")
    group = chips * 2
    chip, core = me // 2, lax.rem(me, 2)
    net = Exchange(chips, chip, core, "mp")
    rows, width = pieces.shape
    entry_count = counts_col.shape[0]
    slots = rows // entry_count
    columns = weights.shape[4]
    half_columns = columns // 2
    head_columns = columns // 4
    heads = width // HD
    blocks = rows // ROW_BLOCK
    total_sum = Total(
        net,
        dp,
        dp_count,
        Scatter(
            net,
            part,
            near,
            far,
            (scatter_near.at[0], scatter_near.at[1], scatter_far_send, scatter_far_recv),
        ),
        mine,
        x_land,
        z_land,
        final,
        (x_sem.at[0], x_sem.at[1], z_send, z_recv, g_send, g_recv, l_sem.at[0], l_sem.at[1]),
    )
    stages = (
        total_sum.near_middle,
        total_sum.far_middle,
        total_sum.x_middle,
        total_sum.z_middle,
        total_sum.g_middle,
        total_sum.finish,
    )

    def run(step):
        for offset, stage in enumerate(stages):
            if 0 <= step - offset < PARTS:
                stage(step - offset)

    flag = pltpu.get_barrier_semaphore()
    pl.semaphore_signal(flag, inc=1, device_id=net.sibling(), device_id_type=MESH)
    for other in net.others():
        pl.semaphore_signal(flag, inc=1, device_id=net.peer(other), device_id_type=MESH)

    def each_dp(body):
        @pl.loop(1, dp_count)
        def _(j):
            body(lax.rem(dp + j, dp_count))

    each_dp(
        lambda target: pl.semaphore_signal(
            flag, inc=1, device_id={"dp": target}, device_id_type=MESH
        )
    )
    loads = [
        pltpu.make_async_copy(weights_hbm.at[k], weights.at[k], weight_sem.at[k])
        for k in (1, 2, 0)
    ]
    for copy in loads:
        copy.start()
    pl.semaphore_wait(flag, chips + dp_count - 1)

    def put(k, c, y, values):
        part[k, c, y] = values[:, :half_columns].astype(BF16)
        part[k + 1, c, y] = values[:, half_columns:].astype(BF16)

    token_total = token_rows.shape[0]
    dp_step = max(1, ROW_BLOCK // entry_count)

    @pl.loop(0, dp_count // dp_step)
    def _(block):
        row = lax.broadcasted_iota(jnp.int32, (dp_step * entry_count, token_total), 0)
        owner = block * dp_step + row // entry_count
        number = (owner * group + me) * entry_count + lax.rem(row, entry_count)
        chosen = jnp.where(number == token_row[...], 1.0, 0.0).astype(BF16)
        sums = dot_nn(chosen, token_rows[...]).astype(BF16)
        for j in range(dp_step):
            entry_part[block * dp_step + j] = sums[j * entry_count : (j + 1) * entry_count]

    def entry_copy(target, slot):
        return pltpu.make_async_remote_copy(
            src_ref=entry_part.at[target],
            dst_ref=entry_land.at[slot],
            send_sem=entry_send.at[target],
            recv_sem=entry_recv.at[slot],
            device_id={"dp": target},
            device_id_type=MESH,
        )

    each_dp(lambda target: entry_copy(target, dp).start())
    pooled_t = pooled_own[...].T

    def proj_shard(c, y, span):
        put(0, c, y, dot_nn(pooled_t, embed_rows[:, span]))

    each_shard(chips, columns, proj_shard)
    total_sum.start(0)
    total_sum.start(1)
    bias_sums = jnp.sum(embed_rows[...].astype(F32), axis=0, keepdims=True)
    for j in range(4):
        small_part[4 + j : 5 + j, :] = bias_sums[:, j * width : (j + 1) * width]
    loads[0].wait()
    run(0)

    pool = pool_matrix(counts_col[...], entry_count, rows).astype(BF16)
    spread = spread_matrix(counts_row[...], entry_count, rows)
    valid = jnp.sum(spread, axis=1, keepdims=True)
    spread = spread.astype(BF16)
    for b in range(blocks):
        bias[b] = slot_bias(valid[b * ROW_BLOCK : (b + 1) * ROW_BLOCK], slots)
    ffn_t[...] = ffn_in[...].T

    def hidden_shard(c, y, span):
        before = dot_nn(ffn_in[...], weights[1, c, y])
        hidden_pre[:, span] = before
        hidden[:, span] = dot_nn(pool, gelu_parts(before)[0].astype(BF16)).astype(BF16)

    each_shard(chips, columns, hidden_shard)
    run(1)
    each_dp(lambda source: entry_copy(source, source).wait_recv())
    pooled_grad = entry_part[dp].astype(F32)
    for j in range(1, dp_count):
        pooled_grad = pooled_grad + entry_land[lax.rem(dp + j, dp_count)].astype(F32)
    entry_low = (pooled_grad / counts_col[...]).astype(BF16)
    out_rows = dot_nn(spread, entry_low)
    entry_t = entry_low.T
    loads[1].wait()
    out_low = out_rows.astype(BF16)
    row_total[...] = jnp.zeros_like(row_total)

    def unit_shard(c, y, span):
        put(2, c, y, dot_nn(entry_t, hidden[:, span]))
        act_grad = dot_nn(out_low, weights[2, c, y])
        pre_grad = (act_grad * gelu_parts(hidden_pre[:, span])[1]).astype(BF16)
        put(4, c, y, dot_nn(ffn_t[...], pre_grad))
        row_total[...] += dot_nt(pre_grad, weights[1, c, y])

    each_shard(chips, columns, unit_shard)
    for k in (2, 3, 4, 5):
        total_sum.start(k)
    run(2)
    back, gain_grad, shift_grad = norm_back(residual[...], row_total[...], gain_two[...])
    small_part[2:3, :] = gain_grad
    small_part[3:4, :] = shift_grad
    residual_grad = out_rows + back
    pieces_grad[...] = residual_grad
    attn_grad = residual_grad.astype(BF16)
    loads[2].wait()
    for m, c, y in shards_of(chips):
        span = slice(m * head_columns, (m + 1) * head_columns)
        d_out_n[:, span] = dot_nn(attn_grad, weights[0, c, y, :, 3 * head_columns :]).astype(BF16)
    out_grad = dot_nn(attn_grad.T, attended[...])
    for m, c, y in shards_of(chips):
        span = slice(m * head_columns, (m + 1) * head_columns)
        part[7, c, y, :, head_columns:] = out_grad[:, span].astype(BF16)
    for b in range(blocks):
        block_rows = slice(b * ROW_BLOCK, (b + 1) * ROW_BLOCK)
        q_t[b] = q_n[block_rows, :].T
        k_t[b] = k_n[block_rows, :].T
        out_t[b] = attended[block_rows, :].T
        d_out_t[b] = d_out_n[block_rows, :].T
    run(3)

    @pl.loop(0, heads // 2)
    def _(pair):
        pair_span = pl.ds(pl.multiple_of(pair * 2 * HD, 2 * HD), 2 * HD)
        for b in range(blocks):
            block_rows = slice(b * ROW_BLOCK, (b + 1) * ROW_BLOCK)
            key_pair = k_n[block_rows, pair_span]
            value_pair = v_n[block_rows, pair_span]
            query_pair = q_n[block_rows, pair_span]
            grad_pair = d_out_n[block_rows, pair_span]
            key_sums, value_sums = [], []
            for odd in range(2):
                h = pair * 2 + odd
                span = pl.ds(pl.multiple_of(h * HD, HD), HD)
                lanes = slice(odd * HD, (odd + 1) * HD)
                scores = dot_nn(key_pair[:, lanes], q_t[b, span, :]) + bias[b]
                probs = jnp.exp(scores - logs[b, h])
                grad_t = d_out_t[b, span, :]
                centre = jnp.sum(
                    grad_t.astype(F32) * out_t[b, span, :].astype(F32), axis=0, keepdims=True
                )
                value_sums.append(dot_nn(probs.astype(BF16), grad_pair[:, lanes]))
                score_grad = (probs * (dot_nn(value_pair[:, lanes], grad_t) - centre)).astype(BF16)
                key_sums.append(dot_nn(score_grad, query_pair[:, lanes]))
                d_query_t[b, span, :] = (
                    dot_nn(k_t[b, span, :], score_grad) * (HD**-0.5)
                ).astype(BF16)
            d_key[block_rows, pair_span] = jnp.concatenate(key_sums, axis=1).astype(BF16)
            d_value[block_rows, pair_span] = jnp.concatenate(value_sums, axis=1).astype(BF16)

    for b in range(blocks):
        d_query[b * ROW_BLOCK : (b + 1) * ROW_BLOCK, :] = d_query_t[b].T
    run(4)
    rows_t = attn_in[...].T
    for place, (k, lanes, source) in enumerate(
        ((6, 0, d_query), (6, 1, d_key), (7, 0, d_value))
    ):
        grads = dot_nn(rows_t, source[...])
        for m, c, y in shards_of(chips):
            span = slice(m * head_columns, (m + 1) * head_columns)
            part[k, c, y, :, lanes * head_columns : (lanes + 1) * head_columns] = grads[
                :, span
            ].astype(BF16)
    total_sum.start(6)
    total_sum.start(7)
    normed = jnp.zeros((rows, width), F32)
    for m, c, y in shards_of(chips):
        span = slice(m * head_columns, (m + 1) * head_columns)
        for j, source in enumerate((d_query, d_key, d_value)):
            normed = normed + dot_nt(
                source[:, span], weights[0, c, y, :, j * head_columns : (j + 1) * head_columns]
            )
    back, gain_grad, shift_grad = norm_back(pieces[...].astype(F32), normed, gain_one[...])
    small_part[0:1, :] = gain_grad
    small_part[1:2, :] = shift_grad
    pieces_grad[...] += back

    small_copy = net.to_sibling(small_part, small_near, small_sem.at[0], small_sem.at[1])
    small_copy.start()

    def small_far_copy(other, owner):
        return net.to_peer(
            other,
            small_far.at[owner],
            small_far.at[owner],
            small_far_send.at[other],
            small_far_recv.at[owner],
        )

    def small_dp_copy(other, owner):
        return pltpu.make_async_remote_copy(
            src_ref=small_dp.at[owner],
            dst_ref=small_dp.at[owner],
            send_sem=small_dp_send.at[other],
            recv_sem=small_dp_recv.at[owner],
            device_id={"dp": other},
            device_id_type=MESH,
        )

    def small_near_done():
        small_copy.wait_recv()
        small_far[chip] = small_part[...] + small_near[...]
        for other in net.others():
            small_far_copy(other, chip).start()

    def small_far_done():
        for other in net.others():
            small_far_copy(other, other).wait_recv()
        total = small_far[0]
        for j in range(1, chips):
            total = total + small_far[j]
        small_dp[dp] = total
        each_dp(lambda other: small_dp_copy(other, dp).start())

    @pl.loop(5, PARTS + 5)
    def _(step):
        for offset, stage in enumerate(stages):
            k = step - offset

            @pl.when((k >= 0) & (k < PARTS))
            def _():
                stage(k)

        pl.when(step == 5)(small_near_done)
        pl.when(step == 7)(small_far_done)

    each_dp(lambda other: small_dp_copy(other, other).wait_recv())
    total = small_dp[0]
    for j in range(1, dp_count):
        total = total + small_dp[j]
    small_total[...] = total

    small_copy.wait_send()
    for other in net.others():
        small_far_copy(other, chip).wait_send()
    each_dp(lambda other: small_dp_copy(other, dp).wait_send())
    each_dp(lambda other: entry_copy(other, dp).wait_send())

    @pl.loop(0, PARTS)
    def _(k):
        total_sum.sent(k)


def hyper_backward(
    group,
    dp_count,
    embed_rows,
    pooled_own,
    token_rows,
    token_row,
    pieces,
    counts_col,
    counts_row,
    gain_one,
    gain_two,
    saved,
    weights,
):
    chips = group // 2
    rows, width = pieces.shape
    entry_count = counts_col.shape[0]
    kinds, columns = weights.shape[0], weights.shape[4]
    half_columns = columns // 2
    heads = width // HD
    blocks = rows // ROW_BLOCK
    spots = dp_count // 2
    vmem = pl.BlockSpec(memory_space=pltpu.VMEM)
    hbm = pl.BlockSpec(memory_space=pl.ANY)
    dma = pltpu.SemaphoreType.DMA
    final = (PARTS, 2, spots, width // (2 * spots), half_columns)
    units = columns * group

    def low(*shape):
        return pltpu.VMEM(shape, BF16)

    def wide(*shape):
        return pltpu.VMEM(shape, F32)

    return pl.pallas_call(
        partial(back_body, chips, dp_count),
        out_shape=(
            jax.ShapeDtypeStruct((rows, width), F32),
            jax.ShapeDtypeStruct(final, BF16),
            jax.ShapeDtypeStruct((8, width), F32),
        ),
        in_specs=[vmem] * 17 + [hbm],
        out_specs=(vmem, vmem, vmem),
        scratch_shapes=[
            low(kinds, 2, chips, width, columns),
            low(PARTS, 2, chips, width, half_columns),
            low(PARTS, chips, width, half_columns),
            low(PARTS, chips - 1, width, half_columns),
            low(*final),
            low(PARTS, spots, width // (2 * spots), half_columns),
            low(PARTS, spots, width // (2 * spots), half_columns),
            low(dp_count, entry_count, width),
            low(dp_count, entry_count, width),
            low(entry_count, units),
            wide(rows, units),
            low(width, rows),
            wide(rows, width),
            low(rows, width),
            low(rows, width),
            low(rows, width),
            low(rows, width),
        ]
        + [low(blocks, width, ROW_BLOCK)] * 5
        + [
            wide(blocks, ROW_BLOCK, ROW_BLOCK),
            wide(8, width),
            wide(chips, 8, width),
            wide(dp_count, 8, width),
            wide(8, width),
            dma((kinds,)),
            dma((dp_count,)),
            dma((dp_count,)),
            dma((2, PARTS)),
            dma((PARTS, chips)),
            dma((PARTS, chips)),
            dma((2, PARTS)),
            dma((PARTS, spots)),
            dma((PARTS, spots)),
            dma((PARTS, spots)),
            dma((PARTS, spots)),
            dma((2, PARTS)),
            dma((2,)),
            dma((chips,)),
            dma((chips,)),
            dma((dp_count,)),
            dma((dp_count,)),
        ],
        compiler_params=pltpu.CompilerParams(
            collective_id=2, has_side_effects=True, vmem_limit_bytes=62 * 1024 * 1024
        ),
        cost_estimate=pl.CostEstimate(
            flops=60 * 10**9, bytes_accessed=20 * 10**6, transcendentals=5 * 10**6
        ),
    )(
        embed_rows,
        pooled_own,
        token_rows,
        token_row,
        pieces,
        counts_col,
        counts_row,
        gain_one,
        gain_two,
        *saved,
        weights,
    )


def spread_body(sums, query, key, value, out, up, down, proj):
    half_columns = sums.shape[2]
    head_columns = query.shape[1]
    for first, target in ((0, proj), (2, down), (4, up)):
        target[:, :half_columns] = sums[first].astype(F32)
        target[:, half_columns:] = sums[first + 1].astype(F32)
    for k, lanes, target in ((6, 0, query), (6, 1, key), (7, 0, value), (7, 1, out)):
        target[...] = sums[k, :, lanes * head_columns : (lanes + 1) * head_columns].astype(F32)


def spread_sums(sums):
    _, width, half_columns = sums.shape
    small = jax.ShapeDtypeStruct((width, half_columns // 2), F32)
    large = jax.ShapeDtypeStruct((width, half_columns * 2), F32)
    vmem = pl.BlockSpec(memory_space=pltpu.VMEM)
    return pl.pallas_call(
        spread_body,
        out_shape=(small,) * 4 + (large,) * 3,
        in_specs=[vmem],
        out_specs=(vmem,) * 7,
        compiler_params=pltpu.CompilerParams(vmem_limit_bytes=40 * 1024 * 1024),
    )(sums)


def on_device(
    pieces,
    counts,
    entry_ids,
    segment_ids,
    norm1_gain,
    norm1_shift,
    query_weight,
    key_weight,
    value_weight,
    out_weight,
    norm2_gain,
    norm2_shift,
    up_weight,
    down_weight,
    proj_weight,
    proj_bias,
    text_norm1_gain,
    text_query,
    text_key,
    text_value,
    text_out_proj,
    text_norm2_gain,
    text_gate,
    text_up,
    text_down,
    token_grad,
):
    group, dp_count = lax.axis_size("mp"), lax.axis_size("dp")
    me = lax.axis_index("mp")
    entry_count, slot_count, width = pieces.shape
    text_width = token_grad.shape[1]
    length = segment_ids.shape[1]
    chunk_rows = length // CHUNKS
    pieces_rows = pieces.reshape(entry_count * slot_count, width)
    entries, weights, *saved, counts_col, counts_row, bias_full = hyper_forward(
        group,
        dp_count,
        pieces_rows,
        counts[None, :],
        norm1_gain[None, :],
        norm1_shift[None, :],
        norm2_gain[None, :],
        norm2_shift[None, :],
        (query_weight, key_weight, value_weight, out_weight),
        proj_bias[None, :],
        (up_weight, down_weight, proj_weight),
    )
    head_width = text_query.shape[1]
    kv_index = me * (head_width // FHD) // (QHEADS // KVHEADS)
    key_local = lax.dynamic_slice_in_dim(text_key, kv_index * FHD, FHD, 1)
    value_local = lax.dynamic_slice_in_dim(text_value, kv_index * FHD, FHD, 1)
    key_value = jnp.concatenate([key_local, value_local], axis=1)
    cos_t, sin_t = rope_tables(length)
    out_part, embed_rows, pooled_own, token_rows = text_layer(
        group,
        dp_count,
        entry_count,
        entry_ids.reshape(CHUNKS, 1, chunk_rows),
        segment_ids.reshape(CHUNKS, 1, chunk_rows),
        cos_t,
        sin_t,
        bias_full,
        text_norm1_gain[None, :],
        text_norm2_gain[None, :],
        key_value,
        entries.reshape(-1, width),
        weights,
        token_grad,
        text_query,
        text_out_proj,
        text_gate,
        text_up,
        text_down,
    )
    text_out = lax.psum_scatter(
        out_part.reshape(length, text_width), "mp", scatter_dimension=0, tiled=True
    ).astype(jnp.float32)
    pieces_grad, final, small = hyper_backward(
        group,
        dp_count,
        embed_rows.reshape(-1, text_width),
        pooled_own.reshape(-1, width),
        token_rows.reshape(length, width),
        entry_ids[None, :],
        pieces_rows,
        counts_col,
        counts_row,
        norm1_gain[None, :],
        norm2_gain[None, :],
        saved,
        weights,
    )
    query_grad, key_grad, value_grad, out_grad, up_grad, down_grad, proj_grad = spread_sums(
        final.reshape(PARTS, width, -1)
    )
    bias_share = proj_bias.shape[0]
    proj_bias_grad = lax.dynamic_slice_in_dim(
        small[4:].reshape(-1), me * bias_share, bias_share
    )
    return (
        text_out,
        pieces_grad.reshape(pieces.shape),
        small[0],
        small[1],
        query_grad,
        key_grad,
        value_grad,
        out_grad,
        small[2],
        small[3],
        up_grad,
        down_grad,
        proj_grad,
        proj_bias_grad,
    )


def solution(mesh):
    return jax.shard_map(
        on_device,
        mesh=mesh,
        in_specs=(
            P(("dp", "mp"), None, None),
            P("dp"),
            P("dp"),
            P("dp", None),
            P(),
            P(),
            P(None, "mp"),
            P(None, "mp"),
            P(None, "mp"),
            P(None, "mp"),
            P(),
            P(),
            P(None, "mp"),
            P(None, "mp"),
            P(None, "mp"),
            P("mp"),
            P(),
            P(None, "mp"),
            P(),
            P(),
            P(None, "mp"),
            P(),
            P(None, "mp"),
            P(None, "mp"),
            P(None, "mp"),
            P(("dp", "mp"), None),
        ),
        out_specs=(
            P(("dp", "mp"), None),
            P(("dp", "mp"), None, None),
            P(),
            P(),
            P(None, "mp"),
            P(None, "mp"),
            P(None, "mp"),
            P(None, "mp"),
            P(),
            P(),
            P(None, "mp"),
            P(None, "mp"),
            P(None, "mp"),
            P("mp"),
        ),
        check_vma=False,
    )
```

```python
from functools import partial
import math

import jax
import jax.numpy as jnp
import numpy as np
from jax import lax
from jax.experimental import pallas as pl
from jax.experimental.pallas import tpu as pltpu
from jax.sharding import PartitionSpec as P

HD = 64
QHEADS = 32
KVHEADS = 4
FHD = 64


def rope_tables(length):
    positions = np.arange(length, dtype=np.float32)
    rates = np.exp(
        np.arange(FHD // 2, dtype=np.float32) * np.float32(-2.0 * math.log(10000.0) / FHD)
    ).astype(np.float32)
    angles = (positions[None, :] * rates[:, None]).reshape(FHD // 2, CHUNKS, length // CHUNKS)
    angles = angles.transpose(1, 0, 2)
    return jnp.asarray(np.cos(angles)), jnp.asarray(np.sin(angles))


MESH = pl.DeviceIdType.MESH
F32 = jnp.float32
BF16 = jnp.bfloat16
CHUNKS = 4
FAR = -1e30


def dot_nn(a, b):
    return lax.dot_general(a, b, (((1,), (0,)), ((), ())), preferred_element_type=F32)


def dot_nt(a, b):
    return lax.dot_general(a, b, (((1,), (1,)), ((), ())), preferred_element_type=F32)


def column_tiles(total, width, body):
    full = total // width
    if full > 0:

        @pl.loop(0, full)
        def _(t):
            body(pl.ds(pl.multiple_of(t * width, width), width))

    if total % width:
        body(pl.ds(full * width, total % width))


def rms_scale(values):
    return lax.rsqrt(jnp.mean(values * values, axis=-1, keepdims=True) + 1e-05)


def rms_back(values, grad, gain):
    scale = rms_scale(values)
    scaled = grad * gain
    return scale * (
        scaled - values * (scale * scale) * jnp.mean(scaled * values, axis=-1, keepdims=True)
    )


class Exchange:
    def __init__(self, chips, chip, core, group_axis):
        self.chips, self.chip, self.core = chips, chip, core
        self.axis = group_axis

    def sibling(self):
        return {self.axis: self.chip * 2 + 1 - self.core}

    def peer(self, other):
        return {self.axis: other * 2 + self.core}

    def others(self):
        return [lax.rem(self.chip + step, self.chips) for step in range(1, self.chips)]

    def barrier(self):
        flag = pltpu.get_barrier_semaphore()
        pl.semaphore_signal(flag, inc=1, device_id=self.sibling(), device_id_type=MESH)
        for other in self.others():
            pl.semaphore_signal(flag, inc=1, device_id=self.peer(other), device_id_type=MESH)
        pl.semaphore_wait(flag, self.chips)

    def to_sibling(self, source, target, send, recv):
        return pltpu.make_async_remote_copy(
            src_ref=source,
            dst_ref=target,
            send_sem=send,
            recv_sem=recv,
            device_id=self.sibling(),
            device_id_type=MESH,
        )

    def to_peer(self, other, source, target, send, recv):
        return pltpu.make_async_remote_copy(
            src_ref=source,
            dst_ref=target,
            send_sem=send,
            recv_sem=recv,
            device_id=self.peer(other),
            device_id_type=MESH,
        )


class Scatter:
    def __init__(self, net, part, near, far, sems):
        self.net, self.part, self.near, self.far = net, part, near, far
        self.slots = None if part.shape[0] == near.shape[0] else part.shape[0]
        self.near_send, self.near_recv, self.far_send, self.far_recv = sems

    def slot(self, i):
        return i if self.slots is None else i % self.slots

    def landing(self, source, target):
        return lax.rem(source - target + self.net.chips - 1, self.net.chips)

    def near_copy(self, i):
        net = self.net
        return net.to_sibling(
            self.part.at[self.slot(i), 1 - net.core],
            self.near.at[i],
            self.near_send.at[i],
            self.near_recv.at[i],
        )

    def far_copy(self, i, other):
        net = self.net
        return net.to_peer(
            other,
            self.part.at[self.slot(i), net.core, other],
            self.far.at[i, self.landing(net.chip, other)],
            self.far_send.at[i, other],
            self.far_recv.at[i, net.chip],
        )

    def far_landing(self, i, other):
        net = self.net
        return net.to_peer(
            other,
            self.part.at[self.slot(i), net.core, other],
            self.far.at[i, self.landing(other, net.chip)],
            self.far_send.at[i, other],
            self.far_recv.at[i, other],
        )

    def start(self, i):
        self.near_copy(i).start()

    def middle(self, i):
        net = self.net
        self.near_copy(i).wait_recv()
        slot = self.slot(i)
        for other in net.others():
            total = self.part[slot, net.core, other].astype(F32) + self.near[
                i, other
            ].astype(F32)
            self.part[slot, net.core, other] = total.astype(BF16)
            self.far_copy(i, other).start()

    def finish(self, i):
        net = self.net
        slot = self.slot(i)
        total = self.part[slot, net.core, net.chip].astype(F32) + self.near[
            i, net.chip
        ].astype(F32)
        for other in net.others():
            self.far_landing(i, other).wait_recv()
            total = total + self.far[i, self.landing(other, net.chip)].astype(F32)
        return total

    def sent(self, i):
        self.near_copy(i).wait_send()
        for other in self.net.others():
            self.far_copy(i, other).wait_send()


class Gather:
    def __init__(self, net, full, sems, single=False):
        self.net, self.full, self.single = net, full, single
        self.far_send, self.far_recv, self.near_send, self.near_recv = sems

    def block(self, i, *place):
        return self.full.at[place] if self.single else self.full.at[(i, *place)]

    def far_copy(self, i, other):
        net = self.net
        block = self.block(i, net.core, net.chip)
        return net.to_peer(
            other, block, block, self.far_send.at[i, other], self.far_recv.at[i, net.chip]
        )

    def far_landing(self, i, other):
        net = self.net
        block = self.block(i, net.core, other)
        return net.to_peer(
            other, block, block, self.far_send.at[i, other], self.far_recv.at[i, other]
        )

    def near_copy(self, i):
        block = self.block(i, self.net.core)
        return self.net.to_sibling(block, block, self.near_send.at[i], self.near_recv.at[i])

    def near_landing(self, i):
        block = self.block(i, 1 - self.net.core)
        return self.net.to_sibling(block, block, self.near_send.at[i], self.near_recv.at[i])

    def start(self, i):
        for other in self.net.others():
            self.far_copy(i, other).start()

    def middle(self, i):
        for other in self.net.others():
            self.far_landing(i, other).wait_recv()
        self.near_copy(i).start()

    def finish(self, i):
        self.near_landing(i).wait_recv()

    def sent(self, i):
        for other in self.net.others():
            self.far_copy(i, other).wait_send()
        self.near_copy(i).wait_send()


STEPS = (
    ("attend", 0),
    ("attn_part", 0),
    ("attend", 2),
    ("attn_far", 0),
    ("attend", 1),
    ("attn_part", 1),
    ("norm", 0),
    ("attn_part", 2),
    ("attn_far", 1),
    ("attend", 3),
    ("rows_near", 0),
    ("attn_part", 3),
    ("attn_far", 2),
    ("units_low", 0),
    ("norm", 1),
    ("units_high", 0),
    ("unit_grads", 0),
    ("attn_far", 3),
    ("outputs", 0),
    ("rows_near", 1),
    ("norm", 2),
    ("units_far", 0),
    ("units_low", 1),
    ("units_high", 1),
    ("outputs", 1),
    ("norm", 3),
    ("rows_near", 2),
    ("unit_grads", 1),
    ("units_low", 2),
    ("residual", 0),
    ("units_high", 2),
    ("outputs", 2),
    ("rows_near", 3),
    ("units_far", 1),
    ("unit_grads", 2),
    ("units_low", 3),
    ("back_near", 0),
    ("units_far", 2),
    ("residual", 1),
    ("units_high", 3),
    ("unit_grads", 3),
    ("units_far", 3),
    ("residual", 2),
    ("attend_back", 0),
    ("back_near", 1),
    ("normed_part", 0),
    ("back_near", 2),
    ("attend_back", 1),
    ("residual", 3),
    ("normed_part", 1),
    ("normed_far", 0),
    ("outputs", 3),
    ("normed_far", 1),
    ("attend_back", 2),
    ("back_near", 3),
    ("embed_grad", 0),
    ("normed_part", 2),
    ("attend_back", 3),
    ("normed_far", 2),
    ("normed_part", 3),
    ("token_near", 0),
    ("embed_grad", 1),
    ("normed_far", 3),
    ("embed_grad", 2),
    ("token_near", 1),
    ("token_near", 2),
    ("embed_grad", 3),
    ("token_near", 3),
)


def column_of(row):
    return jnp.broadcast_to(row, (8, row.shape[1])).T[:, :1]


def text_body(
    chips,
    dp_count,
    entry_count,
    head_count,
    entry_ids,
    segments,
    cos_t,
    sin_t,
    bias_full,
    gain_one,
    gain_two,
    w_kv,
    entries_hbm,
    weights_hbm,
    token_grad,
    w_query_hbm,
    w_out_hbm,
    w_gate_hbm,
    w_up_hbm,
    w_down_hbm,
    out_part,
    embed_grad,
    pooled_own,
    token_full,
    proj,
    w_query,
    w_out,
    w_gate,
    w_up,
    w_down,
    part_a,
    near_a,
    far_a,
    part_b,
    near_b,
    far_b,
    full,
    grad_full,
    embeds_own,
    q_t,
    q_n,
    k_n,
    v_n,
    k_t,
    v_t,
    out_t,
    logs,
    bias,
    residual,
    weight_sem,
    local_sem,
    stage_sem,
    scatter_near,
    scatter_far_send,
    scatter_far_recv,
    gather_near,
    gather_far_send,
    gather_far_recv,
    grad_near,
    grad_far_send,
    grad_far_recv,
):
    me = lax.axis_index("mp")
    chip, core = me // 2, lax.rem(me, 2)
    net = Exchange(chips, chip, core, "mp")
    group = chips * 2
    chunk_rows = q_n.shape[1]
    width = embeds_own.shape[2]
    units = w_gate.shape[1]
    own_rows = embeds_own.shape[1]
    head_width = FHD * head_count
    columns = proj.shape[3]
    entry_total, entry_width = entries_hbm.shape
    owned = token_grad.shape[0]
    first_own = pl.multiple_of((core * chips + chip) * own_rows, own_rows)
    owners = group // CHUNKS if group > CHUNKS else 1

    def scatter_of(kind, part, near, far):
        return Scatter(
            net,
            part,
            near,
            far,
            (
                scatter_near.at[kind, 0],
                scatter_near.at[kind, 1],
                scatter_far_send.at[kind],
                scatter_far_recv.at[kind],
            ),
        )

    def gather_of(kind, ref):
        return Gather(
            net,
            ref,
            (
                gather_far_send.at[kind],
                gather_far_recv.at[kind],
                gather_near.at[kind, 0],
                gather_near.at[kind, 1],
            ),
        )

    attn_sum = scatter_of(0, part_a, near_a, far_a)
    mlp_sum = scatter_of(1, part_b, near_b, far_b)
    normed_sum = scatter_of(2, part_a, near_a, far_a)
    mlp_rows = gather_of(0, full)
    back_rows = gather_of(1, full)
    token_rows = gather_of(2, token_full)

    def load(k, source, target):
        return pltpu.make_async_copy(source, target, weight_sem.at[k])

    load_proj = load(1, weights_hbm.at[3], proj)
    load_query = load(2, w_query_hbm, w_query)
    load_out = load(3, w_out_hbm, w_out)
    load_units = [
        load(4, w_gate_hbm, w_gate),
        load(5, w_up_hbm, w_up),
        load(6, w_down_hbm, w_down),
    ]

    def grad_far(owner_chip, other):
        return net.to_peer(
            other,
            token_grad,
            grad_full.at[owner_chip * 2 + core],
            grad_far_send.at[other],
            grad_far_recv.at[owner_chip],
        )

    def grad_near_copy(owner_chip, owner_core):
        block = grad_full.at[owner_chip * 2 + owner_core]
        return net.to_sibling(
            block, block, grad_near.at[0, owner_chip], grad_near.at[1, owner_chip]
        )

    grad_local = pltpu.make_async_copy(token_grad, grad_full.at[me], local_sem)

    def grad_start():
        for other in net.others():
            grad_far(chip, other).start()

    def grad_middle():
        grad_local.wait()
        grad_near_copy(chip, core).start()
        for other in net.others():
            grad_far(other, other).wait_recv()
            grad_near_copy(other, core).start()

    def grad_chunk(i):
        return grad_full[i * owners : (i + 1) * owners].reshape(chunk_rows, width)

    def grad_finish(i):
        for owner in range(i * owners, (i + 1) * owners):

            @pl.when(core != owner % 2)
            def _():
                grad_near_copy(owner // 2, owner % 2).wait_recv()

    def embed(entries, pooled, embeds):
        load_entries = load(0, entries_hbm, entries)
        load_entries.start()
        for copy in (load_proj, load_query, load_out, *load_units):
            copy.start()
        grad_local.start()
        net.barrier()
        pl.when(core == 1)(grad_start)
        load_entries.wait()
        load_proj.wait()
        load_query.wait()

        @pl.loop(0, CHUNKS)
        def _(i):
            ids = entry_ids[i]
            owner = ids // entry_count
            owner_mp, owner_dp = lax.rem(owner, group), owner // group
            place = (lax.rem(owner_mp, 2) * chips + owner_mp // 2) * dp_count + owner_dp
            spots = column_of(
                (place * entry_count + lax.rem(ids, entry_count)).astype(F32)
            ).astype(jnp.int32)
            numbers = lax.broadcasted_iota(jnp.int32, (chunk_rows, entry_total), 1)
            chosen = jnp.where(numbers == spots, 1.0, 0.0).astype(BF16)
            pooled[...] = dot_nn(chosen, entries[...]).astype(BF16)
            pooled_own[i] = pooled[pl.ds(first_own, own_rows), :]
            for m, c, y in shards_of(chips):
                span = slice(m * columns, (m + 1) * columns)
                embeds[:, span] = (dot_nn(pooled[...], proj[c, y]) + bias_full[c, y]).astype(BF16)
            embeds_own[i] = embeds[pl.ds(first_own, own_rows), :]
            values = embeds[...].astype(F32)
            embeds[...] = (values * rms_scale(values) * gain_one[...]).astype(BF16)
            cosine, sine = cos_t[i], sin_t[i]

            def turned(block):
                low_half, high_half = block[: FHD // 2], block[FHD // 2 :]
                return jnp.concatenate(
                    [low_half * cosine - high_half * sine, high_half * cosine + low_half * sine],
                    axis=0,
                )

            queries = dot_nn(embeds[...], w_query[...]).T
            for h in range(head_count):
                span = slice(h * FHD, (h + 1) * FHD)
                q_t[i, span, :] = (
                    turned(queries[span]).astype(BF16).astype(F32) * FHD**-0.5
                ).astype(BF16)
            q_n[i] = q_t[i].T
            both = dot_nn(embeds[...], w_kv[...])
            keys_t = turned(both.T[:FHD]).astype(BF16)
            k_t[i] = keys_t
            k_n[i] = keys_t.T
            v_n[i] = both[:, FHD:].astype(BF16)
            v_t[i] = both.T[FHD:].astype(BF16)

        pl.when(core == 0)(grad_start)
        pl.when(core == 1)(grad_middle)

    pl.run_scoped(
        embed,
        pltpu.VMEM((entry_total, entry_width), BF16),
        pltpu.VMEM((chunk_rows, entry_width), BF16),
        pltpu.VMEM((chunk_rows, width), BF16),
    )

    def put_rows(part, slot, columns, values):
        half = chunk_rows // 2
        for k in range(2):
            for j in range(chips):
                first = k * half + j * own_rows
                part[slot, k, j, :, columns] = values[first : first + own_rows].astype(BF16)

    def rows_of(ref, i):
        return ref[i].reshape(chunk_rows, width)

    def make_bias(i):
        query_spots = i * chunk_rows + lax.broadcasted_iota(jnp.int32, (chunk_rows, chunk_rows), 1)
        query_segments = segments[i].astype(F32)
        for kb in range(i + 1):
            allowed = column_of(segments[kb].astype(F32)) == query_segments
            if kb == i:
                key_spots = kb * chunk_rows + lax.broadcasted_iota(
                    jnp.int32, (chunk_rows, chunk_rows), 0
                )
                allowed = allowed & (key_spots <= query_spots)
            bias[kb] = jnp.where(allowed, 0.0, FAR)

    def head_span(h):
        return pl.ds(pl.multiple_of(h * FHD, FHD), FHD)

    def layer(
        mixed,
        gate_grad,
        up_grad,
        out_tile,
        out_stage,
        d_out_t,
        d_out_n,
        d_query_t,
        value_even,
        value_odd,
        key_even,
        key_odd,
    ):
        for ref in (value_even, value_odd, key_even, key_odd):
            ref[...] = jnp.zeros_like(ref)

        def stage_copy(i, tile):
            slot = lax.rem(tile, 2)
            columns = pl.ds(pl.multiple_of(tile * 512, 512), 512)
            return pltpu.make_async_copy(
                out_stage.at[slot], out_part.at[i, :, columns], stage_sem.at[slot]
            )

        def attend(i):
            make_bias(i)

            @pl.loop(0, head_count)
            def _(h):
                query = q_t[i, head_span(h), :]
                scores = [dot_nn(k_n[kb], query) + bias[kb] for kb in range(i + 1)]
                top = jnp.max(scores[0], axis=0, keepdims=True)
                for block in scores[1:]:
                    top = jnp.maximum(top, jnp.max(block, axis=0, keepdims=True))
                total = jnp.zeros_like(top)
                attended = jnp.zeros((FHD, chunk_rows), F32)
                for kb in range(i + 1):
                    weights_block = jnp.exp(scores[kb] - top)
                    total = total + jnp.sum(weights_block, axis=0, keepdims=True)
                    attended = attended + dot_nn(v_t[kb], weights_block.astype(BF16))
                logs[i, h] = top + jnp.log(total)
                out_t[i, head_span(h), :] = (attended / total).astype(BF16)

        def attn_part(i):
            if i == CHUNKS - 1:
                load_out.wait()
            attended = out_t[i].T

            def tile(columns):
                put_rows(part_a, i, columns, dot_nt(attended, w_out[columns, :]))

            column_tiles(width, 512, tile)
            attn_sum.start(i)

        def norm(i):
            values = embeds_own[i].astype(F32) + attn_sum.finish(i)
            residual[i] = values
            full[i, core, chip] = (values * rms_scale(values) * gain_two[...]).astype(BF16)
            mlp_rows.start(i)

        def unit_tile(i, columns):
            rows = rows_of(full, i)
            gate_pre = dot_nn(rows, w_gate[:, columns])
            up_pre = dot_nn(rows, w_up[:, columns])
            act_grad = dot_nn(grad_chunk(i), w_down[:, columns])
            inverse = 1.0 / (1.0 + jnp.exp(-gate_pre))
            silu = gate_pre * inverse
            mixed[:, columns] = (silu * up_pre).astype(BF16)
            up_grad[:, columns] = (act_grad * silu).astype(BF16)
            slope = inverse * (1.0 + gate_pre * (1.0 - inverse))
            gate_grad[:, columns] = (act_grad * up_pre * slope).astype(BF16)

        tile_width = 512 if units >= 1024 else 256
        tiles = units // tile_width
        middle_tile = (tiles + 1) // 2

        def unit_tiles(i, first, last):
            @pl.loop(first, last)
            def _(t):
                unit_tile(i, pl.ds(pl.multiple_of(t * tile_width, tile_width), tile_width))

        def units_low(i):
            if i == CHUNKS - 1:
                pl.when(core == 0)(grad_middle)
                for copy in load_units:
                    copy.wait()
            grad_finish(i)
            mlp_rows.finish(i)
            unit_tiles(i, 0, middle_tile)

        def units_high(i):
            unit_tiles(i, middle_tile, tiles)
            if units % tile_width:
                unit_tile(i, pl.ds(tiles * tile_width, units % tile_width))
            mlp_rows.sent(i)

        def unit_grads(i):
            if i + 2 < CHUNKS:
                mlp_sum.sent(i + 2)

            def tile(columns):
                put_rows(
                    part_b,
                    i % 2,
                    columns,
                    dot_nt(gate_grad[...], w_gate[columns, :])
                    + dot_nt(up_grad[...], w_up[columns, :]),
                )

            column_tiles(width, 512, tile)
            mlp_sum.start(i)

        def outputs(i):
            @pl.loop(0, width // 512)
            def _(t):
                columns = pl.ds(pl.multiple_of(t * 512, 512), 512)
                out_tile[...] = dot_nt(mixed[...], w_down[columns, :])
                out_tile[pl.ds(first_own, own_rows), :] += residual[i, :, columns]
                if i == CHUNKS - 1:
                    pl.when(t >= 2)(lambda: stage_copy(i, t).wait())
                else:
                    stage_copy(i, t).wait()
                out_stage[lax.rem(t, 2)] = out_tile[...].astype(BF16)
                stage_copy(i, t).start()

        def residual_back(i):
            grad = mlp_sum.finish(i)
            block = i * owners + first_own // owned
            start = pl.multiple_of(lax.rem(first_own, owned), own_rows)
            own_grad = grad_full[block, pl.ds(start, own_rows), :].astype(F32)
            values = own_grad + rms_back(residual[i], grad, gain_two[...])
            full[i, core, chip] = values.astype(BF16)
            back_rows.start(i)

        def attend_back(i):
            back_rows.finish(i)
            attended_grad = dot_nn(rows_of(full, i), w_out[...]).astype(BF16)
            d_out_n[...] = attended_grad
            d_out_t[...] = attended_grad.T
            make_bias(i)
            cosine, sine = cos_t[i], sin_t[i]

            @pl.loop(0, head_count // 2)
            def _(pair):
                pair_span = pl.ds(pl.multiple_of(pair * 2 * FHD, 2 * FHD), 2 * FHD)
                query_pair = q_n[i, :, pair_span]
                grad_pair = d_out_n[:, pair_span]
                for odd in range(2):
                    h = pair * 2 + odd
                    query = q_t[i, head_span(h), :]
                    grad = d_out_t[head_span(h), :]
                    log_row = logs[i, h]
                    centre = jnp.sum(
                        grad.astype(F32) * out_t[i, head_span(h), :].astype(F32),
                        axis=0,
                        keepdims=True,
                    )
                    value_total = value_odd if odd else value_even
                    key_total = key_odd if odd else key_even
                    query_grad = jnp.zeros((FHD, chunk_rows), F32)
                    for kb in range(i + 1):
                        probs = jnp.exp(dot_nn(k_n[kb], query) + bias[kb] - log_row)
                        value_total[kb] += dot_nn(probs.astype(BF16), grad_pair)
                        score_grad = (probs * (dot_nn(v_n[kb], grad) - centre)).astype(BF16)
                        key_total[kb] += dot_nn(score_grad, query_pair)
                        query_grad = query_grad + dot_nn(k_t[kb], score_grad)
                    query_grad = query_grad * (FHD**-0.5)
                    low_half, high_half = query_grad[: FHD // 2], query_grad[FHD // 2 :]
                    d_query_t[head_span(h), :] = jnp.concatenate(
                        [
                            low_half * cosine + high_half * sine,
                            high_half * cosine - low_half * sine,
                        ],
                        axis=0,
                    ).astype(BF16)

        def normed_part(i):
            attn_sum.sent(i)
            key_grad = (key_even[i][:, :FHD] + key_odd[i][:, FHD:]).T
            cosine, sine = cos_t[i], sin_t[i]
            low_half, high_half = key_grad[: FHD // 2], key_grad[FHD // 2 :]
            value_grad = (value_even[i][:, :FHD] + value_odd[i][:, FHD:]).T
            both = jnp.concatenate(
                [
                    low_half * cosine + high_half * sine,
                    high_half * cosine - low_half * sine,
                    value_grad,
                ],
                axis=0,
            )
            both_rows = both.T.astype(BF16)
            query_rows = d_query_t[...].T

            def tile(columns):
                put_rows(
                    part_a,
                    i,
                    columns,
                    dot_nt(query_rows, w_query[columns, :]) + dot_nt(both_rows, w_kv[columns, :]),
                )

            column_tiles(width, 512, tile)
            normed_sum.start(i)

        def embed_back(i):
            grad = normed_sum.finish(i)
            kept = full[i, core, chip].astype(F32)
            values = kept + rms_back(embeds_own[i].astype(F32), grad, gain_one[...])
            embed_grad[i] = values.astype(BF16)
            total = jnp.zeros((own_rows, entry_width), F32)
            for m, c, y in shards_of(chips):
                total = total + dot_nt(
                    embed_grad[i, :, m * columns : (m + 1) * columns], proj[c, y]
                )
            token_full[i, core, chip] = total.astype(BF16)
            token_rows.start(i)

        stages = {
            "attend": attend,
            "attn_part": attn_part,
            "attn_far": attn_sum.middle,
            "norm": norm,
            "rows_near": mlp_rows.middle,
            "units_low": units_low,
            "units_high": units_high,
            "unit_grads": unit_grads,
            "outputs": outputs,
            "units_far": mlp_sum.middle,
            "residual": residual_back,
            "back_near": back_rows.middle,
            "attend_back": attend_back,
            "normed_part": normed_part,
            "normed_far": normed_sum.middle,
            "embed_grad": embed_back,
            "token_near": token_rows.middle,
        }
        for name, turn in STEPS:
            stages[name](CHUNKS - 1 - turn)

        for tile in range(2):
            stage_copy(0, tile).wait()

    lines = (chunk_rows, units)
    keys = (CHUNKS, chunk_rows, 2 * FHD)
    pl.run_scoped(
        layer,
        pltpu.VMEM(lines, BF16),
        pltpu.VMEM(lines, BF16),
        pltpu.VMEM(lines, BF16),
        pltpu.VMEM((chunk_rows, 512), F32),
        pltpu.VMEM((2, chunk_rows, 512), BF16),
        pltpu.VMEM((head_width, chunk_rows), BF16),
        pltpu.VMEM((chunk_rows, head_width), BF16),
        pltpu.VMEM((head_width, chunk_rows), BF16),
        pltpu.VMEM(keys, F32),
        pltpu.VMEM(keys, F32),
        pltpu.VMEM(keys, F32),
        pltpu.VMEM(keys, F32),
    )

    @pl.loop(0, CHUNKS)
    def _(i):
        token_rows.finish(i)
        token_rows.sent(i)
        normed_sum.sent(i)
        back_rows.sent(i)

    for i in range(2):
        mlp_sum.sent(i)
    for other in net.others():
        grad_far(chip, other).wait_send()
    for owner_chip in range(chips):
        grad_near_copy(owner_chip, core).wait_send()


def text_layer(
    group,
    dp_count,
    entry_count,
    entry_ids,
    segments,
    cos_t,
    sin_t,
    bias_full,
    gain_one,
    gain_two,
    w_kv,
    entries,
    weights,
    token_grad,
    w_query,
    w_out,
    w_gate,
    w_up,
    w_down,
):
    chips = group // 2
    chunks, _, chunk_rows = entry_ids.shape
    own_rows = chunk_rows // group
    owned, width = token_grad.shape
    head_width = w_query.shape[1]
    head_count = head_width // FHD
    entry_width = entries.shape[1]
    vmem = pl.BlockSpec(memory_space=pltpu.VMEM)
    hbm = pl.BlockSpec(memory_space=pl.ANY)
    dma = pltpu.SemaphoreType.DMA

    def low(*shape):
        return pltpu.VMEM(shape, BF16)

    return pl.pallas_call(
        partial(text_body, chips, dp_count, entry_count, head_count),
        out_shape=(
            jax.ShapeDtypeStruct((chunks, chunk_rows, width), BF16),
            jax.ShapeDtypeStruct((chunks, own_rows, width), BF16),
            jax.ShapeDtypeStruct((chunks, own_rows, entry_width), BF16),
            jax.ShapeDtypeStruct((chunks, 2, chips, own_rows, entry_width), BF16),
        ),
        in_specs=[vmem] * 8 + [hbm] * 8,
        out_specs=(hbm, vmem, vmem, vmem),
        scratch_shapes=[
            low(*weights.shape[1:]),
            low(*w_query.shape),
            low(*w_out.shape),
            low(*w_gate.shape),
            low(*w_up.shape),
            low(*w_down.shape),
            low(chunks, 2, chips, own_rows, width),
            low(chunks, chips, own_rows, width),
            low(chunks, chips - 1, own_rows, width),
            low(2, 2, chips, own_rows, width),
            low(chunks, chips, own_rows, width),
            low(chunks, chips - 1, own_rows, width),
            low(chunks, 2, chips, own_rows, width),
            low(group, owned, width),
            low(chunks, own_rows, width),
            low(chunks, head_width, chunk_rows),
            low(chunks, chunk_rows, head_width),
            low(chunks, chunk_rows, FHD),
            low(chunks, chunk_rows, FHD),
            low(chunks, FHD, chunk_rows),
            low(chunks, FHD, chunk_rows),
            low(chunks, head_width, chunk_rows),
            pltpu.VMEM((chunks, head_count, 1, chunk_rows), F32),
            pltpu.VMEM((chunks, chunk_rows, chunk_rows), F32),
            pltpu.VMEM((chunks, own_rows, width), F32),
            dma((7,)),
            dma,
            dma((2,)),
            dma((3, 2, chunks)),
            dma((3, chunks, chips)),
            dma((3, chunks, chips)),
            dma((3, 2, chunks)),
            dma((3, chunks, chips)),
            dma((3, chunks, chips)),
            dma((2, chips)),
            dma((chips,)),
            dma((chips,)),
        ],
        compiler_params=pltpu.CompilerParams(
            collective_id=0, has_side_effects=True, vmem_limit_bytes=65280 * 1024
        ),
        cost_estimate=pl.CostEstimate(
            flops=90 * 10**9, bytes_accessed=40 * 10**6, transcendentals=20 * 10**6
        ),
    )(
        entry_ids,
        segments,
        cos_t,
        sin_t,
        bias_full,
        gain_one,
        gain_two,
        w_kv,
        entries,
        weights,
        token_grad,
        w_query,
        w_out,
        w_gate,
        w_up,
        w_down,
    )


def norm_parts(values):
    average = jnp.mean(values, axis=-1, keepdims=True)
    centred = values - average
    scale = lax.rsqrt(jnp.mean(centred * centred, axis=-1, keepdims=True) + 1e-05)
    return centred * scale, scale


def norm_back(values, grad, gain):
    unit, scale = norm_parts(values)
    scaled = grad * gain
    back = scale * (
        scaled
        - jnp.mean(scaled, axis=-1, keepdims=True)
        - unit * jnp.mean(scaled * unit, axis=-1, keepdims=True)
    )
    return (
        back,
        jnp.sum(grad * unit, axis=0, keepdims=True),
        jnp.sum(grad, axis=0, keepdims=True),
    )


def gelu_parts(values):
    root = math.sqrt(2.0 / math.pi)
    squared = values * values
    bent = jnp.tanh(root * values * (1.0 + 0.044715 * squared))
    half = 0.5 * (1.0 + bent)
    slope = half + 0.5 * values * (1.0 - bent * bent) * root * (1.0 + 3 * 0.044715 * squared)
    return values * half, slope


def pool_matrix(counts_col, entries, rows):
    entry = lax.broadcasted_iota(jnp.int32, (entries, rows), 0)
    row = lax.broadcasted_iota(jnp.int32, (entries, rows), 1)
    slots = rows // entries
    inside = (row // slots == entry) & (lax.rem(row, slots).astype(F32) < counts_col)
    return jnp.where(inside, 1.0, 0.0)


def spread_matrix(counts_row, entries, rows):
    row = lax.broadcasted_iota(jnp.int32, (rows, entries), 0)
    entry = lax.broadcasted_iota(jnp.int32, (rows, entries), 1)
    slots = rows // entries
    inside = (row // slots == entry) & (lax.rem(row, slots).astype(F32) < counts_row)
    return jnp.where(inside, 1.0, 0.0)


def slot_bias(valid_col, slots):
    rows = valid_col.shape[0]
    key = lax.broadcasted_iota(jnp.int32, (rows, rows), 0)
    query = lax.broadcasted_iota(jnp.int32, (rows, rows), 1)
    return jnp.where((key // slots == query // slots) & (valid_col > 0.5), 0.0, FAR)


ROW_BLOCK = 256


def shards_of(chips):
    return [(y * 2 + c, c, y) for y in range(chips) for c in range(2)]


def each_shard(chips, columns, body):
    @pl.loop(0, 2)
    def _(c):
        @pl.loop(0, chips)
        def _(y):
            first = pl.multiple_of((y * 2 + c) * columns, columns)
            body(c, y, pl.ds(first, columns))


def hyper_body(
    chips,
    dp_count,
    pieces,
    counts_all,
    gain_one,
    shift_one,
    gain_two,
    shift_two,
    w_query,
    w_key,
    w_value,
    w_out,
    bias_own,
    w_up_hbm,
    w_down_hbm,
    w_proj_hbm,
    entries,
    weights_out,
    attn_in,
    q_n,
    k_n,
    v_n,
    attended,
    logs,
    residual,
    ffn_in,
    counts_col,
    counts_row,
    bias_full,
    full,
    q_t,
    v_t,
    out_t,
    bias,
    hidden,
    counts_scratch,
    local_sem,
    store_sem,
    far_send,
    far_recv,
    x_send,
    x_recv,
    near_send,
    near_recv,
    z_send,
    z_recv,
    mate_send,
    mate_recv,
    y_send,
    y_recv,
    last_send,
    last_recv,
    bias_far_send,
    bias_far_recv,
    bias_near,
):
    me = lax.axis_index("mp")
    dp = lax.axis_index("dp")
    chip, core = me // 2, lax.rem(me, 2)
    net = Exchange(chips, chip, core, "mp")
    side = lax.rem(dp, 2)
    mate = dp + 1 - 2 * side
    spot, spots = dp // 2, dp_count // 2
    kinds, _, _, width, columns = full.shape
    sources = (None, w_up_hbm, w_down_hbm, w_proj_hbm)
    rows = pieces.shape[0]
    entry_count = counts_col.shape[0]
    slots = rows // entry_count
    head_columns = columns // 4
    half = width // 2
    heads = width // HD

    flag = pltpu.get_barrier_semaphore()
    pl.semaphore_signal(flag, inc=1, device_id=net.sibling(), device_id_type=MESH)
    for other in net.others():
        pl.semaphore_signal(flag, inc=1, device_id=net.peer(other), device_id_type=MESH)

    pl.semaphore_signal(flag, inc=1, device_id={"dp": mate}, device_id_type=MESH)

    @pl.loop(1, spots)
    def _(j):
        target = lax.rem(spot + j, spots) * 2 + side
        pl.semaphore_signal(flag, inc=1, device_id={"dp": target}, device_id_type=MESH)

    local = [
        pltpu.make_async_copy(sources[k], full.at[k, core, chip], local_sem.at[k - 1])
        for k in range(1, kinds)
    ]
    for copy in local:
        copy.start()
    for j, source in enumerate((w_query, w_key, w_value, w_out)):
        full[0, core, chip, :, j * head_columns : (j + 1) * head_columns] = source[...]
    bias_full[core, chip] = bias_own[...]
    pl.semaphore_wait(flag, chips + spots)

    def rows_half(which):
        return pl.ds(pl.multiple_of(which * half, half), half)

    def far_copy(k, other):
        return net.to_peer(
            other,
            sources[k].at[rows_half(side)] if k else full.at[0, core, chip, rows_half(side)],
            full.at[k, core, chip, rows_half(side)],
            far_send.at[k, other],
            far_recv.at[k, chip],
        )

    def far_landing(k, other):
        block = full.at[k, core, other, rows_half(side)]
        return net.to_peer(other, block, block, far_send.at[k, other], far_recv.at[k, other])

    def x_copy(k, other, which):
        block = full.at[k, core, other, rows_half(which)]
        return pltpu.make_async_remote_copy(
            src_ref=block,
            dst_ref=block,
            send_sem=x_send.at[k, other],
            recv_sem=x_recv.at[k, other],
            device_id={"dp": mate},
            device_id_type=MESH,
        )

    def near_copy(k, which):
        block = full.at[k, which]
        return net.to_sibling(block, block, near_send.at[k], near_recv.at[k])

    def far_middle(k):
        for other in net.others():
            far_landing(k, other).wait_recv()
            x_copy(k, other, side).start()

    def x_middle(k):
        for other in net.others():
            x_copy(k, other, 1 - side).wait_recv()
        if k:
            local[k - 1].wait()
        near_copy(k, core).start()

    def store(k):
        return pltpu.make_async_copy(full.at[k], weights_out.at[k], store_sem.at[k])

    def near_finish(k):
        near_copy(k, 1 - core).wait_recv()
        store(k).start()

    bias_rows = Gather(
        net, bias_full, (bias_far_send, bias_far_recv, bias_near.at[0], bias_near.at[1]), True
    )
    def far_start(k):
        for other in net.others():
            far_copy(k, other).start()

    far_start(0)
    bias_rows.start(0)
    counts_scratch[...] = column_of(counts_all[...].astype(F32))
    own_counts = counts_scratch[pl.ds(pl.multiple_of(me * entry_count, entry_count), entry_count)]
    counts_col[...] = own_counts
    counts_row[...] = jnp.broadcast_to(own_counts, (entry_count, 128)).T[:1]

    values = pieces[...].astype(F32)
    attn_in[...] = (norm_parts(values)[0] * gain_one[...] + shift_one[...]).astype(BF16)
    blocks = rows // ROW_BLOCK
    valid = jnp.sum(spread_matrix(counts_row[...], entry_count, rows), axis=1, keepdims=True)
    for b in range(blocks):
        bias[b] = slot_bias(valid[b * ROW_BLOCK : (b + 1) * ROW_BLOCK], slots)

    far_middle(0)
    far_start(1)
    bias_rows.middle(0)
    far_middle(1)
    far_start(2)
    x_middle(0)
    near_finish(0)
    for m, c, y in shards_of(chips):
        span = slice(m * head_columns, (m + 1) * head_columns)
        projected = dot_nn(attn_in[...], full[0, c, y, :, : 3 * head_columns])
        q_n[:, span] = (projected[:, :head_columns].astype(BF16).astype(F32) * HD**-0.5).astype(
            BF16
        )
        k_n[:, span] = projected[:, head_columns : 2 * head_columns].astype(BF16)
        v_n[:, span] = projected[:, 2 * head_columns :].astype(BF16)
    far_middle(2)
    far_start(3)
    x_middle(1)
    for b in range(blocks):
        block_rows = slice(b * ROW_BLOCK, (b + 1) * ROW_BLOCK)
        q_t[b] = q_n[block_rows, :].T
        v_t[b] = v_n[block_rows, :].T

    def attend_pair(pair):
        pair_span = pl.ds(pl.multiple_of(pair * 2 * HD, 2 * HD), 2 * HD)
        for b in range(blocks):
            key_pair = k_n[b * ROW_BLOCK : (b + 1) * ROW_BLOCK, pair_span]
            for odd in range(2):
                h = pair * 2 + odd
                span = pl.ds(pl.multiple_of(h * HD, HD), HD)
                scores = dot_nn(key_pair[:, odd * HD : (odd + 1) * HD], q_t[b, span, :]) + bias[b]
                top = jnp.max(scores, axis=0, keepdims=True)
                weights = jnp.exp(scores - top)
                total = jnp.sum(weights, axis=0, keepdims=True)
                logs[b, h] = top + jnp.log(total)
                out_t[b, span, :] = (dot_nn(v_t[b, span, :], weights.astype(BF16)) / total).astype(
                    BF16
                )

    pl.loop(0, heads // 4)(attend_pair)
    far_middle(3)
    x_middle(2)
    pl.loop(heads // 4, heads // 2)(attend_pair)
    for b in range(blocks):
        attended[b * ROW_BLOCK : (b + 1) * ROW_BLOCK, :] = out_t[b].T
    total = values
    for m, c, y in shards_of(chips):
        span = slice(m * head_columns, (m + 1) * head_columns)
        total = total + dot_nt(attended[:, span], full[0, c, y, :, 3 * head_columns :])
    residual[...] = total
    ffn_in[...] = (norm_parts(total)[0] * gain_two[...] + shift_two[...]).astype(BF16)
    near_finish(1)
    x_middle(3)
    pool = pool_matrix(counts_col[...], entry_count, rows).astype(BF16)

    def up_shard(c, y, span):
        act = gelu_parts(dot_nn(ffn_in[...], full[1, c, y]))[0]
        hidden[:, span] = dot_nn(pool, act.astype(BF16)).astype(BF16)

    each_shard(chips, columns, up_shard)
    near_finish(2)
    pooled = jnp.sum(
        (residual[...] * valid).reshape(entry_count, slots, width), axis=1
    )
    for m, c, y in shards_of(chips):
        pooled = pooled + dot_nt(hidden[:, m * columns : (m + 1) * columns], full[2, c, y])
    entries[core, chip, dp] = (pooled / counts_col[...]).astype(BF16)

    def z_copy(target, owner):
        piece = entries.at[core, chip, owner * 2 + side]
        return pltpu.make_async_remote_copy(
            src_ref=piece,
            dst_ref=piece,
            send_sem=z_send.at[target],
            recv_sem=z_recv.at[owner],
            device_id={"dp": target * 2 + side},
            device_id_type=MESH,
        )

    def mate_copy(owner, which):
        piece = entries.at[core, chip, owner * 2 + which]
        return pltpu.make_async_remote_copy(
            src_ref=piece,
            dst_ref=piece,
            send_sem=mate_send.at[owner],
            recv_sem=mate_recv.at[owner],
            device_id={"dp": mate},
            device_id_type=MESH,
        )

    def y_copy(other, owner, block):
        piece = entries.at[core, owner, block]
        return net.to_peer(
            other, piece, piece, y_send.at[other, block], y_recv.at[owner, block]
        )

    def y_start(block):
        for other in net.others():
            y_copy(other, chip, block).start()

    @pl.loop(1, spots)
    def _(j):
        z_copy(lax.rem(spot + j, spots), spot).start()

    mate_copy(spot, side).start()
    y_start(dp)
    near_finish(3)
    bias_rows.finish(0)

    @pl.loop(1, spots)
    def _(j):
        source = lax.rem(spot + spots - j, spots)
        z_copy(source, source).wait_recv()
        mate_copy(source, side).start()
        y_start(source * 2 + side)

    @pl.loop(0, spots)
    def _(j):
        source = lax.rem(spot + spots - j, spots)
        mate_copy(source, 1 - side).wait_recv()
        y_start(source * 2 + 1 - side)

    def last_copy(part, c, owner):
        piece = entries.at[c, owner]
        return net.to_sibling(piece, piece, last_send.at[part], last_recv.at[owner])

    last_copy(chip, core, chip).start()
    for other in net.others():

        @pl.loop(0, dp_count)
        def _(block):
            y_copy(other, other, block).wait_recv()

        last_copy(other, core, other).start()
    last_copy(chip, 1 - core, chip).wait_recv()
    for other in net.others():
        last_copy(other, 1 - core, other).wait_recv()

    bias_rows.sent(0)
    for k in range(kinds):
        store(k).wait()
        near_copy(k, core).wait_send()
        for other in net.others():
            far_copy(k, other).wait_send()
            x_copy(k, other, side).wait_send()

    @pl.loop(1, spots)
    def _(j):
        z_copy(lax.rem(spot + j, spots), spot).wait_send()

    @pl.loop(0, spots)
    def _(j):
        mate_copy(j, side).wait_send()

    last_copy(chip, core, chip).wait_send()
    for other in net.others():
        last_copy(other, core, other).wait_send()

        @pl.loop(0, dp_count)
        def _(block):
            y_copy(other, chip, block).wait_send()


def hyper_forward(
    group,
    dp_count,
    pieces,
    counts,
    gain_one,
    shift_one,
    gain_two,
    shift_two,
    head_weights,
    bias_own,
    unit_weights,
):
    chips = group // 2
    rows, width = pieces.shape
    columns = unit_weights[0].shape[1]
    kinds = 4
    entry_count = counts.shape[1] // group
    heads = width // HD
    blocks = rows // ROW_BLOCK
    vmem = pl.BlockSpec(memory_space=pltpu.VMEM)
    hbm = pl.BlockSpec(memory_space=pl.ANY)
    row_shape = jax.ShapeDtypeStruct((rows, width), BF16)
    dma = pltpu.SemaphoreType.DMA
    return pl.pallas_call(
        partial(hyper_body, chips, dp_count),
        out_shape=(
            jax.ShapeDtypeStruct((2, chips, dp_count, entry_count, width), BF16),
            jax.ShapeDtypeStruct((kinds, 2, chips, width, columns), BF16),
            row_shape,
            row_shape,
            row_shape,
            row_shape,
            row_shape,
            jax.ShapeDtypeStruct((blocks, heads, 1, ROW_BLOCK), F32),
            jax.ShapeDtypeStruct((rows, width), F32),
            row_shape,
            jax.ShapeDtypeStruct((entry_count, 1), F32),
            jax.ShapeDtypeStruct((1, entry_count), F32),
            jax.ShapeDtypeStruct((2, chips, 1, columns), F32),
        ),
        in_specs=[vmem] * 11 + [hbm] * 3,
        out_specs=(vmem, hbm) + (vmem,) * 11,
        scratch_shapes=[
            pltpu.VMEM((kinds, 2, chips, width, columns), BF16),
            pltpu.VMEM((blocks, width, ROW_BLOCK), BF16),
            pltpu.VMEM((blocks, width, ROW_BLOCK), BF16),
            pltpu.VMEM((blocks, width, ROW_BLOCK), BF16),
            pltpu.VMEM((blocks, ROW_BLOCK, ROW_BLOCK), F32),
            pltpu.VMEM((entry_count, columns * group), BF16),
            pltpu.VMEM((counts.shape[1], 1), F32),
            dma((kinds - 1,)),
            dma((kinds,)),
            dma((kinds, chips)),
            dma((kinds, chips)),
            dma((kinds, chips)),
            dma((kinds, chips)),
            dma((kinds,)),
            dma((kinds,)),
            dma((dp_count // 2,)),
            dma((dp_count // 2,)),
            dma((dp_count // 2,)),
            dma((dp_count // 2,)),
            dma((chips, dp_count)),
            dma((chips, dp_count)),
            dma((chips,)),
            dma((chips,)),
            dma((1, chips)),
            dma((1, chips)),
            dma((2, 1)),
        ],
        compiler_params=pltpu.CompilerParams(
            collective_id=1, has_side_effects=True, vmem_limit_bytes=60 * 1024 * 1024
        ),
        cost_estimate=pl.CostEstimate(
            flops=60 * 10**9, bytes_accessed=20 * 10**6, transcendentals=5 * 10**6
        ),
    )(
        pieces,
        counts,
        gain_one,
        shift_one,
        gain_two,
        shift_two,
        *head_weights,
        bias_own,
        *unit_weights,
    )


class Total:
    def __init__(self, net, dp, dp_count, scatter, mine, x_land, z_land, final, sems):
        self.net, self.scatter, self.mine = net, scatter, mine
        self.x_land, self.z_land, self.final = x_land, z_land, final
        self.x_send, self.x_recv, self.z_send, self.z_recv = sems[:4]
        self.g_send, self.g_recv, self.l_send, self.l_recv = sems[4:]
        self.side = lax.rem(dp, 2)
        self.spot = dp // 2
        self.mate = dp + 1 - 2 * self.side
        self.spots = dp_count // 2

    def remote(self, source, target, send, recv, device):
        return pltpu.make_async_remote_copy(
            src_ref=source,
            dst_ref=target,
            send_sem=send,
            recv_sem=recv,
            device_id={"dp": device},
            device_id_type=MESH,
        )

    def x_copy(self, k):
        return self.remote(
            self.mine.at[k, 1 - self.side],
            self.x_land.at[k],
            self.x_send.at[k],
            self.x_recv.at[k],
            self.mate,
        )

    def z_copy(self, k, spot, slot):
        return self.remote(
            self.mine.at[k, self.side, spot],
            self.z_land.at[k, slot],
            self.z_send.at[k, spot],
            self.z_recv.at[k, slot],
            spot * 2 + self.side,
        )

    def g_copy(self, k, spot, owner):
        block = self.final.at[k, self.side, owner]
        return self.remote(
            block, block, self.g_send.at[k, spot], self.g_recv.at[k, owner], spot * 2 + self.side
        )

    def l_copy(self, k, side):
        block = self.final.at[k, side]
        return self.remote(block, block, self.l_send.at[k], self.l_recv.at[k], self.mate)

    def each_spot(self, body):
        if self.spots > 1:

            @pl.loop(1, self.spots)
            def _(j):
                body(lax.rem(self.spot + j, self.spots))

    def start(self, k):
        self.scatter.start(k)

    def near_middle(self, k):
        self.scatter.middle(k)

    def far_middle(self, k):
        total = self.scatter.finish(k)
        self.mine[k] = total.astype(BF16).reshape(self.mine.shape[1:])
        self.x_copy(k).start()

    def x_middle(self, k):
        self.x_copy(k).wait_recv()
        block = self.mine[k, self.side].astype(F32) + self.x_land[k].astype(F32)
        self.mine[k, self.side] = block.astype(BF16)
        self.each_spot(lambda spot: self.z_copy(k, spot, self.spot).start())

    def z_middle(self, k):
        def add(spot):
            self.z_copy(k, spot, spot).wait_recv()

        self.each_spot(add)
        total = self.mine[k, self.side, self.spot].astype(F32)
        for j in range(1, self.spots):
            spot = lax.rem(self.spot + j, self.spots)
            total = total + self.z_land[k, spot].astype(F32)
        self.final[k, self.side, self.spot] = total.astype(BF16)
        self.each_spot(lambda spot: self.g_copy(k, spot, self.spot).start())

    def g_middle(self, k):
        self.each_spot(lambda spot: self.g_copy(k, spot, spot).wait_recv())
        self.l_copy(k, self.side).start()

    def finish(self, k):
        self.l_copy(k, 1 - self.side).wait_recv()

    def sent(self, k):
        self.scatter.sent(k)
        self.x_copy(k).wait_send()
        self.each_spot(lambda spot: self.z_copy(k, spot, self.spot).wait_send())
        self.each_spot(lambda spot: self.g_copy(k, spot, self.spot).wait_send())
        self.l_copy(k, self.side).wait_send()


PARTS = 8


def back_body(
    chips,
    dp_count,
    embed_rows,
    pooled_own,
    token_rows,
    token_row,
    pieces,
    counts_col,
    counts_row,
    gain_one,
    gain_two,
    attn_in,
    q_n,
    k_n,
    v_n,
    attended,
    logs,
    residual,
    ffn_in,
    weights_hbm,
    out_part,
    pieces_grad,
    final,
    small_total,
    text_out,
    weights,
    part,
    near,
    far,
    mine,
    x_land,
    z_land,
    entry_part,
    entry_land,
    hidden,
    hidden_pre,
    ffn_t,
    row_total,
    d_out_n,
    d_query,
    d_key,
    d_value,
    q_t,
    out_t,
    d_out_t,
    k_t,
    d_query_t,
    bias,
    small_near,
    small_far,
    small_dp,
    small_part,
    out_own,
    out_near,
    out_far,
    weight_sem,
    out_local,
    out_near_sem,
    out_far_send,
    out_far_recv,
    entry_send,
    entry_recv,
    scatter_near,
    scatter_far_send,
    scatter_far_recv,
    x_sem,
    z_send,
    z_recv,
    g_send,
    g_recv,
    l_sem,
    small_sem,
    small_far_send,
    small_far_recv,
    small_dp_send,
    small_dp_recv,
):
    me = lax.axis_index("mp")
    dp = lax.axis_index("dp")
    group = chips * 2
    chip, core = me // 2, lax.rem(me, 2)
    net = Exchange(chips, chip, core, "mp")
    rows, width = pieces.shape
    entry_count = counts_col.shape[0]
    slots = rows // entry_count
    columns = weights.shape[4]
    half_columns = columns // 2
    head_columns = columns // 4
    heads = width // HD
    blocks = rows // ROW_BLOCK
    total_sum = Total(
        net,
        dp,
        dp_count,
        Scatter(
            net,
            part,
            near,
            far,
            (scatter_near.at[0], scatter_near.at[1], scatter_far_send, scatter_far_recv),
        ),
        mine,
        x_land,
        z_land,
        final,
        (x_sem.at[0], x_sem.at[1], z_send, z_recv, g_send, g_recv, l_sem.at[0], l_sem.at[1]),
    )
    stages = (
        total_sum.near_middle,
        total_sum.far_middle,
        total_sum.x_middle,
        total_sum.z_middle,
        total_sum.g_middle,
        total_sum.finish,
    )

    def run(step):
        for offset, stage in enumerate(stages):
            if 0 <= step - offset < PARTS:
                stage(step - offset)

    flag = pltpu.get_barrier_semaphore()
    pl.semaphore_signal(flag, inc=1, device_id=net.sibling(), device_id_type=MESH)
    for other in net.others():
        pl.semaphore_signal(flag, inc=1, device_id=net.peer(other), device_id_type=MESH)

    def each_dp(body):
        @pl.loop(1, dp_count)
        def _(j):
            body(lax.rem(dp + j, dp_count))

    each_dp(
        lambda target: pl.semaphore_signal(
            flag, inc=1, device_id={"dp": target}, device_id_type=MESH
        )
    )
    loads = [
        pltpu.make_async_copy(weights_hbm.at[k], weights.at[k], weight_sem.at[k])
        for k in (1, 2, 0)
    ]
    for copy in loads:
        copy.start()
    out_copies = [
        pltpu.make_async_copy(out_part.at[y * 2 + core], out_own.at[y], out_local.at[y])
        for y in range(chips)
    ]
    for copy in out_copies:
        copy.start()
    pl.semaphore_wait(flag, chips + dp_count - 1)

    def out_near_copy(y):
        return net.to_sibling(
            out_part.at[y * 2 + 1 - core],
            out_near.at[y],
            out_near_sem.at[0, y],
            out_near_sem.at[1, y],
        )

    def out_far_copy(other, source):
        return net.to_peer(
            other,
            out_own.at[other],
            out_far.at[lax.rem(source - chip + chips - 1, chips)]
            if source is not chip
            else out_far.at[lax.rem(chip - other + chips - 1, chips)],
            out_far_send.at[other],
            out_far_recv.at[source],
        )

    for y in range(chips):
        out_near_copy(y).start()

    def put(k, c, y, values):
        part[k, c, y] = values[:, :half_columns].astype(BF16)
        part[k + 1, c, y] = values[:, half_columns:].astype(BF16)

    token_total = token_rows.shape[0]
    dp_step = max(1, ROW_BLOCK // entry_count)

    @pl.loop(0, dp_count // dp_step)
    def _(block):
        row = lax.broadcasted_iota(jnp.int32, (dp_step * entry_count, token_total), 0)
        owner = block * dp_step + row // entry_count
        number = (owner * group + me) * entry_count + lax.rem(row, entry_count)
        chosen = jnp.where(number == token_row[...], 1.0, 0.0).astype(BF16)
        sums = dot_nn(chosen, token_rows[...]).astype(BF16)
        for j in range(dp_step):
            entry_part[block * dp_step + j] = sums[j * entry_count : (j + 1) * entry_count]

    def entry_copy(target, slot):
        return pltpu.make_async_remote_copy(
            src_ref=entry_part.at[target],
            dst_ref=entry_land.at[slot],
            send_sem=entry_send.at[target],
            recv_sem=entry_recv.at[slot],
            device_id={"dp": target},
            device_id_type=MESH,
        )

    each_dp(lambda target: entry_copy(target, dp).start())
    pooled_t = pooled_own[...].T

    def proj_shard(c, y, span):
        put(0, c, y, dot_nn(pooled_t, embed_rows[:, span]))

    each_shard(chips, columns, proj_shard)
    total_sum.start(0)
    total_sum.start(1)
    bias_sums = jnp.sum(embed_rows[...].astype(F32), axis=0, keepdims=True)
    for j in range(4):
        small_part[4 + j : 5 + j, :] = bias_sums[:, j * width : (j + 1) * width]
    loads[0].wait()
    run(0)

    pool = pool_matrix(counts_col[...], entry_count, rows).astype(BF16)
    spread = spread_matrix(counts_row[...], entry_count, rows)
    valid = jnp.sum(spread, axis=1, keepdims=True)
    spread = spread.astype(BF16)
    for b in range(blocks):
        bias[b] = slot_bias(valid[b * ROW_BLOCK : (b + 1) * ROW_BLOCK], slots)
    ffn_t[...] = ffn_in[...].T

    def hidden_shard(c, y, span):
        before = dot_nn(ffn_in[...], weights[1, c, y])
        hidden_pre[:, span] = before
        hidden[:, span] = dot_nn(pool, gelu_parts(before)[0].astype(BF16)).astype(BF16)

    each_shard(chips, columns, hidden_shard)
    run(1)
    each_dp(lambda source: entry_copy(source, source).wait_recv())
    pooled_grad = entry_part[dp].astype(F32)
    for j in range(1, dp_count):
        pooled_grad = pooled_grad + entry_land[lax.rem(dp + j, dp_count)].astype(F32)
    entry_low = (pooled_grad / counts_col[...]).astype(BF16)
    out_rows = dot_nn(spread, entry_low)
    entry_t = entry_low.T
    loads[1].wait()
    out_low = out_rows.astype(BF16)
    row_total[...] = jnp.zeros_like(row_total)

    def unit_shard(c, y, span):
        put(2, c, y, dot_nn(entry_t, hidden[:, span]))
        act_grad = dot_nn(out_low, weights[2, c, y])
        pre_grad = (act_grad * gelu_parts(hidden_pre[:, span])[1]).astype(BF16)
        put(4, c, y, dot_nn(ffn_t[...], pre_grad))
        row_total[...] += dot_nt(pre_grad, weights[1, c, y])

    each_shard(chips, columns, unit_shard)
    for k in (2, 3, 4, 5):
        total_sum.start(k)
    run(2)
    back, gain_grad, shift_grad = norm_back(residual[...], row_total[...], gain_two[...])
    small_part[2:3, :] = gain_grad
    small_part[3:4, :] = shift_grad
    residual_grad = out_rows + back
    pieces_grad[...] = residual_grad
    attn_grad = residual_grad.astype(BF16)
    loads[2].wait()
    for m, c, y in shards_of(chips):
        span = slice(m * head_columns, (m + 1) * head_columns)
        d_out_n[:, span] = dot_nn(attn_grad, weights[0, c, y, :, 3 * head_columns :]).astype(BF16)
    out_grad = dot_nn(attn_grad.T, attended[...])
    for m, c, y in shards_of(chips):
        span = slice(m * head_columns, (m + 1) * head_columns)
        part[7, c, y, :, head_columns:] = out_grad[:, span].astype(BF16)
    for b in range(blocks):
        block_rows = slice(b * ROW_BLOCK, (b + 1) * ROW_BLOCK)
        q_t[b] = q_n[block_rows, :].T
        k_t[b] = k_n[block_rows, :].T
        out_t[b] = attended[block_rows, :].T
        d_out_t[b] = d_out_n[block_rows, :].T
    run(3)

    @pl.loop(0, heads // 2)
    def _(pair):
        pair_span = pl.ds(pl.multiple_of(pair * 2 * HD, 2 * HD), 2 * HD)
        for b in range(blocks):
            block_rows = slice(b * ROW_BLOCK, (b + 1) * ROW_BLOCK)
            key_pair = k_n[block_rows, pair_span]
            value_pair = v_n[block_rows, pair_span]
            query_pair = q_n[block_rows, pair_span]
            grad_pair = d_out_n[block_rows, pair_span]
            key_sums, value_sums = [], []
            for odd in range(2):
                h = pair * 2 + odd
                span = pl.ds(pl.multiple_of(h * HD, HD), HD)
                lanes = slice(odd * HD, (odd + 1) * HD)
                scores = dot_nn(key_pair[:, lanes], q_t[b, span, :]) + bias[b]
                probs = jnp.exp(scores - logs[b, h])
                grad_t = d_out_t[b, span, :]
                centre = jnp.sum(
                    grad_t.astype(F32) * out_t[b, span, :].astype(F32), axis=0, keepdims=True
                )
                value_sums.append(dot_nn(probs.astype(BF16), grad_pair[:, lanes]))
                score_grad = (probs * (dot_nn(value_pair[:, lanes], grad_t) - centre)).astype(BF16)
                key_sums.append(dot_nn(score_grad, query_pair[:, lanes]))
                d_query_t[b, span, :] = (
                    dot_nn(k_t[b, span, :], score_grad) * (HD**-0.5)
                ).astype(BF16)
            d_key[block_rows, pair_span] = jnp.concatenate(key_sums, axis=1).astype(BF16)
            d_value[block_rows, pair_span] = jnp.concatenate(value_sums, axis=1).astype(BF16)

    for b in range(blocks):
        d_query[b * ROW_BLOCK : (b + 1) * ROW_BLOCK, :] = d_query_t[b].T
    run(4)
    rows_t = attn_in[...].T
    for place, (k, lanes, source) in enumerate(
        ((6, 0, d_query), (6, 1, d_key), (7, 0, d_value))
    ):
        grads = dot_nn(rows_t, source[...])
        for m, c, y in shards_of(chips):
            span = slice(m * head_columns, (m + 1) * head_columns)
            part[k, c, y, :, lanes * head_columns : (lanes + 1) * head_columns] = grads[
                :, span
            ].astype(BF16)
    total_sum.start(6)
    total_sum.start(7)
    normed = jnp.zeros((rows, width), F32)
    for m, c, y in shards_of(chips):
        span = slice(m * head_columns, (m + 1) * head_columns)
        for j, source in enumerate((d_query, d_key, d_value)):
            normed = normed + dot_nt(
                source[:, span], weights[0, c, y, :, j * head_columns : (j + 1) * head_columns]
            )
    back, gain_grad, shift_grad = norm_back(pieces[...].astype(F32), normed, gain_one[...])
    small_part[0:1, :] = gain_grad
    small_part[1:2, :] = shift_grad
    pieces_grad[...] += back

    def out_middle():
        for y in range(chips):
            out_copies[y].wait()
            out_near_copy(y).wait_recv()
        for other in net.others():
            out_own[other] = (
                out_own[other].astype(F32) + out_near[other].astype(F32)
            ).astype(BF16)
            out_far_copy(other, chip).start()

    def out_finish():
        text_out[...] = out_own[chip].astype(F32) + out_near[chip].astype(F32)
        for other in net.others():
            out_far_copy(other, other).wait_recv()
            slot = lax.rem(other - chip + chips - 1, chips)
            text_out[...] += out_far[slot].astype(F32)

    small_copy = net.to_sibling(small_part, small_near, small_sem.at[0], small_sem.at[1])
    small_copy.start()

    def small_far_copy(other, owner):
        return net.to_peer(
            other,
            small_far.at[owner],
            small_far.at[owner],
            small_far_send.at[other],
            small_far_recv.at[owner],
        )

    def small_dp_copy(other, owner):
        return pltpu.make_async_remote_copy(
            src_ref=small_dp.at[owner],
            dst_ref=small_dp.at[owner],
            send_sem=small_dp_send.at[other],
            recv_sem=small_dp_recv.at[owner],
            device_id={"dp": other},
            device_id_type=MESH,
        )

    def small_near_done():
        small_copy.wait_recv()
        small_far[chip] = small_part[...] + small_near[...]
        for other in net.others():
            small_far_copy(other, chip).start()

    def small_far_done():
        for other in net.others():
            small_far_copy(other, other).wait_recv()
        total = small_far[0]
        for j in range(1, chips):
            total = total + small_far[j]
        small_dp[dp] = total
        each_dp(lambda other: small_dp_copy(other, dp).start())

    @pl.loop(5, PARTS + 5)
    def _(step):
        for offset, stage in enumerate(stages):
            k = step - offset

            @pl.when((k >= 0) & (k < PARTS))
            def _():
                stage(k)

        pl.when(step == 5)(small_near_done)
        pl.when(step == 7)(small_far_done)
        pl.when(step == PARTS)(out_middle)

    out_finish()
    each_dp(lambda other: small_dp_copy(other, other).wait_recv())
    total = small_dp[0]
    for j in range(1, dp_count):
        total = total + small_dp[j]
    small_total[...] = total

    for y in range(chips):
        out_near_copy(y).wait_send()
    for other in net.others():
        out_far_copy(other, chip).wait_send()
    small_copy.wait_send()
    for other in net.others():
        small_far_copy(other, chip).wait_send()
    each_dp(lambda other: small_dp_copy(other, dp).wait_send())
    each_dp(lambda other: entry_copy(other, dp).wait_send())

    @pl.loop(0, PARTS)
    def _(k):
        total_sum.sent(k)


def hyper_backward(
    group,
    dp_count,
    embed_rows,
    pooled_own,
    token_rows,
    token_row,
    pieces,
    counts_col,
    counts_row,
    gain_one,
    gain_two,
    saved,
    weights,
    out_part,
):
    chips = group // 2
    rows, width = pieces.shape
    entry_count = counts_col.shape[0]
    kinds, columns = weights.shape[0], weights.shape[4]
    half_columns = columns // 2
    heads = width // HD
    blocks = rows // ROW_BLOCK
    spots = dp_count // 2
    vmem = pl.BlockSpec(memory_space=pltpu.VMEM)
    hbm = pl.BlockSpec(memory_space=pl.ANY)
    dma = pltpu.SemaphoreType.DMA
    final = (PARTS, 2, spots, width // (2 * spots), half_columns)
    units = columns * group

    def low(*shape):
        return pltpu.VMEM(shape, BF16)

    def wide(*shape):
        return pltpu.VMEM(shape, F32)

    return pl.pallas_call(
        partial(back_body, chips, dp_count),
        out_shape=(
            jax.ShapeDtypeStruct((rows, width), F32),
            jax.ShapeDtypeStruct(final, BF16),
            jax.ShapeDtypeStruct((8, width), F32),
            jax.ShapeDtypeStruct(out_part.shape[1:], F32),
        ),
        in_specs=[vmem] * 17 + [hbm] * 2,
        out_specs=(vmem,) * 4,
        scratch_shapes=[
            low(kinds, 2, chips, width, columns),
            low(PARTS, 2, chips, width, half_columns),
            low(PARTS, chips, width, half_columns),
            low(PARTS, chips - 1, width, half_columns),
            low(*final),
            low(PARTS, spots, width // (2 * spots), half_columns),
            low(PARTS, spots, width // (2 * spots), half_columns),
            low(dp_count, entry_count, width),
            low(dp_count, entry_count, width),
            low(entry_count, units),
            wide(rows, units),
            low(width, rows),
            wide(rows, width),
            low(rows, width),
            low(rows, width),
            low(rows, width),
            low(rows, width),
        ]
        + [low(blocks, width, ROW_BLOCK)] * 5
        + [
            wide(blocks, ROW_BLOCK, ROW_BLOCK),
            wide(8, width),
            wide(chips, 8, width),
            wide(dp_count, 8, width),
            wide(8, width),
            low(chips, *out_part.shape[1:]),
            low(chips, *out_part.shape[1:]),
            low(chips - 1, *out_part.shape[1:]),
            dma((kinds,)),
            dma((chips,)),
            dma((2, chips)),
            dma((chips,)),
            dma((chips,)),
            dma((dp_count,)),
            dma((dp_count,)),
            dma((2, PARTS)),
            dma((PARTS, chips)),
            dma((PARTS, chips)),
            dma((2, PARTS)),
            dma((PARTS, spots)),
            dma((PARTS, spots)),
            dma((PARTS, spots)),
            dma((PARTS, spots)),
            dma((2, PARTS)),
            dma((2,)),
            dma((chips,)),
            dma((chips,)),
            dma((dp_count,)),
            dma((dp_count,)),
        ],
        compiler_params=pltpu.CompilerParams(
            collective_id=2, has_side_effects=True, vmem_limit_bytes=62 * 1024 * 1024
        ),
        cost_estimate=pl.CostEstimate(
            flops=60 * 10**9, bytes_accessed=20 * 10**6, transcendentals=5 * 10**6
        ),
    )(
        embed_rows,
        pooled_own,
        token_rows,
        token_row,
        pieces,
        counts_col,
        counts_row,
        gain_one,
        gain_two,
        *saved,
        weights,
        out_part,
    )


def spread_body(sums, query, key, value, out, up, down, proj):
    half_columns = sums.shape[2]
    head_columns = query.shape[1]
    for first, target in ((0, proj), (2, down), (4, up)):
        target[:, :half_columns] = sums[first].astype(F32)
        target[:, half_columns:] = sums[first + 1].astype(F32)
    for k, lanes, target in ((6, 0, query), (6, 1, key), (7, 0, value), (7, 1, out)):
        target[...] = sums[k, :, lanes * head_columns : (lanes + 1) * head_columns].astype(F32)


def spread_sums(sums):
    _, width, half_columns = sums.shape
    small = jax.ShapeDtypeStruct((width, half_columns // 2), F32)
    large = jax.ShapeDtypeStruct((width, half_columns * 2), F32)
    vmem = pl.BlockSpec(memory_space=pltpu.VMEM)
    return pl.pallas_call(
        spread_body,
        out_shape=(small,) * 4 + (large,) * 3,
        in_specs=[vmem],
        out_specs=(vmem,) * 7,
        compiler_params=pltpu.CompilerParams(vmem_limit_bytes=40 * 1024 * 1024),
    )(sums)


def on_device(
    pieces,
    counts,
    entry_ids,
    segment_ids,
    norm1_gain,
    norm1_shift,
    query_weight,
    key_weight,
    value_weight,
    out_weight,
    norm2_gain,
    norm2_shift,
    up_weight,
    down_weight,
    proj_weight,
    proj_bias,
    text_norm1_gain,
    text_query,
    text_key,
    text_value,
    text_out_proj,
    text_norm2_gain,
    text_gate,
    text_up,
    text_down,
    token_grad,
):
    group, dp_count = lax.axis_size("mp"), lax.axis_size("dp")
    me = lax.axis_index("mp")
    entry_count, slot_count, width = pieces.shape
    text_width = token_grad.shape[1]
    length = segment_ids.shape[1]
    chunk_rows = length // CHUNKS
    pieces_rows = pieces.reshape(entry_count * slot_count, width)
    entries, weights, *saved, counts_col, counts_row, bias_full = hyper_forward(
        group,
        dp_count,
        pieces_rows,
        counts[None, :],
        norm1_gain[None, :],
        norm1_shift[None, :],
        norm2_gain[None, :],
        norm2_shift[None, :],
        (query_weight, key_weight, value_weight, out_weight),
        proj_bias[None, :],
        (up_weight, down_weight, proj_weight),
    )
    head_width = text_query.shape[1]
    kv_index = me * (head_width // FHD) // (QHEADS // KVHEADS)
    key_local = lax.dynamic_slice_in_dim(text_key, kv_index * FHD, FHD, 1)
    value_local = lax.dynamic_slice_in_dim(text_value, kv_index * FHD, FHD, 1)
    key_value = jnp.concatenate([key_local, value_local], axis=1)
    cos_t, sin_t = rope_tables(length)
    out_part, embed_rows, pooled_own, token_rows = text_layer(
        group,
        dp_count,
        entry_count,
        entry_ids.reshape(CHUNKS, 1, chunk_rows),
        segment_ids.reshape(CHUNKS, 1, chunk_rows),
        cos_t,
        sin_t,
        bias_full,
        text_norm1_gain[None, :],
        text_norm2_gain[None, :],
        key_value,
        entries.reshape(-1, width),
        weights,
        token_grad,
        text_query,
        text_out_proj,
        text_gate,
        text_up,
        text_down,
    )
    pieces_grad, final, small, text_out = hyper_backward(
        group,
        dp_count,
        embed_rows.reshape(-1, text_width),
        pooled_own.reshape(-1, width),
        token_rows.reshape(length, width),
        entry_ids[None, :],
        pieces_rows,
        counts_col,
        counts_row,
        norm1_gain[None, :],
        norm2_gain[None, :],
        saved,
        weights,
        out_part.reshape(group, -1, text_width),
    )
    query_grad, key_grad, value_grad, out_grad, up_grad, down_grad, proj_grad = spread_sums(
        final.reshape(PARTS, width, -1)
    )
    bias_share = proj_bias.shape[0]
    proj_bias_grad = lax.dynamic_slice_in_dim(
        small[4:].reshape(-1), me * bias_share, bias_share
    )
    return (
        text_out,
        pieces_grad.reshape(pieces.shape),
        small[0],
        small[1],
        query_grad,
        key_grad,
        value_grad,
        out_grad,
        small[2],
        small[3],
        up_grad,
        down_grad,
        proj_grad,
        proj_bias_grad,
    )


def solution(mesh):
    return jax.shard_map(
        on_device,
        mesh=mesh,
        in_specs=(
            P(("dp", "mp"), None, None),
            P("dp"),
            P("dp"),
            P("dp", None),
            P(),
            P(),
            P(None, "mp"),
            P(None, "mp"),
            P(None, "mp"),
            P(None, "mp"),
            P(),
            P(),
            P(None, "mp"),
            P(None, "mp"),
            P(None, "mp"),
            P("mp"),
            P(),
            P(None, "mp"),
            P(),
            P(),
            P(None, "mp"),
            P(),
            P(None, "mp"),
            P(None, "mp"),
            P(None, "mp"),
            P(("dp", "mp"), None),
        ),
        out_specs=(
            P(("dp", "mp"), None),
            P(("dp", "mp"), None, None),
            P(),
            P(),
            P(None, "mp"),
            P(None, "mp"),
            P(None, "mp"),
            P(None, "mp"),
            P(),
            P(),
            P(None, "mp"),
            P(None, "mp"),
            P(None, "mp"),
            P("mp"),
        ),
        check_vma=False,
    )
```

```python
from functools import partial
import math

import jax
import jax.numpy as jnp
import numpy as np
from jax import lax
from jax.experimental import pallas as pl
from jax.experimental.pallas import tpu as pltpu
from jax.sharding import PartitionSpec as P

HD = 64
QHEADS = 32
KVHEADS = 4
FHD = 64


def rope_tables(length):
    positions = np.arange(length, dtype=np.float32)
    rates = np.exp(
        np.arange(FHD // 2, dtype=np.float32) * np.float32(-2.0 * math.log(10000.0) / FHD)
    ).astype(np.float32)
    angles = (positions[None, :] * rates[:, None]).reshape(FHD // 2, CHUNKS, length // CHUNKS)
    angles = angles.transpose(1, 0, 2)
    return jnp.asarray(np.cos(angles)), jnp.asarray(np.sin(angles))


MESH = pl.DeviceIdType.MESH
F32 = jnp.float32
BF16 = jnp.bfloat16
CHUNKS = 4
FAR = -1e30


def dot_nn(a, b):
    return lax.dot_general(a, b, (((1,), (0,)), ((), ())), preferred_element_type=F32)


def dot_nt(a, b):
    return lax.dot_general(a, b, (((1,), (1,)), ((), ())), preferred_element_type=F32)


def column_tiles(total, width, body):
    full = total // width
    if full > 0:

        @pl.loop(0, full)
        def _(t):
            body(pl.ds(pl.multiple_of(t * width, width), width))

    if total % width:
        body(pl.ds(full * width, total % width))


def rms_scale(values):
    return lax.rsqrt(jnp.mean(values * values, axis=-1, keepdims=True) + 1e-05)


def rms_back(values, grad, gain):
    scale = rms_scale(values)
    scaled = grad * gain
    return scale * (
        scaled - values * (scale * scale) * jnp.mean(scaled * values, axis=-1, keepdims=True)
    )


class Exchange:
    def __init__(self, chips, chip, core, group_axis):
        self.chips, self.chip, self.core = chips, chip, core
        self.axis = group_axis

    def sibling(self):
        return {self.axis: self.chip * 2 + 1 - self.core}

    def peer(self, other):
        return {self.axis: other * 2 + self.core}

    def others(self):
        return [lax.rem(self.chip + step, self.chips) for step in range(1, self.chips)]

    def barrier(self):
        flag = pltpu.get_barrier_semaphore()
        pl.semaphore_signal(flag, inc=1, device_id=self.sibling(), device_id_type=MESH)
        for other in self.others():
            pl.semaphore_signal(flag, inc=1, device_id=self.peer(other), device_id_type=MESH)
        pl.semaphore_wait(flag, self.chips)

    def to_sibling(self, source, target, send, recv):
        return pltpu.make_async_remote_copy(
            src_ref=source,
            dst_ref=target,
            send_sem=send,
            recv_sem=recv,
            device_id=self.sibling(),
            device_id_type=MESH,
        )

    def to_peer(self, other, source, target, send, recv):
        return pltpu.make_async_remote_copy(
            src_ref=source,
            dst_ref=target,
            send_sem=send,
            recv_sem=recv,
            device_id=self.peer(other),
            device_id_type=MESH,
        )


class Scatter:
    def __init__(self, net, part, near, far, sems):
        self.net, self.part, self.near, self.far = net, part, near, far
        self.slots = None if part.shape[0] == near.shape[0] else part.shape[0]
        self.near_send, self.near_recv, self.far_send, self.far_recv = sems

    def slot(self, i):
        return i if self.slots is None else i % self.slots

    def landing(self, source, target):
        return lax.rem(source - target + self.net.chips - 1, self.net.chips)

    def near_copy(self, i):
        net = self.net
        return net.to_sibling(
            self.part.at[self.slot(i), 1 - net.core],
            self.near.at[i],
            self.near_send.at[i],
            self.near_recv.at[i],
        )

    def far_copy(self, i, other):
        net = self.net
        return net.to_peer(
            other,
            self.part.at[self.slot(i), net.core, other],
            self.far.at[i, self.landing(net.chip, other)],
            self.far_send.at[i, other],
            self.far_recv.at[i, net.chip],
        )

    def far_landing(self, i, other):
        net = self.net
        return net.to_peer(
            other,
            self.part.at[self.slot(i), net.core, other],
            self.far.at[i, self.landing(other, net.chip)],
            self.far_send.at[i, other],
            self.far_recv.at[i, other],
        )

    def start(self, i):
        self.near_copy(i).start()

    def middle(self, i):
        net = self.net
        self.near_copy(i).wait_recv()
        slot = self.slot(i)
        for other in net.others():
            total = self.part[slot, net.core, other].astype(F32) + self.near[
                i, other
            ].astype(F32)
            self.part[slot, net.core, other] = total.astype(BF16)
            self.far_copy(i, other).start()

    def finish(self, i):
        net = self.net
        slot = self.slot(i)
        total = self.part[slot, net.core, net.chip].astype(F32) + self.near[
            i, net.chip
        ].astype(F32)
        for other in net.others():
            self.far_landing(i, other).wait_recv()
            total = total + self.far[i, self.landing(other, net.chip)].astype(F32)
        return total

    def sent(self, i):
        self.near_copy(i).wait_send()
        for other in self.net.others():
            self.far_copy(i, other).wait_send()


class Gather:
    def __init__(self, net, full, sems, single=False):
        self.net, self.full, self.single = net, full, single
        self.far_send, self.far_recv, self.near_send, self.near_recv = sems

    def block(self, i, *place):
        return self.full.at[place] if self.single else self.full.at[(i, *place)]

    def far_copy(self, i, other):
        net = self.net
        block = self.block(i, net.core, net.chip)
        return net.to_peer(
            other, block, block, self.far_send.at[i, other], self.far_recv.at[i, net.chip]
        )

    def far_landing(self, i, other):
        net = self.net
        block = self.block(i, net.core, other)
        return net.to_peer(
            other, block, block, self.far_send.at[i, other], self.far_recv.at[i, other]
        )

    def near_copy(self, i):
        block = self.block(i, self.net.core)
        return self.net.to_sibling(block, block, self.near_send.at[i], self.near_recv.at[i])

    def near_landing(self, i):
        block = self.block(i, 1 - self.net.core)
        return self.net.to_sibling(block, block, self.near_send.at[i], self.near_recv.at[i])

    def start(self, i):
        for other in self.net.others():
            self.far_copy(i, other).start()

    def middle(self, i):
        for other in self.net.others():
            self.far_landing(i, other).wait_recv()
        self.near_copy(i).start()

    def finish(self, i):
        self.near_landing(i).wait_recv()

    def sent(self, i):
        for other in self.net.others():
            self.far_copy(i, other).wait_send()
        self.near_copy(i).wait_send()


STEPS = (
    ("attend", 0),
    ("attn_part", 0),
    ("attend", 2),
    ("attn_far", 0),
    ("attend", 1),
    ("attn_part", 2),
    ("norm", 0),
    ("attn_part", 1),
    ("attend", 3),
    ("attn_far", 1),
    ("attn_far", 2),
    ("attn_part", 3),
    ("rows_near", 0),
    ("units_low", 0),
    ("norm", 1),
    ("units_high", 0),
    ("unit_grads", 0),
    ("norm", 2),
    ("rows_near", 1),
    ("outputs", 0),
    ("attn_far", 3),
    ("units_far", 0),
    ("units_low", 1),
    ("units_high", 1),
    ("rows_near", 2),
    ("unit_grads", 1),
    ("norm", 3),
    ("outputs", 1),
    ("units_far", 1),
    ("residual", 0),
    ("units_low", 2),
    ("units_high", 2),
    ("rows_near", 3),
    ("unit_grads", 2),
    ("residual", 1),
    ("outputs", 2),
    ("units_low", 3),
    ("units_far", 2),
    ("back_near", 0),
    ("units_high", 3),
    ("back_near", 1),
    ("unit_grads", 3),
    ("residual", 2),
    ("attend_back", 0),
    ("units_far", 3),
    ("back_near", 2),
    ("normed_part", 0),
    ("attend_back", 1),
    ("residual", 3),
    ("normed_part", 1),
    ("normed_far", 0),
    ("attend_back", 2),
    ("normed_far", 1),
    ("back_near", 3),
    ("normed_part", 2),
    ("attend_back", 3),
    ("normed_far", 2),
    ("normed_part", 3),
    ("embed_grad", 0),
    ("outputs", 3),
    ("normed_far", 3),
    ("embed_grad", 1),
    ("token_near", 0),
    ("embed_grad", 2),
    ("token_near", 1),
    ("embed_grad", 3),
    ("token_near", 2),
    ("token_near", 3),
)


def column_of(row):
    return jnp.broadcast_to(row, (8, row.shape[1])).T[:, :1]


def text_body(
    chips,
    dp_count,
    entry_count,
    head_count,
    entry_ids,
    segments,
    cos_t,
    sin_t,
    bias_full,
    gain_one,
    gain_two,
    w_kv,
    entries_hbm,
    weights_hbm,
    token_grad,
    w_query_hbm,
    w_out_hbm,
    w_gate_hbm,
    w_up_hbm,
    w_down_hbm,
    out_part,
    embed_grad,
    pooled_own,
    token_full,
    proj,
    w_query,
    w_out,
    w_gate,
    w_up,
    w_down,
    part_a,
    near_a,
    far_a,
    part_b,
    near_b,
    far_b,
    full,
    grad_full,
    embeds_own,
    q_t,
    q_n,
    k_n,
    v_n,
    k_t,
    v_t,
    out_t,
    logs,
    bias,
    residual,
    weight_sem,
    local_sem,
    stage_sem,
    scatter_near,
    scatter_far_send,
    scatter_far_recv,
    gather_near,
    gather_far_send,
    gather_far_recv,
    grad_near,
    grad_far_send,
    grad_far_recv,
):
    me = lax.axis_index("mp")
    chip, core = me // 2, lax.rem(me, 2)
    net = Exchange(chips, chip, core, "mp")
    group = chips * 2
    chunk_rows = q_n.shape[1]
    width = embeds_own.shape[2]
    units = w_gate.shape[1]
    own_rows = embeds_own.shape[1]
    head_width = FHD * head_count
    columns = proj.shape[3]
    entry_total, entry_width = entries_hbm.shape
    owned = token_grad.shape[0]
    first_own = pl.multiple_of((core * chips + chip) * own_rows, own_rows)
    owners = group // CHUNKS if group > CHUNKS else 1

    def scatter_of(kind, part, near, far):
        return Scatter(
            net,
            part,
            near,
            far,
            (
                scatter_near.at[kind, 0],
                scatter_near.at[kind, 1],
                scatter_far_send.at[kind],
                scatter_far_recv.at[kind],
            ),
        )

    def gather_of(kind, ref):
        return Gather(
            net,
            ref,
            (
                gather_far_send.at[kind],
                gather_far_recv.at[kind],
                gather_near.at[kind, 0],
                gather_near.at[kind, 1],
            ),
        )

    attn_sum = scatter_of(0, part_a, near_a, far_a)
    mlp_sum = scatter_of(1, part_b, near_b, far_b)
    normed_sum = scatter_of(2, part_a, near_a, far_a)
    mlp_rows = gather_of(0, full)
    back_rows = gather_of(1, full)
    token_rows = gather_of(2, token_full)

    def load(k, source, target):
        return pltpu.make_async_copy(source, target, weight_sem.at[k])

    load_proj = load(1, weights_hbm.at[3], proj)
    load_query = load(2, w_query_hbm, w_query)
    load_out = load(3, w_out_hbm, w_out)
    load_units = [
        load(4, w_gate_hbm, w_gate),
        load(5, w_up_hbm, w_up),
        load(6, w_down_hbm, w_down),
    ]

    def grad_far(owner_chip, other):
        return net.to_peer(
            other,
            token_grad,
            grad_full.at[owner_chip * 2 + core],
            grad_far_send.at[other],
            grad_far_recv.at[owner_chip],
        )

    def grad_near_copy(owner_chip, owner_core):
        block = grad_full.at[owner_chip * 2 + owner_core]
        return net.to_sibling(
            block, block, grad_near.at[0, owner_chip], grad_near.at[1, owner_chip]
        )

    grad_local = pltpu.make_async_copy(token_grad, grad_full.at[me], local_sem)

    def grad_start():
        for other in net.others():
            grad_far(chip, other).start()

    def grad_middle():
        grad_local.wait()
        grad_near_copy(chip, core).start()
        for other in net.others():
            grad_far(other, other).wait_recv()
            grad_near_copy(other, core).start()

    def grad_chunk(i):
        return grad_full[i * owners : (i + 1) * owners].reshape(chunk_rows, width)

    def grad_finish(i):
        for owner in range(i * owners, (i + 1) * owners):

            @pl.when(core != owner % 2)
            def _():
                grad_near_copy(owner // 2, owner % 2).wait_recv()

    def embed(entries, pooled, embeds):
        load_entries = load(0, entries_hbm, entries)
        load_entries.start()
        for copy in (load_proj, load_query, load_out, *load_units):
            copy.start()
        grad_local.start()
        net.barrier()
        pl.when(core == 1)(grad_start)
        load_entries.wait()
        load_proj.wait()
        load_query.wait()

        @pl.loop(0, CHUNKS)
        def _(i):
            ids = entry_ids[i]
            owner = ids // entry_count
            owner_mp, owner_dp = lax.rem(owner, group), owner // group
            place = (lax.rem(owner_mp, 2) * chips + owner_mp // 2) * dp_count + owner_dp
            spots = column_of(
                (place * entry_count + lax.rem(ids, entry_count)).astype(F32)
            ).astype(jnp.int32)
            numbers = lax.broadcasted_iota(jnp.int32, (chunk_rows, entry_total), 1)
            chosen = jnp.where(numbers == spots, 1.0, 0.0).astype(BF16)
            pooled[...] = dot_nn(chosen, entries[...]).astype(BF16)
            pooled_own[i] = pooled[pl.ds(first_own, own_rows), :]
            for m, c, y in shards_of(chips):
                span = slice(m * columns, (m + 1) * columns)
                embeds[:, span] = (dot_nn(pooled[...], proj[c, y]) + bias_full[c, y]).astype(BF16)
            embeds_own[i] = embeds[pl.ds(first_own, own_rows), :]
            values = embeds[...].astype(F32)
            embeds[...] = (values * rms_scale(values) * gain_one[...]).astype(BF16)
            cosine, sine = cos_t[i], sin_t[i]

            def turned(block):
                low_half, high_half = block[: FHD // 2], block[FHD // 2 :]
                return jnp.concatenate(
                    [low_half * cosine - high_half * sine, high_half * cosine + low_half * sine],
                    axis=0,
                )

            queries = dot_nn(embeds[...], w_query[...]).T
            for h in range(head_count):
                span = slice(h * FHD, (h + 1) * FHD)
                q_t[i, span, :] = (
                    turned(queries[span]).astype(BF16).astype(F32) * FHD**-0.5
                ).astype(BF16)
            q_n[i] = q_t[i].T
            both = dot_nn(embeds[...], w_kv[...])
            keys_t = turned(both.T[:FHD]).astype(BF16)
            k_t[i] = keys_t
            k_n[i] = keys_t.T
            v_n[i] = both[:, FHD:].astype(BF16)
            v_t[i] = both.T[FHD:].astype(BF16)

        pl.when(core == 0)(grad_start)
        pl.when(core == 1)(grad_middle)

    pl.run_scoped(
        embed,
        pltpu.VMEM((entry_total, entry_width), BF16),
        pltpu.VMEM((chunk_rows, entry_width), BF16),
        pltpu.VMEM((chunk_rows, width), BF16),
    )

    def put_rows(part, slot, columns, values):
        half = chunk_rows // 2
        for k in range(2):
            for j in range(chips):
                first = k * half + j * own_rows
                part[slot, k, j, :, columns] = values[first : first + own_rows]

    def rows_of(ref, i):
        return ref[i].reshape(chunk_rows, width)

    def turned_back(sums_t):
        return sums_t.astype(BF16).T

    def make_bias(i):
        query_spots = i * chunk_rows + lax.broadcasted_iota(jnp.int32, (chunk_rows, chunk_rows), 1)
        query_segments = segments[i].astype(F32)
        for kb in range(i + 1):
            allowed = column_of(segments[kb].astype(F32)) == query_segments
            if kb == i:
                key_spots = kb * chunk_rows + lax.broadcasted_iota(
                    jnp.int32, (chunk_rows, chunk_rows), 0
                )
                allowed = allowed & (key_spots <= query_spots)
            bias[kb] = jnp.where(allowed, 0.0, FAR)

    def head_span(h):
        return pl.ds(pl.multiple_of(h * FHD, FHD), FHD)

    def layer(
        mixed,
        gate_grad,
        up_grad,
        out_stage,
        d_out_t,
        d_out_n,
        d_query_t,
        value_even,
        value_odd,
        key_even,
        key_odd,
    ):
        for ref in (value_even, value_odd, key_even, key_odd):
            ref[...] = jnp.zeros_like(ref)

        def stage_copy(i, tile):
            slot = lax.rem(tile, 2)
            columns = pl.ds(pl.multiple_of(tile * 512, 512), 512)
            return pltpu.make_async_copy(
                out_stage.at[slot], out_part.at[i, :, columns], stage_sem.at[slot]
            )

        def attend(i):
            make_bias(i)

            @pl.loop(0, head_count, unroll=2)
            def _(h):
                query = q_t[i, head_span(h), :]
                scores = [dot_nn(k_n[kb], query) + bias[kb] for kb in range(i + 1)]
                top = jnp.max(scores[0], axis=0, keepdims=True)
                for block in scores[1:]:
                    top = jnp.maximum(top, jnp.max(block, axis=0, keepdims=True))
                total = jnp.zeros_like(top)
                attended = jnp.zeros((FHD, chunk_rows), F32)
                for kb in range(i + 1):
                    weights_block = jnp.exp(scores[kb] - top)
                    total = total + jnp.sum(weights_block, axis=0, keepdims=True)
                    attended = attended + dot_nn(v_t[kb], weights_block.astype(BF16))
                logs[i, h] = top + jnp.log(total)
                out_t[i, head_span(h), :] = (attended / total).astype(BF16)

        def attn_part(i):
            if i == CHUNKS - 1:
                load_out.wait()

            def tile(columns):
                put_rows(part_a, i, columns, turned_back(dot_nn(w_out[columns, :], out_t[i])))

            column_tiles(width, 512, tile)
            attn_sum.start(i)

        def norm(i):
            values = embeds_own[i].astype(F32) + attn_sum.finish(i)
            residual[i] = values
            full[i, core, chip] = (values * rms_scale(values) * gain_two[...]).astype(BF16)
            mlp_rows.start(i)

        def unit_tile(i, columns):
            rows = rows_of(full, i)
            gate_pre = dot_nn(rows, w_gate[:, columns])
            up_pre = dot_nn(rows, w_up[:, columns])
            act_grad = dot_nn(grad_chunk(i), w_down[:, columns])
            inverse = 1.0 / (1.0 + jnp.exp(-gate_pre))
            silu = gate_pre * inverse
            mixed[columns, :] = turned_back(silu * up_pre)
            up_grad[columns, :] = turned_back(act_grad * silu)
            slope = inverse * (1.0 + gate_pre * (1.0 - inverse))
            gate_grad[columns, :] = turned_back(act_grad * up_pre * slope)

        tile_width = 512 if units >= 1024 else 256
        tiles = units // tile_width
        middle_tile = (tiles + 1) // 2

        def unit_tiles(i, first, last):
            @pl.loop(first, last)
            def _(t):
                unit_tile(i, pl.ds(pl.multiple_of(t * tile_width, tile_width), tile_width))

        def units_low(i):
            if i == CHUNKS - 1:
                pl.when(core == 0)(grad_middle)
                for copy in load_units:
                    copy.wait()
            grad_finish(i)
            mlp_rows.finish(i)
            unit_tiles(i, 0, middle_tile)

        def units_high(i):
            unit_tiles(i, middle_tile, tiles)
            if units % tile_width:
                unit_tile(i, pl.ds(tiles * tile_width, units % tile_width))
            mlp_rows.sent(i)

        def unit_grads(i):
            if i + 2 < CHUNKS:
                mlp_sum.sent(i + 2)

            def tile(columns):
                put_rows(
                    part_b,
                    i % 2,
                    columns,
                    turned_back(
                        dot_nn(w_gate[columns, :], gate_grad[...])
                        + dot_nn(w_up[columns, :], up_grad[...])
                    ),
                )

            column_tiles(width, 512, tile)
            mlp_sum.start(i)

        def outputs(i):
            @pl.loop(0, width // 512)
            def _(t):
                columns = pl.ds(pl.multiple_of(t * 512, 512), 512)
                slot = lax.rem(t, 2)
                tile = turned_back(dot_nn(w_down[columns, :], mixed[...]))
                if i == CHUNKS - 1:
                    pl.when(t >= 2)(lambda: stage_copy(i, t).wait())
                else:
                    stage_copy(i, t).wait()
                out_stage[slot] = tile
                own = pl.ds(first_own, own_rows)
                out_stage[slot, own, :] = (
                    out_stage[slot, own, :].astype(F32) + residual[i, :, columns]
                ).astype(BF16)
                stage_copy(i, t).start()

        def residual_back(i):
            grad = mlp_sum.finish(i)
            block = i * owners + first_own // owned
            start = pl.multiple_of(lax.rem(first_own, owned), own_rows)
            own_grad = grad_full[block, pl.ds(start, own_rows), :].astype(F32)
            values = own_grad + rms_back(residual[i], grad, gain_two[...])
            full[i, core, chip] = values.astype(BF16)
            back_rows.start(i)

        def attend_back(i):
            back_rows.finish(i)
            attended_grad = dot_nn(rows_of(full, i), w_out[...]).astype(BF16)
            d_out_n[...] = attended_grad
            d_out_t[...] = attended_grad.T
            make_bias(i)
            cosine, sine = cos_t[i], sin_t[i]

            @pl.loop(0, head_count // 2)
            def _(pair):
                pair_span = pl.ds(pl.multiple_of(pair * 2 * FHD, 2 * FHD), 2 * FHD)
                query_pair = q_n[i, :, pair_span]
                grad_pair = d_out_n[:, pair_span]
                for odd in range(2):
                    h = pair * 2 + odd
                    query = q_t[i, head_span(h), :]
                    grad = d_out_t[head_span(h), :]
                    log_row = logs[i, h]
                    centre = jnp.sum(
                        grad.astype(F32) * out_t[i, head_span(h), :].astype(F32),
                        axis=0,
                        keepdims=True,
                    )
                    value_total = value_odd if odd else value_even
                    key_total = key_odd if odd else key_even
                    query_grad = jnp.zeros((FHD, chunk_rows), F32)
                    for kb in range(i + 1):
                        probs = jnp.exp(dot_nn(k_n[kb], query) + bias[kb] - log_row)
                        value_total[kb] += dot_nn(probs.astype(BF16), grad_pair)
                        score_grad = (probs * (dot_nn(v_n[kb], grad) - centre)).astype(BF16)
                        key_total[kb] += dot_nn(score_grad, query_pair)
                        query_grad = query_grad + dot_nn(k_t[kb], score_grad)
                    query_grad = query_grad * (FHD**-0.5)
                    low_half, high_half = query_grad[: FHD // 2], query_grad[FHD // 2 :]
                    d_query_t[head_span(h), :] = jnp.concatenate(
                        [
                            low_half * cosine + high_half * sine,
                            high_half * cosine - low_half * sine,
                        ],
                        axis=0,
                    ).astype(BF16)

        def normed_part(i):
            attn_sum.sent(i)
            key_grad = (key_even[i][:, :FHD] + key_odd[i][:, FHD:]).T
            cosine, sine = cos_t[i], sin_t[i]
            low_half, high_half = key_grad[: FHD // 2], key_grad[FHD // 2 :]
            value_grad = (value_even[i][:, :FHD] + value_odd[i][:, FHD:]).T
            both = jnp.concatenate(
                [
                    low_half * cosine + high_half * sine,
                    high_half * cosine - low_half * sine,
                    value_grad,
                ],
                axis=0,
            )
            both = both.astype(BF16)

            def tile(columns):
                put_rows(
                    part_a,
                    i,
                    columns,
                    turned_back(
                        dot_nn(w_query[columns, :], d_query_t[...])
                        + dot_nn(w_kv[columns, :], both)
                    ),
                )

            column_tiles(width, 512, tile)
            normed_sum.start(i)

        def embed_back(i):
            grad = normed_sum.finish(i)
            kept = full[i, core, chip].astype(F32)
            values = kept + rms_back(embeds_own[i].astype(F32), grad, gain_one[...])
            embed_grad[i] = values.astype(BF16)
            total = jnp.zeros((own_rows, entry_width), F32)
            for m, c, y in shards_of(chips):
                total = total + dot_nt(
                    embed_grad[i, :, m * columns : (m + 1) * columns], proj[c, y]
                )
            token_full[i, core, chip] = total.astype(BF16)
            token_rows.start(i)

        stages = {
            "attend": attend,
            "attn_part": attn_part,
            "attn_far": attn_sum.middle,
            "norm": norm,
            "rows_near": mlp_rows.middle,
            "units_low": units_low,
            "units_high": units_high,
            "unit_grads": unit_grads,
            "outputs": outputs,
            "units_far": mlp_sum.middle,
            "residual": residual_back,
            "back_near": back_rows.middle,
            "attend_back": attend_back,
            "normed_part": normed_part,
            "normed_far": normed_sum.middle,
            "embed_grad": embed_back,
            "token_near": token_rows.middle,
        }
        for name, turn in STEPS:
            stages[name](CHUNKS - 1 - turn)

        for tile in range(2):
            stage_copy(0, tile).wait()

    lines = (units, chunk_rows)
    keys = (CHUNKS, chunk_rows, 2 * FHD)
    pl.run_scoped(
        layer,
        pltpu.VMEM(lines, BF16),
        pltpu.VMEM(lines, BF16),
        pltpu.VMEM(lines, BF16),
        pltpu.VMEM((2, chunk_rows, 512), BF16),
        pltpu.VMEM((head_width, chunk_rows), BF16),
        pltpu.VMEM((chunk_rows, head_width), BF16),
        pltpu.VMEM((head_width, chunk_rows), BF16),
        pltpu.VMEM(keys, F32),
        pltpu.VMEM(keys, F32),
        pltpu.VMEM(keys, F32),
        pltpu.VMEM(keys, F32),
    )

    @pl.loop(0, CHUNKS)
    def _(i):
        token_rows.finish(i)
        token_rows.sent(i)
        normed_sum.sent(i)
        back_rows.sent(i)

    for i in range(2):
        mlp_sum.sent(i)
    for other in net.others():
        grad_far(chip, other).wait_send()
    for owner_chip in range(chips):
        grad_near_copy(owner_chip, core).wait_send()


def text_layer(
    group,
    dp_count,
    entry_count,
    entry_ids,
    segments,
    cos_t,
    sin_t,
    bias_full,
    gain_one,
    gain_two,
    w_kv,
    entries,
    weights,
    token_grad,
    w_query,
    w_out,
    w_gate,
    w_up,
    w_down,
):
    chips = group // 2
    chunks, _, chunk_rows = entry_ids.shape
    own_rows = chunk_rows // group
    owned, width = token_grad.shape
    head_width = w_query.shape[1]
    head_count = head_width // FHD
    entry_width = entries.shape[1]
    vmem = pl.BlockSpec(memory_space=pltpu.VMEM)
    hbm = pl.BlockSpec(memory_space=pl.ANY)
    dma = pltpu.SemaphoreType.DMA

    def low(*shape):
        return pltpu.VMEM(shape, BF16)

    return pl.pallas_call(
        partial(text_body, chips, dp_count, entry_count, head_count),
        out_shape=(
            jax.ShapeDtypeStruct((chunks, chunk_rows, width), BF16),
            jax.ShapeDtypeStruct((chunks, own_rows, width), BF16),
            jax.ShapeDtypeStruct((chunks, own_rows, entry_width), BF16),
            jax.ShapeDtypeStruct((chunks, 2, chips, own_rows, entry_width), BF16),
        ),
        in_specs=[vmem] * 8 + [hbm] * 8,
        out_specs=(hbm, vmem, vmem, vmem),
        scratch_shapes=[
            low(*weights.shape[1:]),
            low(*w_query.shape),
            low(*w_out.shape),
            low(*w_gate.shape),
            low(*w_up.shape),
            low(*w_down.shape),
            low(chunks, 2, chips, own_rows, width),
            low(chunks, chips, own_rows, width),
            low(chunks, chips - 1, own_rows, width),
            low(2, 2, chips, own_rows, width),
            low(chunks, chips, own_rows, width),
            low(chunks, chips - 1, own_rows, width),
            low(chunks, 2, chips, own_rows, width),
            low(group, owned, width),
            low(chunks, own_rows, width),
            low(chunks, head_width, chunk_rows),
            low(chunks, chunk_rows, head_width),
            low(chunks, chunk_rows, FHD),
            low(chunks, chunk_rows, FHD),
            low(chunks, FHD, chunk_rows),
            low(chunks, FHD, chunk_rows),
            low(chunks, head_width, chunk_rows),
            pltpu.VMEM((chunks, head_count, 1, chunk_rows), F32),
            pltpu.VMEM((chunks, chunk_rows, chunk_rows), F32),
            pltpu.VMEM((chunks, own_rows, width), F32),
            dma((7,)),
            dma,
            dma((2,)),
            dma((3, 2, chunks)),
            dma((3, chunks, chips)),
            dma((3, chunks, chips)),
            dma((3, 2, chunks)),
            dma((3, chunks, chips)),
            dma((3, chunks, chips)),
            dma((2, chips)),
            dma((chips,)),
            dma((chips,)),
        ],
        compiler_params=pltpu.CompilerParams(
            collective_id=0, has_side_effects=True, vmem_limit_bytes=65280 * 1024
        ),
        cost_estimate=pl.CostEstimate(
            flops=90 * 10**9, bytes_accessed=40 * 10**6, transcendentals=20 * 10**6
        ),
    )(
        entry_ids,
        segments,
        cos_t,
        sin_t,
        bias_full,
        gain_one,
        gain_two,
        w_kv,
        entries,
        weights,
        token_grad,
        w_query,
        w_out,
        w_gate,
        w_up,
        w_down,
    )


def norm_parts(values):
    average = jnp.mean(values, axis=-1, keepdims=True)
    centred = values - average
    scale = lax.rsqrt(jnp.mean(centred * centred, axis=-1, keepdims=True) + 1e-05)
    return centred * scale, scale


def norm_back(values, grad, gain):
    unit, scale = norm_parts(values)
    scaled = grad * gain
    back = scale * (
        scaled
        - jnp.mean(scaled, axis=-1, keepdims=True)
        - unit * jnp.mean(scaled * unit, axis=-1, keepdims=True)
    )
    return (
        back,
        jnp.sum(grad * unit, axis=0, keepdims=True),
        jnp.sum(grad, axis=0, keepdims=True),
    )


def gelu_parts(values):
    root = math.sqrt(2.0 / math.pi)
    squared = values * values
    bent = jnp.tanh(root * values * (1.0 + 0.044715 * squared))
    half = 0.5 * (1.0 + bent)
    slope = half + 0.5 * values * (1.0 - bent * bent) * root * (1.0 + 3 * 0.044715 * squared)
    return values * half, slope


def pool_matrix(counts_col, entries, rows):
    entry = lax.broadcasted_iota(jnp.int32, (entries, rows), 0)
    row = lax.broadcasted_iota(jnp.int32, (entries, rows), 1)
    slots = rows // entries
    inside = (row // slots == entry) & (lax.rem(row, slots).astype(F32) < counts_col)
    return jnp.where(inside, 1.0, 0.0)


def spread_matrix(counts_row, entries, rows):
    row = lax.broadcasted_iota(jnp.int32, (rows, entries), 0)
    entry = lax.broadcasted_iota(jnp.int32, (rows, entries), 1)
    slots = rows // entries
    inside = (row // slots == entry) & (lax.rem(row, slots).astype(F32) < counts_row)
    return jnp.where(inside, 1.0, 0.0)


def slot_bias(valid_col, slots):
    rows = valid_col.shape[0]
    key = lax.broadcasted_iota(jnp.int32, (rows, rows), 0)
    query = lax.broadcasted_iota(jnp.int32, (rows, rows), 1)
    return jnp.where((key // slots == query // slots) & (valid_col > 0.5), 0.0, FAR)


ROW_BLOCK = 256


def shards_of(chips):
    return [(y * 2 + c, c, y) for y in range(chips) for c in range(2)]


def each_shard(chips, columns, body):
    @pl.loop(0, 2)
    def _(c):
        @pl.loop(0, chips)
        def _(y):
            first = pl.multiple_of((y * 2 + c) * columns, columns)
            body(c, y, pl.ds(first, columns))


def hyper_body(
    chips,
    dp_count,
    pieces,
    counts_all,
    gain_one,
    shift_one,
    gain_two,
    shift_two,
    w_query,
    w_key,
    w_value,
    w_out,
    bias_own,
    w_up_hbm,
    w_down_hbm,
    w_proj_hbm,
    entries,
    weights_out,
    attn_in,
    q_n,
    k_n,
    v_n,
    attended,
    logs,
    residual,
    ffn_in,
    counts_col,
    counts_row,
    bias_full,
    full,
    q_t,
    v_t,
    out_t,
    bias,
    hidden,
    counts_scratch,
    local_sem,
    store_sem,
    far_send,
    far_recv,
    x_send,
    x_recv,
    near_send,
    near_recv,
    z_send,
    z_recv,
    mate_send,
    mate_recv,
    y_send,
    y_recv,
    last_send,
    last_recv,
    bias_far_send,
    bias_far_recv,
    bias_near,
):
    me = lax.axis_index("mp")
    dp = lax.axis_index("dp")
    chip, core = me // 2, lax.rem(me, 2)
    net = Exchange(chips, chip, core, "mp")
    side = lax.rem(dp, 2)
    mate = dp + 1 - 2 * side
    spot, spots = dp // 2, dp_count // 2
    kinds, _, _, width, columns = full.shape
    sources = (None, w_up_hbm, w_down_hbm, w_proj_hbm)
    rows = pieces.shape[0]
    entry_count = counts_col.shape[0]
    slots = rows // entry_count
    head_columns = columns // 4
    half = width // 2
    heads = width // HD

    flag = pltpu.get_barrier_semaphore()
    pl.semaphore_signal(flag, inc=1, device_id=net.sibling(), device_id_type=MESH)
    for other in net.others():
        pl.semaphore_signal(flag, inc=1, device_id=net.peer(other), device_id_type=MESH)

    pl.semaphore_signal(flag, inc=1, device_id={"dp": mate}, device_id_type=MESH)

    @pl.loop(1, spots)
    def _(j):
        target = lax.rem(spot + j, spots) * 2 + side
        pl.semaphore_signal(flag, inc=1, device_id={"dp": target}, device_id_type=MESH)

    local = [
        pltpu.make_async_copy(sources[k], full.at[k, core, chip], local_sem.at[k - 1])
        for k in range(1, kinds)
    ]
    for copy in local:
        copy.start()
    for j, source in enumerate((w_query, w_key, w_value, w_out)):
        full[0, core, chip, :, j * head_columns : (j + 1) * head_columns] = source[...]
    bias_full[core, chip] = bias_own[...]
    pl.semaphore_wait(flag, chips + spots)

    def rows_half(which):
        return pl.ds(pl.multiple_of(which * half, half), half)

    def far_copy(k, other):
        return net.to_peer(
            other,
            sources[k].at[rows_half(side)] if k else full.at[0, core, chip, rows_half(side)],
            full.at[k, core, chip, rows_half(side)],
            far_send.at[k, other],
            far_recv.at[k, chip],
        )

    def far_landing(k, other):
        block = full.at[k, core, other, rows_half(side)]
        return net.to_peer(other, block, block, far_send.at[k, other], far_recv.at[k, other])

    def x_copy(k, other, which):
        block = full.at[k, core, other, rows_half(which)]
        return pltpu.make_async_remote_copy(
            src_ref=block,
            dst_ref=block,
            send_sem=x_send.at[k, other],
            recv_sem=x_recv.at[k, other],
            device_id={"dp": mate},
            device_id_type=MESH,
        )

    def near_copy(k, which):
        block = full.at[k, which]
        return net.to_sibling(block, block, near_send.at[k], near_recv.at[k])

    def far_middle(k):
        for other in net.others():
            far_landing(k, other).wait_recv()
            x_copy(k, other, side).start()

    def x_middle(k):
        for other in net.others():
            x_copy(k, other, 1 - side).wait_recv()
        if k:
            local[k - 1].wait()
        near_copy(k, core).start()

    def store(k):
        return pltpu.make_async_copy(full.at[k], weights_out.at[k], store_sem.at[k])

    def near_finish(k):
        near_copy(k, 1 - core).wait_recv()
        store(k).start()

    bias_rows = Gather(
        net, bias_full, (bias_far_send, bias_far_recv, bias_near.at[0], bias_near.at[1]), True
    )
    def far_start(k):
        for other in net.others():
            far_copy(k, other).start()

    far_start(0)
    bias_rows.start(0)
    counts_scratch[...] = column_of(counts_all[...].astype(F32))
    own_counts = counts_scratch[pl.ds(pl.multiple_of(me * entry_count, entry_count), entry_count)]
    counts_col[...] = own_counts
    counts_row[...] = jnp.broadcast_to(own_counts, (entry_count, 128)).T[:1]

    values = pieces[...].astype(F32)
    attn_in[...] = (norm_parts(values)[0] * gain_one[...] + shift_one[...]).astype(BF16)
    blocks = rows // ROW_BLOCK
    valid = jnp.sum(spread_matrix(counts_row[...], entry_count, rows), axis=1, keepdims=True)
    for b in range(blocks):
        bias[b] = slot_bias(valid[b * ROW_BLOCK : (b + 1) * ROW_BLOCK], slots)

    far_middle(0)
    far_start(1)
    bias_rows.middle(0)
    far_middle(1)
    far_start(2)
    x_middle(0)
    near_finish(0)
    for m, c, y in shards_of(chips):
        span = slice(m * head_columns, (m + 1) * head_columns)
        projected = dot_nn(attn_in[...], full[0, c, y, :, : 3 * head_columns])
        q_n[:, span] = (projected[:, :head_columns].astype(BF16).astype(F32) * HD**-0.5).astype(
            BF16
        )
        k_n[:, span] = projected[:, head_columns : 2 * head_columns].astype(BF16)
        v_n[:, span] = projected[:, 2 * head_columns :].astype(BF16)
    far_middle(2)
    far_start(3)
    x_middle(1)
    for b in range(blocks):
        block_rows = slice(b * ROW_BLOCK, (b + 1) * ROW_BLOCK)
        q_t[b] = q_n[block_rows, :].T
        v_t[b] = v_n[block_rows, :].T

    def attend_pair(pair):
        pair_span = pl.ds(pl.multiple_of(pair * 2 * HD, 2 * HD), 2 * HD)
        for b in range(blocks):
            key_pair = k_n[b * ROW_BLOCK : (b + 1) * ROW_BLOCK, pair_span]
            for odd in range(2):
                h = pair * 2 + odd
                span = pl.ds(pl.multiple_of(h * HD, HD), HD)
                scores = dot_nn(key_pair[:, odd * HD : (odd + 1) * HD], q_t[b, span, :]) + bias[b]
                top = jnp.max(scores, axis=0, keepdims=True)
                weights = jnp.exp(scores - top)
                total = jnp.sum(weights, axis=0, keepdims=True)
                logs[b, h] = top + jnp.log(total)
                out_t[b, span, :] = (dot_nn(v_t[b, span, :], weights.astype(BF16)) / total).astype(
                    BF16
                )

    pl.loop(0, heads // 4)(attend_pair)
    far_middle(3)
    x_middle(2)
    pl.loop(heads // 4, heads // 2)(attend_pair)
    for b in range(blocks):
        attended[b * ROW_BLOCK : (b + 1) * ROW_BLOCK, :] = out_t[b].T
    total = values
    for m, c, y in shards_of(chips):
        span = slice(m * head_columns, (m + 1) * head_columns)
        total = total + dot_nt(attended[:, span], full[0, c, y, :, 3 * head_columns :])
    residual[...] = total
    ffn_in[...] = (norm_parts(total)[0] * gain_two[...] + shift_two[...]).astype(BF16)
    near_finish(1)
    x_middle(3)
    pool = pool_matrix(counts_col[...], entry_count, rows).astype(BF16)

    def up_shard(c, y, span):
        act = gelu_parts(dot_nn(ffn_in[...], full[1, c, y]))[0]
        hidden[:, span] = dot_nn(pool, act.astype(BF16)).astype(BF16)

    each_shard(chips, columns, up_shard)
    near_finish(2)
    pooled = jnp.sum(
        (residual[...] * valid).reshape(entry_count, slots, width), axis=1
    )
    for m, c, y in shards_of(chips):
        pooled = pooled + dot_nt(hidden[:, m * columns : (m + 1) * columns], full[2, c, y])
    entries[core, chip, dp] = (pooled / counts_col[...]).astype(BF16)

    def z_copy(target, owner):
        piece = entries.at[core, chip, owner * 2 + side]
        return pltpu.make_async_remote_copy(
            src_ref=piece,
            dst_ref=piece,
            send_sem=z_send.at[target],
            recv_sem=z_recv.at[owner],
            device_id={"dp": target * 2 + side},
            device_id_type=MESH,
        )

    def mate_copy(owner, which):
        piece = entries.at[core, chip, owner * 2 + which]
        return pltpu.make_async_remote_copy(
            src_ref=piece,
            dst_ref=piece,
            send_sem=mate_send.at[owner],
            recv_sem=mate_recv.at[owner],
            device_id={"dp": mate},
            device_id_type=MESH,
        )

    def y_copy(other, owner, block):
        piece = entries.at[core, owner, block]
        return net.to_peer(
            other, piece, piece, y_send.at[other, block], y_recv.at[owner, block]
        )

    def y_start(block):
        for other in net.others():
            y_copy(other, chip, block).start()

    @pl.loop(1, spots)
    def _(j):
        z_copy(lax.rem(spot + j, spots), spot).start()

    mate_copy(spot, side).start()
    y_start(dp)
    near_finish(3)
    bias_rows.finish(0)

    @pl.loop(1, spots)
    def _(j):
        source = lax.rem(spot + spots - j, spots)
        z_copy(source, source).wait_recv()
        mate_copy(source, side).start()
        y_start(source * 2 + side)

    @pl.loop(0, spots)
    def _(j):
        source = lax.rem(spot + spots - j, spots)
        mate_copy(source, 1 - side).wait_recv()
        y_start(source * 2 + 1 - side)

    def last_copy(part, c, owner):
        piece = entries.at[c, owner]
        return net.to_sibling(piece, piece, last_send.at[part], last_recv.at[owner])

    last_copy(chip, core, chip).start()
    for other in net.others():

        @pl.loop(0, dp_count)
        def _(block):
            y_copy(other, other, block).wait_recv()

        last_copy(other, core, other).start()
    last_copy(chip, 1 - core, chip).wait_recv()
    for other in net.others():
        last_copy(other, 1 - core, other).wait_recv()

    bias_rows.sent(0)
    for k in range(kinds):
        store(k).wait()
        near_copy(k, core).wait_send()
        for other in net.others():
            far_copy(k, other).wait_send()
            x_copy(k, other, side).wait_send()

    @pl.loop(1, spots)
    def _(j):
        z_copy(lax.rem(spot + j, spots), spot).wait_send()

    @pl.loop(0, spots)
    def _(j):
        mate_copy(j, side).wait_send()

    last_copy(chip, core, chip).wait_send()
    for other in net.others():
        last_copy(other, core, other).wait_send()

        @pl.loop(0, dp_count)
        def _(block):
            y_copy(other, chip, block).wait_send()


def hyper_forward(
    group,
    dp_count,
    pieces,
    counts,
    gain_one,
    shift_one,
    gain_two,
    shift_two,
    head_weights,
    bias_own,
    unit_weights,
):
    chips = group // 2
    rows, width = pieces.shape
    columns = unit_weights[0].shape[1]
    kinds = 4
    entry_count = counts.shape[1] // group
    heads = width // HD
    blocks = rows // ROW_BLOCK
    vmem = pl.BlockSpec(memory_space=pltpu.VMEM)
    hbm = pl.BlockSpec(memory_space=pl.ANY)
    row_shape = jax.ShapeDtypeStruct((rows, width), BF16)
    dma = pltpu.SemaphoreType.DMA
    return pl.pallas_call(
        partial(hyper_body, chips, dp_count),
        out_shape=(
            jax.ShapeDtypeStruct((2, chips, dp_count, entry_count, width), BF16),
            jax.ShapeDtypeStruct((kinds, 2, chips, width, columns), BF16),
            row_shape,
            row_shape,
            row_shape,
            row_shape,
            row_shape,
            jax.ShapeDtypeStruct((blocks, heads, 1, ROW_BLOCK), F32),
            jax.ShapeDtypeStruct((rows, width), F32),
            row_shape,
            jax.ShapeDtypeStruct((entry_count, 1), F32),
            jax.ShapeDtypeStruct((1, entry_count), F32),
            jax.ShapeDtypeStruct((2, chips, 1, columns), F32),
        ),
        in_specs=[vmem] * 11 + [hbm] * 3,
        out_specs=(vmem, hbm) + (vmem,) * 11,
        scratch_shapes=[
            pltpu.VMEM((kinds, 2, chips, width, columns), BF16),
            pltpu.VMEM((blocks, width, ROW_BLOCK), BF16),
            pltpu.VMEM((blocks, width, ROW_BLOCK), BF16),
            pltpu.VMEM((blocks, width, ROW_BLOCK), BF16),
            pltpu.VMEM((blocks, ROW_BLOCK, ROW_BLOCK), F32),
            pltpu.VMEM((entry_count, columns * group), BF16),
            pltpu.VMEM((counts.shape[1], 1), F32),
            dma((kinds - 1,)),
            dma((kinds,)),
            dma((kinds, chips)),
            dma((kinds, chips)),
            dma((kinds, chips)),
            dma((kinds, chips)),
            dma((kinds,)),
            dma((kinds,)),
            dma((dp_count // 2,)),
            dma((dp_count // 2,)),
            dma((dp_count // 2,)),
            dma((dp_count // 2,)),
            dma((chips, dp_count)),
            dma((chips, dp_count)),
            dma((chips,)),
            dma((chips,)),
            dma((1, chips)),
            dma((1, chips)),
            dma((2, 1)),
        ],
        compiler_params=pltpu.CompilerParams(
            collective_id=1, has_side_effects=True, vmem_limit_bytes=60 * 1024 * 1024
        ),
        cost_estimate=pl.CostEstimate(
            flops=60 * 10**9, bytes_accessed=20 * 10**6, transcendentals=5 * 10**6
        ),
    )(
        pieces,
        counts,
        gain_one,
        shift_one,
        gain_two,
        shift_two,
        *head_weights,
        bias_own,
        *unit_weights,
    )


class Total:
    def __init__(self, net, dp, dp_count, scatter, mine, x_land, z_land, final, sems):
        self.net, self.scatter, self.mine = net, scatter, mine
        self.x_land, self.z_land, self.final = x_land, z_land, final
        self.x_send, self.x_recv, self.z_send, self.z_recv = sems[:4]
        self.g_send, self.g_recv, self.l_send, self.l_recv = sems[4:]
        self.side = lax.rem(dp, 2)
        self.spot = dp // 2
        self.mate = dp + 1 - 2 * self.side
        self.spots = dp_count // 2

    def remote(self, source, target, send, recv, device):
        return pltpu.make_async_remote_copy(
            src_ref=source,
            dst_ref=target,
            send_sem=send,
            recv_sem=recv,
            device_id={"dp": device},
            device_id_type=MESH,
        )

    def x_copy(self, k):
        return self.remote(
            self.mine.at[k, 1 - self.side],
            self.x_land.at[k],
            self.x_send.at[k],
            self.x_recv.at[k],
            self.mate,
        )

    def z_copy(self, k, spot, slot):
        return self.remote(
            self.mine.at[k, self.side, spot],
            self.z_land.at[k, slot],
            self.z_send.at[k, spot],
            self.z_recv.at[k, slot],
            spot * 2 + self.side,
        )

    def g_copy(self, k, spot, owner):
        block = self.final.at[k, self.side, owner]
        return self.remote(
            block, block, self.g_send.at[k, spot], self.g_recv.at[k, owner], spot * 2 + self.side
        )

    def l_copy(self, k, side):
        block = self.final.at[k, side]
        return self.remote(block, block, self.l_send.at[k], self.l_recv.at[k], self.mate)

    def each_spot(self, body):
        if self.spots > 1:

            @pl.loop(1, self.spots)
            def _(j):
                body(lax.rem(self.spot + j, self.spots))

    def start(self, k):
        self.scatter.start(k)

    def near_middle(self, k):
        self.scatter.middle(k)

    def far_middle(self, k):
        total = self.scatter.finish(k)
        self.mine[k] = total.astype(BF16).reshape(self.mine.shape[1:])
        self.x_copy(k).start()

    def x_middle(self, k):
        self.x_copy(k).wait_recv()
        block = self.mine[k, self.side].astype(F32) + self.x_land[k].astype(F32)
        self.mine[k, self.side] = block.astype(BF16)
        self.each_spot(lambda spot: self.z_copy(k, spot, self.spot).start())

    def z_middle(self, k):
        def add(spot):
            self.z_copy(k, spot, spot).wait_recv()

        self.each_spot(add)
        total = self.mine[k, self.side, self.spot].astype(F32)
        for j in range(1, self.spots):
            spot = lax.rem(self.spot + j, self.spots)
            total = total + self.z_land[k, spot].astype(F32)
        self.final[k, self.side, self.spot] = total.astype(BF16)
        self.each_spot(lambda spot: self.g_copy(k, spot, self.spot).start())

    def g_middle(self, k):
        self.each_spot(lambda spot: self.g_copy(k, spot, spot).wait_recv())
        self.l_copy(k, self.side).start()

    def finish(self, k):
        self.l_copy(k, 1 - self.side).wait_recv()

    def sent(self, k):
        self.scatter.sent(k)
        self.x_copy(k).wait_send()
        self.each_spot(lambda spot: self.z_copy(k, spot, self.spot).wait_send())
        self.each_spot(lambda spot: self.g_copy(k, spot, self.spot).wait_send())
        self.l_copy(k, self.side).wait_send()


PARTS = 8


def back_body(
    chips,
    dp_count,
    embed_rows,
    pooled_own,
    token_rows,
    token_row,
    pieces,
    counts_col,
    counts_row,
    gain_one,
    gain_two,
    attn_in,
    q_n,
    k_n,
    v_n,
    attended,
    logs,
    residual,
    ffn_in,
    weights_hbm,
    out_part,
    pieces_grad,
    final,
    small_total,
    text_out,
    weights,
    part,
    near,
    far,
    mine,
    x_land,
    z_land,
    entry_part,
    entry_land,
    hidden,
    hidden_pre,
    ffn_t,
    row_total,
    d_out_n,
    d_query,
    d_key,
    d_value,
    q_t,
    out_t,
    d_out_t,
    k_t,
    d_query_t,
    bias,
    small_near,
    small_far,
    small_dp,
    small_part,
    out_own,
    out_near,
    out_far,
    weight_sem,
    out_local,
    out_near_sem,
    out_far_send,
    out_far_recv,
    entry_send,
    entry_recv,
    scatter_near,
    scatter_far_send,
    scatter_far_recv,
    x_sem,
    z_send,
    z_recv,
    g_send,
    g_recv,
    l_sem,
    small_sem,
    small_far_send,
    small_far_recv,
    small_dp_send,
    small_dp_recv,
):
    me = lax.axis_index("mp")
    dp = lax.axis_index("dp")
    group = chips * 2
    chip, core = me // 2, lax.rem(me, 2)
    net = Exchange(chips, chip, core, "mp")
    rows, width = pieces.shape
    entry_count = counts_col.shape[0]
    slots = rows // entry_count
    columns = weights.shape[4]
    half_columns = columns // 2
    head_columns = columns // 4
    heads = width // HD
    blocks = rows // ROW_BLOCK
    total_sum = Total(
        net,
        dp,
        dp_count,
        Scatter(
            net,
            part,
            near,
            far,
            (scatter_near.at[0], scatter_near.at[1], scatter_far_send, scatter_far_recv),
        ),
        mine,
        x_land,
        z_land,
        final,
        (x_sem.at[0], x_sem.at[1], z_send, z_recv, g_send, g_recv, l_sem.at[0], l_sem.at[1]),
    )
    stages = (
        total_sum.near_middle,
        total_sum.far_middle,
        total_sum.x_middle,
        total_sum.z_middle,
        total_sum.g_middle,
        total_sum.finish,
    )

    def run(step):
        for offset, stage in enumerate(stages):
            if 0 <= step - offset < PARTS:
                stage(step - offset)

    flag = pltpu.get_barrier_semaphore()
    pl.semaphore_signal(flag, inc=1, device_id=net.sibling(), device_id_type=MESH)
    for other in net.others():
        pl.semaphore_signal(flag, inc=1, device_id=net.peer(other), device_id_type=MESH)

    def each_dp(body):
        @pl.loop(1, dp_count)
        def _(j):
            body(lax.rem(dp + j, dp_count))

    each_dp(
        lambda target: pl.semaphore_signal(
            flag, inc=1, device_id={"dp": target}, device_id_type=MESH
        )
    )
    loads = [
        pltpu.make_async_copy(weights_hbm.at[k], weights.at[k], weight_sem.at[k])
        for k in (1, 2, 0)
    ]
    for copy in loads:
        copy.start()
    out_copies = [
        pltpu.make_async_copy(out_part.at[y * 2 + core], out_own.at[y], out_local.at[y])
        for y in range(chips)
    ]
    for copy in out_copies:
        copy.start()
    pl.semaphore_wait(flag, chips + dp_count - 1)

    def out_near_copy(y):
        return net.to_sibling(
            out_part.at[y * 2 + 1 - core],
            out_near.at[y],
            out_near_sem.at[0, y],
            out_near_sem.at[1, y],
        )

    out_half = out_part.shape[1] // 2

    def out_far_copy(other, source, half):
        target = chip if source is not chip else other
        span = pl.ds(half * out_half, out_half)
        return net.to_peer(
            other,
            out_own.at[other, span],
            out_far.at[lax.rem(source - target + chips - 1, chips), span],
            out_far_send.at[half, other],
            out_far_recv.at[half, source],
        )

    def out_middle(half):
        span = pl.ds(half * out_half, out_half)
        for y in range(chips):
            if half == 0:
                out_copies[y].wait()
                out_near_copy(y).wait_recv()
        for other in net.others():
            out_own[other, span] = (
                out_own[other, span].astype(F32) + out_near[other, span].astype(F32)
            ).astype(BF16)
            out_far_copy(other, chip, half).start()

    for y in range(chips):
        out_near_copy(y).start()

    def put(k, c, y, values):
        part[k, c, y] = values[:, :half_columns].astype(BF16)
        part[k + 1, c, y] = values[:, half_columns:].astype(BF16)

    token_total = token_rows.shape[0]
    dp_step = max(1, ROW_BLOCK // entry_count)

    @pl.loop(0, dp_count // dp_step)
    def _(block):
        row = lax.broadcasted_iota(jnp.int32, (dp_step * entry_count, token_total), 0)
        owner = block * dp_step + row // entry_count
        number = (owner * group + me) * entry_count + lax.rem(row, entry_count)
        chosen = jnp.where(number == token_row[...], 1.0, 0.0).astype(BF16)
        sums = dot_nn(chosen, token_rows[...]).astype(BF16)
        for j in range(dp_step):
            entry_part[block * dp_step + j] = sums[j * entry_count : (j + 1) * entry_count]

    def entry_copy(target, slot):
        return pltpu.make_async_remote_copy(
            src_ref=entry_part.at[target],
            dst_ref=entry_land.at[slot],
            send_sem=entry_send.at[target],
            recv_sem=entry_recv.at[slot],
            device_id={"dp": target},
            device_id_type=MESH,
        )

    each_dp(lambda target: entry_copy(target, dp).start())
    pooled_t = pooled_own[...].T

    def proj_shard(c, y, span):
        put(0, c, y, dot_nn(pooled_t, embed_rows[:, span]))

    each_shard(chips, columns, proj_shard)
    total_sum.start(0)
    total_sum.start(1)
    bias_sums = jnp.sum(embed_rows[...].astype(F32), axis=0, keepdims=True)
    for j in range(4):
        small_part[4 + j : 5 + j, :] = bias_sums[:, j * width : (j + 1) * width]
    loads[0].wait()
    run(0)

    pool = pool_matrix(counts_col[...], entry_count, rows).astype(BF16)
    spread = spread_matrix(counts_row[...], entry_count, rows)
    valid = jnp.sum(spread, axis=1, keepdims=True)
    spread = spread.astype(BF16)
    for b in range(blocks):
        bias[b] = slot_bias(valid[b * ROW_BLOCK : (b + 1) * ROW_BLOCK], slots)
    ffn_t[...] = ffn_in[...].T

    def hidden_shard(c, y, span):
        before = dot_nn(ffn_in[...], weights[1, c, y])
        hidden_pre[:, span] = before
        hidden[:, span] = dot_nn(pool, gelu_parts(before)[0].astype(BF16)).astype(BF16)

    def some_shards(shards, body):
        @pl.loop(shards * group // 2, (shards + 1) * group // 2)
        def _(m):
            first = pl.multiple_of(m * columns, columns)
            body(lax.rem(m, 2), m // 2, pl.ds(first, columns))

    some_shards(0, hidden_shard)
    run(1)
    some_shards(1, hidden_shard)
    out_middle(0)
    each_dp(lambda source: entry_copy(source, source).wait_recv())
    pooled_grad = entry_part[dp].astype(F32)
    for j in range(1, dp_count):
        pooled_grad = pooled_grad + entry_land[lax.rem(dp + j, dp_count)].astype(F32)
    entry_low = (pooled_grad / counts_col[...]).astype(BF16)
    out_rows = dot_nn(spread, entry_low)
    entry_t = entry_low.T
    loads[1].wait()
    out_low = out_rows.astype(BF16)
    row_total[...] = jnp.zeros_like(row_total)

    def down_shard(c, y, span):
        put(2, c, y, dot_nn(entry_t, hidden[:, span]))

    each_shard(chips, columns, down_shard)
    total_sum.start(2)
    total_sum.start(3)

    def unit_shard(c, y, span):
        act_grad = dot_nn(out_low, weights[2, c, y])
        pre_grad = (act_grad * gelu_parts(hidden_pre[:, span])[1]).astype(BF16)
        put(4, c, y, dot_nn(ffn_t[...], pre_grad))
        row_total[...] += dot_nt(pre_grad, weights[1, c, y])

    some_shards(0, unit_shard)
    run(2)
    some_shards(1, unit_shard)
    total_sum.start(4)
    total_sum.start(5)
    run(3)
    back, gain_grad, shift_grad = norm_back(residual[...], row_total[...], gain_two[...])
    small_part[2:3, :] = gain_grad
    small_part[3:4, :] = shift_grad
    residual_grad = out_rows + back
    pieces_grad[...] = residual_grad
    attn_grad = residual_grad.astype(BF16)
    loads[2].wait()
    for m, c, y in shards_of(chips):
        span = slice(m * head_columns, (m + 1) * head_columns)
        d_out_n[:, span] = dot_nn(attn_grad, weights[0, c, y, :, 3 * head_columns :]).astype(BF16)
    out_grad = dot_nn(attn_grad.T, attended[...])
    for m, c, y in shards_of(chips):
        span = slice(m * head_columns, (m + 1) * head_columns)
        part[7, c, y, :, head_columns:] = out_grad[:, span].astype(BF16)
    for b in range(blocks):
        block_rows = slice(b * ROW_BLOCK, (b + 1) * ROW_BLOCK)
        q_t[b] = q_n[block_rows, :].T
        k_t[b] = k_n[block_rows, :].T
        out_t[b] = attended[block_rows, :].T
        d_out_t[b] = d_out_n[block_rows, :].T
    run(4)

    def attend_pair(pair):
        pair_span = pl.ds(pl.multiple_of(pair * 2 * HD, 2 * HD), 2 * HD)
        for b in range(blocks):
            block_rows = slice(b * ROW_BLOCK, (b + 1) * ROW_BLOCK)
            key_pair = k_n[block_rows, pair_span]
            value_pair = v_n[block_rows, pair_span]
            query_pair = q_n[block_rows, pair_span]
            grad_pair = d_out_n[block_rows, pair_span]
            key_sums, value_sums = [], []
            for odd in range(2):
                h = pair * 2 + odd
                span = pl.ds(pl.multiple_of(h * HD, HD), HD)
                lanes = slice(odd * HD, (odd + 1) * HD)
                scores = dot_nn(key_pair[:, lanes], q_t[b, span, :]) + bias[b]
                probs = jnp.exp(scores - logs[b, h])
                grad_t = d_out_t[b, span, :]
                centre = jnp.sum(
                    grad_t.astype(F32) * out_t[b, span, :].astype(F32), axis=0, keepdims=True
                )
                value_sums.append(dot_nn(probs.astype(BF16), grad_pair[:, lanes]))
                score_grad = (probs * (dot_nn(value_pair[:, lanes], grad_t) - centre)).astype(BF16)
                key_sums.append(dot_nn(score_grad, query_pair[:, lanes]))
                d_query_t[b, span, :] = (
                    dot_nn(k_t[b, span, :], score_grad) * (HD**-0.5)
                ).astype(BF16)
            d_key[block_rows, pair_span] = jnp.concatenate(key_sums, axis=1).astype(BF16)
            d_value[block_rows, pair_span] = jnp.concatenate(value_sums, axis=1).astype(BF16)

    pl.loop(0, heads // 4)(attend_pair)
    run(5)
    pl.loop(heads // 4, heads // 2)(attend_pair)
    for b in range(blocks):
        d_query[b * ROW_BLOCK : (b + 1) * ROW_BLOCK, :] = d_query_t[b].T
    rows_t = attn_in[...].T
    for place, (k, lanes, source) in enumerate(
        ((6, 0, d_query), (6, 1, d_key), (7, 0, d_value))
    ):
        grads = dot_nn(rows_t, source[...])
        for m, c, y in shards_of(chips):
            span = slice(m * head_columns, (m + 1) * head_columns)
            part[k, c, y, :, lanes * head_columns : (lanes + 1) * head_columns] = grads[
                :, span
            ].astype(BF16)
    total_sum.start(6)
    total_sum.start(7)
    run(6)
    normed = jnp.zeros((rows, width), F32)
    for m, c, y in shards_of(chips):
        span = slice(m * head_columns, (m + 1) * head_columns)
        for j, source in enumerate((d_query, d_key, d_value)):
            normed = normed + dot_nt(
                source[:, span], weights[0, c, y, :, j * head_columns : (j + 1) * head_columns]
            )
    back, gain_grad, shift_grad = norm_back(pieces[...].astype(F32), normed, gain_one[...])
    small_part[0:1, :] = gain_grad
    small_part[1:2, :] = shift_grad
    pieces_grad[...] += back

    def out_finish():
        text_out[...] = out_own[chip].astype(F32) + out_near[chip].astype(F32)
        for other in net.others():
            for half in range(2):
                out_far_copy(other, other, half).wait_recv()
            slot = lax.rem(other - chip + chips - 1, chips)
            text_out[...] += out_far[slot].astype(F32)

    small_copy = net.to_sibling(small_part, small_near, small_sem.at[0], small_sem.at[1])
    small_copy.start()

    def small_far_copy(other, owner):
        return net.to_peer(
            other,
            small_far.at[owner],
            small_far.at[owner],
            small_far_send.at[other],
            small_far_recv.at[owner],
        )

    def small_dp_copy(other, owner):
        return pltpu.make_async_remote_copy(
            src_ref=small_dp.at[owner],
            dst_ref=small_dp.at[owner],
            send_sem=small_dp_send.at[other],
            recv_sem=small_dp_recv.at[owner],
            device_id={"dp": other},
            device_id_type=MESH,
        )

    def small_near_done():
        small_copy.wait_recv()
        small_far[chip] = small_part[...] + small_near[...]
        for other in net.others():
            small_far_copy(other, chip).start()

    def small_far_done():
        for other in net.others():
            small_far_copy(other, other).wait_recv()
        total = small_far[0]
        for j in range(1, chips):
            total = total + small_far[j]
        small_dp[dp] = total
        each_dp(lambda other: small_dp_copy(other, dp).start())

    @pl.loop(7, PARTS + 5)
    def _(step):
        for offset, stage in enumerate(stages):
            k = step - offset

            @pl.when((k >= 0) & (k < PARTS))
            def _():
                stage(k)

        pl.when(step == 7)(small_near_done)
        pl.when(step == 9)(small_far_done)
        pl.when(step == PARTS)(lambda: out_middle(1))

    out_finish()
    each_dp(lambda other: small_dp_copy(other, other).wait_recv())
    total = small_dp[0]
    for j in range(1, dp_count):
        total = total + small_dp[j]
    small_total[...] = total

    for y in range(chips):
        out_near_copy(y).wait_send()
    for other in net.others():
        for half in range(2):
            out_far_copy(other, chip, half).wait_send()
    small_copy.wait_send()
    for other in net.others():
        small_far_copy(other, chip).wait_send()
    each_dp(lambda other: small_dp_copy(other, dp).wait_send())
    each_dp(lambda other: entry_copy(other, dp).wait_send())

    @pl.loop(0, PARTS)
    def _(k):
        total_sum.sent(k)


def hyper_backward(
    group,
    dp_count,
    embed_rows,
    pooled_own,
    token_rows,
    token_row,
    pieces,
    counts_col,
    counts_row,
    gain_one,
    gain_two,
    saved,
    weights,
    out_part,
):
    chips = group // 2
    rows, width = pieces.shape
    entry_count = counts_col.shape[0]
    kinds, columns = weights.shape[0], weights.shape[4]
    half_columns = columns // 2
    heads = width // HD
    blocks = rows // ROW_BLOCK
    spots = dp_count // 2
    vmem = pl.BlockSpec(memory_space=pltpu.VMEM)
    hbm = pl.BlockSpec(memory_space=pl.ANY)
    dma = pltpu.SemaphoreType.DMA
    final = (PARTS, 2, spots, width // (2 * spots), half_columns)
    units = columns * group

    def low(*shape):
        return pltpu.VMEM(shape, BF16)

    def wide(*shape):
        return pltpu.VMEM(shape, F32)

    return pl.pallas_call(
        partial(back_body, chips, dp_count),
        out_shape=(
            jax.ShapeDtypeStruct((rows, width), F32),
            jax.ShapeDtypeStruct(final, BF16),
            jax.ShapeDtypeStruct((8, width), F32),
            jax.ShapeDtypeStruct(out_part.shape[1:], F32),
        ),
        in_specs=[vmem] * 17 + [hbm] * 2,
        out_specs=(vmem,) * 4,
        scratch_shapes=[
            low(kinds, 2, chips, width, columns),
            low(PARTS, 2, chips, width, half_columns),
            low(PARTS, chips, width, half_columns),
            low(PARTS, chips - 1, width, half_columns),
            low(*final),
            low(PARTS, spots, width // (2 * spots), half_columns),
            low(PARTS, spots, width // (2 * spots), half_columns),
            low(dp_count, entry_count, width),
            low(dp_count, entry_count, width),
            low(entry_count, units),
            wide(rows, units),
            low(width, rows),
            wide(rows, width),
            low(rows, width),
            low(rows, width),
            low(rows, width),
            low(rows, width),
        ]
        + [low(blocks, width, ROW_BLOCK)] * 5
        + [
            wide(blocks, ROW_BLOCK, ROW_BLOCK),
            wide(8, width),
            wide(chips, 8, width),
            wide(dp_count, 8, width),
            wide(8, width),
            low(chips, *out_part.shape[1:]),
            low(chips, *out_part.shape[1:]),
            low(chips - 1, *out_part.shape[1:]),
            dma((kinds,)),
            dma((chips,)),
            dma((2, chips)),
            dma((2, chips)),
            dma((2, chips)),
            dma((dp_count,)),
            dma((dp_count,)),
            dma((2, PARTS)),
            dma((PARTS, chips)),
            dma((PARTS, chips)),
            dma((2, PARTS)),
            dma((PARTS, spots)),
            dma((PARTS, spots)),
            dma((PARTS, spots)),
            dma((PARTS, spots)),
            dma((2, PARTS)),
            dma((2,)),
            dma((chips,)),
            dma((chips,)),
            dma((dp_count,)),
            dma((dp_count,)),
        ],
        compiler_params=pltpu.CompilerParams(
            collective_id=2, has_side_effects=True, vmem_limit_bytes=62 * 1024 * 1024
        ),
        cost_estimate=pl.CostEstimate(
            flops=60 * 10**9, bytes_accessed=20 * 10**6, transcendentals=5 * 10**6
        ),
    )(
        embed_rows,
        pooled_own,
        token_rows,
        token_row,
        pieces,
        counts_col,
        counts_row,
        gain_one,
        gain_two,
        *saved,
        weights,
        out_part,
    )


def spread_body(sums, query, key, value, out, up, down, proj):
    half_columns = sums.shape[2]
    head_columns = query.shape[1]
    for first, target in ((0, proj), (2, down), (4, up)):
        target[:, :half_columns] = sums[first].astype(F32)
        target[:, half_columns:] = sums[first + 1].astype(F32)
    for k, lanes, target in ((6, 0, query), (6, 1, key), (7, 0, value), (7, 1, out)):
        target[...] = sums[k, :, lanes * head_columns : (lanes + 1) * head_columns].astype(F32)


def spread_sums(sums):
    _, width, half_columns = sums.shape
    small = jax.ShapeDtypeStruct((width, half_columns // 2), F32)
    large = jax.ShapeDtypeStruct((width, half_columns * 2), F32)
    vmem = pl.BlockSpec(memory_space=pltpu.VMEM)
    return pl.pallas_call(
        spread_body,
        out_shape=(small,) * 4 + (large,) * 3,
        in_specs=[vmem],
        out_specs=(vmem,) * 7,
        compiler_params=pltpu.CompilerParams(vmem_limit_bytes=40 * 1024 * 1024),
    )(sums)


def on_device(
    pieces,
    counts,
    entry_ids,
    segment_ids,
    norm1_gain,
    norm1_shift,
    query_weight,
    key_weight,
    value_weight,
    out_weight,
    norm2_gain,
    norm2_shift,
    up_weight,
    down_weight,
    proj_weight,
    proj_bias,
    text_norm1_gain,
    text_query,
    text_key,
    text_value,
    text_out_proj,
    text_norm2_gain,
    text_gate,
    text_up,
    text_down,
    token_grad,
):
    group, dp_count = lax.axis_size("mp"), lax.axis_size("dp")
    me = lax.axis_index("mp")
    entry_count, slot_count, width = pieces.shape
    text_width = token_grad.shape[1]
    length = segment_ids.shape[1]
    chunk_rows = length // CHUNKS
    pieces_rows = pieces.reshape(entry_count * slot_count, width)
    entries, weights, *saved, counts_col, counts_row, bias_full = hyper_forward(
        group,
        dp_count,
        pieces_rows,
        counts[None, :],
        norm1_gain[None, :],
        norm1_shift[None, :],
        norm2_gain[None, :],
        norm2_shift[None, :],
        (query_weight, key_weight, value_weight, out_weight),
        proj_bias[None, :],
        (up_weight, down_weight, proj_weight),
    )
    head_width = text_query.shape[1]
    kv_index = me * (head_width // FHD) // (QHEADS // KVHEADS)
    key_local = lax.dynamic_slice_in_dim(text_key, kv_index * FHD, FHD, 1)
    value_local = lax.dynamic_slice_in_dim(text_value, kv_index * FHD, FHD, 1)
    key_value = jnp.concatenate([key_local, value_local], axis=1)
    cos_t, sin_t = rope_tables(length)
    out_part, embed_rows, pooled_own, token_rows = text_layer(
        group,
        dp_count,
        entry_count,
        entry_ids.reshape(CHUNKS, 1, chunk_rows),
        segment_ids.reshape(CHUNKS, 1, chunk_rows),
        cos_t,
        sin_t,
        bias_full,
        text_norm1_gain[None, :],
        text_norm2_gain[None, :],
        key_value,
        entries.reshape(-1, width),
        weights,
        token_grad,
        text_query,
        text_out_proj,
        text_gate,
        text_up,
        text_down,
    )
    pieces_grad, final, small, text_out = hyper_backward(
        group,
        dp_count,
        embed_rows.reshape(-1, text_width),
        pooled_own.reshape(-1, width),
        token_rows.reshape(length, width),
        entry_ids[None, :],
        pieces_rows,
        counts_col,
        counts_row,
        norm1_gain[None, :],
        norm2_gain[None, :],
        saved,
        weights,
        out_part.reshape(group, -1, text_width),
    )
    query_grad, key_grad, value_grad, out_grad, up_grad, down_grad, proj_grad = spread_sums(
        final.reshape(PARTS, width, -1)
    )
    bias_share = proj_bias.shape[0]
    proj_bias_grad = lax.dynamic_slice_in_dim(
        small[4:].reshape(-1), me * bias_share, bias_share
    )
    return (
        text_out,
        pieces_grad.reshape(pieces.shape),
        small[0],
        small[1],
        query_grad,
        key_grad,
        value_grad,
        out_grad,
        small[2],
        small[3],
        up_grad,
        down_grad,
        proj_grad,
        proj_bias_grad,
    )


def solution(mesh):
    return jax.shard_map(
        on_device,
        mesh=mesh,
        in_specs=(
            P(("dp", "mp"), None, None),
            P("dp"),
            P("dp"),
            P("dp", None),
            P(),
            P(),
            P(None, "mp"),
            P(None, "mp"),
            P(None, "mp"),
            P(None, "mp"),
            P(),
            P(),
            P(None, "mp"),
            P(None, "mp"),
            P(None, "mp"),
            P("mp"),
            P(),
            P(None, "mp"),
            P(),
            P(),
            P(None, "mp"),
            P(),
            P(None, "mp"),
            P(None, "mp"),
            P(None, "mp"),
            P(("dp", "mp"), None),
        ),
        out_specs=(
            P(("dp", "mp"), None),
            P(("dp", "mp"), None, None),
            P(),
            P(),
            P(None, "mp"),
            P(None, "mp"),
            P(None, "mp"),
            P(None, "mp"),
            P(),
            P(),
            P(None, "mp"),
            P(None, "mp"),
            P(None, "mp"),
            P("mp"),
        ),
        check_vma=False,
    )
```

```python
from functools import partial
import math

import jax
import jax.numpy as jnp
import numpy as np
from jax import lax
from jax.experimental import pallas as pl
from jax.experimental.pallas import tpu as pltpu
from jax.sharding import PartitionSpec as P

HD = 64
QHEADS = 32
KVHEADS = 4
FHD = 64


def rope_tables(length):
    positions = np.arange(length, dtype=np.float32)
    rates = np.exp(
        np.arange(FHD // 2, dtype=np.float32) * np.float32(-2.0 * math.log(10000.0) / FHD)
    ).astype(np.float32)
    angles = (positions[None, :] * rates[:, None]).reshape(FHD // 2, CHUNKS, length // CHUNKS)
    angles = angles.transpose(1, 0, 2)
    return jnp.asarray(np.cos(angles)), jnp.asarray(np.sin(angles))


MESH = pl.DeviceIdType.MESH
F32 = jnp.float32
BF16 = jnp.bfloat16
CHUNKS = 4
FAR = -1e30


def dot_nn(a, b):
    return lax.dot_general(a, b, (((1,), (0,)), ((), ())), preferred_element_type=F32)


def dot_nt(a, b):
    return lax.dot_general(a, b, (((1,), (1,)), ((), ())), preferred_element_type=F32)


def column_tiles(total, width, body):
    full = total // width
    if full > 0:

        @pl.loop(0, full)
        def _(t):
            body(pl.ds(pl.multiple_of(t * width, width), width))

    if total % width:
        body(pl.ds(full * width, total % width))


def rms_scale(values):
    return lax.rsqrt(jnp.mean(values * values, axis=-1, keepdims=True) + 1e-05)


def rms_back(values, grad, gain):
    scale = rms_scale(values)
    scaled = grad * gain
    return scale * (
        scaled - values * (scale * scale) * jnp.mean(scaled * values, axis=-1, keepdims=True)
    )


class Exchange:
    def __init__(self, chips, chip, core, group_axis):
        self.chips, self.chip, self.core = chips, chip, core
        self.axis = group_axis

    def sibling(self):
        return {self.axis: self.chip * 2 + 1 - self.core}

    def peer(self, other):
        return {self.axis: other * 2 + self.core}

    def others(self):
        return [lax.rem(self.chip + step, self.chips) for step in range(1, self.chips)]

    def barrier(self):
        flag = pltpu.get_barrier_semaphore()
        pl.semaphore_signal(flag, inc=1, device_id=self.sibling(), device_id_type=MESH)
        for other in self.others():
            pl.semaphore_signal(flag, inc=1, device_id=self.peer(other), device_id_type=MESH)
        pl.semaphore_wait(flag, self.chips)

    def to_sibling(self, source, target, send, recv):
        return pltpu.make_async_remote_copy(
            src_ref=source,
            dst_ref=target,
            send_sem=send,
            recv_sem=recv,
            device_id=self.sibling(),
            device_id_type=MESH,
        )

    def to_peer(self, other, source, target, send, recv):
        return pltpu.make_async_remote_copy(
            src_ref=source,
            dst_ref=target,
            send_sem=send,
            recv_sem=recv,
            device_id=self.peer(other),
            device_id_type=MESH,
        )


class Scatter:
    def __init__(self, net, part, near, far, sems):
        self.net, self.part, self.near, self.far = net, part, near, far
        self.slots = None if part.shape[0] == near.shape[0] else part.shape[0]
        self.near_send, self.near_recv, self.far_send, self.far_recv = sems

    def slot(self, i):
        return i if self.slots is None else i % self.slots

    def landing(self, source, target):
        return lax.rem(source - target + self.net.chips - 1, self.net.chips)

    def near_copy(self, i):
        net = self.net
        return net.to_sibling(
            self.part.at[self.slot(i), 1 - net.core],
            self.near.at[i],
            self.near_send.at[i],
            self.near_recv.at[i],
        )

    def far_copy(self, i, other):
        net = self.net
        return net.to_peer(
            other,
            self.part.at[self.slot(i), net.core, other],
            self.far.at[i, self.landing(net.chip, other)],
            self.far_send.at[i, other],
            self.far_recv.at[i, net.chip],
        )

    def far_landing(self, i, other):
        net = self.net
        return net.to_peer(
            other,
            self.part.at[self.slot(i), net.core, other],
            self.far.at[i, self.landing(other, net.chip)],
            self.far_send.at[i, other],
            self.far_recv.at[i, other],
        )

    def start(self, i):
        self.near_copy(i).start()

    def middle(self, i):
        net = self.net
        self.near_copy(i).wait_recv()
        slot = self.slot(i)
        for other in net.others():
            total = self.part[slot, net.core, other].astype(F32) + self.near[
                i, other
            ].astype(F32)
            self.part[slot, net.core, other] = total.astype(BF16)
            self.far_copy(i, other).start()

    def finish(self, i):
        net = self.net
        slot = self.slot(i)
        total = self.part[slot, net.core, net.chip].astype(F32) + self.near[
            i, net.chip
        ].astype(F32)
        for other in net.others():
            self.far_landing(i, other).wait_recv()
            total = total + self.far[i, self.landing(other, net.chip)].astype(F32)
        return total

    def sent(self, i):
        self.near_copy(i).wait_send()
        for other in self.net.others():
            self.far_copy(i, other).wait_send()


class Gather:
    def __init__(self, net, full, sems, single=False):
        self.net, self.full, self.single = net, full, single
        self.far_send, self.far_recv, self.near_send, self.near_recv = sems

    def block(self, i, *place):
        return self.full.at[place] if self.single else self.full.at[(i, *place)]

    def far_copy(self, i, other):
        net = self.net
        block = self.block(i, net.core, net.chip)
        return net.to_peer(
            other, block, block, self.far_send.at[i, other], self.far_recv.at[i, net.chip]
        )

    def far_landing(self, i, other):
        net = self.net
        block = self.block(i, net.core, other)
        return net.to_peer(
            other, block, block, self.far_send.at[i, other], self.far_recv.at[i, other]
        )

    def near_copy(self, i):
        block = self.block(i, self.net.core)
        return self.net.to_sibling(block, block, self.near_send.at[i], self.near_recv.at[i])

    def near_landing(self, i):
        block = self.block(i, 1 - self.net.core)
        return self.net.to_sibling(block, block, self.near_send.at[i], self.near_recv.at[i])

    def start(self, i):
        for other in self.net.others():
            self.far_copy(i, other).start()

    def middle(self, i):
        for other in self.net.others():
            self.far_landing(i, other).wait_recv()
        self.near_copy(i).start()

    def finish(self, i):
        self.near_landing(i).wait_recv()

    def sent(self, i):
        for other in self.net.others():
            self.far_copy(i, other).wait_send()
        self.near_copy(i).wait_send()


STEPS = (
    ("attend", 0),
    ("attn_part", 0),
    ("attend", 2),
    ("attn_far", 0),
    ("attend", 1),
    ("attn_part", 2),
    ("norm", 0),
    ("attn_part", 1),
    ("attend", 3),
    ("attn_far", 1),
    ("attn_far", 2),
    ("attn_part", 3),
    ("rows_near", 0),
    ("units_low", 0),
    ("norm", 1),
    ("units_high", 0),
    ("unit_grads", 0),
    ("norm", 2),
    ("rows_near", 1),
    ("outputs", 0),
    ("attn_far", 3),
    ("units_far", 0),
    ("units_low", 1),
    ("units_high", 1),
    ("rows_near", 2),
    ("unit_grads", 1),
    ("norm", 3),
    ("outputs", 1),
    ("units_far", 1),
    ("residual", 0),
    ("units_low", 2),
    ("units_high", 2),
    ("rows_near", 3),
    ("unit_grads", 2),
    ("residual", 1),
    ("outputs", 2),
    ("units_low", 3),
    ("units_far", 2),
    ("back_near", 0),
    ("units_high", 3),
    ("back_near", 1),
    ("unit_grads", 3),
    ("residual", 2),
    ("attend_back", 0),
    ("units_far", 3),
    ("back_near", 2),
    ("normed_part", 0),
    ("attend_back", 1),
    ("residual", 3),
    ("normed_part", 1),
    ("normed_far", 0),
    ("attend_back", 2),
    ("normed_far", 1),
    ("back_near", 3),
    ("normed_part", 2),
    ("attend_back", 3),
    ("normed_far", 2),
    ("normed_part", 3),
    ("embed_grad", 0),
    ("outputs", 3),
    ("normed_far", 3),
    ("embed_grad", 1),
    ("token_near", 0),
    ("embed_grad", 2),
    ("token_near", 1),
    ("embed_grad", 3),
    ("token_near", 2),
    ("token_near", 3),
)


def column_of(row):
    return jnp.broadcast_to(row, (8, row.shape[1])).T[:, :1]


def text_body(
    chips,
    dp_count,
    entry_count,
    head_count,
    entry_ids,
    segments,
    cos_t,
    sin_t,
    bias_full,
    gain_one,
    gain_two,
    w_kv,
    entries_hbm,
    weights_hbm,
    token_grad,
    grad_even,
    w_query_hbm,
    w_out_hbm,
    w_gate_hbm,
    w_up_hbm,
    w_down_hbm,
    out_part,
    embed_grad,
    pooled_own,
    token_full,
    proj,
    w_query,
    w_out,
    w_gate,
    w_up,
    w_down,
    part_a,
    near_a,
    far_a,
    part_b,
    near_b,
    far_b,
    full,
    grad_full,
    embeds_own,
    q_t,
    q_n,
    k_n,
    v_n,
    k_t,
    v_t,
    out_t,
    logs,
    bias,
    residual,
    weight_sem,
    local_sem,
    stage_sem,
    scatter_near,
    scatter_far_send,
    scatter_far_recv,
    gather_near,
    gather_far_send,
    gather_far_recv,
    grad_near,
    grad_far_send,
    grad_far_recv,
):
    me = lax.axis_index("mp")
    chip, core = me // 2, lax.rem(me, 2)
    net = Exchange(chips, chip, core, "mp")
    group = chips * 2
    chunk_rows = q_n.shape[1]
    width = embeds_own.shape[2]
    units = w_gate.shape[1]
    own_rows = embeds_own.shape[1]
    head_width = FHD * head_count
    columns = proj.shape[3]
    entry_total, entry_width = entries_hbm.shape
    owned = token_grad.shape[0]
    first_own = pl.multiple_of((core * chips + chip) * own_rows, own_rows)
    owners = group // CHUNKS if group > CHUNKS else 1

    def scatter_of(kind, part, near, far):
        return Scatter(
            net,
            part,
            near,
            far,
            (
                scatter_near.at[kind, 0],
                scatter_near.at[kind, 1],
                scatter_far_send.at[kind],
                scatter_far_recv.at[kind],
            ),
        )

    def gather_of(kind, ref):
        return Gather(
            net,
            ref,
            (
                gather_far_send.at[kind],
                gather_far_recv.at[kind],
                gather_near.at[kind, 0],
                gather_near.at[kind, 1],
            ),
        )

    attn_sum = scatter_of(0, part_a, near_a, far_a)
    mlp_sum = scatter_of(1, part_b, near_b, far_b)
    normed_sum = scatter_of(2, part_a, near_a, far_a)
    mlp_rows = gather_of(0, full)
    back_rows = gather_of(1, full)
    token_rows = gather_of(2, token_full)

    def load(k, source, target):
        return pltpu.make_async_copy(source, target, weight_sem.at[k])

    load_proj = load(1, weights_hbm.at[3], proj)
    load_query = load(2, w_query_hbm, w_query)
    load_out = load(3, w_out_hbm, w_out)
    load_units = [
        load(4, w_gate_hbm, w_gate),
        load(5, w_up_hbm, w_up),
        load(6, w_down_hbm, w_down),
    ]

    def grad_far(owner_chip, other):
        return net.to_peer(
            other,
            token_grad,
            grad_full.at[owner_chip * 2 + core],
            grad_far_send.at[other],
            grad_far_recv.at[owner_chip],
        )

    def grad_near_copy(owner_chip, owner_core):
        block = grad_full.at[owner_chip * 2 + owner_core]
        return net.to_sibling(
            block, block, grad_near.at[0, owner_chip], grad_near.at[1, owner_chip]
        )

    grad_local = pltpu.make_async_copy(token_grad, grad_full.at[me], local_sem.at[chips])
    grad_loads = [
        pltpu.make_async_copy(grad_even.at[y], grad_full.at[y * 2], local_sem.at[y])
        for y in range(chips)
    ]

    def grad_start():
        grad_local.start()
        for other in net.others():
            grad_far(chip, other).start()

    def grad_middle():
        grad_local.wait()
        grad_near_copy(chip, core).start()
        for other in net.others():
            grad_far(other, other).wait_recv()
            grad_near_copy(other, core).start()

    def grad_chunk(i):
        return grad_full[i * owners : (i + 1) * owners].reshape(chunk_rows, width)

    def grad_finish(i):
        for owner in range(i * owners, (i + 1) * owners):
            if owner % 2:

                @pl.when(core == 0)
                def _():
                    grad_near_copy(owner // 2, 1).wait_recv()

            else:
                grad_loads[owner // 2].wait()

    def embed(entries, pooled, embeds):
        load_entries = load(0, entries_hbm, entries)
        load_entries.start()
        for copy in (load_proj, load_query, load_out, *load_units):
            copy.start()
        for copy in grad_loads:
            copy.start()
        net.barrier()
        pl.when(core == 1)(grad_start)
        load_entries.wait()
        load_proj.wait()
        load_query.wait()

        @pl.loop(0, CHUNKS)
        def _(i):
            ids = entry_ids[i]
            owner = ids // entry_count
            owner_mp, owner_dp = lax.rem(owner, group), owner // group
            place = (lax.rem(owner_mp, 2) * chips + owner_mp // 2) * dp_count + owner_dp
            spots = column_of(
                (place * entry_count + lax.rem(ids, entry_count)).astype(F32)
            ).astype(jnp.int32)
            numbers = lax.broadcasted_iota(jnp.int32, (chunk_rows, entry_total), 1)
            chosen = jnp.where(numbers == spots, 1.0, 0.0).astype(BF16)
            pooled[...] = dot_nn(chosen, entries[...]).astype(BF16)
            pooled_own[i] = pooled[pl.ds(first_own, own_rows), :]
            for m, c, y in shards_of(chips):
                span = slice(m * columns, (m + 1) * columns)
                embeds[:, span] = (dot_nn(pooled[...], proj[c, y]) + bias_full[c, y]).astype(BF16)
            embeds_own[i] = embeds[pl.ds(first_own, own_rows), :]
            values = embeds[...].astype(F32)
            embeds[...] = (values * rms_scale(values) * gain_one[...]).astype(BF16)
            cosine, sine = cos_t[i], sin_t[i]

            def turned(block):
                low_half, high_half = block[: FHD // 2], block[FHD // 2 :]
                return jnp.concatenate(
                    [low_half * cosine - high_half * sine, high_half * cosine + low_half * sine],
                    axis=0,
                )

            queries = dot_nn(embeds[...], w_query[...]).T
            for h in range(head_count):
                span = slice(h * FHD, (h + 1) * FHD)
                q_t[i, span, :] = (
                    turned(queries[span]).astype(BF16).astype(F32) * FHD**-0.5
                ).astype(BF16)
            q_n[i] = q_t[i].T
            both = dot_nn(embeds[...], w_kv[...])
            keys_t = turned(both.T[:FHD]).astype(BF16)
            k_t[i] = keys_t
            k_n[i] = keys_t.T
            v_n[i] = both[:, FHD:].astype(BF16)
            v_t[i] = both.T[FHD:].astype(BF16)

        pl.when(core == 1)(grad_middle)

    pl.run_scoped(
        embed,
        pltpu.VMEM((entry_total, entry_width), BF16),
        pltpu.VMEM((chunk_rows, entry_width), BF16),
        pltpu.VMEM((chunk_rows, width), BF16),
    )

    def put_rows(part, slot, columns, values):
        half = chunk_rows // 2
        for k in range(2):
            for j in range(chips):
                first = k * half + j * own_rows
                part[slot, k, j, :, columns] = values[first : first + own_rows]

    def rows_of(ref, i):
        return ref[i].reshape(chunk_rows, width)

    def turned_back(sums_t):
        return sums_t.astype(BF16).T

    def make_bias(i):
        query_spots = i * chunk_rows + lax.broadcasted_iota(jnp.int32, (chunk_rows, chunk_rows), 1)
        query_segments = segments[i].astype(F32)
        for kb in range(i + 1):
            allowed = column_of(segments[kb].astype(F32)) == query_segments
            if kb == i:
                key_spots = kb * chunk_rows + lax.broadcasted_iota(
                    jnp.int32, (chunk_rows, chunk_rows), 0
                )
                allowed = allowed & (key_spots <= query_spots)
            bias[kb] = jnp.where(allowed, 0.0, FAR)

    def head_span(h):
        return pl.ds(pl.multiple_of(h * FHD, FHD), FHD)

    def layer(
        mixed,
        gate_grad,
        up_grad,
        out_stage,
        d_out_t,
        d_out_n,
        d_query_t,
        value_even,
        value_odd,
        key_even,
        key_odd,
    ):
        for ref in (value_even, value_odd, key_even, key_odd):
            ref[...] = jnp.zeros_like(ref)

        def stage_copy(i, tile):
            slot = lax.rem(tile, 2)
            columns = pl.ds(pl.multiple_of(tile * 512, 512), 512)
            return pltpu.make_async_copy(
                out_stage.at[slot], out_part.at[i, :, columns], stage_sem.at[slot]
            )

        def attend(i):
            make_bias(i)

            @pl.loop(0, head_count, unroll=2)
            def _(h):
                query = q_t[i, head_span(h), :]
                scores = [dot_nn(k_n[kb], query) + bias[kb] for kb in range(i + 1)]
                top = jnp.max(scores[0], axis=0, keepdims=True)
                for block in scores[1:]:
                    top = jnp.maximum(top, jnp.max(block, axis=0, keepdims=True))
                total = jnp.zeros_like(top)
                attended = jnp.zeros((FHD, chunk_rows), F32)
                for kb in range(i + 1):
                    weights_block = jnp.exp(scores[kb] - top)
                    total = total + jnp.sum(weights_block, axis=0, keepdims=True)
                    attended = attended + dot_nn(v_t[kb], weights_block.astype(BF16))
                logs[i, h] = top + jnp.log(total)
                out_t[i, head_span(h), :] = (attended / total).astype(BF16)

        def attn_part(i):
            if i == CHUNKS - 1:
                load_out.wait()

            def tile(columns):
                put_rows(part_a, i, columns, turned_back(dot_nn(w_out[columns, :], out_t[i])))

            column_tiles(width, 512, tile)
            attn_sum.start(i)

        def norm(i):
            values = embeds_own[i].astype(F32) + attn_sum.finish(i)
            residual[i] = values
            full[i, core, chip] = (values * rms_scale(values) * gain_two[...]).astype(BF16)
            mlp_rows.start(i)

        def unit_tile(i, columns):
            rows = rows_of(full, i)
            gate_pre = dot_nn(rows, w_gate[:, columns])
            up_pre = dot_nn(rows, w_up[:, columns])
            act_grad = dot_nn(grad_chunk(i), w_down[:, columns])
            inverse = 1.0 / (1.0 + jnp.exp(-gate_pre))
            silu = gate_pre * inverse
            mixed[columns, :] = turned_back(silu * up_pre)
            up_grad[columns, :] = turned_back(act_grad * silu)
            slope = inverse * (1.0 + gate_pre * (1.0 - inverse))
            gate_grad[columns, :] = turned_back(act_grad * up_pre * slope)

        tile_width = 512 if units >= 1024 else 256
        tiles = units // tile_width
        middle_tile = (tiles + 1) // 2

        def unit_tiles(i, first, last):
            @pl.loop(first, last)
            def _(t):
                unit_tile(i, pl.ds(pl.multiple_of(t * tile_width, tile_width), tile_width))

        def units_low(i):
            if i == CHUNKS - 1:
                for copy in load_units:
                    copy.wait()
            grad_finish(i)
            mlp_rows.finish(i)
            unit_tiles(i, 0, middle_tile)

        def units_high(i):
            unit_tiles(i, middle_tile, tiles)
            if units % tile_width:
                unit_tile(i, pl.ds(tiles * tile_width, units % tile_width))
            mlp_rows.sent(i)

        def unit_grads(i):
            if i + 2 < CHUNKS:
                mlp_sum.sent(i + 2)

            def tile(columns):
                put_rows(
                    part_b,
                    i % 2,
                    columns,
                    turned_back(
                        dot_nn(w_gate[columns, :], gate_grad[...])
                        + dot_nn(w_up[columns, :], up_grad[...])
                    ),
                )

            column_tiles(width, 512, tile)
            mlp_sum.start(i)

        def outputs(i):
            @pl.loop(0, width // 512)
            def _(t):
                columns = pl.ds(pl.multiple_of(t * 512, 512), 512)
                slot = lax.rem(t, 2)
                tile = turned_back(dot_nn(w_down[columns, :], mixed[...]))
                if i == CHUNKS - 1:
                    pl.when(t >= 2)(lambda: stage_copy(i, t).wait())
                else:
                    stage_copy(i, t).wait()
                out_stage[slot] = tile
                own = pl.ds(first_own, own_rows)
                out_stage[slot, own, :] = (
                    out_stage[slot, own, :].astype(F32) + residual[i, :, columns]
                ).astype(BF16)
                stage_copy(i, t).start()

        def residual_back(i):
            grad = mlp_sum.finish(i)
            block = i * owners + first_own // owned
            start = pl.multiple_of(lax.rem(first_own, owned), own_rows)
            own_grad = grad_full[block, pl.ds(start, own_rows), :].astype(F32)
            values = own_grad + rms_back(residual[i], grad, gain_two[...])
            full[i, core, chip] = values.astype(BF16)
            back_rows.start(i)

        def attend_back(i):
            back_rows.finish(i)
            attended_grad = dot_nn(rows_of(full, i), w_out[...]).astype(BF16)
            d_out_n[...] = attended_grad
            d_out_t[...] = attended_grad.T
            make_bias(i)
            cosine, sine = cos_t[i], sin_t[i]

            @pl.loop(0, head_count // 2)
            def _(pair):
                pair_span = pl.ds(pl.multiple_of(pair * 2 * FHD, 2 * FHD), 2 * FHD)
                query_pair = q_n[i, :, pair_span]
                grad_pair = d_out_n[:, pair_span]
                for odd in range(2):
                    h = pair * 2 + odd
                    query = q_t[i, head_span(h), :]
                    grad = d_out_t[head_span(h), :]
                    log_row = logs[i, h]
                    centre = jnp.sum(
                        grad.astype(F32) * out_t[i, head_span(h), :].astype(F32),
                        axis=0,
                        keepdims=True,
                    )
                    value_total = value_odd if odd else value_even
                    key_total = key_odd if odd else key_even
                    query_grad = jnp.zeros((FHD, chunk_rows), F32)
                    for kb in range(i + 1):
                        probs = jnp.exp(dot_nn(k_n[kb], query) + bias[kb] - log_row)
                        value_total[kb] += dot_nn(probs.astype(BF16), grad_pair)
                        score_grad = (probs * (dot_nn(v_n[kb], grad) - centre)).astype(BF16)
                        key_total[kb] += dot_nn(score_grad, query_pair)
                        query_grad = query_grad + dot_nn(k_t[kb], score_grad)
                    query_grad = query_grad * (FHD**-0.5)
                    low_half, high_half = query_grad[: FHD // 2], query_grad[FHD // 2 :]
                    d_query_t[head_span(h), :] = jnp.concatenate(
                        [
                            low_half * cosine + high_half * sine,
                            high_half * cosine - low_half * sine,
                        ],
                        axis=0,
                    ).astype(BF16)

        def normed_part(i):
            attn_sum.sent(i)
            key_grad = (key_even[i][:, :FHD] + key_odd[i][:, FHD:]).T
            cosine, sine = cos_t[i], sin_t[i]
            low_half, high_half = key_grad[: FHD // 2], key_grad[FHD // 2 :]
            value_grad = (value_even[i][:, :FHD] + value_odd[i][:, FHD:]).T
            both = jnp.concatenate(
                [
                    low_half * cosine + high_half * sine,
                    high_half * cosine - low_half * sine,
                    value_grad,
                ],
                axis=0,
            )
            both = both.astype(BF16)

            def tile(columns):
                put_rows(
                    part_a,
                    i,
                    columns,
                    turned_back(
                        dot_nn(w_query[columns, :], d_query_t[...])
                        + dot_nn(w_kv[columns, :], both)
                    ),
                )

            column_tiles(width, 512, tile)
            normed_sum.start(i)

        def embed_back(i):
            grad = normed_sum.finish(i)
            kept = full[i, core, chip].astype(F32)
            values = kept + rms_back(embeds_own[i].astype(F32), grad, gain_one[...])
            embed_grad[i] = values.astype(BF16)
            total = jnp.zeros((own_rows, entry_width), F32)
            for m, c, y in shards_of(chips):
                total = total + dot_nt(
                    embed_grad[i, :, m * columns : (m + 1) * columns], proj[c, y]
                )
            token_full[i, core, chip] = total.astype(BF16)
            token_rows.start(i)

        stages = {
            "attend": attend,
            "attn_part": attn_part,
            "attn_far": attn_sum.middle,
            "norm": norm,
            "rows_near": mlp_rows.middle,
            "units_low": units_low,
            "units_high": units_high,
            "unit_grads": unit_grads,
            "outputs": outputs,
            "units_far": mlp_sum.middle,
            "residual": residual_back,
            "back_near": back_rows.middle,
            "attend_back": attend_back,
            "normed_part": normed_part,
            "normed_far": normed_sum.middle,
            "embed_grad": embed_back,
            "token_near": token_rows.middle,
        }
        for name, turn in STEPS:
            stages[name](CHUNKS - 1 - turn)

        for tile in range(2):
            stage_copy(0, tile).wait()

    lines = (units, chunk_rows)
    keys = (CHUNKS, chunk_rows, 2 * FHD)
    pl.run_scoped(
        layer,
        pltpu.VMEM(lines, BF16),
        pltpu.VMEM(lines, BF16),
        pltpu.VMEM(lines, BF16),
        pltpu.VMEM((2, chunk_rows, 512), BF16),
        pltpu.VMEM((head_width, chunk_rows), BF16),
        pltpu.VMEM((chunk_rows, head_width), BF16),
        pltpu.VMEM((head_width, chunk_rows), BF16),
        pltpu.VMEM(keys, F32),
        pltpu.VMEM(keys, F32),
        pltpu.VMEM(keys, F32),
        pltpu.VMEM(keys, F32),
    )

    @pl.loop(0, CHUNKS)
    def _(i):
        token_rows.finish(i)
        token_rows.sent(i)
        normed_sum.sent(i)
        back_rows.sent(i)

    for i in range(2):
        mlp_sum.sent(i)

    @pl.when(core == 1)
    def _():
        for other in net.others():
            grad_far(chip, other).wait_send()
        for owner_chip in range(chips):
            grad_near_copy(owner_chip, core).wait_send()


def text_layer(
    group,
    dp_count,
    entry_count,
    entry_ids,
    segments,
    cos_t,
    sin_t,
    bias_full,
    gain_one,
    gain_two,
    w_kv,
    entries,
    weights,
    token_grad,
    grad_even,
    w_query,
    w_out,
    w_gate,
    w_up,
    w_down,
):
    chips = group // 2
    chunks, _, chunk_rows = entry_ids.shape
    own_rows = chunk_rows // group
    owned, width = token_grad.shape
    head_width = w_query.shape[1]
    head_count = head_width // FHD
    entry_width = entries.shape[1]
    vmem = pl.BlockSpec(memory_space=pltpu.VMEM)
    hbm = pl.BlockSpec(memory_space=pl.ANY)
    dma = pltpu.SemaphoreType.DMA

    def low(*shape):
        return pltpu.VMEM(shape, BF16)

    return pl.pallas_call(
        partial(text_body, chips, dp_count, entry_count, head_count),
        out_shape=(
            jax.ShapeDtypeStruct((chunks, chunk_rows, width), BF16),
            jax.ShapeDtypeStruct((chunks, own_rows, width), BF16),
            jax.ShapeDtypeStruct((chunks, own_rows, entry_width), BF16),
            jax.ShapeDtypeStruct((chunks, 2, chips, own_rows, entry_width), BF16),
        ),
        in_specs=[vmem] * 8 + [hbm] * 9,
        out_specs=(hbm, vmem, vmem, vmem),
        scratch_shapes=[
            low(*weights.shape[1:]),
            low(*w_query.shape),
            low(*w_out.shape),
            low(*w_gate.shape),
            low(*w_up.shape),
            low(*w_down.shape),
            low(chunks, 2, chips, own_rows, width),
            low(chunks, chips, own_rows, width),
            low(chunks, chips - 1, own_rows, width),
            low(2, 2, chips, own_rows, width),
            low(chunks, chips, own_rows, width),
            low(chunks, chips - 1, own_rows, width),
            low(chunks, 2, chips, own_rows, width),
            low(group, owned, width),
            low(chunks, own_rows, width),
            low(chunks, head_width, chunk_rows),
            low(chunks, chunk_rows, head_width),
            low(chunks, chunk_rows, FHD),
            low(chunks, chunk_rows, FHD),
            low(chunks, FHD, chunk_rows),
            low(chunks, FHD, chunk_rows),
            low(chunks, head_width, chunk_rows),
            pltpu.VMEM((chunks, head_count, 1, chunk_rows), F32),
            pltpu.VMEM((chunks, chunk_rows, chunk_rows), F32),
            pltpu.VMEM((chunks, own_rows, width), F32),
            dma((7,)),
            dma((chips + 1,)),
            dma((2,)),
            dma((3, 2, chunks)),
            dma((3, chunks, chips)),
            dma((3, chunks, chips)),
            dma((3, 2, chunks)),
            dma((3, chunks, chips)),
            dma((3, chunks, chips)),
            dma((2, chips)),
            dma((chips,)),
            dma((chips,)),
        ],
        compiler_params=pltpu.CompilerParams(
            collective_id=0, has_side_effects=True, vmem_limit_bytes=65280 * 1024
        ),
        cost_estimate=pl.CostEstimate(
            flops=90 * 10**9, bytes_accessed=40 * 10**6, transcendentals=20 * 10**6
        ),
    )(
        entry_ids,
        segments,
        cos_t,
        sin_t,
        bias_full,
        gain_one,
        gain_two,
        w_kv,
        entries,
        weights,
        token_grad,
        grad_even,
        w_query,
        w_out,
        w_gate,
        w_up,
        w_down,
    )


def norm_parts(values):
    average = jnp.mean(values, axis=-1, keepdims=True)
    centred = values - average
    scale = lax.rsqrt(jnp.mean(centred * centred, axis=-1, keepdims=True) + 1e-05)
    return centred * scale, scale


def norm_back(values, grad, gain):
    unit, scale = norm_parts(values)
    scaled = grad * gain
    back = scale * (
        scaled
        - jnp.mean(scaled, axis=-1, keepdims=True)
        - unit * jnp.mean(scaled * unit, axis=-1, keepdims=True)
    )
    return (
        back,
        jnp.sum(grad * unit, axis=0, keepdims=True),
        jnp.sum(grad, axis=0, keepdims=True),
    )


def gelu_parts(values):
    root = math.sqrt(2.0 / math.pi)
    squared = values * values
    bent = jnp.tanh(root * values * (1.0 + 0.044715 * squared))
    half = 0.5 * (1.0 + bent)
    slope = half + 0.5 * values * (1.0 - bent * bent) * root * (1.0 + 3 * 0.044715 * squared)
    return values * half, slope


def pool_matrix(counts_col, entries, rows):
    entry = lax.broadcasted_iota(jnp.int32, (entries, rows), 0)
    row = lax.broadcasted_iota(jnp.int32, (entries, rows), 1)
    slots = rows // entries
    inside = (row // slots == entry) & (lax.rem(row, slots).astype(F32) < counts_col)
    return jnp.where(inside, 1.0, 0.0)


def spread_matrix(counts_row, entries, rows):
    row = lax.broadcasted_iota(jnp.int32, (rows, entries), 0)
    entry = lax.broadcasted_iota(jnp.int32, (rows, entries), 1)
    slots = rows // entries
    inside = (row // slots == entry) & (lax.rem(row, slots).astype(F32) < counts_row)
    return jnp.where(inside, 1.0, 0.0)


def slot_bias(valid_col, slots):
    rows = valid_col.shape[0]
    key = lax.broadcasted_iota(jnp.int32, (rows, rows), 0)
    query = lax.broadcasted_iota(jnp.int32, (rows, rows), 1)
    return jnp.where((key // slots == query // slots) & (valid_col > 0.5), 0.0, FAR)


ROW_BLOCK = 256


def shards_of(chips):
    return [(y * 2 + c, c, y) for y in range(chips) for c in range(2)]


def each_shard(chips, columns, body):
    @pl.loop(0, 2)
    def _(c):
        @pl.loop(0, chips)
        def _(y):
            first = pl.multiple_of((y * 2 + c) * columns, columns)
            body(c, y, pl.ds(first, columns))


def hyper_body(
    chips,
    dp_count,
    pieces,
    counts_all,
    gain_one,
    shift_one,
    gain_two,
    shift_two,
    w_query,
    w_key,
    w_value,
    w_out,
    bias_own,
    w_up_hbm,
    w_down_hbm,
    w_proj_hbm,
    token_grad,
    entries,
    weights_out,
    attn_in,
    q_n,
    k_n,
    v_n,
    attended,
    logs,
    residual,
    ffn_in,
    counts_col,
    counts_row,
    bias_full,
    grad_even,
    full,
    q_t,
    v_t,
    out_t,
    bias,
    hidden,
    counts_scratch,
    local_sem,
    store_sem,
    far_send,
    far_recv,
    x_send,
    x_recv,
    near_send,
    near_recv,
    z_send,
    z_recv,
    mate_send,
    mate_recv,
    y_send,
    y_recv,
    last_send,
    last_recv,
    bias_far_send,
    bias_far_recv,
    bias_near,
    grad_sem,
    grad_far_send,
    grad_far_recv,
    grad_near,
):
    me = lax.axis_index("mp")
    dp = lax.axis_index("dp")
    chip, core = me // 2, lax.rem(me, 2)
    net = Exchange(chips, chip, core, "mp")
    side = lax.rem(dp, 2)
    mate = dp + 1 - 2 * side
    spot, spots = dp // 2, dp_count // 2
    kinds, _, _, width, columns = full.shape
    sources = (None, w_up_hbm, w_down_hbm, w_proj_hbm)
    rows = pieces.shape[0]
    entry_count = counts_col.shape[0]
    slots = rows // entry_count
    head_columns = columns // 4
    half = width // 2
    heads = width // HD

    flag = pltpu.get_barrier_semaphore()
    pl.semaphore_signal(flag, inc=1, device_id=net.sibling(), device_id_type=MESH)
    for other in net.others():
        pl.semaphore_signal(flag, inc=1, device_id=net.peer(other), device_id_type=MESH)

    pl.semaphore_signal(flag, inc=1, device_id={"dp": mate}, device_id_type=MESH)

    @pl.loop(1, spots)
    def _(j):
        target = lax.rem(spot + j, spots) * 2 + side
        pl.semaphore_signal(flag, inc=1, device_id={"dp": target}, device_id_type=MESH)

    local = [
        pltpu.make_async_copy(sources[k], full.at[k, core, chip], local_sem.at[k - 1])
        for k in range(1, kinds)
    ]
    for copy in local:
        copy.start()
    for j, source in enumerate((w_query, w_key, w_value, w_out)):
        full[0, core, chip, :, j * head_columns : (j + 1) * head_columns] = source[...]
    bias_full[core, chip] = bias_own[...]
    pl.semaphore_wait(flag, chips + spots)

    def rows_half(which):
        return pl.ds(pl.multiple_of(which * half, half), half)

    def far_copy(k, other):
        return net.to_peer(
            other,
            sources[k].at[rows_half(side)] if k else full.at[0, core, chip, rows_half(side)],
            full.at[k, core, chip, rows_half(side)],
            far_send.at[k, other],
            far_recv.at[k, chip],
        )

    def far_landing(k, other):
        block = full.at[k, core, other, rows_half(side)]
        return net.to_peer(other, block, block, far_send.at[k, other], far_recv.at[k, other])

    def x_copy(k, other, which):
        block = full.at[k, core, other, rows_half(which)]
        return pltpu.make_async_remote_copy(
            src_ref=block,
            dst_ref=block,
            send_sem=x_send.at[k, other],
            recv_sem=x_recv.at[k, other],
            device_id={"dp": mate},
            device_id_type=MESH,
        )

    def near_copy(k, which):
        block = full.at[k, which]
        return net.to_sibling(block, block, near_send.at[k], near_recv.at[k])

    def far_middle(k):
        for other in net.others():
            far_landing(k, other).wait_recv()
            x_copy(k, other, side).start()

    def x_middle(k):
        for other in net.others():
            x_copy(k, other, 1 - side).wait_recv()
        if k:
            local[k - 1].wait()
        near_copy(k, core).start()

    def store(k):
        return pltpu.make_async_copy(full.at[k], weights_out.at[k], store_sem.at[k])

    def near_finish(k):
        near_copy(k, 1 - core).wait_recv()
        store(k).start()

    bias_rows = Gather(
        net, bias_full, (bias_far_send, bias_far_recv, bias_near.at[0], bias_near.at[1]), True
    )
    def far_start(k):
        for other in net.others():
            far_copy(k, other).start()

    grad_local = pltpu.make_async_copy(token_grad, grad_even.at[chip], grad_sem)

    def grad_far(other, owner):
        return net.to_peer(
            other,
            token_grad,
            grad_even.at[owner],
            grad_far_send.at[other],
            grad_far_recv.at[owner],
        )

    def grad_across(owner):
        block = grad_even.at[owner]
        return net.to_sibling(block, block, grad_near.at[0, owner], grad_near.at[1, owner])

    def grad_start():
        grad_local.start()
        for other in net.others():
            grad_far(other, chip).start()

    def grad_finish_even():
        grad_local.wait()
        for other in net.others():
            grad_far(other, other).wait_recv()
        for owner in range(chips):
            grad_across(owner).start()
        for other in net.others():
            grad_far(other, chip).wait_send()
        for owner in range(chips):
            grad_across(owner).wait_send()

    def grad_finish_odd():
        for owner in range(chips):
            grad_across(owner).wait_recv()

    far_start(0)
    bias_rows.start(0)
    counts_scratch[...] = column_of(counts_all[...].astype(F32))
    own_counts = counts_scratch[pl.ds(pl.multiple_of(me * entry_count, entry_count), entry_count)]
    counts_col[...] = own_counts
    counts_row[...] = jnp.broadcast_to(own_counts, (entry_count, 128)).T[:1]

    values = pieces[...].astype(F32)
    attn_in[...] = (norm_parts(values)[0] * gain_one[...] + shift_one[...]).astype(BF16)
    blocks = rows // ROW_BLOCK
    valid = jnp.sum(spread_matrix(counts_row[...], entry_count, rows), axis=1, keepdims=True)
    for b in range(blocks):
        bias[b] = slot_bias(valid[b * ROW_BLOCK : (b + 1) * ROW_BLOCK], slots)

    far_middle(0)
    far_start(1)
    bias_rows.middle(0)
    far_middle(1)
    far_start(2)
    x_middle(0)
    near_finish(0)
    for m, c, y in shards_of(chips):
        span = slice(m * head_columns, (m + 1) * head_columns)
        projected = dot_nn(attn_in[...], full[0, c, y, :, : 3 * head_columns])
        q_n[:, span] = (projected[:, :head_columns].astype(BF16).astype(F32) * HD**-0.5).astype(
            BF16
        )
        k_n[:, span] = projected[:, head_columns : 2 * head_columns].astype(BF16)
        v_n[:, span] = projected[:, 2 * head_columns :].astype(BF16)
    far_middle(2)
    far_start(3)
    x_middle(1)
    for b in range(blocks):
        block_rows = slice(b * ROW_BLOCK, (b + 1) * ROW_BLOCK)
        q_t[b] = q_n[block_rows, :].T
        v_t[b] = v_n[block_rows, :].T

    def attend_pair(pair):
        pair_span = pl.ds(pl.multiple_of(pair * 2 * HD, 2 * HD), 2 * HD)
        for b in range(blocks):
            key_pair = k_n[b * ROW_BLOCK : (b + 1) * ROW_BLOCK, pair_span]
            for odd in range(2):
                h = pair * 2 + odd
                span = pl.ds(pl.multiple_of(h * HD, HD), HD)
                scores = dot_nn(key_pair[:, odd * HD : (odd + 1) * HD], q_t[b, span, :]) + bias[b]
                top = jnp.max(scores, axis=0, keepdims=True)
                weights = jnp.exp(scores - top)
                total = jnp.sum(weights, axis=0, keepdims=True)
                logs[b, h] = top + jnp.log(total)
                out_t[b, span, :] = (dot_nn(v_t[b, span, :], weights.astype(BF16)) / total).astype(
                    BF16
                )

    pl.loop(0, heads // 4)(attend_pair)
    far_middle(3)
    pl.when(core == 0)(grad_start)
    x_middle(2)
    pl.loop(heads // 4, heads // 2)(attend_pair)
    for b in range(blocks):
        attended[b * ROW_BLOCK : (b + 1) * ROW_BLOCK, :] = out_t[b].T
    total = values
    for m, c, y in shards_of(chips):
        span = slice(m * head_columns, (m + 1) * head_columns)
        total = total + dot_nt(attended[:, span], full[0, c, y, :, 3 * head_columns :])
    residual[...] = total
    ffn_in[...] = (norm_parts(total)[0] * gain_two[...] + shift_two[...]).astype(BF16)
    near_finish(1)
    x_middle(3)
    pool = pool_matrix(counts_col[...], entry_count, rows).astype(BF16)

    def up_shard(c, y, span):
        act = gelu_parts(dot_nn(ffn_in[...], full[1, c, y]))[0]
        hidden[:, span] = dot_nn(pool, act.astype(BF16)).astype(BF16)

    each_shard(chips, columns, up_shard)
    near_finish(2)
    pooled = jnp.sum(
        (residual[...] * valid).reshape(entry_count, slots, width), axis=1
    )
    for m, c, y in shards_of(chips):
        pooled = pooled + dot_nt(hidden[:, m * columns : (m + 1) * columns], full[2, c, y])
    entries[core, chip, dp] = (pooled / counts_col[...]).astype(BF16)

    def z_copy(target, owner):
        piece = entries.at[core, chip, owner * 2 + side]
        return pltpu.make_async_remote_copy(
            src_ref=piece,
            dst_ref=piece,
            send_sem=z_send.at[target],
            recv_sem=z_recv.at[owner],
            device_id={"dp": target * 2 + side},
            device_id_type=MESH,
        )

    def mate_copy(owner, which):
        piece = entries.at[core, chip, owner * 2 + which]
        return pltpu.make_async_remote_copy(
            src_ref=piece,
            dst_ref=piece,
            send_sem=mate_send.at[owner],
            recv_sem=mate_recv.at[owner],
            device_id={"dp": mate},
            device_id_type=MESH,
        )

    def y_copy(other, owner, block):
        piece = entries.at[core, owner, block]
        return net.to_peer(
            other, piece, piece, y_send.at[other, block], y_recv.at[owner, block]
        )

    def y_start(block):
        for other in net.others():
            y_copy(other, chip, block).start()

    @pl.loop(1, spots)
    def _(j):
        z_copy(lax.rem(spot + j, spots), spot).start()

    mate_copy(spot, side).start()
    y_start(dp)
    near_finish(3)
    bias_rows.finish(0)

    @pl.loop(1, spots)
    def _(j):
        source = lax.rem(spot + spots - j, spots)
        z_copy(source, source).wait_recv()
        mate_copy(source, side).start()
        y_start(source * 2 + side)

    @pl.loop(0, spots)
    def _(j):
        source = lax.rem(spot + spots - j, spots)
        mate_copy(source, 1 - side).wait_recv()
        y_start(source * 2 + 1 - side)

    def last_copy(part, c, owner):
        piece = entries.at[c, owner]
        return net.to_sibling(piece, piece, last_send.at[part], last_recv.at[owner])

    last_copy(chip, core, chip).start()
    for other in net.others():

        @pl.loop(0, dp_count)
        def _(block):
            y_copy(other, other, block).wait_recv()

        last_copy(other, core, other).start()
    last_copy(chip, 1 - core, chip).wait_recv()
    for other in net.others():
        last_copy(other, 1 - core, other).wait_recv()

    pl.when(core == 0)(grad_finish_even)
    pl.when(core == 1)(grad_finish_odd)
    bias_rows.sent(0)
    for k in range(kinds):
        store(k).wait()
        near_copy(k, core).wait_send()
        for other in net.others():
            far_copy(k, other).wait_send()
            x_copy(k, other, side).wait_send()

    @pl.loop(1, spots)
    def _(j):
        z_copy(lax.rem(spot + j, spots), spot).wait_send()

    @pl.loop(0, spots)
    def _(j):
        mate_copy(j, side).wait_send()

    last_copy(chip, core, chip).wait_send()
    for other in net.others():
        last_copy(other, core, other).wait_send()

        @pl.loop(0, dp_count)
        def _(block):
            y_copy(other, chip, block).wait_send()


def hyper_forward(
    group,
    dp_count,
    pieces,
    counts,
    gain_one,
    shift_one,
    gain_two,
    shift_two,
    head_weights,
    bias_own,
    unit_weights,
    token_grad,
):
    chips = group // 2
    rows, width = pieces.shape
    columns = unit_weights[0].shape[1]
    kinds = 4
    entry_count = counts.shape[1] // group
    heads = width // HD
    blocks = rows // ROW_BLOCK
    vmem = pl.BlockSpec(memory_space=pltpu.VMEM)
    hbm = pl.BlockSpec(memory_space=pl.ANY)
    row_shape = jax.ShapeDtypeStruct((rows, width), BF16)
    dma = pltpu.SemaphoreType.DMA
    return pl.pallas_call(
        partial(hyper_body, chips, dp_count),
        out_shape=(
            jax.ShapeDtypeStruct((2, chips, dp_count, entry_count, width), BF16),
            jax.ShapeDtypeStruct((kinds, 2, chips, width, columns), BF16),
            row_shape,
            row_shape,
            row_shape,
            row_shape,
            row_shape,
            jax.ShapeDtypeStruct((blocks, heads, 1, ROW_BLOCK), F32),
            jax.ShapeDtypeStruct((rows, width), F32),
            row_shape,
            jax.ShapeDtypeStruct((entry_count, 1), F32),
            jax.ShapeDtypeStruct((1, entry_count), F32),
            jax.ShapeDtypeStruct((2, chips, 1, columns), F32),
            jax.ShapeDtypeStruct((chips, *token_grad.shape), BF16),
        ),
        in_specs=[vmem] * 11 + [hbm] * 4,
        out_specs=(vmem, hbm) + (vmem,) * 11 + (hbm,),
        scratch_shapes=[
            pltpu.VMEM((kinds, 2, chips, width, columns), BF16),
            pltpu.VMEM((blocks, width, ROW_BLOCK), BF16),
            pltpu.VMEM((blocks, width, ROW_BLOCK), BF16),
            pltpu.VMEM((blocks, width, ROW_BLOCK), BF16),
            pltpu.VMEM((blocks, ROW_BLOCK, ROW_BLOCK), F32),
            pltpu.VMEM((entry_count, columns * group), BF16),
            pltpu.VMEM((counts.shape[1], 1), F32),
            dma((kinds - 1,)),
            dma((kinds,)),
            dma((kinds, chips)),
            dma((kinds, chips)),
            dma((kinds, chips)),
            dma((kinds, chips)),
            dma((kinds,)),
            dma((kinds,)),
            dma((dp_count // 2,)),
            dma((dp_count // 2,)),
            dma((dp_count // 2,)),
            dma((dp_count // 2,)),
            dma((chips, dp_count)),
            dma((chips, dp_count)),
            dma((chips,)),
            dma((chips,)),
            dma((1, chips)),
            dma((1, chips)),
            dma((2, 1)),
            dma,
            dma((chips,)),
            dma((chips,)),
            dma((2, chips)),
        ],
        compiler_params=pltpu.CompilerParams(
            collective_id=1, has_side_effects=True, vmem_limit_bytes=60 * 1024 * 1024
        ),
        cost_estimate=pl.CostEstimate(
            flops=60 * 10**9, bytes_accessed=20 * 10**6, transcendentals=5 * 10**6
        ),
    )(
        pieces,
        counts,
        gain_one,
        shift_one,
        gain_two,
        shift_two,
        *head_weights,
        bias_own,
        *unit_weights,
        token_grad,
    )


class Total:
    def __init__(self, net, dp, dp_count, refs, sems):
        self.net = net
        self.part, self.near, self.far, self.x_land, self.z_land, self.final = refs
        self.n_send, self.n_recv, self.y_send, self.y_recv, self.x_send, self.x_recv = sems[:6]
        self.z_send, self.z_recv, self.g_send, self.g_recv, self.l_send, self.l_recv = sems[6:]
        self.side = lax.rem(dp, 2)
        self.spot = dp // 2
        self.mate = dp + 1 - 2 * self.side
        self.spots = dp_count // 2
        self.chips, self.chip, self.core = net.chips, net.chip, net.core

    def remote(self, source, target, send, recv, device):
        return pltpu.make_async_remote_copy(
            src_ref=source,
            dst_ref=target,
            send_sem=send,
            recv_sem=recv,
            device_id={"dp": device},
            device_id_type=MESH,
        )

    def near_copy(self, k):
        return self.net.to_sibling(
            self.part.at[k, 1 - self.core], self.near.at[k], self.n_send.at[k], self.n_recv.at[k]
        )

    def slot(self, source, target):
        return lax.rem(source - target + self.chips - 1, self.chips)

    def y_copy(self, k, other, half, landing=False):
        source, target = (other, self.chip) if landing else (self.chip, other)
        return self.net.to_peer(
            other,
            self.part.at[k, self.core, other, half],
            self.far.at[k, self.slot(source, target), half],
            self.y_send.at[k, other, half],
            self.y_recv.at[k, source, half],
        )

    def x_copy(self, k, chip):
        return self.remote(
            self.part.at[k, self.core, chip, 1 - self.side],
            self.x_land.at[k, chip],
            self.x_send.at[k, chip],
            self.x_recv.at[k, chip],
            self.mate,
        )

    def z_copy(self, k, spot, slot):
        return self.remote(
            self.part.at[k, self.core, self.chip, self.side, spot],
            self.z_land.at[k, slot],
            self.z_send.at[k, spot],
            self.z_recv.at[k, slot],
            spot * 2 + self.side,
        )

    def g_copy(self, k, spot, owner):
        block = self.final.at[k, self.side, owner]
        return self.remote(
            block, block, self.g_send.at[k, spot], self.g_recv.at[k, owner], spot * 2 + self.side
        )

    def l_copy(self, k, side):
        block = self.final.at[k, side]
        return self.remote(block, block, self.l_send.at[k], self.l_recv.at[k], self.mate)

    def each_spot(self, body):
        if self.spots > 1:

            @pl.loop(1, self.spots)
            def _(j):
                body(lax.rem(self.spot + j, self.spots))

    def by_order(self, k, even, odd):
        if isinstance(k, int):
            (odd if k % 2 else even)(k)
        else:
            pl.when(lax.rem(k, 2) == 0)(lambda: even(k))
            pl.when(lax.rem(k, 2) == 1)(lambda: odd(k))

    def add(self, k, chip, half, *lands):
        total = self.part[k, self.core, chip, half].astype(F32)
        for land in lands:
            total = total + land.astype(F32)
        self.part[k, self.core, chip, half] = total.astype(BF16)

    def start(self, k):
        self.near_copy(k).start()

    def near_even(self, k):
        for other in self.net.others():
            for half in range(2):
                self.add(k, other, half, self.near[k, other, half])
                self.y_copy(k, other, half).start()

    def near_odd(self, k):
        for chip in range(self.chips):
            self.add(k, chip, 1 - self.side, self.near[k, chip, 1 - self.side])
            self.x_copy(k, chip).start()

    def near_middle(self, k):
        self.near_copy(k).wait_recv()
        self.by_order(k, self.near_even, self.near_odd)

    def second_even(self, k):
        chip = self.chip
        for other in self.net.others():
            for half in range(2):
                self.y_copy(k, other, half, True).wait_recv()
        slots = [self.slot(other, chip) for other in self.net.others()]
        half = 1 - self.side
        self.add(k, chip, half, self.near[k, chip, half], *[self.far[k, j, half] for j in slots])
        self.x_copy(k, chip).start()
        half = self.side
        self.add(k, chip, half, self.near[k, chip, half], *[self.far[k, j, half] for j in slots])

    def second_odd(self, k):
        for chip in range(self.chips):
            self.x_copy(k, chip).wait_recv()
        for other in self.net.others():
            self.add(k, other, self.side, self.near[k, other, self.side], self.x_land[k, other])
            self.y_copy(k, other, self.side).start()

    def second(self, k):
        self.by_order(k, self.second_even, self.second_odd)

    def third_even(self, k):
        self.x_copy(k, self.chip).wait_recv()
        self.add(k, self.chip, self.side, self.x_land[k, self.chip])

    def third_odd(self, k):
        chip = self.chip
        lands = [self.near[k, chip, self.side], self.x_land[k, chip]]
        for other in self.net.others():
            self.y_copy(k, other, self.side, True).wait_recv()
            lands.append(self.far[k, self.slot(other, chip), self.side])
        self.add(k, chip, self.side, *lands)

    def third(self, k):
        self.by_order(k, self.third_even, self.third_odd)
        self.each_spot(lambda spot: self.z_copy(k, spot, self.spot).start())

    def z_middle(self, k):
        self.each_spot(lambda spot: self.z_copy(k, spot, spot).wait_recv())
        total = self.part[k, self.core, self.chip, self.side, self.spot].astype(F32)
        for j in range(1, self.spots):
            spot = lax.rem(self.spot + j, self.spots)
            total = total + self.z_land[k, spot].astype(F32)
        self.final[k, self.side, self.spot] = total.astype(BF16)
        self.each_spot(lambda spot: self.g_copy(k, spot, self.spot).start())

    def g_middle(self, k):
        self.each_spot(lambda spot: self.g_copy(k, spot, spot).wait_recv())
        self.l_copy(k, self.side).start()

    def finish(self, k):
        self.l_copy(k, 1 - self.side).wait_recv()

    def sent_even(self, k):
        for other in self.net.others():
            for half in range(2):
                self.y_copy(k, other, half).wait_send()
        self.x_copy(k, self.chip).wait_send()

    def sent_odd(self, k):
        for chip in range(self.chips):
            self.x_copy(k, chip).wait_send()
        for other in self.net.others():
            self.y_copy(k, other, self.side).wait_send()

    def sent(self, k):
        self.near_copy(k).wait_send()
        self.by_order(k, self.sent_even, self.sent_odd)
        self.each_spot(lambda spot: self.z_copy(k, spot, self.spot).wait_send())
        self.each_spot(lambda spot: self.g_copy(k, spot, self.spot).wait_send())
        self.l_copy(k, self.side).wait_send()


PARTS = 8


def back_body(
    chips,
    dp_count,
    embed_rows,
    pooled_own,
    token_rows,
    token_row,
    pieces,
    counts_col,
    counts_row,
    gain_one,
    gain_two,
    attn_in,
    q_n,
    k_n,
    v_n,
    attended,
    logs,
    residual,
    ffn_in,
    weights_hbm,
    out_part,
    pieces_grad,
    final,
    small_total,
    text_out,
    weights,
    part,
    near,
    far,
    x_land,
    z_land,
    entry_part,
    entry_land,
    hidden,
    hidden_pre,
    ffn_t,
    row_total,
    d_out_n,
    d_query,
    d_key,
    d_value,
    q_t,
    out_t,
    d_out_t,
    k_t,
    d_query_t,
    bias,
    small_near,
    small_far,
    small_dp,
    small_part,
    out_own,
    out_near,
    out_far,
    weight_sem,
    out_local,
    out_near_sem,
    out_far_send,
    out_far_recv,
    entry_send,
    entry_recv,
    near_sem,
    far_send,
    far_recv,
    x_sem,
    z_send,
    z_recv,
    g_send,
    g_recv,
    l_sem,
    small_sem,
    small_far_send,
    small_far_recv,
    small_dp_send,
    small_dp_recv,
):
    me = lax.axis_index("mp")
    dp = lax.axis_index("dp")
    group = chips * 2
    chip, core = me // 2, lax.rem(me, 2)
    net = Exchange(chips, chip, core, "mp")
    rows, width = pieces.shape
    entry_count = counts_col.shape[0]
    slots = rows // entry_count
    columns = weights.shape[4]
    half_columns = columns // 2
    head_columns = columns // 4
    heads = width // HD
    blocks = rows // ROW_BLOCK
    total_sum = Total(
        net,
        dp,
        dp_count,
        (part, near, far, x_land, z_land, final),
        (near_sem.at[0], near_sem.at[1], far_send, far_recv, x_sem.at[0], x_sem.at[1])
        + (z_send, z_recv, g_send, g_recv, l_sem.at[0], l_sem.at[1]),
    )
    stages = (
        total_sum.near_middle,
        total_sum.second,
        total_sum.third,
        total_sum.z_middle,
        total_sum.g_middle,
        total_sum.finish,
    )

    def run(step):
        for offset, stage in enumerate(stages):
            if 0 <= step - offset < PARTS:
                stage(step - offset)

    flag = pltpu.get_barrier_semaphore()
    pl.semaphore_signal(flag, inc=1, device_id=net.sibling(), device_id_type=MESH)
    for other in net.others():
        pl.semaphore_signal(flag, inc=1, device_id=net.peer(other), device_id_type=MESH)

    def each_dp(body):
        @pl.loop(1, dp_count)
        def _(j):
            body(lax.rem(dp + j, dp_count))

    each_dp(
        lambda target: pl.semaphore_signal(
            flag, inc=1, device_id={"dp": target}, device_id_type=MESH
        )
    )
    loads = [
        pltpu.make_async_copy(weights_hbm.at[k], weights.at[k], weight_sem.at[k])
        for k in (1, 2, 0)
    ]
    for copy in loads:
        copy.start()
    out_copies = [
        pltpu.make_async_copy(out_part.at[y * 2 + core], out_own.at[y], out_local.at[y])
        for y in range(chips)
    ]
    for copy in out_copies:
        copy.start()
    pl.semaphore_wait(flag, chips + dp_count - 1)

    def out_near_copy(y):
        return net.to_sibling(
            out_part.at[y * 2 + 1 - core],
            out_near.at[y],
            out_near_sem.at[0, y],
            out_near_sem.at[1, y],
        )

    out_half = out_part.shape[1] // 2

    def out_far_copy(other, source, half):
        target = chip if source is not chip else other
        span = pl.ds(half * out_half, out_half)
        return net.to_peer(
            other,
            out_own.at[other, span],
            out_far.at[lax.rem(source - target + chips - 1, chips), span],
            out_far_send.at[half, other],
            out_far_recv.at[half, source],
        )

    def out_middle(half):
        span = pl.ds(half * out_half, out_half)
        for y in range(chips):
            if half == 0:
                out_copies[y].wait()
                out_near_copy(y).wait_recv()
        for other in net.others():
            out_own[other, span] = (
                out_own[other, span].astype(F32) + out_near[other, span].astype(F32)
            ).astype(BF16)
            out_far_copy(other, chip, half).start()

    for y in range(chips):
        out_near_copy(y).start()

    def put(k, c, y, values):
        shape = part.shape[3:]
        part[k, c, y] = values[:, :half_columns].astype(BF16).reshape(shape)
        part[k + 1, c, y] = values[:, half_columns:].astype(BF16).reshape(shape)

    def put_columns(k, c, y, lanes, values):
        columns = slice(lanes * head_columns, (lanes + 1) * head_columns)
        shape = part.shape[3:-1] + (head_columns,)
        part[k, c, y, :, :, :, columns] = values.astype(BF16).reshape(shape)

    token_total = token_rows.shape[0]
    dp_step = max(1, ROW_BLOCK // entry_count)

    @pl.loop(0, dp_count // dp_step)
    def _(block):
        row = lax.broadcasted_iota(jnp.int32, (dp_step * entry_count, token_total), 0)
        owner = block * dp_step + row // entry_count
        number = (owner * group + me) * entry_count + lax.rem(row, entry_count)
        chosen = jnp.where(number == token_row[...], 1.0, 0.0).astype(BF16)
        sums = dot_nn(chosen, token_rows[...]).astype(BF16)
        for j in range(dp_step):
            entry_part[block * dp_step + j] = sums[j * entry_count : (j + 1) * entry_count]

    def entry_copy(target, slot):
        return pltpu.make_async_remote_copy(
            src_ref=entry_part.at[target],
            dst_ref=entry_land.at[slot],
            send_sem=entry_send.at[target],
            recv_sem=entry_recv.at[slot],
            device_id={"dp": target},
            device_id_type=MESH,
        )

    each_dp(lambda target: entry_copy(target, dp).start())
    pooled_t = pooled_own[...].T

    def proj_shard(c, y, span):
        put(0, c, y, dot_nn(pooled_t, embed_rows[:, span]))

    each_shard(chips, columns, proj_shard)
    total_sum.start(0)
    total_sum.start(1)
    bias_sums = jnp.sum(embed_rows[...].astype(F32), axis=0, keepdims=True)
    for j in range(4):
        small_part[4 + j : 5 + j, :] = bias_sums[:, j * width : (j + 1) * width]
    loads[0].wait()
    run(0)

    pool = pool_matrix(counts_col[...], entry_count, rows).astype(BF16)
    spread = spread_matrix(counts_row[...], entry_count, rows)
    valid = jnp.sum(spread, axis=1, keepdims=True)
    spread = spread.astype(BF16)
    for b in range(blocks):
        bias[b] = slot_bias(valid[b * ROW_BLOCK : (b + 1) * ROW_BLOCK], slots)
    ffn_t[...] = ffn_in[...].T

    def hidden_shard(c, y, span):
        before = dot_nn(ffn_in[...], weights[1, c, y])
        hidden_pre[:, span] = before
        hidden[:, span] = dot_nn(pool, gelu_parts(before)[0].astype(BF16)).astype(BF16)

    def some_shards(shards, body):
        @pl.loop(shards * group // 2, (shards + 1) * group // 2)
        def _(m):
            first = pl.multiple_of(m * columns, columns)
            body(lax.rem(m, 2), m // 2, pl.ds(first, columns))

    some_shards(0, hidden_shard)
    run(1)
    some_shards(1, hidden_shard)
    each_dp(lambda source: entry_copy(source, source).wait_recv())
    pooled_grad = entry_part[dp].astype(F32)
    for j in range(1, dp_count):
        pooled_grad = pooled_grad + entry_land[lax.rem(dp + j, dp_count)].astype(F32)
    entry_low = (pooled_grad / counts_col[...]).astype(BF16)
    out_rows = dot_nn(spread, entry_low)
    entry_t = entry_low.T
    loads[1].wait()
    out_low = out_rows.astype(BF16)
    row_total[...] = jnp.zeros_like(row_total)

    def down_shard(c, y, span):
        put(2, c, y, dot_nn(entry_t, hidden[:, span]))

    each_shard(chips, columns, down_shard)
    total_sum.start(2)
    total_sum.start(3)

    def unit_shard(c, y, span):
        act_grad = dot_nn(out_low, weights[2, c, y])
        pre_grad = (act_grad * gelu_parts(hidden_pre[:, span])[1]).astype(BF16)
        put(4, c, y, dot_nn(ffn_t[...], pre_grad))
        row_total[...] += dot_nt(pre_grad, weights[1, c, y])

    some_shards(0, unit_shard)
    run(2)
    some_shards(1, unit_shard)
    total_sum.start(4)
    total_sum.start(5)
    run(3)
    back, gain_grad, shift_grad = norm_back(residual[...], row_total[...], gain_two[...])
    small_part[2:3, :] = gain_grad
    small_part[3:4, :] = shift_grad
    residual_grad = out_rows + back
    pieces_grad[...] = residual_grad
    attn_grad = residual_grad.astype(BF16)
    loads[2].wait()
    for m, c, y in shards_of(chips):
        span = slice(m * head_columns, (m + 1) * head_columns)
        d_out_n[:, span] = dot_nn(attn_grad, weights[0, c, y, :, 3 * head_columns :]).astype(BF16)
    out_grad = dot_nn(attn_grad.T, attended[...])
    for m, c, y in shards_of(chips):
        span = slice(m * head_columns, (m + 1) * head_columns)
        put_columns(7, c, y, 1, out_grad[:, span])
    for b in range(blocks):
        block_rows = slice(b * ROW_BLOCK, (b + 1) * ROW_BLOCK)
        q_t[b] = q_n[block_rows, :].T
        k_t[b] = k_n[block_rows, :].T
        out_t[b] = attended[block_rows, :].T
        d_out_t[b] = d_out_n[block_rows, :].T
    run(4)

    def attend_pair(pair):
        pair_span = pl.ds(pl.multiple_of(pair * 2 * HD, 2 * HD), 2 * HD)
        for b in range(blocks):
            block_rows = slice(b * ROW_BLOCK, (b + 1) * ROW_BLOCK)
            key_pair = k_n[block_rows, pair_span]
            value_pair = v_n[block_rows, pair_span]
            query_pair = q_n[block_rows, pair_span]
            grad_pair = d_out_n[block_rows, pair_span]
            key_sums, value_sums = [], []
            for odd in range(2):
                h = pair * 2 + odd
                span = pl.ds(pl.multiple_of(h * HD, HD), HD)
                lanes = slice(odd * HD, (odd + 1) * HD)
                scores = dot_nn(key_pair[:, lanes], q_t[b, span, :]) + bias[b]
                probs = jnp.exp(scores - logs[b, h])
                grad_t = d_out_t[b, span, :]
                centre = jnp.sum(
                    grad_t.astype(F32) * out_t[b, span, :].astype(F32), axis=0, keepdims=True
                )
                value_sums.append(dot_nn(probs.astype(BF16), grad_pair[:, lanes]))
                score_grad = (probs * (dot_nn(value_pair[:, lanes], grad_t) - centre)).astype(BF16)
                key_sums.append(dot_nn(score_grad, query_pair[:, lanes]))
                d_query_t[b, span, :] = (
                    dot_nn(k_t[b, span, :], score_grad) * (HD**-0.5)
                ).astype(BF16)
            d_key[block_rows, pair_span] = jnp.concatenate(key_sums, axis=1).astype(BF16)
            d_value[block_rows, pair_span] = jnp.concatenate(value_sums, axis=1).astype(BF16)

    pl.loop(0, heads // 4)(attend_pair)
    run(5)
    pl.loop(heads // 4, heads // 2)(attend_pair)
    for b in range(blocks):
        d_query[b * ROW_BLOCK : (b + 1) * ROW_BLOCK, :] = d_query_t[b].T
    rows_t = attn_in[...].T
    for place, (k, lanes, source) in enumerate(
        ((6, 0, d_query), (6, 1, d_key), (7, 0, d_value))
    ):
        grads = dot_nn(rows_t, source[...])
        for m, c, y in shards_of(chips):
            span = slice(m * head_columns, (m + 1) * head_columns)
            put_columns(k, c, y, lanes, grads[:, span])
    total_sum.start(6)
    total_sum.start(7)
    run(6)
    normed = jnp.zeros((rows, width), F32)
    for m, c, y in shards_of(chips):
        span = slice(m * head_columns, (m + 1) * head_columns)
        for j, source in enumerate((d_query, d_key, d_value)):
            normed = normed + dot_nt(
                source[:, span], weights[0, c, y, :, j * head_columns : (j + 1) * head_columns]
            )
    back, gain_grad, shift_grad = norm_back(pieces[...].astype(F32), normed, gain_one[...])
    small_part[0:1, :] = gain_grad
    small_part[1:2, :] = shift_grad
    pieces_grad[...] += back

    def out_finish():
        text_out[...] = out_own[chip].astype(F32) + out_near[chip].astype(F32)
        for other in net.others():
            for half in range(2):
                out_far_copy(other, other, half).wait_recv()
            slot = lax.rem(other - chip + chips - 1, chips)
            text_out[...] += out_far[slot].astype(F32)

    small_copy = net.to_sibling(small_part, small_near, small_sem.at[0], small_sem.at[1])
    small_copy.start()

    def small_far_copy(other, owner):
        return net.to_peer(
            other,
            small_far.at[owner],
            small_far.at[owner],
            small_far_send.at[other],
            small_far_recv.at[owner],
        )

    def small_dp_copy(other, owner):
        return pltpu.make_async_remote_copy(
            src_ref=small_dp.at[owner],
            dst_ref=small_dp.at[owner],
            send_sem=small_dp_send.at[other],
            recv_sem=small_dp_recv.at[owner],
            device_id={"dp": other},
            device_id_type=MESH,
        )

    def small_near_done():
        small_copy.wait_recv()
        small_far[chip] = small_part[...] + small_near[...]
        for other in net.others():
            small_far_copy(other, chip).start()

    def small_far_done():
        for other in net.others():
            small_far_copy(other, other).wait_recv()
        total = small_far[0]
        for j in range(1, chips):
            total = total + small_far[j]
        small_dp[dp] = total
        each_dp(lambda other: small_dp_copy(other, dp).start())

    @pl.loop(7, PARTS + 5)
    def _(step):
        for offset, stage in enumerate(stages):
            k = step - offset

            @pl.when((k >= 0) & (k < PARTS))
            def _():
                stage(k)

        pl.when(step == 7)(small_near_done)
        pl.when(step == 9)(small_far_done)

        @pl.when(step == PARTS)
        def _():
            out_middle(0)
            out_middle(1)

    out_finish()
    each_dp(lambda other: small_dp_copy(other, other).wait_recv())
    total = small_dp[0]
    for j in range(1, dp_count):
        total = total + small_dp[j]
    small_total[...] = total

    for y in range(chips):
        out_near_copy(y).wait_send()
    for other in net.others():
        for half in range(2):
            out_far_copy(other, chip, half).wait_send()
    small_copy.wait_send()
    for other in net.others():
        small_far_copy(other, chip).wait_send()
    each_dp(lambda other: small_dp_copy(other, dp).wait_send())
    each_dp(lambda other: entry_copy(other, dp).wait_send())

    @pl.loop(0, PARTS)
    def _(k):
        total_sum.sent(k)


def hyper_backward(
    group,
    dp_count,
    embed_rows,
    pooled_own,
    token_rows,
    token_row,
    pieces,
    counts_col,
    counts_row,
    gain_one,
    gain_two,
    saved,
    weights,
    out_part,
):
    chips = group // 2
    rows, width = pieces.shape
    entry_count = counts_col.shape[0]
    kinds, columns = weights.shape[0], weights.shape[4]
    half_columns = columns // 2
    heads = width // HD
    blocks = rows // ROW_BLOCK
    spots = dp_count // 2
    vmem = pl.BlockSpec(memory_space=pltpu.VMEM)
    hbm = pl.BlockSpec(memory_space=pl.ANY)
    dma = pltpu.SemaphoreType.DMA
    final = (PARTS, 2, spots, width // (2 * spots), half_columns)
    units = columns * group

    def low(*shape):
        return pltpu.VMEM(shape, BF16)

    def wide(*shape):
        return pltpu.VMEM(shape, F32)

    return pl.pallas_call(
        partial(back_body, chips, dp_count),
        out_shape=(
            jax.ShapeDtypeStruct((rows, width), F32),
            jax.ShapeDtypeStruct(final, BF16),
            jax.ShapeDtypeStruct((8, width), F32),
            jax.ShapeDtypeStruct(out_part.shape[1:], F32),
        ),
        in_specs=[vmem] * 17 + [hbm] * 2,
        out_specs=(vmem,) * 4,
        scratch_shapes=[
            low(kinds, 2, chips, width, columns),
            low(PARTS, 2, chips, *final[1:]),
            low(PARTS, chips, *final[1:]),
            low(PARTS, chips - 1, *final[1:]),
            low(PARTS, chips, *final[2:]),
            low(PARTS, *final[2:]),
            low(dp_count, entry_count, width),
            low(dp_count, entry_count, width),
            low(entry_count, units),
            wide(rows, units),
            low(width, rows),
            wide(rows, width),
            low(rows, width),
            low(rows, width),
            low(rows, width),
            low(rows, width),
        ]
        + [low(blocks, width, ROW_BLOCK)] * 5
        + [
            wide(blocks, ROW_BLOCK, ROW_BLOCK),
            wide(8, width),
            wide(chips, 8, width),
            wide(dp_count, 8, width),
            wide(8, width),
            low(chips, *out_part.shape[1:]),
            low(chips, *out_part.shape[1:]),
            low(chips - 1, *out_part.shape[1:]),
            dma((kinds,)),
            dma((chips,)),
            dma((2, chips)),
            dma((2, chips)),
            dma((2, chips)),
            dma((dp_count,)),
            dma((dp_count,)),
            dma((2, PARTS)),
            dma((PARTS, chips, 2)),
            dma((PARTS, chips, 2)),
            dma((2, PARTS, chips)),
            dma((PARTS, spots)),
            dma((PARTS, spots)),
            dma((PARTS, spots)),
            dma((PARTS, spots)),
            dma((2, PARTS)),
            dma((2,)),
            dma((chips,)),
            dma((chips,)),
            dma((dp_count,)),
            dma((dp_count,)),
        ],
        compiler_params=pltpu.CompilerParams(
            collective_id=2, has_side_effects=True, vmem_limit_bytes=62 * 1024 * 1024
        ),
        cost_estimate=pl.CostEstimate(
            flops=60 * 10**9, bytes_accessed=20 * 10**6, transcendentals=5 * 10**6
        ),
    )(
        embed_rows,
        pooled_own,
        token_rows,
        token_row,
        pieces,
        counts_col,
        counts_row,
        gain_one,
        gain_two,
        *saved,
        weights,
        out_part,
    )


def spread_body(sums, query, key, value, out, up, down, proj):
    half_columns = sums.shape[2]
    head_columns = query.shape[1]
    for first, target in ((0, proj), (2, down), (4, up)):
        target[:, :half_columns] = sums[first].astype(F32)
        target[:, half_columns:] = sums[first + 1].astype(F32)
    for k, lanes, target in ((6, 0, query), (6, 1, key), (7, 0, value), (7, 1, out)):
        target[...] = sums[k, :, lanes * head_columns : (lanes + 1) * head_columns].astype(F32)


def spread_sums(sums):
    _, width, half_columns = sums.shape
    small = jax.ShapeDtypeStruct((width, half_columns // 2), F32)
    large = jax.ShapeDtypeStruct((width, half_columns * 2), F32)
    vmem = pl.BlockSpec(memory_space=pltpu.VMEM)
    return pl.pallas_call(
        spread_body,
        out_shape=(small,) * 4 + (large,) * 3,
        in_specs=[vmem],
        out_specs=(vmem,) * 7,
        compiler_params=pltpu.CompilerParams(vmem_limit_bytes=40 * 1024 * 1024),
    )(sums)


def on_device(
    pieces,
    counts,
    entry_ids,
    segment_ids,
    norm1_gain,
    norm1_shift,
    query_weight,
    key_weight,
    value_weight,
    out_weight,
    norm2_gain,
    norm2_shift,
    up_weight,
    down_weight,
    proj_weight,
    proj_bias,
    text_norm1_gain,
    text_query,
    text_key,
    text_value,
    text_out_proj,
    text_norm2_gain,
    text_gate,
    text_up,
    text_down,
    token_grad,
):
    group, dp_count = lax.axis_size("mp"), lax.axis_size("dp")
    me = lax.axis_index("mp")
    entry_count, slot_count, width = pieces.shape
    text_width = token_grad.shape[1]
    length = segment_ids.shape[1]
    chunk_rows = length // CHUNKS
    pieces_rows = pieces.reshape(entry_count * slot_count, width)
    entries, weights, *saved, counts_col, counts_row, bias_full, grad_even = hyper_forward(
        group,
        dp_count,
        pieces_rows,
        counts[None, :],
        norm1_gain[None, :],
        norm1_shift[None, :],
        norm2_gain[None, :],
        norm2_shift[None, :],
        (query_weight, key_weight, value_weight, out_weight),
        proj_bias[None, :],
        (up_weight, down_weight, proj_weight),
        token_grad,
    )
    head_width = text_query.shape[1]
    kv_index = me * (head_width // FHD) // (QHEADS // KVHEADS)
    key_local = lax.dynamic_slice_in_dim(text_key, kv_index * FHD, FHD, 1)
    value_local = lax.dynamic_slice_in_dim(text_value, kv_index * FHD, FHD, 1)
    key_value = jnp.concatenate([key_local, value_local], axis=1)
    cos_t, sin_t = rope_tables(length)
    out_part, embed_rows, pooled_own, token_rows = text_layer(
        group,
        dp_count,
        entry_count,
        entry_ids.reshape(CHUNKS, 1, chunk_rows),
        segment_ids.reshape(CHUNKS, 1, chunk_rows),
        cos_t,
        sin_t,
        bias_full,
        text_norm1_gain[None, :],
        text_norm2_gain[None, :],
        key_value,
        entries.reshape(-1, width),
        weights,
        token_grad,
        grad_even,
        text_query,
        text_out_proj,
        text_gate,
        text_up,
        text_down,
    )
    pieces_grad, final, small, text_out = hyper_backward(
        group,
        dp_count,
        embed_rows.reshape(-1, text_width),
        pooled_own.reshape(-1, width),
        token_rows.reshape(length, width),
        entry_ids[None, :],
        pieces_rows,
        counts_col,
        counts_row,
        norm1_gain[None, :],
        norm2_gain[None, :],
        saved,
        weights,
        out_part.reshape(group, -1, text_width),
    )
    query_grad, key_grad, value_grad, out_grad, up_grad, down_grad, proj_grad = spread_sums(
        final.reshape(PARTS, width, -1)
    )
    bias_share = proj_bias.shape[0]
    proj_bias_grad = lax.dynamic_slice_in_dim(
        small[4:].reshape(-1), me * bias_share, bias_share
    )
    return (
        text_out,
        pieces_grad.reshape(pieces.shape),
        small[0],
        small[1],
        query_grad,
        key_grad,
        value_grad,
        out_grad,
        small[2],
        small[3],
        up_grad,
        down_grad,
        proj_grad,
        proj_bias_grad,
    )


def solution(mesh):
    return jax.shard_map(
        on_device,
        mesh=mesh,
        in_specs=(
            P(("dp", "mp"), None, None),
            P("dp"),
            P("dp"),
            P("dp", None),
            P(),
            P(),
            P(None, "mp"),
            P(None, "mp"),
            P(None, "mp"),
            P(None, "mp"),
            P(),
            P(),
            P(None, "mp"),
            P(None, "mp"),
            P(None, "mp"),
            P("mp"),
            P(),
            P(None, "mp"),
            P(),
            P(),
            P(None, "mp"),
            P(),
            P(None, "mp"),
            P(None, "mp"),
            P(None, "mp"),
            P(("dp", "mp"), None),
        ),
        out_specs=(
            P(("dp", "mp"), None),
            P(("dp", "mp"), None, None),
            P(),
            P(),
            P(None, "mp"),
            P(None, "mp"),
            P(None, "mp"),
            P(None, "mp"),
            P(),
            P(),
            P(None, "mp"),
            P(None, "mp"),
            P(None, "mp"),
            P("mp"),
        ),
        check_vma=False,
    )
```

```python
from functools import partial
import math

import jax
import jax.numpy as jnp
import numpy as np
from jax import lax
from jax.experimental import pallas as pl
from jax.experimental.pallas import tpu as pltpu
from jax.sharding import PartitionSpec as P

HD = 64
QHEADS = 32
KVHEADS = 4
FHD = 64


def rope_tables(length):
    positions = np.arange(length, dtype=np.float32)
    rates = np.exp(
        np.arange(FHD // 2, dtype=np.float32) * np.float32(-2.0 * math.log(10000.0) / FHD)
    ).astype(np.float32)
    angles = (positions[None, :] * rates[:, None]).reshape(FHD // 2, CHUNKS, length // CHUNKS)
    angles = angles.transpose(1, 0, 2)
    return jnp.asarray(np.cos(angles)), jnp.asarray(np.sin(angles))


MESH = pl.DeviceIdType.MESH
F32 = jnp.float32
BF16 = jnp.bfloat16
CHUNKS = 4
FAR = -1e30


def dot_nn(a, b):
    return lax.dot_general(a, b, (((1,), (0,)), ((), ())), preferred_element_type=F32)


def dot_nt(a, b):
    return lax.dot_general(a, b, (((1,), (1,)), ((), ())), preferred_element_type=F32)


def column_tiles(total, width, body):
    full = total // width
    if full > 0:

        @pl.loop(0, full)
        def _(t):
            body(pl.ds(pl.multiple_of(t * width, width), width))

    if total % width:
        body(pl.ds(full * width, total % width))


def rms_scale(values):
    return lax.rsqrt(jnp.mean(values * values, axis=-1, keepdims=True) + 1e-05)


def rms_back(values, grad, gain):
    scale = rms_scale(values)
    scaled = grad * gain
    return scale * (
        scaled - values * (scale * scale) * jnp.mean(scaled * values, axis=-1, keepdims=True)
    )


class Exchange:
    def __init__(self, chips, chip, core, group_axis):
        self.chips, self.chip, self.core = chips, chip, core
        self.axis = group_axis

    def sibling(self):
        return {self.axis: self.chip * 2 + 1 - self.core}

    def peer(self, other):
        return {self.axis: other * 2 + self.core}

    def others(self):
        return [lax.rem(self.chip + step, self.chips) for step in range(1, self.chips)]

    def barrier(self):
        flag = pltpu.get_barrier_semaphore()
        pl.semaphore_signal(flag, inc=1, device_id=self.sibling(), device_id_type=MESH)
        for other in self.others():
            pl.semaphore_signal(flag, inc=1, device_id=self.peer(other), device_id_type=MESH)
        pl.semaphore_wait(flag, self.chips)

    def to_sibling(self, source, target, send, recv):
        return pltpu.make_async_remote_copy(
            src_ref=source,
            dst_ref=target,
            send_sem=send,
            recv_sem=recv,
            device_id=self.sibling(),
            device_id_type=MESH,
        )

    def to_peer(self, other, source, target, send, recv):
        return pltpu.make_async_remote_copy(
            src_ref=source,
            dst_ref=target,
            send_sem=send,
            recv_sem=recv,
            device_id=self.peer(other),
            device_id_type=MESH,
        )


class Scatter:
    def __init__(self, net, part, near, far, sems):
        self.net, self.part, self.near, self.far = net, part, near, far
        self.slots = None if part.shape[0] == near.shape[0] else part.shape[0]
        self.near_send, self.near_recv, self.far_send, self.far_recv = sems

    def slot(self, i):
        return i if self.slots is None else i % self.slots

    def landing(self, source, target):
        return lax.rem(source - target + self.net.chips - 1, self.net.chips)

    def near_copy(self, i):
        net = self.net
        return net.to_sibling(
            self.part.at[self.slot(i), 1 - net.core],
            self.near.at[i],
            self.near_send.at[i],
            self.near_recv.at[i],
        )

    def far_copy(self, i, other):
        net = self.net
        return net.to_peer(
            other,
            self.part.at[self.slot(i), net.core, other],
            self.far.at[i, self.landing(net.chip, other)],
            self.far_send.at[i, other],
            self.far_recv.at[i, net.chip],
        )

    def far_landing(self, i, other):
        net = self.net
        return net.to_peer(
            other,
            self.part.at[self.slot(i), net.core, other],
            self.far.at[i, self.landing(other, net.chip)],
            self.far_send.at[i, other],
            self.far_recv.at[i, other],
        )

    def start(self, i):
        self.near_copy(i).start()

    def middle(self, i):
        net = self.net
        self.near_copy(i).wait_recv()
        slot = self.slot(i)
        for other in net.others():
            total = self.part[slot, net.core, other].astype(F32) + self.near[
                i, other
            ].astype(F32)
            self.part[slot, net.core, other] = total.astype(BF16)
            self.far_copy(i, other).start()

    def finish(self, i):
        net = self.net
        slot = self.slot(i)
        total = self.part[slot, net.core, net.chip].astype(F32) + self.near[
            i, net.chip
        ].astype(F32)
        for other in net.others():
            self.far_landing(i, other).wait_recv()
            total = total + self.far[i, self.landing(other, net.chip)].astype(F32)
        return total

    def sent(self, i):
        self.near_copy(i).wait_send()
        for other in self.net.others():
            self.far_copy(i, other).wait_send()


class Gather:
    def __init__(self, net, full, sems, single=False):
        self.net, self.full, self.single = net, full, single
        self.far_send, self.far_recv, self.near_send, self.near_recv = sems

    def block(self, i, *place):
        return self.full.at[place] if self.single else self.full.at[(i, *place)]

    def far_copy(self, i, other):
        net = self.net
        block = self.block(i, net.core, net.chip)
        return net.to_peer(
            other, block, block, self.far_send.at[i, other], self.far_recv.at[i, net.chip]
        )

    def far_landing(self, i, other):
        net = self.net
        block = self.block(i, net.core, other)
        return net.to_peer(
            other, block, block, self.far_send.at[i, other], self.far_recv.at[i, other]
        )

    def near_copy(self, i):
        block = self.block(i, self.net.core)
        return self.net.to_sibling(block, block, self.near_send.at[i], self.near_recv.at[i])

    def near_landing(self, i):
        block = self.block(i, 1 - self.net.core)
        return self.net.to_sibling(block, block, self.near_send.at[i], self.near_recv.at[i])

    def start(self, i):
        for other in self.net.others():
            self.far_copy(i, other).start()

    def middle(self, i):
        for other in self.net.others():
            self.far_landing(i, other).wait_recv()
        self.near_copy(i).start()

    def finish(self, i):
        self.near_landing(i).wait_recv()

    def sent(self, i):
        for other in self.net.others():
            self.far_copy(i, other).wait_send()
        self.near_copy(i).wait_send()


STEPS = (
    ("attend", 0),
    ("attn_part", 0),
    ("attend", 2),
    ("attn_far", 0),
    ("attend", 1),
    ("attn_part", 2),
    ("norm", 0),
    ("attn_part", 1),
    ("attend", 3),
    ("attn_far", 1),
    ("attn_far", 2),
    ("attn_part", 3),
    ("rows_near", 0),
    ("units_low", 0),
    ("norm", 1),
    ("units_high", 0),
    ("unit_grads", 0),
    ("norm", 2),
    ("rows_near", 1),
    ("outputs", 0),
    ("attn_far", 3),
    ("units_far", 0),
    ("units_low", 1),
    ("units_high", 1),
    ("rows_near", 2),
    ("unit_grads", 1),
    ("norm", 3),
    ("outputs", 1),
    ("units_far", 1),
    ("residual", 0),
    ("units_low", 2),
    ("units_high", 2),
    ("rows_near", 3),
    ("unit_grads", 2),
    ("residual", 1),
    ("outputs", 2),
    ("units_low", 3),
    ("units_far", 2),
    ("back_near", 0),
    ("units_high", 3),
    ("back_near", 1),
    ("unit_grads", 3),
    ("residual", 2),
    ("attend_back", 0),
    ("units_far", 3),
    ("back_near", 2),
    ("normed_part", 0),
    ("attend_back", 1),
    ("residual", 3),
    ("normed_part", 1),
    ("normed_far", 0),
    ("attend_back", 2),
    ("normed_far", 1),
    ("back_near", 3),
    ("normed_part", 2),
    ("attend_back", 3),
    ("normed_far", 2),
    ("normed_part", 3),
    ("embed_grad", 0),
    ("outputs", 3),
    ("normed_far", 3),
    ("embed_grad", 1),
    ("token_near", 0),
    ("embed_grad", 2),
    ("token_near", 1),
    ("embed_grad", 3),
    ("token_near", 2),
    ("token_near", 3),
)


def column_of(row):
    return jnp.broadcast_to(row, (8, row.shape[1])).T[:, :1]


def text_body(
    chips,
    dp_count,
    entry_count,
    head_count,
    entry_ids,
    segments,
    cos_t,
    sin_t,
    bias_full,
    gain_one,
    gain_two,
    w_kv,
    entries_hbm,
    weights_hbm,
    token_grad,
    w_query_hbm,
    w_out_hbm,
    w_gate_hbm,
    w_up_hbm,
    w_down_hbm,
    out_part,
    embed_grad,
    pooled_own,
    token_full,
    proj,
    w_query,
    w_out,
    w_gate,
    w_up,
    w_down,
    part_a,
    near_a,
    far_a,
    part_b,
    near_b,
    far_b,
    full,
    grad_full,
    embeds_own,
    q_t,
    q_n,
    k_n,
    v_n,
    k_t,
    v_t,
    out_t,
    logs,
    bias,
    residual,
    weight_sem,
    local_sem,
    stage_sem,
    scatter_near,
    scatter_far_send,
    scatter_far_recv,
    gather_near,
    gather_far_send,
    gather_far_recv,
    grad_near,
    grad_far_send,
    grad_far_recv,
):
    me = lax.axis_index("mp")
    chip, core = me // 2, lax.rem(me, 2)
    net = Exchange(chips, chip, core, "mp")
    group = chips * 2
    chunk_rows = q_n.shape[1]
    width = embeds_own.shape[2]
    units = w_gate.shape[1]
    own_rows = embeds_own.shape[1]
    head_width = FHD * head_count
    columns = proj.shape[3]
    entry_total, entry_width = entries_hbm.shape
    owned = token_grad.shape[0]
    first_own = pl.multiple_of((core * chips + chip) * own_rows, own_rows)
    owners = group // CHUNKS if group > CHUNKS else 1

    def scatter_of(kind, part, near, far):
        return Scatter(
            net,
            part,
            near,
            far,
            (
                scatter_near.at[kind, 0],
                scatter_near.at[kind, 1],
                scatter_far_send.at[kind],
                scatter_far_recv.at[kind],
            ),
        )

    def gather_of(kind, ref):
        return Gather(
            net,
            ref,
            (
                gather_far_send.at[kind],
                gather_far_recv.at[kind],
                gather_near.at[kind, 0],
                gather_near.at[kind, 1],
            ),
        )

    attn_sum = scatter_of(0, part_a, near_a, far_a)
    mlp_sum = scatter_of(1, part_b, near_b, far_b)
    normed_sum = scatter_of(2, part_a, near_a, far_a)
    mlp_rows = gather_of(0, full)
    back_rows = gather_of(1, full)
    token_rows = gather_of(2, token_full)

    def load(k, source, target):
        return pltpu.make_async_copy(source, target, weight_sem.at[k])

    load_proj = load(1, weights_hbm.at[3], proj)
    load_query = load(2, w_query_hbm, w_query)
    load_out = load(3, w_out_hbm, w_out)
    load_units = [
        load(4, w_gate_hbm, w_gate),
        load(5, w_up_hbm, w_up),
        load(6, w_down_hbm, w_down),
    ]

    def grad_far(owner_chip, other):
        return net.to_peer(
            other,
            token_grad,
            grad_full.at[owner_chip * 2 + core],
            grad_far_send.at[other],
            grad_far_recv.at[owner_chip],
        )

    def grad_near_copy(owner_chip, owner_core):
        block = grad_full.at[owner_chip * 2 + owner_core]
        return net.to_sibling(
            block, block, grad_near.at[0, owner_chip], grad_near.at[1, owner_chip]
        )

    grad_local = pltpu.make_async_copy(token_grad, grad_full.at[me], local_sem)

    def grad_start():
        for other in net.others():
            grad_far(chip, other).start()

    def grad_middle():
        grad_local.wait()
        grad_near_copy(chip, core).start()
        for other in net.others():
            grad_far(other, other).wait_recv()
            grad_near_copy(other, core).start()

    def grad_chunk(i):
        return grad_full[i * owners : (i + 1) * owners].reshape(chunk_rows, width)

    def grad_finish(i):
        for owner in range(i * owners, (i + 1) * owners):

            @pl.when(core != owner % 2)
            def _():
                grad_near_copy(owner // 2, owner % 2).wait_recv()

    def embed(entries, pooled, embeds):
        load_entries = load(0, entries_hbm, entries)
        load_entries.start()
        for copy in (load_proj, load_query, load_out, *load_units):
            copy.start()
        grad_local.start()
        net.barrier()
        pl.when(core == 1)(grad_start)
        load_entries.wait()
        load_proj.wait()
        load_query.wait()

        @pl.loop(0, CHUNKS)
        def _(i):
            ids = entry_ids[i]
            owner = ids // entry_count
            owner_mp, owner_dp = lax.rem(owner, group), owner // group
            place = (lax.rem(owner_mp, 2) * chips + owner_mp // 2) * dp_count + owner_dp
            spots = column_of(
                (place * entry_count + lax.rem(ids, entry_count)).astype(F32)
            ).astype(jnp.int32)
            numbers = lax.broadcasted_iota(jnp.int32, (chunk_rows, entry_total), 1)
            chosen = jnp.where(numbers == spots, 1.0, 0.0).astype(BF16)
            pooled[...] = dot_nn(chosen, entries[...]).astype(BF16)
            pooled_own[i] = pooled[pl.ds(first_own, own_rows), :]
            for m, c, y in shards_of(chips):
                span = slice(m * columns, (m + 1) * columns)
                embeds[:, span] = (dot_nn(pooled[...], proj[c, y]) + bias_full[c, y]).astype(BF16)
            embeds_own[i] = embeds[pl.ds(first_own, own_rows), :]
            values = embeds[...].astype(F32)
            embeds[...] = (values * rms_scale(values) * gain_one[...]).astype(BF16)
            cosine, sine = cos_t[i], sin_t[i]

            def turned(block):
                low_half, high_half = block[: FHD // 2], block[FHD // 2 :]
                return jnp.concatenate(
                    [low_half * cosine - high_half * sine, high_half * cosine + low_half * sine],
                    axis=0,
                )

            queries = dot_nn(embeds[...], w_query[...]).T
            for h in range(head_count):
                span = slice(h * FHD, (h + 1) * FHD)
                q_t[i, span, :] = (
                    turned(queries[span]).astype(BF16).astype(F32) * FHD**-0.5
                ).astype(BF16)
            q_n[i] = q_t[i].T
            both = dot_nn(embeds[...], w_kv[...])
            keys_t = turned(both.T[:FHD]).astype(BF16)
            k_t[i] = keys_t
            k_n[i] = keys_t.T
            v_n[i] = both[:, FHD:].astype(BF16)
            v_t[i] = both.T[FHD:].astype(BF16)

        pl.when(core == 0)(grad_start)
        pl.when(core == 1)(grad_middle)

    pl.run_scoped(
        embed,
        pltpu.VMEM((entry_total, entry_width), BF16),
        pltpu.VMEM((chunk_rows, entry_width), BF16),
        pltpu.VMEM((chunk_rows, width), BF16),
    )

    def put_rows(part, slot, columns, values):
        half = chunk_rows // 2
        for k in range(2):
            for j in range(chips):
                first = k * half + j * own_rows
                part[slot, k, j, :, columns] = values[first : first + own_rows]

    def rows_of(ref, i):
        return ref[i].reshape(chunk_rows, width)

    def turned_back(sums_t):
        return sums_t.astype(BF16).T

    def make_bias(i):
        query_spots = i * chunk_rows + lax.broadcasted_iota(jnp.int32, (chunk_rows, chunk_rows), 1)
        query_segments = segments[i].astype(F32)
        for kb in range(i + 1):
            allowed = column_of(segments[kb].astype(F32)) == query_segments
            if kb == i:
                key_spots = kb * chunk_rows + lax.broadcasted_iota(
                    jnp.int32, (chunk_rows, chunk_rows), 0
                )
                allowed = allowed & (key_spots <= query_spots)
            bias[kb] = jnp.where(allowed, 0.0, FAR)

    def head_span(h):
        return pl.ds(pl.multiple_of(h * FHD, FHD), FHD)

    def layer(
        mixed,
        gate_grad,
        up_grad,
        out_stage,
        d_out_t,
        d_out_n,
        d_query_t,
        value_total,
        key_total,
    ):
        for ref in (value_total, key_total):
            ref[...] = jnp.zeros_like(ref)

        def stage_copy(i, tile):
            slot = lax.rem(tile, 2)
            columns = pl.ds(pl.multiple_of(tile * 512, 512), 512)
            return pltpu.make_async_copy(
                out_stage.at[slot], out_part.at[i, :, columns], stage_sem.at[slot]
            )

        def pair_t(ref, pair):
            return jnp.concatenate(
                [ref[head_span(pair * 2), :], ref[head_span(pair * 2 + 1), :]], axis=1
            )

        def pair_bias(kb):
            return jnp.concatenate([bias[kb], bias[kb]], axis=1)

        def attend(i):
            make_bias(i)

            @pl.loop(0, head_count // 2)
            def _(pair):
                query = pair_t(q_t.at[i], pair)
                scores = [dot_nn(k_n[kb], query) + pair_bias(kb) for kb in range(i + 1)]
                top = jnp.max(scores[0], axis=0, keepdims=True)
                for block in scores[1:]:
                    top = jnp.maximum(top, jnp.max(block, axis=0, keepdims=True))
                total = jnp.zeros_like(top)
                attended = jnp.zeros((FHD, 2 * chunk_rows), F32)
                for kb in range(i + 1):
                    weights_block = jnp.exp(scores[kb] - top)
                    total = total + jnp.sum(weights_block, axis=0, keepdims=True)
                    attended = attended + dot_nn(v_t[kb], weights_block.astype(BF16))
                logs[i, pair] = top + jnp.log(total)
                attended = (attended / total).astype(BF16)
                out_t[i, head_span(pair * 2), :] = attended[:, :chunk_rows]
                out_t[i, head_span(pair * 2 + 1), :] = attended[:, chunk_rows:]

        def attn_part(i):
            if i == CHUNKS - 1:
                load_out.wait()

            def tile(columns):
                put_rows(part_a, i, columns, turned_back(dot_nn(w_out[columns, :], out_t[i])))

            column_tiles(width, 512, tile)
            attn_sum.start(i)

        def norm(i):
            values = embeds_own[i].astype(F32) + attn_sum.finish(i)
            residual[i] = values
            full[i, core, chip] = (values * rms_scale(values) * gain_two[...]).astype(BF16)
            mlp_rows.start(i)

        def unit_tile(i, columns):
            rows = rows_of(full, i)
            gate_pre = dot_nn(rows, w_gate[:, columns])
            up_pre = dot_nn(rows, w_up[:, columns])
            act_grad = dot_nn(grad_chunk(i), w_down[:, columns])
            inverse = 1.0 / (1.0 + jnp.exp(-gate_pre))
            silu = gate_pre * inverse
            mixed[columns, :] = turned_back(silu * up_pre)
            up_grad[columns, :] = turned_back(act_grad * silu)
            slope = inverse * (1.0 + gate_pre * (1.0 - inverse))
            gate_grad[columns, :] = turned_back(act_grad * up_pre * slope)

        tile_width = 512 if units >= 1024 else 256
        tiles = units // tile_width
        middle_tile = (tiles + 1) // 2

        def unit_tiles(i, first, last):
            @pl.loop(first, last)
            def _(t):
                unit_tile(i, pl.ds(pl.multiple_of(t * tile_width, tile_width), tile_width))

        def units_low(i):
            if i == CHUNKS - 1:
                pl.when(core == 0)(grad_middle)
                for copy in load_units:
                    copy.wait()
            grad_finish(i)
            mlp_rows.finish(i)
            unit_tiles(i, 0, middle_tile)

        def units_high(i):
            unit_tiles(i, middle_tile, tiles)
            if units % tile_width:
                unit_tile(i, pl.ds(tiles * tile_width, units % tile_width))
            mlp_rows.sent(i)

        def unit_grads(i):
            if i + 2 < CHUNKS:
                mlp_sum.sent(i + 2)

            def tile(columns):
                put_rows(
                    part_b,
                    i % 2,
                    columns,
                    turned_back(
                        dot_nn(w_gate[columns, :], gate_grad[...])
                        + dot_nn(w_up[columns, :], up_grad[...])
                    ),
                )

            column_tiles(width, 512, tile)
            mlp_sum.start(i)

        def outputs(i):
            @pl.loop(0, width // 512)
            def _(t):
                columns = pl.ds(pl.multiple_of(t * 512, 512), 512)
                slot = lax.rem(t, 2)
                tile = turned_back(dot_nn(w_down[columns, :], mixed[...]))
                if i == CHUNKS - 1:
                    pl.when(t >= 2)(lambda: stage_copy(i, t).wait())
                else:
                    stage_copy(i, t).wait()
                out_stage[slot] = tile
                own = pl.ds(first_own, own_rows)
                out_stage[slot, own, :] = (
                    out_stage[slot, own, :].astype(F32) + residual[i, :, columns]
                ).astype(BF16)
                stage_copy(i, t).start()

        def residual_back(i):
            grad = mlp_sum.finish(i)
            block = i * owners + first_own // owned
            start = pl.multiple_of(lax.rem(first_own, owned), own_rows)
            own_grad = grad_full[block, pl.ds(start, own_rows), :].astype(F32)
            values = own_grad + rms_back(residual[i], grad, gain_two[...])
            full[i, core, chip] = values.astype(BF16)
            back_rows.start(i)

        def attend_back(i):
            back_rows.finish(i)
            attended_grad = dot_nn(rows_of(full, i), w_out[...]).astype(BF16)
            d_out_n[...] = attended_grad
            d_out_t[...] = attended_grad.T
            make_bias(i)
            cosine, sine = cos_t[i], sin_t[i]

            first_head = (
                lax.broadcasted_iota(jnp.int32, (chunk_rows, 2 * FHD), 1) < FHD
            )

            def stacked(rows):
                wide = rows.astype(F32)
                return jnp.concatenate(
                    [jnp.where(first_head, wide, 0.0), jnp.where(first_head, 0.0, wide)], axis=0
                ).astype(BF16)

            @pl.loop(0, head_count // 2)
            def _(pair):
                pair_span = pl.ds(pl.multiple_of(pair * 2 * FHD, 2 * FHD), 2 * FHD)
                query_rows = stacked(q_n[i, :, pair_span])
                grad_rows = stacked(d_out_n[:, pair_span])
                query = pair_t(q_t.at[i], pair)
                grad = pair_t(d_out_t, pair)
                log_row = logs[i, pair]
                centre = jnp.sum(
                    grad.astype(F32) * pair_t(out_t.at[i], pair).astype(F32),
                    axis=0,
                    keepdims=True,
                )
                query_grad = jnp.zeros((FHD, 2 * chunk_rows), F32)
                for kb in range(i + 1):
                    probs = jnp.exp(dot_nn(k_n[kb], query) + pair_bias(kb) - log_row)
                    value_total[kb] += dot_nn(probs.astype(BF16), grad_rows)
                    score_grad = (probs * (dot_nn(v_n[kb], grad) - centre)).astype(BF16)
                    key_total[kb] += dot_nn(score_grad, query_rows)
                    query_grad = query_grad + dot_nn(k_t[kb], score_grad)
                query_grad = query_grad * (FHD**-0.5)
                for odd in range(2):
                    lanes = slice(odd * chunk_rows, (odd + 1) * chunk_rows)
                    low_half = query_grad[: FHD // 2, lanes]
                    high_half = query_grad[FHD // 2 :, lanes]
                    d_query_t[head_span(pair * 2 + odd), :] = jnp.concatenate(
                        [
                            low_half * cosine + high_half * sine,
                            high_half * cosine - low_half * sine,
                        ],
                        axis=0,
                    ).astype(BF16)

        def normed_part(i):
            attn_sum.sent(i)
            key_grad = (key_total[i][:, :FHD] + key_total[i][:, FHD:]).T
            cosine, sine = cos_t[i], sin_t[i]
            low_half, high_half = key_grad[: FHD // 2], key_grad[FHD // 2 :]
            value_grad = (value_total[i][:, :FHD] + value_total[i][:, FHD:]).T
            both = jnp.concatenate(
                [
                    low_half * cosine + high_half * sine,
                    high_half * cosine - low_half * sine,
                    value_grad,
                ],
                axis=0,
            )
            both = both.astype(BF16)

            def tile(columns):
                put_rows(
                    part_a,
                    i,
                    columns,
                    turned_back(
                        dot_nn(w_query[columns, :], d_query_t[...])
                        + dot_nn(w_kv[columns, :], both)
                    ),
                )

            column_tiles(width, 512, tile)
            normed_sum.start(i)

        def embed_back(i):
            grad = normed_sum.finish(i)
            kept = full[i, core, chip].astype(F32)
            values = kept + rms_back(embeds_own[i].astype(F32), grad, gain_one[...])
            embed_grad[i] = values.astype(BF16)
            total = jnp.zeros((own_rows, entry_width), F32)
            for m, c, y in shards_of(chips):
                total = total + dot_nt(
                    embed_grad[i, :, m * columns : (m + 1) * columns], proj[c, y]
                )
            token_full[i, core, chip] = total.astype(BF16)
            token_rows.start(i)

        stages = {
            "attend": attend,
            "attn_part": attn_part,
            "attn_far": attn_sum.middle,
            "norm": norm,
            "rows_near": mlp_rows.middle,
            "units_low": units_low,
            "units_high": units_high,
            "unit_grads": unit_grads,
            "outputs": outputs,
            "units_far": mlp_sum.middle,
            "residual": residual_back,
            "back_near": back_rows.middle,
            "attend_back": attend_back,
            "normed_part": normed_part,
            "normed_far": normed_sum.middle,
            "embed_grad": embed_back,
            "token_near": token_rows.middle,
        }
        for name, turn in STEPS:
            stages[name](CHUNKS - 1 - turn)

        for tile in range(2):
            stage_copy(0, tile).wait()

    lines = (units, chunk_rows)
    keys = (CHUNKS, chunk_rows, 2 * FHD)
    pl.run_scoped(
        layer,
        pltpu.VMEM(lines, BF16),
        pltpu.VMEM(lines, BF16),
        pltpu.VMEM(lines, BF16),
        pltpu.VMEM((2, chunk_rows, 512), BF16),
        pltpu.VMEM((head_width, chunk_rows), BF16),
        pltpu.VMEM((chunk_rows, head_width), BF16),
        pltpu.VMEM((head_width, chunk_rows), BF16),
        pltpu.VMEM(keys, F32),
        pltpu.VMEM(keys, F32),
    )

    @pl.loop(0, CHUNKS)
    def _(i):
        token_rows.finish(i)
        token_rows.sent(i)
        normed_sum.sent(i)
        back_rows.sent(i)

    for i in range(2):
        mlp_sum.sent(i)
    for other in net.others():
        grad_far(chip, other).wait_send()
    for owner_chip in range(chips):
        grad_near_copy(owner_chip, core).wait_send()


def text_layer(
    group,
    dp_count,
    entry_count,
    entry_ids,
    segments,
    cos_t,
    sin_t,
    bias_full,
    gain_one,
    gain_two,
    w_kv,
    entries,
    weights,
    token_grad,
    w_query,
    w_out,
    w_gate,
    w_up,
    w_down,
):
    chips = group // 2
    chunks, _, chunk_rows = entry_ids.shape
    own_rows = chunk_rows // group
    owned, width = token_grad.shape
    head_width = w_query.shape[1]
    head_count = head_width // FHD
    entry_width = entries.shape[1]
    vmem = pl.BlockSpec(memory_space=pltpu.VMEM)
    hbm = pl.BlockSpec(memory_space=pl.ANY)
    dma = pltpu.SemaphoreType.DMA

    def low(*shape):
        return pltpu.VMEM(shape, BF16)

    return pl.pallas_call(
        partial(text_body, chips, dp_count, entry_count, head_count),
        out_shape=(
            jax.ShapeDtypeStruct((chunks, chunk_rows, width), BF16),
            jax.ShapeDtypeStruct((chunks, own_rows, width), BF16),
            jax.ShapeDtypeStruct((chunks, own_rows, entry_width), BF16),
            jax.ShapeDtypeStruct((chunks, 2, chips, own_rows, entry_width), BF16),
        ),
        in_specs=[vmem] * 8 + [hbm] * 8,
        out_specs=(hbm, vmem, vmem, vmem),
        scratch_shapes=[
            low(*weights.shape[1:]),
            low(*w_query.shape),
            low(*w_out.shape),
            low(*w_gate.shape),
            low(*w_up.shape),
            low(*w_down.shape),
            low(chunks, 2, chips, own_rows, width),
            low(chunks, chips, own_rows, width),
            low(chunks, chips - 1, own_rows, width),
            low(2, 2, chips, own_rows, width),
            low(chunks, chips, own_rows, width),
            low(chunks, chips - 1, own_rows, width),
            low(chunks, 2, chips, own_rows, width),
            low(group, owned, width),
            low(chunks, own_rows, width),
            low(chunks, head_width, chunk_rows),
            low(chunks, chunk_rows, head_width),
            low(chunks, chunk_rows, FHD),
            low(chunks, chunk_rows, FHD),
            low(chunks, FHD, chunk_rows),
            low(chunks, FHD, chunk_rows),
            low(chunks, head_width, chunk_rows),
            pltpu.VMEM((chunks, head_count // 2, 1, 2 * chunk_rows), F32),
            pltpu.VMEM((chunks, chunk_rows, chunk_rows), F32),
            pltpu.VMEM((chunks, own_rows, width), F32),
            dma((7,)),
            dma,
            dma((2,)),
            dma((3, 2, chunks)),
            dma((3, chunks, chips)),
            dma((3, chunks, chips)),
            dma((3, 2, chunks)),
            dma((3, chunks, chips)),
            dma((3, chunks, chips)),
            dma((2, chips)),
            dma((chips,)),
            dma((chips,)),
        ],
        compiler_params=pltpu.CompilerParams(
            collective_id=0, has_side_effects=True, vmem_limit_bytes=65280 * 1024
        ),
        cost_estimate=pl.CostEstimate(
            flops=90 * 10**9, bytes_accessed=40 * 10**6, transcendentals=20 * 10**6
        ),
    )(
        entry_ids,
        segments,
        cos_t,
        sin_t,
        bias_full,
        gain_one,
        gain_two,
        w_kv,
        entries,
        weights,
        token_grad,
        w_query,
        w_out,
        w_gate,
        w_up,
        w_down,
    )


def norm_parts(values):
    average = jnp.mean(values, axis=-1, keepdims=True)
    centred = values - average
    scale = lax.rsqrt(jnp.mean(centred * centred, axis=-1, keepdims=True) + 1e-05)
    return centred * scale, scale


def norm_back(values, grad, gain):
    unit, scale = norm_parts(values)
    scaled = grad * gain
    back = scale * (
        scaled
        - jnp.mean(scaled, axis=-1, keepdims=True)
        - unit * jnp.mean(scaled * unit, axis=-1, keepdims=True)
    )
    return (
        back,
        jnp.sum(grad * unit, axis=0, keepdims=True),
        jnp.sum(grad, axis=0, keepdims=True),
    )


def gelu_parts(values):
    root = math.sqrt(2.0 / math.pi)
    squared = values * values
    bent = jnp.tanh(root * values * (1.0 + 0.044715 * squared))
    half = 0.5 * (1.0 + bent)
    slope = half + 0.5 * values * (1.0 - bent * bent) * root * (1.0 + 3 * 0.044715 * squared)
    return values * half, slope


def pool_matrix(counts_col, entries, rows):
    entry = lax.broadcasted_iota(jnp.int32, (entries, rows), 0)
    row = lax.broadcasted_iota(jnp.int32, (entries, rows), 1)
    slots = rows // entries
    inside = (row // slots == entry) & (lax.rem(row, slots).astype(F32) < counts_col)
    return jnp.where(inside, 1.0, 0.0)


def spread_matrix(counts_row, entries, rows):
    row = lax.broadcasted_iota(jnp.int32, (rows, entries), 0)
    entry = lax.broadcasted_iota(jnp.int32, (rows, entries), 1)
    slots = rows // entries
    inside = (row // slots == entry) & (lax.rem(row, slots).astype(F32) < counts_row)
    return jnp.where(inside, 1.0, 0.0)


def slot_bias(valid_col, slots):
    rows = valid_col.shape[0]
    key = lax.broadcasted_iota(jnp.int32, (rows, rows), 0)
    query = lax.broadcasted_iota(jnp.int32, (rows, rows), 1)
    return jnp.where((key // slots == query // slots) & (valid_col > 0.5), 0.0, FAR)


ROW_BLOCK = 128


def fill_diagonal(ref, columns_t, heads):
    for h in range(heads):
        span = slice(h * HD, (h + 1) * HD)
        ref[span, h * ROW_BLOCK : (h + 1) * ROW_BLOCK] = columns_t[span, :]


def pair_blocks(both):
    return jnp.concatenate([both[:HD, :ROW_BLOCK], both[HD:, ROW_BLOCK:]], axis=0)


def tiled(block, count):
    return jnp.concatenate([block] * count, axis=1)


def shards_of(chips):
    return [(y * 2 + c, c, y) for y in range(chips) for c in range(2)]


def each_shard(chips, columns, body):
    @pl.loop(0, 2)
    def _(c):
        @pl.loop(0, chips)
        def _(y):
            first = pl.multiple_of((y * 2 + c) * columns, columns)
            body(c, y, pl.ds(first, columns))


def hyper_body(
    chips,
    dp_count,
    pieces,
    counts_all,
    gain_one,
    shift_one,
    gain_two,
    shift_two,
    w_query,
    w_key,
    w_value,
    w_out,
    bias_own,
    w_up_hbm,
    w_down_hbm,
    w_proj_hbm,
    entries,
    weights_out,
    attn_in,
    q_n,
    k_n,
    v_n,
    attended,
    logs,
    residual,
    ffn_in,
    counts_col,
    counts_row,
    bias_full,
    full,
    q_t,
    v_t,
    out_t,
    bias,
    diagonal,
    hidden,
    counts_scratch,
    local_sem,
    store_sem,
    far_send,
    far_recv,
    x_send,
    x_recv,
    near_send,
    near_recv,
    z_send,
    z_recv,
    mate_send,
    mate_recv,
    y_send,
    y_recv,
    last_send,
    last_recv,
    bias_far_send,
    bias_far_recv,
    bias_near,
):
    me = lax.axis_index("mp")
    dp = lax.axis_index("dp")
    chip, core = me // 2, lax.rem(me, 2)
    net = Exchange(chips, chip, core, "mp")
    side = lax.rem(dp, 2)
    mate = dp + 1 - 2 * side
    spot, spots = dp // 2, dp_count // 2
    kinds, _, _, width, columns = full.shape
    sources = (None, w_up_hbm, w_down_hbm, w_proj_hbm)
    rows = pieces.shape[0]
    entry_count = counts_col.shape[0]
    slots = rows // entry_count
    head_columns = columns // 4
    half = width // 2
    heads = width // HD

    flag = pltpu.get_barrier_semaphore()
    pl.semaphore_signal(flag, inc=1, device_id=net.sibling(), device_id_type=MESH)
    for other in net.others():
        pl.semaphore_signal(flag, inc=1, device_id=net.peer(other), device_id_type=MESH)

    pl.semaphore_signal(flag, inc=1, device_id={"dp": mate}, device_id_type=MESH)

    @pl.loop(1, spots)
    def _(j):
        target = lax.rem(spot + j, spots) * 2 + side
        pl.semaphore_signal(flag, inc=1, device_id={"dp": target}, device_id_type=MESH)

    local = [
        pltpu.make_async_copy(sources[k], full.at[k, core, chip], local_sem.at[k - 1])
        for k in range(1, kinds)
    ]
    for copy in local:
        copy.start()
    for j, source in enumerate((w_query, w_key, w_value, w_out)):
        full[0, core, chip, :, j * head_columns : (j + 1) * head_columns] = source[...]
    bias_full[core, chip] = bias_own[...]
    pl.semaphore_wait(flag, chips + spots)

    def rows_half(which):
        return pl.ds(pl.multiple_of(which * half, half), half)

    def far_copy(k, other):
        return net.to_peer(
            other,
            sources[k].at[rows_half(side)] if k else full.at[0, core, chip, rows_half(side)],
            full.at[k, core, chip, rows_half(side)],
            far_send.at[k, other],
            far_recv.at[k, chip],
        )

    def far_landing(k, other):
        block = full.at[k, core, other, rows_half(side)]
        return net.to_peer(other, block, block, far_send.at[k, other], far_recv.at[k, other])

    def x_copy(k, other, which):
        block = full.at[k, core, other, rows_half(which)]
        return pltpu.make_async_remote_copy(
            src_ref=block,
            dst_ref=block,
            send_sem=x_send.at[k, other],
            recv_sem=x_recv.at[k, other],
            device_id={"dp": mate},
            device_id_type=MESH,
        )

    def near_copy(k, which):
        block = full.at[k, which]
        return net.to_sibling(block, block, near_send.at[k], near_recv.at[k])

    def far_middle(k):
        for other in net.others():
            far_landing(k, other).wait_recv()
            x_copy(k, other, side).start()

    def x_middle(k):
        for other in net.others():
            x_copy(k, other, 1 - side).wait_recv()
        if k:
            local[k - 1].wait()
        near_copy(k, core).start()

    def store(k):
        return pltpu.make_async_copy(full.at[k], weights_out.at[k], store_sem.at[k])

    def near_finish(k):
        near_copy(k, 1 - core).wait_recv()
        store(k).start()

    bias_rows = Gather(
        net, bias_full, (bias_far_send, bias_far_recv, bias_near.at[0], bias_near.at[1]), True
    )
    def far_start(k):
        for other in net.others():
            far_copy(k, other).start()

    far_start(0)
    bias_rows.start(0)
    counts_scratch[...] = column_of(counts_all[...].astype(F32))
    own_counts = counts_scratch[pl.ds(pl.multiple_of(me * entry_count, entry_count), entry_count)]
    counts_col[...] = own_counts
    counts_row[...] = jnp.broadcast_to(own_counts, (entry_count, 128)).T[:1]

    values = pieces[...].astype(F32)
    attn_in[...] = (norm_parts(values)[0] * gain_one[...] + shift_one[...]).astype(BF16)
    blocks = rows // ROW_BLOCK
    valid = jnp.sum(spread_matrix(counts_row[...], entry_count, rows), axis=1, keepdims=True)
    for b in range(blocks):
        bias[b] = slot_bias(valid[b * ROW_BLOCK : (b + 1) * ROW_BLOCK], slots)

    far_middle(0)
    far_start(1)
    bias_rows.middle(0)
    far_middle(1)
    far_start(2)
    x_middle(0)
    near_finish(0)
    for m, c, y in shards_of(chips):
        span = slice(m * head_columns, (m + 1) * head_columns)
        projected = dot_nn(attn_in[...], full[0, c, y, :, : 3 * head_columns])
        q_n[:, span] = (projected[:, :head_columns].astype(BF16).astype(F32) * HD**-0.5).astype(
            BF16
        )
        k_n[:, span] = projected[:, head_columns : 2 * head_columns].astype(BF16)
        v_n[:, span] = projected[:, 2 * head_columns :].astype(BF16)
    far_middle(2)
    far_start(3)
    x_middle(1)
    for b in range(blocks):
        block_rows = slice(b * ROW_BLOCK, (b + 1) * ROW_BLOCK)
        q_t[b] = q_n[block_rows, :].T
        v_t[b] = v_n[block_rows, :].T

    diagonal[...] = jnp.zeros_like(diagonal)

    def attend_block(b):
        block_rows = pl.ds(pl.multiple_of(b * ROW_BLOCK, ROW_BLOCK), ROW_BLOCK)
        fill_diagonal(diagonal, q_t[b], heads)
        scores = dot_nn(k_n[block_rows, :], diagonal[...]) + tiled(bias[b], heads)
        top = jnp.max(scores, axis=0, keepdims=True)
        weights = jnp.exp(scores - top)
        total = jnp.sum(weights, axis=0, keepdims=True)
        logs[b] = top + jnp.log(total)
        weights = (weights / total).astype(BF16)
        for pair in range(heads // 2):
            span = slice(pair * 2 * HD, (pair + 1) * 2 * HD)
            lanes = slice(pair * 2 * ROW_BLOCK, (pair + 1) * 2 * ROW_BLOCK)
            both = dot_nn(v_t[b, span, :], weights[:, lanes])
            out_t[b, span, :] = pair_blocks(both).astype(BF16)

    pl.loop(0, blocks // 2)(attend_block)
    far_middle(3)
    x_middle(2)
    pl.loop(blocks // 2, blocks)(attend_block)
    for b in range(blocks):
        attended[b * ROW_BLOCK : (b + 1) * ROW_BLOCK, :] = out_t[b].T
    total = values
    for m, c, y in shards_of(chips):
        span = slice(m * head_columns, (m + 1) * head_columns)
        total = total + dot_nt(attended[:, span], full[0, c, y, :, 3 * head_columns :])
    residual[...] = total
    ffn_in[...] = (norm_parts(total)[0] * gain_two[...] + shift_two[...]).astype(BF16)
    near_finish(1)
    x_middle(3)
    pool = pool_matrix(counts_col[...], entry_count, rows).astype(BF16)

    def up_shard(c, y, span):
        act = gelu_parts(dot_nn(ffn_in[...], full[1, c, y]))[0]
        hidden[:, span] = dot_nn(pool, act.astype(BF16)).astype(BF16)

    each_shard(chips, columns, up_shard)
    near_finish(2)
    pooled = jnp.sum(
        (residual[...] * valid).reshape(entry_count, slots, width), axis=1
    )
    for m, c, y in shards_of(chips):
        pooled = pooled + dot_nt(hidden[:, m * columns : (m + 1) * columns], full[2, c, y])
    entries[core, chip, dp] = (pooled / counts_col[...]).astype(BF16)

    def z_copy(target, owner):
        piece = entries.at[core, chip, owner * 2 + side]
        return pltpu.make_async_remote_copy(
            src_ref=piece,
            dst_ref=piece,
            send_sem=z_send.at[target],
            recv_sem=z_recv.at[owner],
            device_id={"dp": target * 2 + side},
            device_id_type=MESH,
        )

    def mate_copy(owner, which):
        piece = entries.at[core, chip, owner * 2 + which]
        return pltpu.make_async_remote_copy(
            src_ref=piece,
            dst_ref=piece,
            send_sem=mate_send.at[owner],
            recv_sem=mate_recv.at[owner],
            device_id={"dp": mate},
            device_id_type=MESH,
        )

    def y_copy(other, owner, block):
        piece = entries.at[core, owner, block]
        return net.to_peer(
            other, piece, piece, y_send.at[other, block], y_recv.at[owner, block]
        )

    def y_start(block):
        for other in net.others():
            y_copy(other, chip, block).start()

    @pl.loop(1, spots)
    def _(j):
        z_copy(lax.rem(spot + j, spots), spot).start()

    mate_copy(spot, side).start()
    y_start(dp)
    near_finish(3)
    bias_rows.finish(0)

    @pl.loop(1, spots)
    def _(j):
        source = lax.rem(spot + spots - j, spots)
        z_copy(source, source).wait_recv()
        mate_copy(source, side).start()
        y_start(source * 2 + side)

    @pl.loop(0, spots)
    def _(j):
        source = lax.rem(spot + spots - j, spots)
        mate_copy(source, 1 - side).wait_recv()
        y_start(source * 2 + 1 - side)

    def last_copy(part, c, owner):
        piece = entries.at[c, owner]
        return net.to_sibling(piece, piece, last_send.at[part], last_recv.at[owner])

    last_copy(chip, core, chip).start()
    for other in net.others():

        @pl.loop(0, dp_count)
        def _(block):
            y_copy(other, other, block).wait_recv()

        last_copy(other, core, other).start()
    last_copy(chip, 1 - core, chip).wait_recv()
    for other in net.others():
        last_copy(other, 1 - core, other).wait_recv()

    bias_rows.sent(0)
    for k in range(kinds):
        store(k).wait()
        near_copy(k, core).wait_send()
        for other in net.others():
            far_copy(k, other).wait_send()
            x_copy(k, other, side).wait_send()

    @pl.loop(1, spots)
    def _(j):
        z_copy(lax.rem(spot + j, spots), spot).wait_send()

    @pl.loop(0, spots)
    def _(j):
        mate_copy(j, side).wait_send()

    last_copy(chip, core, chip).wait_send()
    for other in net.others():
        last_copy(other, core, other).wait_send()

        @pl.loop(0, dp_count)
        def _(block):
            y_copy(other, chip, block).wait_send()


def hyper_forward(
    group,
    dp_count,
    pieces,
    counts,
    gain_one,
    shift_one,
    gain_two,
    shift_two,
    head_weights,
    bias_own,
    unit_weights,
):
    chips = group // 2
    rows, width = pieces.shape
    columns = unit_weights[0].shape[1]
    kinds = 4
    entry_count = counts.shape[1] // group
    heads = width // HD
    blocks = rows // ROW_BLOCK
    vmem = pl.BlockSpec(memory_space=pltpu.VMEM)
    hbm = pl.BlockSpec(memory_space=pl.ANY)
    row_shape = jax.ShapeDtypeStruct((rows, width), BF16)
    dma = pltpu.SemaphoreType.DMA
    return pl.pallas_call(
        partial(hyper_body, chips, dp_count),
        out_shape=(
            jax.ShapeDtypeStruct((2, chips, dp_count, entry_count, width), BF16),
            jax.ShapeDtypeStruct((kinds, 2, chips, width, columns), BF16),
            row_shape,
            row_shape,
            row_shape,
            row_shape,
            row_shape,
            jax.ShapeDtypeStruct((blocks, 1, heads * ROW_BLOCK), F32),
            jax.ShapeDtypeStruct((rows, width), F32),
            row_shape,
            jax.ShapeDtypeStruct((entry_count, 1), F32),
            jax.ShapeDtypeStruct((1, entry_count), F32),
            jax.ShapeDtypeStruct((2, chips, 1, columns), F32),
        ),
        in_specs=[vmem] * 11 + [hbm] * 3,
        out_specs=(vmem, hbm) + (vmem,) * 11,
        scratch_shapes=[
            pltpu.VMEM((kinds, 2, chips, width, columns), BF16),
            pltpu.VMEM((blocks, width, ROW_BLOCK), BF16),
            pltpu.VMEM((blocks, width, ROW_BLOCK), BF16),
            pltpu.VMEM((blocks, width, ROW_BLOCK), BF16),
            pltpu.VMEM((blocks, ROW_BLOCK, ROW_BLOCK), F32),
            pltpu.VMEM((width, heads * ROW_BLOCK), BF16),
            pltpu.VMEM((entry_count, columns * group), BF16),
            pltpu.VMEM((counts.shape[1], 1), F32),
            dma((kinds - 1,)),
            dma((kinds,)),
            dma((kinds, chips)),
            dma((kinds, chips)),
            dma((kinds, chips)),
            dma((kinds, chips)),
            dma((kinds,)),
            dma((kinds,)),
            dma((dp_count // 2,)),
            dma((dp_count // 2,)),
            dma((dp_count // 2,)),
            dma((dp_count // 2,)),
            dma((chips, dp_count)),
            dma((chips, dp_count)),
            dma((chips,)),
            dma((chips,)),
            dma((1, chips)),
            dma((1, chips)),
            dma((2, 1)),
        ],
        compiler_params=pltpu.CompilerParams(
            collective_id=1, has_side_effects=True, vmem_limit_bytes=60 * 1024 * 1024
        ),
        cost_estimate=pl.CostEstimate(
            flops=60 * 10**9, bytes_accessed=20 * 10**6, transcendentals=5 * 10**6
        ),
    )(
        pieces,
        counts,
        gain_one,
        shift_one,
        gain_two,
        shift_two,
        *head_weights,
        bias_own,
        *unit_weights,
    )


class Total:
    def __init__(self, net, dp, dp_count, scatter, mine, x_land, z_land, final, sems):
        self.net, self.scatter, self.mine = net, scatter, mine
        self.x_land, self.z_land, self.final = x_land, z_land, final
        self.x_send, self.x_recv, self.z_send, self.z_recv = sems[:4]
        self.g_send, self.g_recv, self.l_send, self.l_recv = sems[4:]
        self.side = lax.rem(dp, 2)
        self.spot = dp // 2
        self.mate = dp + 1 - 2 * self.side
        self.spots = dp_count // 2

    def remote(self, source, target, send, recv, device):
        return pltpu.make_async_remote_copy(
            src_ref=source,
            dst_ref=target,
            send_sem=send,
            recv_sem=recv,
            device_id={"dp": device},
            device_id_type=MESH,
        )

    def x_copy(self, k):
        return self.remote(
            self.mine.at[k, 1 - self.side],
            self.x_land.at[k],
            self.x_send.at[k],
            self.x_recv.at[k],
            self.mate,
        )

    def z_copy(self, k, spot, slot):
        return self.remote(
            self.mine.at[k, self.side, spot],
            self.z_land.at[k, slot],
            self.z_send.at[k, spot],
            self.z_recv.at[k, slot],
            spot * 2 + self.side,
        )

    def g_copy(self, k, spot, owner):
        block = self.final.at[k, self.side, owner]
        return self.remote(
            block, block, self.g_send.at[k, spot], self.g_recv.at[k, owner], spot * 2 + self.side
        )

    def l_copy(self, k, side):
        block = self.final.at[k, side]
        return self.remote(block, block, self.l_send.at[k], self.l_recv.at[k], self.mate)

    def each_spot(self, body):
        if self.spots > 1:

            @pl.loop(1, self.spots)
            def _(j):
                body(lax.rem(self.spot + j, self.spots))

    def start(self, k):
        self.scatter.start(k)

    def near_middle(self, k):
        self.scatter.middle(k)

    def far_middle(self, k):
        total = self.scatter.finish(k)
        self.mine[k] = total.astype(BF16).reshape(self.mine.shape[1:])
        self.x_copy(k).start()

    def x_middle(self, k):
        self.x_copy(k).wait_recv()
        block = self.mine[k, self.side].astype(F32) + self.x_land[k].astype(F32)
        self.mine[k, self.side] = block.astype(BF16)
        self.each_spot(lambda spot: self.z_copy(k, spot, self.spot).start())

    def z_middle(self, k):
        def add(spot):
            self.z_copy(k, spot, spot).wait_recv()

        self.each_spot(add)
        total = self.mine[k, self.side, self.spot].astype(F32)
        for j in range(1, self.spots):
            spot = lax.rem(self.spot + j, self.spots)
            total = total + self.z_land[k, spot].astype(F32)
        self.final[k, self.side, self.spot] = total.astype(BF16)
        self.each_spot(lambda spot: self.g_copy(k, spot, self.spot).start())

    def g_middle(self, k):
        self.each_spot(lambda spot: self.g_copy(k, spot, spot).wait_recv())
        self.l_copy(k, self.side).start()

    def finish(self, k):
        self.l_copy(k, 1 - self.side).wait_recv()

    def sent(self, k):
        self.scatter.sent(k)
        self.x_copy(k).wait_send()
        self.each_spot(lambda spot: self.z_copy(k, spot, self.spot).wait_send())
        self.each_spot(lambda spot: self.g_copy(k, spot, self.spot).wait_send())
        self.l_copy(k, self.side).wait_send()


PARTS = 8


def back_body(
    chips,
    dp_count,
    embed_rows,
    pooled_own,
    token_rows,
    token_row,
    pieces,
    counts_col,
    counts_row,
    gain_one,
    gain_two,
    attn_in,
    q_n,
    k_n,
    v_n,
    attended,
    logs,
    residual,
    ffn_in,
    weights_hbm,
    out_part,
    pieces_grad,
    final,
    small_total,
    text_out,
    weights,
    part,
    near,
    far,
    mine,
    x_land,
    z_land,
    entry_part,
    entry_land,
    hidden,
    slopes,
    ffn_t,
    row_total,
    d_out_n,
    d_query,
    d_key,
    d_value,
    q_t,
    out_t,
    d_out_t,
    k_t,
    d_query_t,
    bias,
    query_wide,
    grad_wide,
    small_near,
    small_far,
    small_dp,
    small_part,
    out_own,
    out_near,
    out_far,
    weight_sem,
    out_local,
    out_near_sem,
    out_far_send,
    out_far_recv,
    entry_send,
    entry_recv,
    scatter_near,
    scatter_far_send,
    scatter_far_recv,
    x_sem,
    z_send,
    z_recv,
    g_send,
    g_recv,
    l_sem,
    small_sem,
    small_far_send,
    small_far_recv,
    small_dp_send,
    small_dp_recv,
):
    me = lax.axis_index("mp")
    dp = lax.axis_index("dp")
    group = chips * 2
    chip, core = me // 2, lax.rem(me, 2)
    net = Exchange(chips, chip, core, "mp")
    rows, width = pieces.shape
    entry_count = counts_col.shape[0]
    slots = rows // entry_count
    columns = weights.shape[4]
    half_columns = columns // 2
    head_columns = columns // 4
    heads = width // HD
    blocks = rows // ROW_BLOCK
    total_sum = Total(
        net,
        dp,
        dp_count,
        Scatter(
            net,
            part,
            near,
            far,
            (scatter_near.at[0], scatter_near.at[1], scatter_far_send, scatter_far_recv),
        ),
        mine,
        x_land,
        z_land,
        final,
        (x_sem.at[0], x_sem.at[1], z_send, z_recv, g_send, g_recv, l_sem.at[0], l_sem.at[1]),
    )
    stages = (
        total_sum.near_middle,
        total_sum.far_middle,
        total_sum.x_middle,
        total_sum.z_middle,
        total_sum.g_middle,
        total_sum.finish,
    )

    def run(step):
        for offset, stage in enumerate(stages):
            if 0 <= step - offset < PARTS:
                stage(step - offset)

    flag = pltpu.get_barrier_semaphore()
    pl.semaphore_signal(flag, inc=1, device_id=net.sibling(), device_id_type=MESH)
    for other in net.others():
        pl.semaphore_signal(flag, inc=1, device_id=net.peer(other), device_id_type=MESH)

    def each_dp(body):
        @pl.loop(1, dp_count)
        def _(j):
            body(lax.rem(dp + j, dp_count))

    each_dp(
        lambda target: pl.semaphore_signal(
            flag, inc=1, device_id={"dp": target}, device_id_type=MESH
        )
    )
    loads = [
        pltpu.make_async_copy(weights_hbm.at[k], weights.at[k], weight_sem.at[k])
        for k in (1, 2, 0)
    ]
    for copy in loads:
        copy.start()
    out_copies = [
        pltpu.make_async_copy(out_part.at[y * 2 + core], out_own.at[y], out_local.at[y])
        for y in range(chips)
    ]
    for copy in out_copies:
        copy.start()
    pl.semaphore_wait(flag, chips + dp_count - 1)

    def out_near_copy(y):
        return net.to_sibling(
            out_part.at[y * 2 + 1 - core],
            out_near.at[y],
            out_near_sem.at[0, y],
            out_near_sem.at[1, y],
        )

    def out_far_copy(other, source):
        return net.to_peer(
            other,
            out_own.at[other],
            out_far.at[lax.rem(source - chip + chips - 1, chips)]
            if source is not chip
            else out_far.at[lax.rem(chip - other + chips - 1, chips)],
            out_far_send.at[other],
            out_far_recv.at[source],
        )

    for y in range(chips):
        out_near_copy(y).start()

    def put(k, c, y, values):
        part[k, c, y] = values[:, :half_columns].astype(BF16)
        part[k + 1, c, y] = values[:, half_columns:].astype(BF16)

    token_total = token_rows.shape[0]
    dp_step = max(1, 256 // entry_count)

    @pl.loop(0, dp_count // dp_step)
    def _(block):
        row = lax.broadcasted_iota(jnp.int32, (dp_step * entry_count, token_total), 0)
        owner = block * dp_step + row // entry_count
        number = (owner * group + me) * entry_count + lax.rem(row, entry_count)
        chosen = jnp.where(number == token_row[...], 1.0, 0.0).astype(BF16)
        sums = dot_nn(chosen, token_rows[...]).astype(BF16)
        for j in range(dp_step):
            entry_part[block * dp_step + j] = sums[j * entry_count : (j + 1) * entry_count]

    def entry_copy(target, slot):
        return pltpu.make_async_remote_copy(
            src_ref=entry_part.at[target],
            dst_ref=entry_land.at[slot],
            send_sem=entry_send.at[target],
            recv_sem=entry_recv.at[slot],
            device_id={"dp": target},
            device_id_type=MESH,
        )

    each_dp(lambda target: entry_copy(target, dp).start())
    pooled_t = pooled_own[...].T

    def proj_shard(c, y, span):
        put(0, c, y, dot_nn(pooled_t, embed_rows[:, span]))

    each_shard(chips, columns, proj_shard)
    total_sum.start(0)
    total_sum.start(1)
    bias_sums = jnp.sum(embed_rows[...].astype(F32), axis=0, keepdims=True)
    for j in range(4):
        small_part[4 + j : 5 + j, :] = bias_sums[:, j * width : (j + 1) * width]
    loads[0].wait()
    run(0)

    pool = pool_matrix(counts_col[...], entry_count, rows).astype(BF16)
    spread = spread_matrix(counts_row[...], entry_count, rows)
    valid = jnp.sum(spread, axis=1, keepdims=True)
    spread = spread.astype(BF16)
    for b in range(blocks):
        bias[b] = slot_bias(valid[b * ROW_BLOCK : (b + 1) * ROW_BLOCK], slots)
    ffn_t[...] = ffn_in[...].T

    def hidden_shard(c, y, span):
        act, slope = gelu_parts(dot_nn(ffn_in[...], weights[1, c, y]))
        slopes[:, span] = slope.astype(BF16)
        hidden[:, span] = dot_nn(pool, act.astype(BF16)).astype(BF16)

    each_shard(chips, columns, hidden_shard)
    run(1)
    each_dp(lambda source: entry_copy(source, source).wait_recv())
    pooled_grad = entry_part[dp].astype(F32)
    for j in range(1, dp_count):
        pooled_grad = pooled_grad + entry_land[lax.rem(dp + j, dp_count)].astype(F32)
    entry_low = (pooled_grad / counts_col[...]).astype(BF16)
    out_rows = dot_nn(spread, entry_low)
    entry_t = entry_low.T
    loads[1].wait()
    out_low = out_rows.astype(BF16)
    row_total[...] = jnp.zeros_like(row_total)

    def unit_shard(c, y, span):
        put(2, c, y, dot_nn(entry_t, hidden[:, span]))
        act_grad = dot_nn(out_low, weights[2, c, y])
        pre_grad = (act_grad * slopes[:, span].astype(F32)).astype(BF16)
        put(4, c, y, dot_nn(ffn_t[...], pre_grad))
        row_total[...] += dot_nt(pre_grad, weights[1, c, y])

    each_shard(chips, columns, unit_shard)
    for k in (2, 3, 4, 5):
        total_sum.start(k)
    run(2)
    back, gain_grad, shift_grad = norm_back(residual[...], row_total[...], gain_two[...])
    small_part[2:3, :] = gain_grad
    small_part[3:4, :] = shift_grad
    residual_grad = out_rows + back
    pieces_grad[...] = residual_grad
    attn_grad = residual_grad.astype(BF16)
    loads[2].wait()
    for m, c, y in shards_of(chips):
        span = slice(m * head_columns, (m + 1) * head_columns)
        d_out_n[:, span] = dot_nn(attn_grad, weights[0, c, y, :, 3 * head_columns :]).astype(BF16)
    out_grad = dot_nn(attn_grad.T, attended[...])
    for m, c, y in shards_of(chips):
        span = slice(m * head_columns, (m + 1) * head_columns)
        part[7, c, y, :, head_columns:] = out_grad[:, span].astype(BF16)
    for b in range(blocks):
        block_rows = slice(b * ROW_BLOCK, (b + 1) * ROW_BLOCK)
        q_t[b] = q_n[block_rows, :].T
        k_t[b] = k_n[block_rows, :].T
        out_t[b] = attended[block_rows, :].T
        d_out_t[b] = d_out_n[block_rows, :].T
    run(3)

    for ref in (query_wide, grad_wide):
        ref[...] = jnp.zeros_like(ref)

    @pl.loop(0, blocks)
    def _(b):
        block_rows = pl.ds(pl.multiple_of(b * ROW_BLOCK, ROW_BLOCK), ROW_BLOCK)
        fill_diagonal(query_wide, q_t[b], heads)
        fill_diagonal(grad_wide, d_out_t[b], heads)
        scores = dot_nn(k_n[block_rows, :], query_wide[...]) + tiled(bias[b], heads)
        probs = jnp.exp(scores - logs[b])
        d_value[block_rows, :] = dot_nt(probs.astype(BF16), grad_wide[...]).astype(BF16)
        moved = d_out_t[b].astype(F32) * out_t[b].astype(F32)
        centre = jnp.concatenate(
            [
                jnp.sum(moved[h * HD : (h + 1) * HD], axis=0, keepdims=True)
                for h in range(heads)
            ],
            axis=1,
        )
        score_grad = (probs * (dot_nn(v_n[block_rows, :], grad_wide[...]) - centre)).astype(BF16)
        d_key[block_rows, :] = dot_nt(score_grad, query_wide[...]).astype(BF16)
        for pair in range(heads // 2):
            span = slice(pair * 2 * HD, (pair + 1) * 2 * HD)
            lanes = slice(pair * 2 * ROW_BLOCK, (pair + 1) * 2 * ROW_BLOCK)
            both = dot_nn(k_t[b, span, :], score_grad[:, lanes]) * (HD**-0.5)
            d_query_t[b, span, :] = pair_blocks(both).astype(BF16)

    for b in range(blocks):
        d_query[b * ROW_BLOCK : (b + 1) * ROW_BLOCK, :] = d_query_t[b].T
    run(4)
    rows_t = attn_in[...].T
    for place, (k, lanes, source) in enumerate(
        ((6, 0, d_query), (6, 1, d_key), (7, 0, d_value))
    ):
        grads = dot_nn(rows_t, source[...])
        for m, c, y in shards_of(chips):
            span = slice(m * head_columns, (m + 1) * head_columns)
            part[k, c, y, :, lanes * head_columns : (lanes + 1) * head_columns] = grads[
                :, span
            ].astype(BF16)
    total_sum.start(6)
    total_sum.start(7)
    normed = jnp.zeros((rows, width), F32)
    for m, c, y in shards_of(chips):
        span = slice(m * head_columns, (m + 1) * head_columns)
        for j, source in enumerate((d_query, d_key, d_value)):
            normed = normed + dot_nt(
                source[:, span], weights[0, c, y, :, j * head_columns : (j + 1) * head_columns]
            )
    back, gain_grad, shift_grad = norm_back(pieces[...].astype(F32), normed, gain_one[...])
    small_part[0:1, :] = gain_grad
    small_part[1:2, :] = shift_grad
    pieces_grad[...] += back

    def out_middle():
        for y in range(chips):
            out_copies[y].wait()
            out_near_copy(y).wait_recv()
        for other in net.others():
            out_own[other] = (
                out_own[other].astype(F32) + out_near[other].astype(F32)
            ).astype(BF16)
            out_far_copy(other, chip).start()

    def out_finish():
        text_out[...] = out_own[chip].astype(F32) + out_near[chip].astype(F32)
        for other in net.others():
            out_far_copy(other, other).wait_recv()
            slot = lax.rem(other - chip + chips - 1, chips)
            text_out[...] += out_far[slot].astype(F32)

    small_copy = net.to_sibling(small_part, small_near, small_sem.at[0], small_sem.at[1])
    small_copy.start()

    def small_far_copy(other, owner):
        return net.to_peer(
            other,
            small_far.at[owner],
            small_far.at[owner],
            small_far_send.at[other],
            small_far_recv.at[owner],
        )

    def small_dp_copy(other, owner):
        return pltpu.make_async_remote_copy(
            src_ref=small_dp.at[owner],
            dst_ref=small_dp.at[owner],
            send_sem=small_dp_send.at[other],
            recv_sem=small_dp_recv.at[owner],
            device_id={"dp": other},
            device_id_type=MESH,
        )

    def small_near_done():
        small_copy.wait_recv()
        small_far[chip] = small_part[...] + small_near[...]
        for other in net.others():
            small_far_copy(other, chip).start()

    def small_far_done():
        for other in net.others():
            small_far_copy(other, other).wait_recv()
        total = small_far[0]
        for j in range(1, chips):
            total = total + small_far[j]
        small_dp[dp] = total
        each_dp(lambda other: small_dp_copy(other, dp).start())

    @pl.loop(5, PARTS + 5)
    def _(step):
        for offset, stage in enumerate(stages):
            k = step - offset

            @pl.when((k >= 0) & (k < PARTS))
            def _():
                stage(k)

        pl.when(step == 5)(small_near_done)
        pl.when(step == 7)(small_far_done)
        pl.when(step == PARTS)(out_middle)

    out_finish()
    each_dp(lambda other: small_dp_copy(other, other).wait_recv())
    total = small_dp[0]
    for j in range(1, dp_count):
        total = total + small_dp[j]
    small_total[...] = total

    for y in range(chips):
        out_near_copy(y).wait_send()
    for other in net.others():
        out_far_copy(other, chip).wait_send()
    small_copy.wait_send()
    for other in net.others():
        small_far_copy(other, chip).wait_send()
    each_dp(lambda other: small_dp_copy(other, dp).wait_send())
    each_dp(lambda other: entry_copy(other, dp).wait_send())

    @pl.loop(0, PARTS)
    def _(k):
        total_sum.sent(k)


def hyper_backward(
    group,
    dp_count,
    embed_rows,
    pooled_own,
    token_rows,
    token_row,
    pieces,
    counts_col,
    counts_row,
    gain_one,
    gain_two,
    saved,
    weights,
    out_part,
):
    chips = group // 2
    rows, width = pieces.shape
    entry_count = counts_col.shape[0]
    kinds, columns = weights.shape[0], weights.shape[4]
    half_columns = columns // 2
    heads = width // HD
    blocks = rows // ROW_BLOCK
    spots = dp_count // 2
    vmem = pl.BlockSpec(memory_space=pltpu.VMEM)
    hbm = pl.BlockSpec(memory_space=pl.ANY)
    dma = pltpu.SemaphoreType.DMA
    final = (PARTS, 2, spots, width // (2 * spots), half_columns)
    units = columns * group

    def low(*shape):
        return pltpu.VMEM(shape, BF16)

    def wide(*shape):
        return pltpu.VMEM(shape, F32)

    return pl.pallas_call(
        partial(back_body, chips, dp_count),
        out_shape=(
            jax.ShapeDtypeStruct((rows, width), F32),
            jax.ShapeDtypeStruct(final, BF16),
            jax.ShapeDtypeStruct((8, width), F32),
            jax.ShapeDtypeStruct(out_part.shape[1:], F32),
        ),
        in_specs=[vmem] * 17 + [hbm] * 2,
        out_specs=(vmem,) * 4,
        scratch_shapes=[
            low(kinds, 2, chips, width, columns),
            low(PARTS, 2, chips, width, half_columns),
            low(PARTS, chips, width, half_columns),
            low(PARTS, chips - 1, width, half_columns),
            low(*final),
            low(PARTS, spots, width // (2 * spots), half_columns),
            low(PARTS, spots, width // (2 * spots), half_columns),
            low(dp_count, entry_count, width),
            low(dp_count, entry_count, width),
            low(entry_count, units),
            low(rows, units),
            low(width, rows),
            wide(rows, width),
            low(rows, width),
            low(rows, width),
            low(rows, width),
            low(rows, width),
        ]
        + [low(blocks, width, ROW_BLOCK)] * 5
        + [
            wide(blocks, ROW_BLOCK, ROW_BLOCK),
            low(width, heads * ROW_BLOCK),
            low(width, heads * ROW_BLOCK),
            wide(8, width),
            wide(chips, 8, width),
            wide(dp_count, 8, width),
            wide(8, width),
            low(chips, *out_part.shape[1:]),
            low(chips, *out_part.shape[1:]),
            low(chips - 1, *out_part.shape[1:]),
            dma((kinds,)),
            dma((chips,)),
            dma((2, chips)),
            dma((chips,)),
            dma((chips,)),
            dma((dp_count,)),
            dma((dp_count,)),
            dma((2, PARTS)),
            dma((PARTS, chips)),
            dma((PARTS, chips)),
            dma((2, PARTS)),
            dma((PARTS, spots)),
            dma((PARTS, spots)),
            dma((PARTS, spots)),
            dma((PARTS, spots)),
            dma((2, PARTS)),
            dma((2,)),
            dma((chips,)),
            dma((chips,)),
            dma((dp_count,)),
            dma((dp_count,)),
        ],
        compiler_params=pltpu.CompilerParams(
            collective_id=2, has_side_effects=True, vmem_limit_bytes=62 * 1024 * 1024
        ),
        cost_estimate=pl.CostEstimate(
            flops=60 * 10**9, bytes_accessed=20 * 10**6, transcendentals=5 * 10**6
        ),
    )(
        embed_rows,
        pooled_own,
        token_rows,
        token_row,
        pieces,
        counts_col,
        counts_row,
        gain_one,
        gain_two,
        *saved,
        weights,
        out_part,
    )


def spread_body(sums, query, key, value, out, up, down, proj):
    half_columns = sums.shape[2]
    head_columns = query.shape[1]
    for first, target in ((0, proj), (2, down), (4, up)):
        target[:, :half_columns] = sums[first].astype(F32)
        target[:, half_columns:] = sums[first + 1].astype(F32)
    for k, lanes, target in ((6, 0, query), (6, 1, key), (7, 0, value), (7, 1, out)):
        target[...] = sums[k, :, lanes * head_columns : (lanes + 1) * head_columns].astype(F32)


def spread_sums(sums):
    _, width, half_columns = sums.shape
    small = jax.ShapeDtypeStruct((width, half_columns // 2), F32)
    large = jax.ShapeDtypeStruct((width, half_columns * 2), F32)
    vmem = pl.BlockSpec(memory_space=pltpu.VMEM)
    return pl.pallas_call(
        spread_body,
        out_shape=(small,) * 4 + (large,) * 3,
        in_specs=[vmem],
        out_specs=(vmem,) * 7,
        compiler_params=pltpu.CompilerParams(vmem_limit_bytes=40 * 1024 * 1024),
    )(sums)


def on_device(
    pieces,
    counts,
    entry_ids,
    segment_ids,
    norm1_gain,
    norm1_shift,
    query_weight,
    key_weight,
    value_weight,
    out_weight,
    norm2_gain,
    norm2_shift,
    up_weight,
    down_weight,
    proj_weight,
    proj_bias,
    text_norm1_gain,
    text_query,
    text_key,
    text_value,
    text_out_proj,
    text_norm2_gain,
    text_gate,
    text_up,
    text_down,
    token_grad,
):
    group, dp_count = lax.axis_size("mp"), lax.axis_size("dp")
    me = lax.axis_index("mp")
    entry_count, slot_count, width = pieces.shape
    text_width = token_grad.shape[1]
    length = segment_ids.shape[1]
    chunk_rows = length // CHUNKS
    pieces_rows = pieces.reshape(entry_count * slot_count, width)
    entries, weights, *saved, counts_col, counts_row, bias_full = hyper_forward(
        group,
        dp_count,
        pieces_rows,
        counts[None, :],
        norm1_gain[None, :],
        norm1_shift[None, :],
        norm2_gain[None, :],
        norm2_shift[None, :],
        (query_weight, key_weight, value_weight, out_weight),
        proj_bias[None, :],
        (up_weight, down_weight, proj_weight),
    )
    head_width = text_query.shape[1]
    kv_index = me * (head_width // FHD) // (QHEADS // KVHEADS)
    key_local = lax.dynamic_slice_in_dim(text_key, kv_index * FHD, FHD, 1)
    value_local = lax.dynamic_slice_in_dim(text_value, kv_index * FHD, FHD, 1)
    key_value = jnp.concatenate([key_local, value_local], axis=1)
    cos_t, sin_t = rope_tables(length)
    out_part, embed_rows, pooled_own, token_rows = text_layer(
        group,
        dp_count,
        entry_count,
        entry_ids.reshape(CHUNKS, 1, chunk_rows),
        segment_ids.reshape(CHUNKS, 1, chunk_rows),
        cos_t,
        sin_t,
        bias_full,
        text_norm1_gain[None, :],
        text_norm2_gain[None, :],
        key_value,
        entries.reshape(-1, width),
        weights,
        token_grad,
        text_query,
        text_out_proj,
        text_gate,
        text_up,
        text_down,
    )
    pieces_grad, final, small, text_out = hyper_backward(
        group,
        dp_count,
        embed_rows.reshape(-1, text_width),
        pooled_own.reshape(-1, width),
        token_rows.reshape(length, width),
        entry_ids[None, :],
        pieces_rows,
        counts_col,
        counts_row,
        norm1_gain[None, :],
        norm2_gain[None, :],
        saved,
        weights,
        out_part.reshape(group, -1, text_width),
    )
    query_grad, key_grad, value_grad, out_grad, up_grad, down_grad, proj_grad = spread_sums(
        final.reshape(PARTS, width, -1)
    )
    bias_share = proj_bias.shape[0]
    proj_bias_grad = lax.dynamic_slice_in_dim(
        small[4:].reshape(-1), me * bias_share, bias_share
    )
    return (
        text_out,
        pieces_grad.reshape(pieces.shape),
        small[0],
        small[1],
        query_grad,
        key_grad,
        value_grad,
        out_grad,
        small[2],
        small[3],
        up_grad,
        down_grad,
        proj_grad,
        proj_bias_grad,
    )


def solution(mesh):
    return jax.shard_map(
        on_device,
        mesh=mesh,
        in_specs=(
            P(("dp", "mp"), None, None),
            P("dp"),
            P("dp"),
            P("dp", None),
            P(),
            P(),
            P(None, "mp"),
            P(None, "mp"),
            P(None, "mp"),
            P(None, "mp"),
            P(),
            P(),
            P(None, "mp"),
            P(None, "mp"),
            P(None, "mp"),
            P("mp"),
            P(),
            P(None, "mp"),
            P(),
            P(),
            P(None, "mp"),
            P(),
            P(None, "mp"),
            P(None, "mp"),
            P(None, "mp"),
            P(("dp", "mp"), None),
        ),
        out_specs=(
            P(("dp", "mp"), None),
            P(("dp", "mp"), None, None),
            P(),
            P(),
            P(None, "mp"),
            P(None, "mp"),
            P(None, "mp"),
            P(None, "mp"),
            P(),
            P(),
            P(None, "mp"),
            P(None, "mp"),
            P(None, "mp"),
            P("mp"),
        ),
        check_vma=False,
    )
```

```python
from functools import partial
import math

import jax
import jax.numpy as jnp
import numpy as np
from jax import lax
from jax.experimental import pallas as pl
from jax.experimental.pallas import tpu as pltpu
from jax.sharding import PartitionSpec as P

HD = 64
QHEADS = 32
KVHEADS = 4
FHD = 64


def rope_tables(length):
    positions = np.arange(length, dtype=np.float32)
    rates = np.exp(
        np.arange(FHD // 2, dtype=np.float32) * np.float32(-2.0 * math.log(10000.0) / FHD)
    ).astype(np.float32)
    angles = (positions[None, :] * rates[:, None]).reshape(FHD // 2, CHUNKS, length // CHUNKS)
    angles = angles.transpose(1, 0, 2)
    return jnp.asarray(np.cos(angles)), jnp.asarray(np.sin(angles))


MESH = pl.DeviceIdType.MESH
F32 = jnp.float32
BF16 = jnp.bfloat16
CHUNKS = 4
FAR = -1e30


def dot_nn(a, b):
    return lax.dot_general(a, b, (((1,), (0,)), ((), ())), preferred_element_type=F32)


def dot_nt(a, b):
    return lax.dot_general(a, b, (((1,), (1,)), ((), ())), preferred_element_type=F32)


def column_tiles(total, width, body):
    full = total // width
    if full > 0:

        @pl.loop(0, full)
        def _(t):
            body(pl.ds(pl.multiple_of(t * width, width), width))

    if total % width:
        body(pl.ds(full * width, total % width))


def rms_scale(values):
    return lax.rsqrt(jnp.mean(values * values, axis=-1, keepdims=True) + 1e-05)


def rms_back(values, grad, gain):
    scale = rms_scale(values)
    scaled = grad * gain
    return scale * (
        scaled - values * (scale * scale) * jnp.mean(scaled * values, axis=-1, keepdims=True)
    )


def piece_indices(shape, row_pieces):
    places = [()]
    for size in shape[:-2]:
        places = [place + (j,) for place in places for j in range(size)]
    rows = shape[-2]
    if rows % (16 * row_pieces):
        return places
    step = rows // row_pieces
    return [place + (pl.ds(j * step, step),) for place in places for j in range(row_pieces)]


class Pieces:
    def __init__(self, source, target, send, recv, device, row_pieces=2):
        self.parts = (source, target, send, recv, device)
        self.row_pieces = row_pieces

    def copy(self, source, target):
        _, _, send, recv, device = self.parts
        return pltpu.make_async_remote_copy(
            src_ref=source,
            dst_ref=target,
            send_sem=send,
            recv_sem=recv,
            device_id=device,
            device_id_type=MESH,
        )

    def start(self):
        source, target = self.parts[:2]
        for place in piece_indices(source.shape, self.row_pieces):
            if place:
                self.copy(source.at[place], target.at[place]).start()
            else:
                self.copy(source, target).start()

    def wait_send(self):
        self.copy(*self.parts[:2]).wait_send()

    def wait_recv(self):
        self.copy(*self.parts[:2]).wait_recv()


class Exchange:
    def __init__(self, chips, chip, core, group_axis):
        self.chips, self.chip, self.core = chips, chip, core
        self.axis = group_axis

    def sibling(self):
        return {self.axis: self.chip * 2 + 1 - self.core}

    def peer(self, other):
        return {self.axis: other * 2 + self.core}

    def others(self):
        return [lax.rem(self.chip + step, self.chips) for step in range(1, self.chips)]

    def barrier(self):
        flag = pltpu.get_barrier_semaphore()
        pl.semaphore_signal(flag, inc=1, device_id=self.sibling(), device_id_type=MESH)
        for other in self.others():
            pl.semaphore_signal(flag, inc=1, device_id=self.peer(other), device_id_type=MESH)
        pl.semaphore_wait(flag, self.chips)

    def to_sibling(self, source, target, send, recv):
        return Pieces(source, target, send, recv, self.sibling())

    def to_peer(self, other, source, target, send, recv):
        return Pieces(source, target, send, recv, self.peer(other))


class Scatter:
    def __init__(self, net, part, near, far, sems):
        self.net, self.part, self.near, self.far = net, part, near, far
        self.slots = None if part.shape[0] == near.shape[0] else part.shape[0]
        self.near_send, self.near_recv, self.far_send, self.far_recv = sems

    def slot(self, i):
        return i if self.slots is None else i % self.slots

    def landing(self, source, target):
        return lax.rem(source - target + self.net.chips - 1, self.net.chips)

    def near_copy(self, i):
        net = self.net
        return net.to_sibling(
            self.part.at[self.slot(i), 1 - net.core],
            self.near.at[i],
            self.near_send.at[i],
            self.near_recv.at[i],
        )

    def far_copy(self, i, other):
        net = self.net
        return net.to_peer(
            other,
            self.part.at[self.slot(i), net.core, other],
            self.far.at[i, self.landing(net.chip, other)],
            self.far_send.at[i, other],
            self.far_recv.at[i, net.chip],
        )

    def far_landing(self, i, other):
        net = self.net
        return net.to_peer(
            other,
            self.part.at[self.slot(i), net.core, other],
            self.far.at[i, self.landing(other, net.chip)],
            self.far_send.at[i, other],
            self.far_recv.at[i, other],
        )

    def start(self, i):
        self.near_copy(i).start()

    def middle(self, i):
        net = self.net
        self.near_copy(i).wait_recv()
        slot = self.slot(i)
        for other in net.others():
            total = self.part[slot, net.core, other].astype(F32) + self.near[
                i, other
            ].astype(F32)
            self.part[slot, net.core, other] = total.astype(BF16)
            self.far_copy(i, other).start()

    def finish(self, i):
        net = self.net
        slot = self.slot(i)
        total = self.part[slot, net.core, net.chip].astype(F32) + self.near[
            i, net.chip
        ].astype(F32)
        for other in net.others():
            self.far_landing(i, other).wait_recv()
            total = total + self.far[i, self.landing(other, net.chip)].astype(F32)
        return total

    def sent(self, i):
        self.near_copy(i).wait_send()
        for other in self.net.others():
            self.far_copy(i, other).wait_send()


class Gather:
    def __init__(self, net, full, sems, single=False):
        self.net, self.full, self.single = net, full, single
        self.far_send, self.far_recv, self.near_send, self.near_recv = sems

    def block(self, i, *place):
        return self.full.at[place] if self.single else self.full.at[(i, *place)]

    def far_copy(self, i, other):
        net = self.net
        block = self.block(i, net.core, net.chip)
        return net.to_peer(
            other, block, block, self.far_send.at[i, other], self.far_recv.at[i, net.chip]
        )

    def far_landing(self, i, other):
        net = self.net
        block = self.block(i, net.core, other)
        return net.to_peer(
            other, block, block, self.far_send.at[i, other], self.far_recv.at[i, other]
        )

    def near_copy(self, i):
        block = self.block(i, self.net.core)
        return self.net.to_sibling(block, block, self.near_send.at[i], self.near_recv.at[i])

    def near_landing(self, i):
        block = self.block(i, 1 - self.net.core)
        return self.net.to_sibling(block, block, self.near_send.at[i], self.near_recv.at[i])

    def start(self, i):
        for other in self.net.others():
            self.far_copy(i, other).start()

    def middle(self, i):
        for other in self.net.others():
            self.far_landing(i, other).wait_recv()
        self.near_copy(i).start()

    def finish(self, i):
        self.near_landing(i).wait_recv()

    def sent(self, i):
        for other in self.net.others():
            self.far_copy(i, other).wait_send()
        self.near_copy(i).wait_send()


STEPS = (
    ("attend", 0),
    ("attn_part", 0),
    ("attend", 2),
    ("attn_far", 0),
    ("attend", 1),
    ("attn_part", 2),
    ("norm", 0),
    ("attn_part", 1),
    ("attend", 3),
    ("attn_far", 1),
    ("attn_far", 2),
    ("attn_part", 3),
    ("rows_near", 0),
    ("units_low", 0),
    ("norm", 1),
    ("units_high", 0),
    ("unit_grads", 0),
    ("norm", 2),
    ("rows_near", 1),
    ("outputs", 0),
    ("attn_far", 3),
    ("units_far", 0),
    ("units_low", 1),
    ("units_high", 1),
    ("rows_near", 2),
    ("unit_grads", 1),
    ("norm", 3),
    ("outputs", 1),
    ("units_far", 1),
    ("residual", 0),
    ("units_low", 2),
    ("units_high", 2),
    ("rows_near", 3),
    ("unit_grads", 2),
    ("residual", 1),
    ("outputs", 2),
    ("units_low", 3),
    ("units_far", 2),
    ("back_near", 0),
    ("units_high", 3),
    ("back_near", 1),
    ("unit_grads", 3),
    ("residual", 2),
    ("attend_back", 0),
    ("units_far", 3),
    ("back_near", 2),
    ("normed_part", 0),
    ("attend_back", 1),
    ("residual", 3),
    ("normed_part", 1),
    ("normed_far", 0),
    ("attend_back", 2),
    ("normed_far", 1),
    ("back_near", 3),
    ("normed_part", 2),
    ("attend_back", 3),
    ("normed_far", 2),
    ("normed_part", 3),
    ("embed_grad", 0),
    ("outputs", 3),
    ("normed_far", 3),
    ("embed_grad", 1),
    ("token_near", 0),
    ("embed_grad", 2),
    ("token_near", 1),
    ("embed_grad", 3),
    ("token_near", 2),
    ("token_near", 3),
)


def column_of(row):
    return jnp.broadcast_to(row, (8, row.shape[1])).T[:, :1]


def text_body(
    chips,
    dp_count,
    entry_count,
    head_count,
    entry_ids,
    segments,
    cos_t,
    sin_t,
    bias_full,
    gain_one,
    gain_two,
    w_kv,
    entries_hbm,
    weights_hbm,
    token_grad,
    w_query_hbm,
    w_out_hbm,
    w_gate_hbm,
    w_up_hbm,
    w_down_hbm,
    out_part,
    embed_grad,
    pooled_own,
    token_full,
    proj,
    w_query,
    w_out,
    w_gate,
    w_up,
    w_down,
    part_a,
    near_a,
    far_a,
    part_b,
    near_b,
    far_b,
    full,
    grad_full,
    embeds_own,
    q_t,
    q_n,
    k_n,
    v_n,
    k_t,
    v_t,
    out_t,
    logs,
    bias,
    residual,
    weight_sem,
    local_sem,
    stage_sem,
    scatter_near,
    scatter_far_send,
    scatter_far_recv,
    gather_near,
    gather_far_send,
    gather_far_recv,
    grad_near,
    grad_far_send,
    grad_far_recv,
):
    me = lax.axis_index("mp")
    chip, core = me // 2, lax.rem(me, 2)
    net = Exchange(chips, chip, core, "mp")
    group = chips * 2
    chunk_rows = q_n.shape[1]
    width = embeds_own.shape[2]
    units = w_gate.shape[1]
    own_rows = embeds_own.shape[1]
    head_width = FHD * head_count
    columns = proj.shape[3]
    entry_total, entry_width = entries_hbm.shape
    owned = token_grad.shape[0]
    first_own = pl.multiple_of((core * chips + chip) * own_rows, own_rows)
    owners = group // CHUNKS if group > CHUNKS else 1

    def scatter_of(kind, part, near, far):
        return Scatter(
            net,
            part,
            near,
            far,
            (
                scatter_near.at[kind, 0],
                scatter_near.at[kind, 1],
                scatter_far_send.at[kind],
                scatter_far_recv.at[kind],
            ),
        )

    def gather_of(kind, ref):
        return Gather(
            net,
            ref,
            (
                gather_far_send.at[kind],
                gather_far_recv.at[kind],
                gather_near.at[kind, 0],
                gather_near.at[kind, 1],
            ),
        )

    attn_sum = scatter_of(0, part_a, near_a, far_a)
    mlp_sum = scatter_of(1, part_b, near_b, far_b)
    normed_sum = scatter_of(2, part_a, near_a, far_a)
    mlp_rows = gather_of(0, full)
    back_rows = gather_of(1, full)
    token_rows = gather_of(2, token_full)

    def load(k, source, target):
        return pltpu.make_async_copy(source, target, weight_sem.at[k])

    load_proj = load(1, weights_hbm.at[3], proj)
    load_query = load(2, w_query_hbm, w_query)
    load_out = load(3, w_out_hbm, w_out)
    load_units = [
        load(4, w_gate_hbm, w_gate),
        load(5, w_up_hbm, w_up),
        load(6, w_down_hbm, w_down),
    ]

    def grad_far(owner_chip, other):
        return net.to_peer(
            other,
            token_grad,
            grad_full.at[owner_chip * 2 + core],
            grad_far_send.at[other],
            grad_far_recv.at[owner_chip],
        )

    def grad_near_copy(owner_chip, owner_core):
        block = grad_full.at[owner_chip * 2 + owner_core]
        return net.to_sibling(
            block, block, grad_near.at[0, owner_chip], grad_near.at[1, owner_chip]
        )

    grad_local = pltpu.make_async_copy(token_grad, grad_full.at[me], local_sem)

    def grad_start():
        for other in net.others():
            grad_far(chip, other).start()

    def grad_middle():
        grad_local.wait()
        grad_near_copy(chip, core).start()
        for other in net.others():
            grad_far(other, other).wait_recv()
            grad_near_copy(other, core).start()

    def grad_chunk(i):
        return grad_full[i * owners : (i + 1) * owners].reshape(chunk_rows, width)

    def grad_finish(i):
        for owner in range(i * owners, (i + 1) * owners):

            @pl.when(core != owner % 2)
            def _():
                grad_near_copy(owner // 2, owner % 2).wait_recv()

    def embed(entries, pooled, embeds):
        load_entries = load(0, entries_hbm, entries)
        load_entries.start()
        for copy in (load_proj, load_query, load_out, *load_units):
            copy.start()
        grad_local.start()
        net.barrier()
        pl.when(core == 1)(grad_start)
        load_entries.wait()
        load_proj.wait()
        load_query.wait()

        @pl.loop(0, CHUNKS)
        def _(i):
            ids = entry_ids[i]
            owner = ids // entry_count
            owner_mp, owner_dp = lax.rem(owner, group), owner // group
            place = (lax.rem(owner_mp, 2) * chips + owner_mp // 2) * dp_count + owner_dp
            spots = column_of(
                (place * entry_count + lax.rem(ids, entry_count)).astype(F32)
            ).astype(jnp.int32)
            numbers = lax.broadcasted_iota(jnp.int32, (chunk_rows, entry_total), 1)
            chosen = jnp.where(numbers == spots, 1.0, 0.0).astype(BF16)
            pooled[...] = dot_nn(chosen, entries[...]).astype(BF16)
            pooled_own[i] = pooled[pl.ds(first_own, own_rows), :]
            for m, c, y in shards_of(chips):
                span = slice(m * columns, (m + 1) * columns)
                embeds[:, span] = (dot_nn(pooled[...], proj[c, y]) + bias_full[c, y]).astype(BF16)
            embeds_own[i] = embeds[pl.ds(first_own, own_rows), :]
            values = embeds[...].astype(F32)
            embeds[...] = (values * rms_scale(values) * gain_one[...]).astype(BF16)
            cosine, sine = cos_t[i], sin_t[i]

            def turned(block):
                low_half, high_half = block[: FHD // 2], block[FHD // 2 :]
                return jnp.concatenate(
                    [low_half * cosine - high_half * sine, high_half * cosine + low_half * sine],
                    axis=0,
                )

            queries = dot_nn(embeds[...], w_query[...]).T
            for h in range(head_count):
                span = slice(h * FHD, (h + 1) * FHD)
                q_t[i, span, :] = (
                    turned(queries[span]).astype(BF16).astype(F32) * FHD**-0.5
                ).astype(BF16)
            q_n[i] = q_t[i].T
            both = dot_nn(embeds[...], w_kv[...])
            keys_t = turned(both.T[:FHD]).astype(BF16)
            k_t[i] = keys_t
            k_n[i] = keys_t.T
            v_n[i] = both[:, FHD:].astype(BF16)
            v_t[i] = both.T[FHD:].astype(BF16)

        pl.when(core == 0)(grad_start)
        pl.when(core == 1)(grad_middle)

    pl.run_scoped(
        embed,
        pltpu.VMEM((entry_total, entry_width), BF16),
        pltpu.VMEM((chunk_rows, entry_width), BF16),
        pltpu.VMEM((chunk_rows, width), BF16),
    )

    def put_rows(part, slot, columns, values):
        half = chunk_rows // 2
        for k in range(2):
            for j in range(chips):
                first = k * half + j * own_rows
                part[slot, k, j, :, columns] = values[first : first + own_rows]

    def rows_of(ref, i):
        return ref[i].reshape(chunk_rows, width)

    def turned_back(sums_t):
        return sums_t.astype(BF16).T

    def make_bias(i):
        query_spots = i * chunk_rows + lax.broadcasted_iota(jnp.int32, (chunk_rows, chunk_rows), 1)
        query_segments = segments[i].astype(F32)
        for kb in range(i + 1):
            allowed = column_of(segments[kb].astype(F32)) == query_segments
            if kb == i:
                key_spots = kb * chunk_rows + lax.broadcasted_iota(
                    jnp.int32, (chunk_rows, chunk_rows), 0
                )
                allowed = allowed & (key_spots <= query_spots)
            bias[kb] = jnp.where(allowed, 0.0, FAR)

    def head_span(h):
        return pl.ds(pl.multiple_of(h * FHD, FHD), FHD)

    def layer(
        mixed,
        gate_grad,
        up_grad,
        out_stage,
        d_out_t,
        d_out_n,
        d_query_t,
        value_total,
        key_total,
    ):
        for ref in (value_total, key_total):
            ref[...] = jnp.zeros_like(ref)

        def stage_copy(i, tile):
            slot = lax.rem(tile, 2)
            columns = pl.ds(pl.multiple_of(tile * 512, 512), 512)
            return pltpu.make_async_copy(
                out_stage.at[slot], out_part.at[i, :, columns], stage_sem.at[slot]
            )

        def pair_t(ref, pair):
            return jnp.concatenate(
                [ref[head_span(pair * 2), :], ref[head_span(pair * 2 + 1), :]], axis=1
            )

        def pair_bias(kb):
            return jnp.concatenate([bias[kb], bias[kb]], axis=1)

        def attend(i):
            make_bias(i)

            @pl.loop(0, head_count // 2)
            def _(pair):
                query = pair_t(q_t.at[i], pair)
                scores = [dot_nn(k_n[kb], query) + pair_bias(kb) for kb in range(i + 1)]
                top = jnp.max(scores[0], axis=0, keepdims=True)
                for block in scores[1:]:
                    top = jnp.maximum(top, jnp.max(block, axis=0, keepdims=True))
                total = jnp.zeros_like(top)
                attended = jnp.zeros((FHD, 2 * chunk_rows), F32)
                for kb in range(i + 1):
                    weights_block = jnp.exp(scores[kb] - top)
                    total = total + jnp.sum(weights_block, axis=0, keepdims=True)
                    attended = attended + dot_nn(v_t[kb], weights_block.astype(BF16))
                logs[i, pair] = top + jnp.log(total)
                attended = (attended / total).astype(BF16)
                out_t[i, head_span(pair * 2), :] = attended[:, :chunk_rows]
                out_t[i, head_span(pair * 2 + 1), :] = attended[:, chunk_rows:]

        def attn_part(i):
            if i == CHUNKS - 1:
                load_out.wait()

            def tile(columns):
                put_rows(part_a, i, columns, turned_back(dot_nn(w_out[columns, :], out_t[i])))

            column_tiles(width, 512, tile)
            attn_sum.start(i)

        def norm(i):
            values = embeds_own[i].astype(F32) + attn_sum.finish(i)
            residual[i] = values
            full[i, core, chip] = (values * rms_scale(values) * gain_two[...]).astype(BF16)
            mlp_rows.start(i)

        def unit_tile(i, columns):
            rows = rows_of(full, i)
            gate_pre = dot_nn(rows, w_gate[:, columns])
            up_pre = dot_nn(rows, w_up[:, columns])
            act_grad = dot_nn(grad_chunk(i), w_down[:, columns])
            inverse = 1.0 / (1.0 + jnp.exp(-gate_pre))
            silu = gate_pre * inverse
            mixed[columns, :] = turned_back(silu * up_pre)
            up_grad[columns, :] = turned_back(act_grad * silu)
            slope = inverse * (1.0 + gate_pre * (1.0 - inverse))
            gate_grad[columns, :] = turned_back(act_grad * up_pre * slope)

        tile_width = 512 if units >= 1024 else 256
        tiles = units // tile_width
        middle_tile = (tiles + 1) // 2

        def unit_tiles(i, first, last):
            @pl.loop(first, last)
            def _(t):
                unit_tile(i, pl.ds(pl.multiple_of(t * tile_width, tile_width), tile_width))

        def units_low(i):
            if i == CHUNKS - 1:
                pl.when(core == 0)(grad_middle)
                for copy in load_units:
                    copy.wait()
            grad_finish(i)
            mlp_rows.finish(i)
            unit_tiles(i, 0, middle_tile)

        def units_high(i):
            unit_tiles(i, middle_tile, tiles)
            if units % tile_width:
                unit_tile(i, pl.ds(tiles * tile_width, units % tile_width))
            mlp_rows.sent(i)

        def unit_grads(i):
            if i + 2 < CHUNKS:
                mlp_sum.sent(i + 2)

            def tile(columns):
                put_rows(
                    part_b,
                    i % 2,
                    columns,
                    turned_back(
                        dot_nn(w_gate[columns, :], gate_grad[...])
                        + dot_nn(w_up[columns, :], up_grad[...])
                    ),
                )

            column_tiles(width, 512, tile)
            mlp_sum.start(i)

        def outputs(i):
            @pl.loop(0, width // 512)
            def _(t):
                columns = pl.ds(pl.multiple_of(t * 512, 512), 512)
                slot = lax.rem(t, 2)
                tile = turned_back(dot_nn(w_down[columns, :], mixed[...]))
                if i == CHUNKS - 1:
                    pl.when(t >= 2)(lambda: stage_copy(i, t).wait())
                else:
                    stage_copy(i, t).wait()
                out_stage[slot] = tile
                own = pl.ds(first_own, own_rows)
                out_stage[slot, own, :] = (
                    out_stage[slot, own, :].astype(F32) + residual[i, :, columns]
                ).astype(BF16)
                stage_copy(i, t).start()

        def residual_back(i):
            grad = mlp_sum.finish(i)
            block = i * owners + first_own // owned
            start = pl.multiple_of(lax.rem(first_own, owned), own_rows)
            own_grad = grad_full[block, pl.ds(start, own_rows), :].astype(F32)
            values = own_grad + rms_back(residual[i], grad, gain_two[...])
            full[i, core, chip] = values.astype(BF16)
            back_rows.start(i)

        def attend_back(i):
            back_rows.finish(i)
            attended_grad = dot_nn(rows_of(full, i), w_out[...]).astype(BF16)
            d_out_n[...] = attended_grad
            d_out_t[...] = attended_grad.T
            make_bias(i)
            cosine, sine = cos_t[i], sin_t[i]

            first_head = (
                lax.broadcasted_iota(jnp.int32, (chunk_rows, 2 * FHD), 1) < FHD
            )

            def stacked(rows):
                wide = rows.astype(F32)
                return jnp.concatenate(
                    [jnp.where(first_head, wide, 0.0), jnp.where(first_head, 0.0, wide)], axis=0
                ).astype(BF16)

            @pl.loop(0, head_count // 2)
            def _(pair):
                pair_span = pl.ds(pl.multiple_of(pair * 2 * FHD, 2 * FHD), 2 * FHD)
                query_rows = stacked(q_n[i, :, pair_span])
                grad_rows = stacked(d_out_n[:, pair_span])
                query = pair_t(q_t.at[i], pair)
                grad = pair_t(d_out_t, pair)
                log_row = logs[i, pair]
                centre = jnp.sum(
                    grad.astype(F32) * pair_t(out_t.at[i], pair).astype(F32),
                    axis=0,
                    keepdims=True,
                )
                query_grad = jnp.zeros((FHD, 2 * chunk_rows), F32)
                for kb in range(i + 1):
                    probs = jnp.exp(dot_nn(k_n[kb], query) + pair_bias(kb) - log_row)
                    value_total[kb] += dot_nn(probs.astype(BF16), grad_rows)
                    score_grad = (probs * (dot_nn(v_n[kb], grad) - centre)).astype(BF16)
                    key_total[kb] += dot_nn(score_grad, query_rows)
                    query_grad = query_grad + dot_nn(k_t[kb], score_grad)
                query_grad = query_grad * (FHD**-0.5)
                for odd in range(2):
                    lanes = slice(odd * chunk_rows, (odd + 1) * chunk_rows)
                    low_half = query_grad[: FHD // 2, lanes]
                    high_half = query_grad[FHD // 2 :, lanes]
                    d_query_t[head_span(pair * 2 + odd), :] = jnp.concatenate(
                        [
                            low_half * cosine + high_half * sine,
                            high_half * cosine - low_half * sine,
                        ],
                        axis=0,
                    ).astype(BF16)

        def normed_part(i):
            attn_sum.sent(i)
            key_grad = (key_total[i][:, :FHD] + key_total[i][:, FHD:]).T
            cosine, sine = cos_t[i], sin_t[i]
            low_half, high_half = key_grad[: FHD // 2], key_grad[FHD // 2 :]
            value_grad = (value_total[i][:, :FHD] + value_total[i][:, FHD:]).T
            both = jnp.concatenate(
                [
                    low_half * cosine + high_half * sine,
                    high_half * cosine - low_half * sine,
                    value_grad,
                ],
                axis=0,
            )
            both = both.astype(BF16)

            def tile(columns):
                put_rows(
                    part_a,
                    i,
                    columns,
                    turned_back(
                        dot_nn(w_query[columns, :], d_query_t[...])
                        + dot_nn(w_kv[columns, :], both)
                    ),
                )

            column_tiles(width, 512, tile)
            normed_sum.start(i)

        def embed_back(i):
            grad = normed_sum.finish(i)
            kept = full[i, core, chip].astype(F32)
            values = kept + rms_back(embeds_own[i].astype(F32), grad, gain_one[...])
            embed_grad[i] = values.astype(BF16)
            total = jnp.zeros((own_rows, entry_width), F32)
            for m, c, y in shards_of(chips):
                total = total + dot_nt(
                    embed_grad[i, :, m * columns : (m + 1) * columns], proj[c, y]
                )
            token_full[i, core, chip] = total.astype(BF16)
            token_rows.start(i)

        stages = {
            "attend": attend,
            "attn_part": attn_part,
            "attn_far": attn_sum.middle,
            "norm": norm,
            "rows_near": mlp_rows.middle,
            "units_low": units_low,
            "units_high": units_high,
            "unit_grads": unit_grads,
            "outputs": outputs,
            "units_far": mlp_sum.middle,
            "residual": residual_back,
            "back_near": back_rows.middle,
            "attend_back": attend_back,
            "normed_part": normed_part,
            "normed_far": normed_sum.middle,
            "embed_grad": embed_back,
            "token_near": token_rows.middle,
        }
        for name, turn in STEPS:
            stages[name](CHUNKS - 1 - turn)

        for tile in range(2):
            stage_copy(0, tile).wait()

    lines = (units, chunk_rows)
    keys = (CHUNKS, chunk_rows, 2 * FHD)
    pl.run_scoped(
        layer,
        pltpu.VMEM(lines, BF16),
        pltpu.VMEM(lines, BF16),
        pltpu.VMEM(lines, BF16),
        pltpu.VMEM((2, chunk_rows, 512), BF16),
        pltpu.VMEM((head_width, chunk_rows), BF16),
        pltpu.VMEM((chunk_rows, head_width), BF16),
        pltpu.VMEM((head_width, chunk_rows), BF16),
        pltpu.VMEM(keys, F32),
        pltpu.VMEM(keys, F32),
    )

    @pl.loop(0, CHUNKS)
    def _(i):
        token_rows.finish(i)
        token_rows.sent(i)
        normed_sum.sent(i)
        back_rows.sent(i)

    for i in range(2):
        mlp_sum.sent(i)
    for other in net.others():
        grad_far(chip, other).wait_send()
    for owner_chip in range(chips):
        grad_near_copy(owner_chip, core).wait_send()


def text_layer(
    group,
    dp_count,
    entry_count,
    entry_ids,
    segments,
    cos_t,
    sin_t,
    bias_full,
    gain_one,
    gain_two,
    w_kv,
    entries,
    weights,
    token_grad,
    w_query,
    w_out,
    w_gate,
    w_up,
    w_down,
):
    chips = group // 2
    chunks, _, chunk_rows = entry_ids.shape
    own_rows = chunk_rows // group
    owned, width = token_grad.shape
    head_width = w_query.shape[1]
    head_count = head_width // FHD
    entry_width = entries.shape[1]
    vmem = pl.BlockSpec(memory_space=pltpu.VMEM)
    hbm = pl.BlockSpec(memory_space=pl.ANY)
    dma = pltpu.SemaphoreType.DMA

    def low(*shape):
        return pltpu.VMEM(shape, BF16)

    return pl.pallas_call(
        partial(text_body, chips, dp_count, entry_count, head_count),
        out_shape=(
            jax.ShapeDtypeStruct((chunks, chunk_rows, width), BF16),
            jax.ShapeDtypeStruct((chunks, own_rows, width), BF16),
            jax.ShapeDtypeStruct((chunks, own_rows, entry_width), BF16),
            jax.ShapeDtypeStruct((chunks, 2, chips, own_rows, entry_width), BF16),
        ),
        in_specs=[vmem] * 8 + [hbm] * 8,
        out_specs=(hbm, vmem, vmem, vmem),
        scratch_shapes=[
            low(*weights.shape[1:]),
            low(*w_query.shape),
            low(*w_out.shape),
            low(*w_gate.shape),
            low(*w_up.shape),
            low(*w_down.shape),
            low(chunks, 2, chips, own_rows, width),
            low(chunks, chips, own_rows, width),
            low(chunks, chips - 1, own_rows, width),
            low(2, 2, chips, own_rows, width),
            low(chunks, chips, own_rows, width),
            low(chunks, chips - 1, own_rows, width),
            low(chunks, 2, chips, own_rows, width),
            low(group, owned, width),
            low(chunks, own_rows, width),
            low(chunks, head_width, chunk_rows),
            low(chunks, chunk_rows, head_width),
            low(chunks, chunk_rows, FHD),
            low(chunks, chunk_rows, FHD),
            low(chunks, FHD, chunk_rows),
            low(chunks, FHD, chunk_rows),
            low(chunks, head_width, chunk_rows),
            pltpu.VMEM((chunks, head_count // 2, 1, 2 * chunk_rows), F32),
            pltpu.VMEM((chunks, chunk_rows, chunk_rows), F32),
            pltpu.VMEM((chunks, own_rows, width), F32),
            dma((7,)),
            dma,
            dma((2,)),
            dma((3, 2, chunks)),
            dma((3, chunks, chips)),
            dma((3, chunks, chips)),
            dma((3, 2, chunks)),
            dma((3, chunks, chips)),
            dma((3, chunks, chips)),
            dma((2, chips)),
            dma((chips,)),
            dma((chips,)),
        ],
        compiler_params=pltpu.CompilerParams(
            collective_id=0, has_side_effects=True, vmem_limit_bytes=65280 * 1024
        ),
        cost_estimate=pl.CostEstimate(
            flops=90 * 10**9, bytes_accessed=40 * 10**6, transcendentals=20 * 10**6
        ),
    )(
        entry_ids,
        segments,
        cos_t,
        sin_t,
        bias_full,
        gain_one,
        gain_two,
        w_kv,
        entries,
        weights,
        token_grad,
        w_query,
        w_out,
        w_gate,
        w_up,
        w_down,
    )


def norm_parts(values):
    average = jnp.mean(values, axis=-1, keepdims=True)
    centred = values - average
    scale = lax.rsqrt(jnp.mean(centred * centred, axis=-1, keepdims=True) + 1e-05)
    return centred * scale, scale


def norm_back(values, grad, gain):
    unit, scale = norm_parts(values)
    scaled = grad * gain
    back = scale * (
        scaled
        - jnp.mean(scaled, axis=-1, keepdims=True)
        - unit * jnp.mean(scaled * unit, axis=-1, keepdims=True)
    )
    return (
        back,
        jnp.sum(grad * unit, axis=0, keepdims=True),
        jnp.sum(grad, axis=0, keepdims=True),
    )


def gelu_parts(values):
    root = math.sqrt(2.0 / math.pi)
    squared = values * values
    bent = jnp.tanh(root * values * (1.0 + 0.044715 * squared))
    half = 0.5 * (1.0 + bent)
    slope = half + 0.5 * values * (1.0 - bent * bent) * root * (1.0 + 3 * 0.044715 * squared)
    return values * half, slope


def pool_matrix(counts_col, entries, rows):
    entry = lax.broadcasted_iota(jnp.int32, (entries, rows), 0)
    row = lax.broadcasted_iota(jnp.int32, (entries, rows), 1)
    slots = rows // entries
    inside = (row // slots == entry) & (lax.rem(row, slots).astype(F32) < counts_col)
    return jnp.where(inside, 1.0, 0.0)


def spread_matrix(counts_row, entries, rows):
    row = lax.broadcasted_iota(jnp.int32, (rows, entries), 0)
    entry = lax.broadcasted_iota(jnp.int32, (rows, entries), 1)
    slots = rows // entries
    inside = (row // slots == entry) & (lax.rem(row, slots).astype(F32) < counts_row)
    return jnp.where(inside, 1.0, 0.0)


def slot_bias(valid_col, slots):
    rows = valid_col.shape[0]
    key = lax.broadcasted_iota(jnp.int32, (rows, rows), 0)
    query = lax.broadcasted_iota(jnp.int32, (rows, rows), 1)
    return jnp.where((key // slots == query // slots) & (valid_col > 0.5), 0.0, FAR)


ROW_BLOCK = 128


def fill_diagonal(ref, columns_t, heads):
    for h in range(heads):
        span = slice(h * HD, (h + 1) * HD)
        ref[span, h * ROW_BLOCK : (h + 1) * ROW_BLOCK] = columns_t[span, :]


def pair_blocks(both):
    return jnp.concatenate([both[:HD, :ROW_BLOCK], both[HD:, ROW_BLOCK:]], axis=0)


def tiled(block, count):
    return jnp.concatenate([block] * count, axis=1)


def shards_of(chips):
    return [(y * 2 + c, c, y) for y in range(chips) for c in range(2)]


def each_shard(chips, columns, body):
    @pl.loop(0, 2)
    def _(c):
        @pl.loop(0, chips)
        def _(y):
            first = pl.multiple_of((y * 2 + c) * columns, columns)
            body(c, y, pl.ds(first, columns))


def hyper_body(
    chips,
    dp_count,
    pieces,
    counts_all,
    gain_one,
    shift_one,
    gain_two,
    shift_two,
    w_query,
    w_key,
    w_value,
    w_out,
    bias_own,
    w_up_hbm,
    w_down_hbm,
    w_proj_hbm,
    entries,
    weights_out,
    attn_in,
    q_n,
    k_n,
    v_n,
    attended,
    logs,
    residual,
    ffn_in,
    counts_col,
    counts_row,
    bias_full,
    full,
    q_t,
    v_t,
    out_t,
    bias,
    diagonal,
    hidden,
    counts_scratch,
    local_sem,
    store_sem,
    far_send,
    far_recv,
    x_send,
    x_recv,
    near_send,
    near_recv,
    z_send,
    z_recv,
    mate_send,
    mate_recv,
    y_send,
    y_recv,
    last_send,
    last_recv,
    bias_far_send,
    bias_far_recv,
    bias_near,
):
    me = lax.axis_index("mp")
    dp = lax.axis_index("dp")
    chip, core = me // 2, lax.rem(me, 2)
    net = Exchange(chips, chip, core, "mp")
    side = lax.rem(dp, 2)
    mate = dp + 1 - 2 * side
    spot, spots = dp // 2, dp_count // 2
    kinds, _, _, width, columns = full.shape
    sources = (None, w_up_hbm, w_down_hbm, w_proj_hbm)
    rows = pieces.shape[0]
    entry_count = counts_col.shape[0]
    slots = rows // entry_count
    head_columns = columns // 4
    half = width // 2
    heads = width // HD

    flag = pltpu.get_barrier_semaphore()
    pl.semaphore_signal(flag, inc=1, device_id=net.sibling(), device_id_type=MESH)
    for other in net.others():
        pl.semaphore_signal(flag, inc=1, device_id=net.peer(other), device_id_type=MESH)

    pl.semaphore_signal(flag, inc=1, device_id={"dp": mate}, device_id_type=MESH)

    @pl.loop(1, spots)
    def _(j):
        target = lax.rem(spot + j, spots) * 2 + side
        pl.semaphore_signal(flag, inc=1, device_id={"dp": target}, device_id_type=MESH)

    local = [
        pltpu.make_async_copy(sources[k], full.at[k, core, chip], local_sem.at[k - 1])
        for k in range(1, kinds)
    ]
    for copy in local:
        copy.start()
    for j, source in enumerate((w_query, w_key, w_value, w_out)):
        full[0, core, chip, :, j * head_columns : (j + 1) * head_columns] = source[...]
    bias_full[core, chip] = bias_own[...]
    pl.semaphore_wait(flag, chips + spots)

    def rows_half(which):
        return pl.ds(pl.multiple_of(which * half, half), half)

    def far_copy(k, other):
        return net.to_peer(
            other,
            sources[k].at[rows_half(side)] if k else full.at[0, core, chip, rows_half(side)],
            full.at[k, core, chip, rows_half(side)],
            far_send.at[k, other],
            far_recv.at[k, chip],
        )

    def far_landing(k, other):
        block = full.at[k, core, other, rows_half(side)]
        return net.to_peer(other, block, block, far_send.at[k, other], far_recv.at[k, other])

    def x_copy(k, other, which):
        block = full.at[k, core, other, rows_half(which)]
        return pltpu.make_async_remote_copy(
            src_ref=block,
            dst_ref=block,
            send_sem=x_send.at[k, other],
            recv_sem=x_recv.at[k, other],
            device_id={"dp": mate},
            device_id_type=MESH,
        )

    def near_copy(k, which):
        block = full.at[k, which]
        return net.to_sibling(block, block, near_send.at[k], near_recv.at[k])

    def far_middle(k):
        for other in net.others():
            far_landing(k, other).wait_recv()
            x_copy(k, other, side).start()

    def x_middle(k):
        for other in net.others():
            x_copy(k, other, 1 - side).wait_recv()
        if k:
            local[k - 1].wait()
        near_copy(k, core).start()

    def store(k):
        return pltpu.make_async_copy(full.at[k], weights_out.at[k], store_sem.at[k])

    def near_finish(k):
        near_copy(k, 1 - core).wait_recv()
        store(k).start()

    bias_rows = Gather(
        net, bias_full, (bias_far_send, bias_far_recv, bias_near.at[0], bias_near.at[1]), True
    )
    def far_start(k):
        for other in net.others():
            far_copy(k, other).start()

    far_start(0)
    bias_rows.start(0)
    counts_scratch[...] = column_of(counts_all[...].astype(F32))
    own_counts = counts_scratch[pl.ds(pl.multiple_of(me * entry_count, entry_count), entry_count)]
    counts_col[...] = own_counts
    counts_row[...] = jnp.broadcast_to(own_counts, (entry_count, 128)).T[:1]

    values = pieces[...].astype(F32)
    attn_in[...] = (norm_parts(values)[0] * gain_one[...] + shift_one[...]).astype(BF16)
    blocks = rows // ROW_BLOCK
    valid = jnp.sum(spread_matrix(counts_row[...], entry_count, rows), axis=1, keepdims=True)
    for b in range(blocks):
        bias[b] = slot_bias(valid[b * ROW_BLOCK : (b + 1) * ROW_BLOCK], slots)

    far_middle(0)
    far_start(1)
    bias_rows.middle(0)
    far_middle(1)
    far_start(2)
    x_middle(0)
    near_finish(0)
    for m, c, y in shards_of(chips):
        span = slice(m * head_columns, (m + 1) * head_columns)
        projected = dot_nn(attn_in[...], full[0, c, y, :, : 3 * head_columns])
        q_n[:, span] = (projected[:, :head_columns].astype(BF16).astype(F32) * HD**-0.5).astype(
            BF16
        )
        k_n[:, span] = projected[:, head_columns : 2 * head_columns].astype(BF16)
        v_n[:, span] = projected[:, 2 * head_columns :].astype(BF16)
    far_middle(2)
    far_start(3)
    x_middle(1)
    for b in range(blocks):
        block_rows = slice(b * ROW_BLOCK, (b + 1) * ROW_BLOCK)
        q_t[b] = q_n[block_rows, :].T
        v_t[b] = v_n[block_rows, :].T

    diagonal[...] = jnp.zeros_like(diagonal)

    def attend_block(b):
        block_rows = pl.ds(pl.multiple_of(b * ROW_BLOCK, ROW_BLOCK), ROW_BLOCK)
        fill_diagonal(diagonal, q_t[b], heads)
        scores = dot_nn(k_n[block_rows, :], diagonal[...]) + tiled(bias[b], heads)
        top = jnp.max(scores, axis=0, keepdims=True)
        weights = jnp.exp(scores - top)
        total = jnp.sum(weights, axis=0, keepdims=True)
        logs[b] = top + jnp.log(total)
        weights = (weights / total).astype(BF16)
        for pair in range(heads // 2):
            span = slice(pair * 2 * HD, (pair + 1) * 2 * HD)
            lanes = slice(pair * 2 * ROW_BLOCK, (pair + 1) * 2 * ROW_BLOCK)
            both = dot_nn(v_t[b, span, :], weights[:, lanes])
            out_t[b, span, :] = pair_blocks(both).astype(BF16)

    pl.loop(0, blocks // 2)(attend_block)
    far_middle(3)
    x_middle(2)
    pl.loop(blocks // 2, blocks)(attend_block)
    for b in range(blocks):
        attended[b * ROW_BLOCK : (b + 1) * ROW_BLOCK, :] = out_t[b].T
    total = values
    for m, c, y in shards_of(chips):
        span = slice(m * head_columns, (m + 1) * head_columns)
        total = total + dot_nt(attended[:, span], full[0, c, y, :, 3 * head_columns :])
    residual[...] = total
    ffn_in[...] = (norm_parts(total)[0] * gain_two[...] + shift_two[...]).astype(BF16)
    near_finish(1)
    x_middle(3)
    pool = pool_matrix(counts_col[...], entry_count, rows).astype(BF16)

    def up_shard(c, y, span):
        act = gelu_parts(dot_nn(ffn_in[...], full[1, c, y]))[0]
        hidden[:, span] = dot_nn(pool, act.astype(BF16)).astype(BF16)

    each_shard(chips, columns, up_shard)
    near_finish(2)
    pooled = jnp.sum(
        (residual[...] * valid).reshape(entry_count, slots, width), axis=1
    )
    for m, c, y in shards_of(chips):
        pooled = pooled + dot_nt(hidden[:, m * columns : (m + 1) * columns], full[2, c, y])
    entries[core, chip, dp] = (pooled / counts_col[...]).astype(BF16)

    def z_copy(target, owner):
        piece = entries.at[core, chip, owner * 2 + side]
        return pltpu.make_async_remote_copy(
            src_ref=piece,
            dst_ref=piece,
            send_sem=z_send.at[target],
            recv_sem=z_recv.at[owner],
            device_id={"dp": target * 2 + side},
            device_id_type=MESH,
        )

    def mate_copy(owner, which):
        piece = entries.at[core, chip, owner * 2 + which]
        return pltpu.make_async_remote_copy(
            src_ref=piece,
            dst_ref=piece,
            send_sem=mate_send.at[owner],
            recv_sem=mate_recv.at[owner],
            device_id={"dp": mate},
            device_id_type=MESH,
        )

    def y_copy(other, owner, block):
        piece = entries.at[core, owner, block]
        return net.to_peer(
            other, piece, piece, y_send.at[other, block], y_recv.at[owner, block]
        )

    def y_start(block):
        for other in net.others():
            y_copy(other, chip, block).start()

    @pl.loop(1, spots)
    def _(j):
        z_copy(lax.rem(spot + j, spots), spot).start()

    mate_copy(spot, side).start()
    y_start(dp)
    near_finish(3)
    bias_rows.finish(0)

    @pl.loop(1, spots)
    def _(j):
        source = lax.rem(spot + spots - j, spots)
        z_copy(source, source).wait_recv()
        mate_copy(source, side).start()
        y_start(source * 2 + side)

    @pl.loop(0, spots)
    def _(j):
        source = lax.rem(spot + spots - j, spots)
        mate_copy(source, 1 - side).wait_recv()
        y_start(source * 2 + 1 - side)

    def last_copy(part, c, owner):
        piece = entries.at[c, owner]
        return net.to_sibling(piece, piece, last_send.at[part], last_recv.at[owner])

    last_copy(chip, core, chip).start()
    for other in net.others():

        @pl.loop(0, dp_count)
        def _(block):
            y_copy(other, other, block).wait_recv()

        last_copy(other, core, other).start()
    last_copy(chip, 1 - core, chip).wait_recv()
    for other in net.others():
        last_copy(other, 1 - core, other).wait_recv()

    bias_rows.sent(0)
    for k in range(kinds):
        store(k).wait()
        near_copy(k, core).wait_send()
        for other in net.others():
            far_copy(k, other).wait_send()
            x_copy(k, other, side).wait_send()

    @pl.loop(1, spots)
    def _(j):
        z_copy(lax.rem(spot + j, spots), spot).wait_send()

    @pl.loop(0, spots)
    def _(j):
        mate_copy(j, side).wait_send()

    last_copy(chip, core, chip).wait_send()
    for other in net.others():
        last_copy(other, core, other).wait_send()

        @pl.loop(0, dp_count)
        def _(block):
            y_copy(other, chip, block).wait_send()


def hyper_forward(
    group,
    dp_count,
    pieces,
    counts,
    gain_one,
    shift_one,
    gain_two,
    shift_two,
    head_weights,
    bias_own,
    unit_weights,
):
    chips = group // 2
    rows, width = pieces.shape
    columns = unit_weights[0].shape[1]
    kinds = 4
    entry_count = counts.shape[1] // group
    heads = width // HD
    blocks = rows // ROW_BLOCK
    vmem = pl.BlockSpec(memory_space=pltpu.VMEM)
    hbm = pl.BlockSpec(memory_space=pl.ANY)
    row_shape = jax.ShapeDtypeStruct((rows, width), BF16)
    dma = pltpu.SemaphoreType.DMA
    return pl.pallas_call(
        partial(hyper_body, chips, dp_count),
        out_shape=(
            jax.ShapeDtypeStruct((2, chips, dp_count, entry_count, width), BF16),
            jax.ShapeDtypeStruct((kinds, 2, chips, width, columns), BF16),
            row_shape,
            row_shape,
            row_shape,
            row_shape,
            row_shape,
            jax.ShapeDtypeStruct((blocks, 1, heads * ROW_BLOCK), F32),
            jax.ShapeDtypeStruct((rows, width), F32),
            row_shape,
            jax.ShapeDtypeStruct((entry_count, 1), F32),
            jax.ShapeDtypeStruct((1, entry_count), F32),
            jax.ShapeDtypeStruct((2, chips, 1, columns), F32),
        ),
        in_specs=[vmem] * 11 + [hbm] * 3,
        out_specs=(vmem, hbm) + (vmem,) * 11,
        scratch_shapes=[
            pltpu.VMEM((kinds, 2, chips, width, columns), BF16),
            pltpu.VMEM((blocks, width, ROW_BLOCK), BF16),
            pltpu.VMEM((blocks, width, ROW_BLOCK), BF16),
            pltpu.VMEM((blocks, width, ROW_BLOCK), BF16),
            pltpu.VMEM((blocks, ROW_BLOCK, ROW_BLOCK), F32),
            pltpu.VMEM((width, heads * ROW_BLOCK), BF16),
            pltpu.VMEM((entry_count, columns * group), BF16),
            pltpu.VMEM((counts.shape[1], 1), F32),
            dma((kinds - 1,)),
            dma((kinds,)),
            dma((kinds, chips)),
            dma((kinds, chips)),
            dma((kinds, chips)),
            dma((kinds, chips)),
            dma((kinds,)),
            dma((kinds,)),
            dma((dp_count // 2,)),
            dma((dp_count // 2,)),
            dma((dp_count // 2,)),
            dma((dp_count // 2,)),
            dma((chips, dp_count)),
            dma((chips, dp_count)),
            dma((chips,)),
            dma((chips,)),
            dma((1, chips)),
            dma((1, chips)),
            dma((2, 1)),
        ],
        compiler_params=pltpu.CompilerParams(
            collective_id=1, has_side_effects=True, vmem_limit_bytes=60 * 1024 * 1024
        ),
        cost_estimate=pl.CostEstimate(
            flops=60 * 10**9, bytes_accessed=20 * 10**6, transcendentals=5 * 10**6
        ),
    )(
        pieces,
        counts,
        gain_one,
        shift_one,
        gain_two,
        shift_two,
        *head_weights,
        bias_own,
        *unit_weights,
    )


class Total:
    def __init__(self, net, dp, dp_count, scatter, mine, x_land, z_land, final, sems):
        self.net, self.scatter, self.mine = net, scatter, mine
        self.x_land, self.z_land, self.final = x_land, z_land, final
        self.x_send, self.x_recv, self.z_send, self.z_recv = sems[:4]
        self.g_send, self.g_recv, self.l_send, self.l_recv = sems[4:]
        self.side = lax.rem(dp, 2)
        self.spot = dp // 2
        self.mate = dp + 1 - 2 * self.side
        self.spots = dp_count // 2

    def remote(self, source, target, send, recv, device):
        return Pieces(source, target, send, recv, {"dp": device}, 1)

    def x_copy(self, k):
        return self.remote(
            self.mine.at[k, 1 - self.side],
            self.x_land.at[k],
            self.x_send.at[k],
            self.x_recv.at[k],
            self.mate,
        )

    def z_copy(self, k, spot, slot):
        return self.remote(
            self.mine.at[k, self.side, spot],
            self.z_land.at[k, slot],
            self.z_send.at[k, spot],
            self.z_recv.at[k, slot],
            spot * 2 + self.side,
        )

    def g_copy(self, k, spot, owner):
        block = self.final.at[k, self.side, owner]
        return self.remote(
            block, block, self.g_send.at[k, spot], self.g_recv.at[k, owner], spot * 2 + self.side
        )

    def l_copy(self, k, side):
        block = self.final.at[k, side]
        return self.remote(block, block, self.l_send.at[k], self.l_recv.at[k], self.mate)

    def each_spot(self, body):
        if self.spots > 1:

            @pl.loop(1, self.spots)
            def _(j):
                body(lax.rem(self.spot + j, self.spots))

    def start(self, k):
        self.scatter.start(k)

    def near_middle(self, k):
        self.scatter.middle(k)

    def far_middle(self, k):
        total = self.scatter.finish(k)
        self.mine[k] = total.astype(BF16).reshape(self.mine.shape[1:])
        self.x_copy(k).start()

    def x_middle(self, k):
        self.x_copy(k).wait_recv()
        block = self.mine[k, self.side].astype(F32) + self.x_land[k].astype(F32)
        self.mine[k, self.side] = block.astype(BF16)
        self.each_spot(lambda spot: self.z_copy(k, spot, self.spot).start())

    def z_middle(self, k):
        def add(spot):
            self.z_copy(k, spot, spot).wait_recv()

        self.each_spot(add)
        total = self.mine[k, self.side, self.spot].astype(F32)
        for j in range(1, self.spots):
            spot = lax.rem(self.spot + j, self.spots)
            total = total + self.z_land[k, spot].astype(F32)
        self.final[k, self.side, self.spot] = total.astype(BF16)
        self.each_spot(lambda spot: self.g_copy(k, spot, self.spot).start())

    def g_middle(self, k):
        self.each_spot(lambda spot: self.g_copy(k, spot, spot).wait_recv())
        self.l_copy(k, self.side).start()

    def finish(self, k):
        self.l_copy(k, 1 - self.side).wait_recv()

    def sent(self, k):
        self.scatter.sent(k)
        self.x_copy(k).wait_send()
        self.each_spot(lambda spot: self.z_copy(k, spot, self.spot).wait_send())
        self.each_spot(lambda spot: self.g_copy(k, spot, self.spot).wait_send())
        self.l_copy(k, self.side).wait_send()


PARTS = 8


def back_body(
    chips,
    dp_count,
    embed_rows,
    pooled_own,
    token_rows,
    token_row,
    pieces,
    counts_col,
    counts_row,
    gain_one,
    gain_two,
    attn_in,
    q_n,
    k_n,
    v_n,
    attended,
    logs,
    residual,
    ffn_in,
    weights_hbm,
    out_part,
    pieces_grad,
    final,
    small_total,
    text_out,
    weights,
    part,
    near,
    far,
    mine,
    x_land,
    z_land,
    entry_part,
    entry_land,
    hidden,
    slopes,
    ffn_t,
    row_total,
    d_out_n,
    d_query,
    d_key,
    d_value,
    q_t,
    out_t,
    d_out_t,
    k_t,
    d_query_t,
    bias,
    query_wide,
    grad_wide,
    small_near,
    small_far,
    small_dp,
    small_part,
    out_own,
    out_near,
    out_far,
    weight_sem,
    out_local,
    out_near_sem,
    out_far_send,
    out_far_recv,
    entry_send,
    entry_recv,
    scatter_near,
    scatter_far_send,
    scatter_far_recv,
    x_sem,
    z_send,
    z_recv,
    g_send,
    g_recv,
    l_sem,
    small_sem,
    small_far_send,
    small_far_recv,
    small_dp_send,
    small_dp_recv,
):
    me = lax.axis_index("mp")
    dp = lax.axis_index("dp")
    group = chips * 2
    chip, core = me // 2, lax.rem(me, 2)
    net = Exchange(chips, chip, core, "mp")
    rows, width = pieces.shape
    entry_count = counts_col.shape[0]
    slots = rows // entry_count
    columns = weights.shape[4]
    half_columns = columns // 2
    head_columns = columns // 4
    heads = width // HD
    blocks = rows // ROW_BLOCK
    total_sum = Total(
        net,
        dp,
        dp_count,
        Scatter(
            net,
            part,
            near,
            far,
            (scatter_near.at[0], scatter_near.at[1], scatter_far_send, scatter_far_recv),
        ),
        mine,
        x_land,
        z_land,
        final,
        (x_sem.at[0], x_sem.at[1], z_send, z_recv, g_send, g_recv, l_sem.at[0], l_sem.at[1]),
    )
    stages = (
        total_sum.near_middle,
        total_sum.far_middle,
        total_sum.x_middle,
        total_sum.z_middle,
        total_sum.g_middle,
        total_sum.finish,
    )

    def run(step):
        for offset, stage in enumerate(stages):
            if 0 <= step - offset < PARTS:
                stage(step - offset)

    flag = pltpu.get_barrier_semaphore()
    pl.semaphore_signal(flag, inc=1, device_id=net.sibling(), device_id_type=MESH)
    for other in net.others():
        pl.semaphore_signal(flag, inc=1, device_id=net.peer(other), device_id_type=MESH)

    def each_dp(body):
        @pl.loop(1, dp_count)
        def _(j):
            body(lax.rem(dp + j, dp_count))

    each_dp(
        lambda target: pl.semaphore_signal(
            flag, inc=1, device_id={"dp": target}, device_id_type=MESH
        )
    )
    loads = [
        pltpu.make_async_copy(weights_hbm.at[k], weights.at[k], weight_sem.at[k])
        for k in (1, 2, 0)
    ]
    for copy in loads:
        copy.start()
    out_copies = [
        pltpu.make_async_copy(out_part.at[y * 2 + core], out_own.at[y], out_local.at[y])
        for y in range(chips)
    ]
    for copy in out_copies:
        copy.start()
    pl.semaphore_wait(flag, chips + dp_count - 1)

    def out_near_copy(y):
        return net.to_sibling(
            out_part.at[y * 2 + 1 - core],
            out_near.at[y],
            out_near_sem.at[0, y],
            out_near_sem.at[1, y],
        )

    def out_far_copy(other, source):
        return net.to_peer(
            other,
            out_own.at[other],
            out_far.at[lax.rem(source - chip + chips - 1, chips)]
            if source is not chip
            else out_far.at[lax.rem(chip - other + chips - 1, chips)],
            out_far_send.at[other],
            out_far_recv.at[source],
        )

    for y in range(chips):
        out_near_copy(y).start()

    def put(k, c, y, values):
        part[k, c, y] = values[:, :half_columns].astype(BF16)
        part[k + 1, c, y] = values[:, half_columns:].astype(BF16)

    token_total = token_rows.shape[0]
    dp_step = max(1, 256 // entry_count)

    @pl.loop(0, dp_count // dp_step)
    def _(block):
        row = lax.broadcasted_iota(jnp.int32, (dp_step * entry_count, token_total), 0)
        owner = block * dp_step + row // entry_count
        number = (owner * group + me) * entry_count + lax.rem(row, entry_count)
        chosen = jnp.where(number == token_row[...], 1.0, 0.0).astype(BF16)
        sums = dot_nn(chosen, token_rows[...]).astype(BF16)
        for j in range(dp_step):
            entry_part[block * dp_step + j] = sums[j * entry_count : (j + 1) * entry_count]

    def entry_copy(target, slot):
        return pltpu.make_async_remote_copy(
            src_ref=entry_part.at[target],
            dst_ref=entry_land.at[slot],
            send_sem=entry_send.at[target],
            recv_sem=entry_recv.at[slot],
            device_id={"dp": target},
            device_id_type=MESH,
        )

    each_dp(lambda target: entry_copy(target, dp).start())
    pooled_t = pooled_own[...].T

    def proj_shard(c, y, span):
        put(0, c, y, dot_nn(pooled_t, embed_rows[:, span]))

    each_shard(chips, columns, proj_shard)
    total_sum.start(0)
    total_sum.start(1)
    bias_sums = jnp.sum(embed_rows[...].astype(F32), axis=0, keepdims=True)
    for j in range(4):
        small_part[4 + j : 5 + j, :] = bias_sums[:, j * width : (j + 1) * width]
    loads[0].wait()
    run(0)

    pool = pool_matrix(counts_col[...], entry_count, rows).astype(BF16)
    spread = spread_matrix(counts_row[...], entry_count, rows)
    valid = jnp.sum(spread, axis=1, keepdims=True)
    spread = spread.astype(BF16)
    for b in range(blocks):
        bias[b] = slot_bias(valid[b * ROW_BLOCK : (b + 1) * ROW_BLOCK], slots)
    ffn_t[...] = ffn_in[...].T

    def hidden_shard(c, y, span):
        act, slope = gelu_parts(dot_nn(ffn_in[...], weights[1, c, y]))
        slopes[:, span] = slope.astype(BF16)
        hidden[:, span] = dot_nn(pool, act.astype(BF16)).astype(BF16)

    each_shard(chips, columns, hidden_shard)
    run(1)
    each_dp(lambda source: entry_copy(source, source).wait_recv())
    pooled_grad = entry_part[dp].astype(F32)
    for j in range(1, dp_count):
        pooled_grad = pooled_grad + entry_land[lax.rem(dp + j, dp_count)].astype(F32)
    entry_low = (pooled_grad / counts_col[...]).astype(BF16)
    out_rows = dot_nn(spread, entry_low)
    entry_t = entry_low.T
    loads[1].wait()
    out_low = out_rows.astype(BF16)
    row_total[...] = jnp.zeros_like(row_total)

    def unit_shard(c, y, span):
        put(2, c, y, dot_nn(entry_t, hidden[:, span]))
        act_grad = dot_nn(out_low, weights[2, c, y])
        pre_grad = (act_grad * slopes[:, span].astype(F32)).astype(BF16)
        put(4, c, y, dot_nn(ffn_t[...], pre_grad))
        row_total[...] += dot_nt(pre_grad, weights[1, c, y])

    each_shard(chips, columns, unit_shard)
    for k in (2, 3, 4, 5):
        total_sum.start(k)
    run(2)
    back, gain_grad, shift_grad = norm_back(residual[...], row_total[...], gain_two[...])
    small_part[2:3, :] = gain_grad
    small_part[3:4, :] = shift_grad
    residual_grad = out_rows + back
    pieces_grad[...] = residual_grad
    attn_grad = residual_grad.astype(BF16)
    loads[2].wait()
    for m, c, y in shards_of(chips):
        span = slice(m * head_columns, (m + 1) * head_columns)
        d_out_n[:, span] = dot_nn(attn_grad, weights[0, c, y, :, 3 * head_columns :]).astype(BF16)
    out_grad = dot_nn(attn_grad.T, attended[...])
    for m, c, y in shards_of(chips):
        span = slice(m * head_columns, (m + 1) * head_columns)
        part[7, c, y, :, head_columns:] = out_grad[:, span].astype(BF16)
    for b in range(blocks):
        block_rows = slice(b * ROW_BLOCK, (b + 1) * ROW_BLOCK)
        q_t[b] = q_n[block_rows, :].T
        k_t[b] = k_n[block_rows, :].T
        out_t[b] = attended[block_rows, :].T
        d_out_t[b] = d_out_n[block_rows, :].T
    run(3)

    for ref in (query_wide, grad_wide):
        ref[...] = jnp.zeros_like(ref)

    @pl.loop(0, blocks)
    def _(b):
        block_rows = pl.ds(pl.multiple_of(b * ROW_BLOCK, ROW_BLOCK), ROW_BLOCK)
        fill_diagonal(query_wide, q_t[b], heads)
        fill_diagonal(grad_wide, d_out_t[b], heads)
        scores = dot_nn(k_n[block_rows, :], query_wide[...]) + tiled(bias[b], heads)
        probs = jnp.exp(scores - logs[b])
        d_value[block_rows, :] = dot_nt(probs.astype(BF16), grad_wide[...]).astype(BF16)
        moved = d_out_t[b].astype(F32) * out_t[b].astype(F32)
        centre = jnp.concatenate(
            [
                jnp.sum(moved[h * HD : (h + 1) * HD], axis=0, keepdims=True)
                for h in range(heads)
            ],
            axis=1,
        )
        score_grad = (probs * (dot_nn(v_n[block_rows, :], grad_wide[...]) - centre)).astype(BF16)
        d_key[block_rows, :] = dot_nt(score_grad, query_wide[...]).astype(BF16)
        for pair in range(heads // 2):
            span = slice(pair * 2 * HD, (pair + 1) * 2 * HD)
            lanes = slice(pair * 2 * ROW_BLOCK, (pair + 1) * 2 * ROW_BLOCK)
            both = dot_nn(k_t[b, span, :], score_grad[:, lanes]) * (HD**-0.5)
            d_query_t[b, span, :] = pair_blocks(both).astype(BF16)

    for b in range(blocks):
        d_query[b * ROW_BLOCK : (b + 1) * ROW_BLOCK, :] = d_query_t[b].T
    run(4)
    rows_t = attn_in[...].T
    for place, (k, lanes, source) in enumerate(
        ((6, 0, d_query), (6, 1, d_key), (7, 0, d_value))
    ):
        grads = dot_nn(rows_t, source[...])
        for m, c, y in shards_of(chips):
            span = slice(m * head_columns, (m + 1) * head_columns)
            part[k, c, y, :, lanes * head_columns : (lanes + 1) * head_columns] = grads[
                :, span
            ].astype(BF16)
    total_sum.start(6)
    total_sum.start(7)
    normed = jnp.zeros((rows, width), F32)
    for m, c, y in shards_of(chips):
        span = slice(m * head_columns, (m + 1) * head_columns)
        for j, source in enumerate((d_query, d_key, d_value)):
            normed = normed + dot_nt(
                source[:, span], weights[0, c, y, :, j * head_columns : (j + 1) * head_columns]
            )
    back, gain_grad, shift_grad = norm_back(pieces[...].astype(F32), normed, gain_one[...])
    small_part[0:1, :] = gain_grad
    small_part[1:2, :] = shift_grad
    pieces_grad[...] += back

    def out_middle():
        for y in range(chips):
            out_copies[y].wait()
            out_near_copy(y).wait_recv()
        for other in net.others():
            out_own[other] = (
                out_own[other].astype(F32) + out_near[other].astype(F32)
            ).astype(BF16)
            out_far_copy(other, chip).start()

    def out_finish():
        text_out[...] = out_own[chip].astype(F32) + out_near[chip].astype(F32)
        for other in net.others():
            out_far_copy(other, other).wait_recv()
            slot = lax.rem(other - chip + chips - 1, chips)
            text_out[...] += out_far[slot].astype(F32)

    small_copy = net.to_sibling(small_part, small_near, small_sem.at[0], small_sem.at[1])
    small_copy.start()

    def small_far_copy(other, owner):
        return net.to_peer(
            other,
            small_far.at[owner],
            small_far.at[owner],
            small_far_send.at[other],
            small_far_recv.at[owner],
        )

    def small_dp_copy(other, owner):
        return pltpu.make_async_remote_copy(
            src_ref=small_dp.at[owner],
            dst_ref=small_dp.at[owner],
            send_sem=small_dp_send.at[other],
            recv_sem=small_dp_recv.at[owner],
            device_id={"dp": other},
            device_id_type=MESH,
        )

    def small_near_done():
        small_copy.wait_recv()
        small_far[chip] = small_part[...] + small_near[...]
        for other in net.others():
            small_far_copy(other, chip).start()

    def small_far_done():
        for other in net.others():
            small_far_copy(other, other).wait_recv()
        total = small_far[0]
        for j in range(1, chips):
            total = total + small_far[j]
        small_dp[dp] = total
        each_dp(lambda other: small_dp_copy(other, dp).start())

    @pl.loop(5, PARTS + 5)
    def _(step):
        for offset, stage in enumerate(stages):
            k = step - offset

            @pl.when((k >= 0) & (k < PARTS))
            def _():
                stage(k)

        pl.when(step == 5)(small_near_done)
        pl.when(step == 7)(small_far_done)
        pl.when(step == PARTS)(out_middle)

    out_finish()
    each_dp(lambda other: small_dp_copy(other, other).wait_recv())
    total = small_dp[0]
    for j in range(1, dp_count):
        total = total + small_dp[j]
    small_total[...] = total

    for y in range(chips):
        out_near_copy(y).wait_send()
    for other in net.others():
        out_far_copy(other, chip).wait_send()
    small_copy.wait_send()
    for other in net.others():
        small_far_copy(other, chip).wait_send()
    each_dp(lambda other: small_dp_copy(other, dp).wait_send())
    each_dp(lambda other: entry_copy(other, dp).wait_send())

    @pl.loop(0, PARTS)
    def _(k):
        total_sum.sent(k)


def hyper_backward(
    group,
    dp_count,
    embed_rows,
    pooled_own,
    token_rows,
    token_row,
    pieces,
    counts_col,
    counts_row,
    gain_one,
    gain_two,
    saved,
    weights,
    out_part,
):
    chips = group // 2
    rows, width = pieces.shape
    entry_count = counts_col.shape[0]
    kinds, columns = weights.shape[0], weights.shape[4]
    half_columns = columns // 2
    heads = width // HD
    blocks = rows // ROW_BLOCK
    spots = dp_count // 2
    vmem = pl.BlockSpec(memory_space=pltpu.VMEM)
    hbm = pl.BlockSpec(memory_space=pl.ANY)
    dma = pltpu.SemaphoreType.DMA
    final = (PARTS, 2, spots, width // (2 * spots), half_columns)
    units = columns * group

    def low(*shape):
        return pltpu.VMEM(shape, BF16)

    def wide(*shape):
        return pltpu.VMEM(shape, F32)

    return pl.pallas_call(
        partial(back_body, chips, dp_count),
        out_shape=(
            jax.ShapeDtypeStruct((rows, width), F32),
            jax.ShapeDtypeStruct(final, BF16),
            jax.ShapeDtypeStruct((8, width), F32),
            jax.ShapeDtypeStruct(out_part.shape[1:], F32),
        ),
        in_specs=[vmem] * 17 + [hbm] * 2,
        out_specs=(vmem,) * 4,
        scratch_shapes=[
            low(kinds, 2, chips, width, columns),
            low(PARTS, 2, chips, width, half_columns),
            low(PARTS, chips, width, half_columns),
            low(PARTS, chips - 1, width, half_columns),
            low(*final),
            low(PARTS, spots, width // (2 * spots), half_columns),
            low(PARTS, spots, width // (2 * spots), half_columns),
            low(dp_count, entry_count, width),
            low(dp_count, entry_count, width),
            low(entry_count, units),
            low(rows, units),
            low(width, rows),
            wide(rows, width),
            low(rows, width),
            low(rows, width),
            low(rows, width),
            low(rows, width),
        ]
        + [low(blocks, width, ROW_BLOCK)] * 5
        + [
            wide(blocks, ROW_BLOCK, ROW_BLOCK),
            low(width, heads * ROW_BLOCK),
            low(width, heads * ROW_BLOCK),
            wide(8, width),
            wide(chips, 8, width),
            wide(dp_count, 8, width),
            wide(8, width),
            low(chips, *out_part.shape[1:]),
            low(chips, *out_part.shape[1:]),
            low(chips - 1, *out_part.shape[1:]),
            dma((kinds,)),
            dma((chips,)),
            dma((2, chips)),
            dma((chips,)),
            dma((chips,)),
            dma((dp_count,)),
            dma((dp_count,)),
            dma((2, PARTS)),
            dma((PARTS, chips)),
            dma((PARTS, chips)),
            dma((2, PARTS)),
            dma((PARTS, spots)),
            dma((PARTS, spots)),
            dma((PARTS, spots)),
            dma((PARTS, spots)),
            dma((2, PARTS)),
            dma((2,)),
            dma((chips,)),
            dma((chips,)),
            dma((dp_count,)),
            dma((dp_count,)),
        ],
        compiler_params=pltpu.CompilerParams(
            collective_id=2, has_side_effects=True, vmem_limit_bytes=62 * 1024 * 1024
        ),
        cost_estimate=pl.CostEstimate(
            flops=60 * 10**9, bytes_accessed=20 * 10**6, transcendentals=5 * 10**6
        ),
    )(
        embed_rows,
        pooled_own,
        token_rows,
        token_row,
        pieces,
        counts_col,
        counts_row,
        gain_one,
        gain_two,
        *saved,
        weights,
        out_part,
    )


def spread_body(sums, query, key, value, out, up, down, proj):
    half_columns = sums.shape[2]
    head_columns = query.shape[1]
    for first, target in ((0, proj), (2, down), (4, up)):
        target[:, :half_columns] = sums[first].astype(F32)
        target[:, half_columns:] = sums[first + 1].astype(F32)
    for k, lanes, target in ((6, 0, query), (6, 1, key), (7, 0, value), (7, 1, out)):
        target[...] = sums[k, :, lanes * head_columns : (lanes + 1) * head_columns].astype(F32)


def spread_sums(sums):
    _, width, half_columns = sums.shape
    small = jax.ShapeDtypeStruct((width, half_columns // 2), F32)
    large = jax.ShapeDtypeStruct((width, half_columns * 2), F32)
    vmem = pl.BlockSpec(memory_space=pltpu.VMEM)
    return pl.pallas_call(
        spread_body,
        out_shape=(small,) * 4 + (large,) * 3,
        in_specs=[vmem],
        out_specs=(vmem,) * 7,
        compiler_params=pltpu.CompilerParams(vmem_limit_bytes=40 * 1024 * 1024),
    )(sums)


def on_device(
    pieces,
    counts,
    entry_ids,
    segment_ids,
    norm1_gain,
    norm1_shift,
    query_weight,
    key_weight,
    value_weight,
    out_weight,
    norm2_gain,
    norm2_shift,
    up_weight,
    down_weight,
    proj_weight,
    proj_bias,
    text_norm1_gain,
    text_query,
    text_key,
    text_value,
    text_out_proj,
    text_norm2_gain,
    text_gate,
    text_up,
    text_down,
    token_grad,
):
    group, dp_count = lax.axis_size("mp"), lax.axis_size("dp")
    me = lax.axis_index("mp")
    entry_count, slot_count, width = pieces.shape
    text_width = token_grad.shape[1]
    length = segment_ids.shape[1]
    chunk_rows = length // CHUNKS
    pieces_rows = pieces.reshape(entry_count * slot_count, width)
    entries, weights, *saved, counts_col, counts_row, bias_full = hyper_forward(
        group,
        dp_count,
        pieces_rows,
        counts[None, :],
        norm1_gain[None, :],
        norm1_shift[None, :],
        norm2_gain[None, :],
        norm2_shift[None, :],
        (query_weight, key_weight, value_weight, out_weight),
        proj_bias[None, :],
        (up_weight, down_weight, proj_weight),
    )
    head_width = text_query.shape[1]
    kv_index = me * (head_width // FHD) // (QHEADS // KVHEADS)
    key_local = lax.dynamic_slice_in_dim(text_key, kv_index * FHD, FHD, 1)
    value_local = lax.dynamic_slice_in_dim(text_value, kv_index * FHD, FHD, 1)
    key_value = jnp.concatenate([key_local, value_local], axis=1)
    cos_t, sin_t = rope_tables(length)
    out_part, embed_rows, pooled_own, token_rows = text_layer(
        group,
        dp_count,
        entry_count,
        entry_ids.reshape(CHUNKS, 1, chunk_rows),
        segment_ids.reshape(CHUNKS, 1, chunk_rows),
        cos_t,
        sin_t,
        bias_full,
        text_norm1_gain[None, :],
        text_norm2_gain[None, :],
        key_value,
        entries.reshape(-1, width),
        weights,
        token_grad,
        text_query,
        text_out_proj,
        text_gate,
        text_up,
        text_down,
    )
    pieces_grad, final, small, text_out = hyper_backward(
        group,
        dp_count,
        embed_rows.reshape(-1, text_width),
        pooled_own.reshape(-1, width),
        token_rows.reshape(length, width),
        entry_ids[None, :],
        pieces_rows,
        counts_col,
        counts_row,
        norm1_gain[None, :],
        norm2_gain[None, :],
        saved,
        weights,
        out_part.reshape(group, -1, text_width),
    )
    query_grad, key_grad, value_grad, out_grad, up_grad, down_grad, proj_grad = spread_sums(
        final.reshape(PARTS, width, -1)
    )
    bias_share = proj_bias.shape[0]
    proj_bias_grad = lax.dynamic_slice_in_dim(
        small[4:].reshape(-1), me * bias_share, bias_share
    )
    return (
        text_out,
        pieces_grad.reshape(pieces.shape),
        small[0],
        small[1],
        query_grad,
        key_grad,
        value_grad,
        out_grad,
        small[2],
        small[3],
        up_grad,
        down_grad,
        proj_grad,
        proj_bias_grad,
    )


def solution(mesh):
    return jax.shard_map(
        on_device,
        mesh=mesh,
        in_specs=(
            P(("dp", "mp"), None, None),
            P("dp"),
            P("dp"),
            P("dp", None),
            P(),
            P(),
            P(None, "mp"),
            P(None, "mp"),
            P(None, "mp"),
            P(None, "mp"),
            P(),
            P(),
            P(None, "mp"),
            P(None, "mp"),
            P(None, "mp"),
            P("mp"),
            P(),
            P(None, "mp"),
            P(),
            P(),
            P(None, "mp"),
            P(),
            P(None, "mp"),
            P(None, "mp"),
            P(None, "mp"),
            P(("dp", "mp"), None),
        ),
        out_specs=(
            P(("dp", "mp"), None),
            P(("dp", "mp"), None, None),
            P(),
            P(),
            P(None, "mp"),
            P(None, "mp"),
            P(None, "mp"),
            P(None, "mp"),
            P(),
            P(),
            P(None, "mp"),
            P(None, "mp"),
            P(None, "mp"),
            P("mp"),
        ),
        check_vma=False,
    )
```

```python
from functools import partial
import math

import jax
import jax.numpy as jnp
import numpy as np
from jax import lax
from jax.experimental import pallas as pl
from jax.experimental.pallas import tpu as pltpu
from jax.sharding import PartitionSpec as P

HD = 64
QHEADS = 32
KVHEADS = 4
FHD = 64


def rope_tables(length):
    positions = np.arange(length, dtype=np.float32)
    rates = np.exp(
        np.arange(FHD // 2, dtype=np.float32) * np.float32(-2.0 * math.log(10000.0) / FHD)
    ).astype(np.float32)
    angles = (positions[None, :] * rates[:, None]).reshape(FHD // 2, CHUNKS, length // CHUNKS)
    angles = angles.transpose(1, 0, 2)
    return jnp.asarray(np.cos(angles)), jnp.asarray(np.sin(angles))


MESH = pl.DeviceIdType.MESH
F32 = jnp.float32
BF16 = jnp.bfloat16
CHUNKS = 4
FAR = -1e30


def dot_nn(a, b):
    return lax.dot_general(a, b, (((1,), (0,)), ((), ())), preferred_element_type=F32)


def dot_nt(a, b):
    return lax.dot_general(a, b, (((1,), (1,)), ((), ())), preferred_element_type=F32)


def column_tiles(total, width, body):
    full = total // width
    if full > 0:

        @pl.loop(0, full)
        def _(t):
            body(pl.ds(pl.multiple_of(t * width, width), width))

    if total % width:
        body(pl.ds(full * width, total % width))


def rms_scale(values):
    return lax.rsqrt(jnp.mean(values * values, axis=-1, keepdims=True) + 1e-05)


def rms_back(values, grad, gain):
    scale = rms_scale(values)
    scaled = grad * gain
    return scale * (
        scaled - values * (scale * scale) * jnp.mean(scaled * values, axis=-1, keepdims=True)
    )


def piece_indices(shape, row_pieces):
    places = [()]
    for size in shape[:-2]:
        places = [place + (j,) for place in places for j in range(size)]
    rows = shape[-2]
    if rows % (16 * row_pieces):
        return places
    step = rows // row_pieces
    return [place + (pl.ds(j * step, step),) for place in places for j in range(row_pieces)]


class Pieces:
    def __init__(self, source, target, send, recv, device, row_pieces=2):
        self.parts = (source, target, send, recv, device)
        self.row_pieces = row_pieces

    def copy(self, source, target):
        _, _, send, recv, device = self.parts
        return pltpu.make_async_remote_copy(
            src_ref=source,
            dst_ref=target,
            send_sem=send,
            recv_sem=recv,
            device_id=device,
            device_id_type=MESH,
        )

    def start(self):
        source, target = self.parts[:2]
        for place in piece_indices(source.shape, self.row_pieces):
            if place:
                self.copy(source.at[place], target.at[place]).start()
            else:
                self.copy(source, target).start()

    def wait_send(self):
        self.copy(*self.parts[:2]).wait_send()

    def wait_recv(self):
        self.copy(*self.parts[:2]).wait_recv()


class Exchange:
    def __init__(self, chips, chip, core, group_axis):
        self.chips, self.chip, self.core = chips, chip, core
        self.axis = group_axis

    def sibling(self):
        return {self.axis: self.chip * 2 + 1 - self.core}

    def peer(self, other):
        return {self.axis: other * 2 + self.core}

    def others(self):
        return [lax.rem(self.chip + step, self.chips) for step in range(1, self.chips)]

    def barrier(self):
        flag = pltpu.get_barrier_semaphore()
        pl.semaphore_signal(flag, inc=1, device_id=self.sibling(), device_id_type=MESH)
        for other in self.others():
            pl.semaphore_signal(flag, inc=1, device_id=self.peer(other), device_id_type=MESH)
        pl.semaphore_wait(flag, self.chips)

    def to_sibling(self, source, target, send, recv):
        return Pieces(source, target, send, recv, self.sibling())

    def to_peer(self, other, source, target, send, recv):
        return Pieces(source, target, send, recv, self.peer(other))


class Scatter:
    def __init__(self, net, part, near, far, sems):
        self.net, self.part, self.near, self.far = net, part, near, far
        self.slots = None if part.shape[0] == near.shape[0] else part.shape[0]
        self.near_send, self.near_recv, self.far_send, self.far_recv = sems

    def slot(self, i):
        return i if self.slots is None else i % self.slots

    def landing(self, source, target):
        return lax.rem(source - target + self.net.chips - 1, self.net.chips)

    def near_copy(self, i):
        net = self.net
        return net.to_sibling(
            self.part.at[self.slot(i), 1 - net.core],
            self.near.at[i],
            self.near_send.at[i],
            self.near_recv.at[i],
        )

    def far_copy(self, i, other):
        net = self.net
        return net.to_peer(
            other,
            self.part.at[self.slot(i), net.core, other],
            self.far.at[i, self.landing(net.chip, other)],
            self.far_send.at[i, other],
            self.far_recv.at[i, net.chip],
        )

    def far_landing(self, i, other):
        net = self.net
        return net.to_peer(
            other,
            self.part.at[self.slot(i), net.core, other],
            self.far.at[i, self.landing(other, net.chip)],
            self.far_send.at[i, other],
            self.far_recv.at[i, other],
        )

    def start(self, i):
        self.near_copy(i).start()

    def middle(self, i):
        net = self.net
        self.near_copy(i).wait_recv()
        slot = self.slot(i)
        for other in net.others():
            total = self.part[slot, net.core, other].astype(F32) + self.near[
                i, other
            ].astype(F32)
            self.part[slot, net.core, other] = total.astype(BF16)
            self.far_copy(i, other).start()

    def finish(self, i):
        net = self.net
        slot = self.slot(i)
        total = self.part[slot, net.core, net.chip].astype(F32) + self.near[
            i, net.chip
        ].astype(F32)
        for other in net.others():
            self.far_landing(i, other).wait_recv()
            total = total + self.far[i, self.landing(other, net.chip)].astype(F32)
        return total

    def sent(self, i):
        self.near_copy(i).wait_send()
        for other in self.net.others():
            self.far_copy(i, other).wait_send()


class Gather:
    def __init__(self, net, full, sems, single=False):
        self.net, self.full, self.single = net, full, single
        self.far_send, self.far_recv, self.near_send, self.near_recv = sems

    def block(self, i, *place):
        return self.full.at[place] if self.single else self.full.at[(i, *place)]

    def far_copy(self, i, other):
        net = self.net
        block = self.block(i, net.core, net.chip)
        return net.to_peer(
            other, block, block, self.far_send.at[i, other], self.far_recv.at[i, net.chip]
        )

    def far_landing(self, i, other):
        net = self.net
        block = self.block(i, net.core, other)
        return net.to_peer(
            other, block, block, self.far_send.at[i, other], self.far_recv.at[i, other]
        )

    def near_copy(self, i):
        block = self.block(i, self.net.core)
        return self.net.to_sibling(block, block, self.near_send.at[i], self.near_recv.at[i])

    def near_landing(self, i):
        block = self.block(i, 1 - self.net.core)
        return self.net.to_sibling(block, block, self.near_send.at[i], self.near_recv.at[i])

    def start(self, i):
        for other in self.net.others():
            self.far_copy(i, other).start()

    def middle(self, i):
        for other in self.net.others():
            self.far_landing(i, other).wait_recv()
        self.near_copy(i).start()

    def finish(self, i):
        self.near_landing(i).wait_recv()

    def sent(self, i):
        for other in self.net.others():
            self.far_copy(i, other).wait_send()
        self.near_copy(i).wait_send()


STEPS = (
    ("attend", 0),
    ("attn_part", 0),
    ("attend", 2),
    ("attn_far", 0),
    ("attend", 1),
    ("attn_part", 2),
    ("norm", 0),
    ("attn_part", 1),
    ("attend", 3),
    ("attn_far", 1),
    ("attn_far", 2),
    ("attn_part", 3),
    ("rows_near", 0),
    ("units_low", 0),
    ("norm", 1),
    ("units_high", 0),
    ("unit_grads", 0),
    ("norm", 2),
    ("rows_near", 1),
    ("outputs", 0),
    ("attn_far", 3),
    ("units_far", 0),
    ("units_low", 1),
    ("units_high", 1),
    ("rows_near", 2),
    ("unit_grads", 1),
    ("norm", 3),
    ("outputs", 1),
    ("units_far", 1),
    ("residual", 0),
    ("units_low", 2),
    ("units_high", 2),
    ("rows_near", 3),
    ("unit_grads", 2),
    ("residual", 1),
    ("outputs", 2),
    ("units_low", 3),
    ("units_far", 2),
    ("back_near", 0),
    ("units_high", 3),
    ("back_near", 1),
    ("unit_grads", 3),
    ("residual", 2),
    ("attend_back", 0),
    ("units_far", 3),
    ("back_near", 2),
    ("normed_part", 0),
    ("attend_back", 1),
    ("residual", 3),
    ("normed_part", 1),
    ("normed_far", 0),
    ("attend_back", 2),
    ("normed_far", 1),
    ("back_near", 3),
    ("normed_part", 2),
    ("attend_back", 3),
    ("normed_far", 2),
    ("normed_part", 3),
    ("embed_grad", 0),
    ("outputs", 3),
    ("normed_far", 3),
    ("embed_grad", 1),
    ("token_near", 0),
    ("embed_grad", 2),
    ("token_near", 1),
    ("embed_grad", 3),
    ("token_near", 2),
    ("token_near", 3),
)


def column_of(row):
    return jnp.broadcast_to(row, (8, row.shape[1])).T[:, :1]


def text_body(
    chips,
    dp_count,
    entry_count,
    head_count,
    entry_ids,
    segments,
    cos_t,
    sin_t,
    bias_full,
    gain_one,
    gain_two,
    w_kv,
    entries_hbm,
    weights_hbm,
    token_grad,
    w_query_hbm,
    w_out_hbm,
    w_gate_hbm,
    w_up_hbm,
    w_down_hbm,
    out_part,
    embed_grad,
    pooled_own,
    token_full,
    proj,
    w_query,
    w_out,
    w_gate,
    w_up,
    w_down,
    part_a,
    near_a,
    far_a,
    part_b,
    near_b,
    far_b,
    full,
    grad_full,
    embeds_own,
    q_t,
    q_n,
    k_n,
    v_n,
    k_t,
    v_t,
    out_t,
    logs,
    bias,
    residual,
    weight_sem,
    local_sem,
    stage_sem,
    scatter_near,
    scatter_far_send,
    scatter_far_recv,
    gather_near,
    gather_far_send,
    gather_far_recv,
    grad_near,
    grad_far_send,
    grad_far_recv,
):
    me = lax.axis_index("mp")
    chip, core = me // 2, lax.rem(me, 2)
    net = Exchange(chips, chip, core, "mp")
    group = chips * 2
    chunk_rows = q_n.shape[1]
    width = embeds_own.shape[2]
    units = w_gate.shape[1]
    own_rows = embeds_own.shape[1]
    head_width = FHD * head_count
    columns = proj.shape[3]
    entry_total, entry_width = entries_hbm.shape
    owned = token_grad.shape[0]
    first_own = pl.multiple_of((core * chips + chip) * own_rows, own_rows)
    owners = group // CHUNKS if group > CHUNKS else 1

    def scatter_of(kind, part, near, far):
        return Scatter(
            net,
            part,
            near,
            far,
            (
                scatter_near.at[kind, 0],
                scatter_near.at[kind, 1],
                scatter_far_send.at[kind],
                scatter_far_recv.at[kind],
            ),
        )

    def gather_of(kind, ref):
        return Gather(
            net,
            ref,
            (
                gather_far_send.at[kind],
                gather_far_recv.at[kind],
                gather_near.at[kind, 0],
                gather_near.at[kind, 1],
            ),
        )

    attn_sum = scatter_of(0, part_a, near_a, far_a)
    mlp_sum = scatter_of(1, part_b, near_b, far_b)
    normed_sum = scatter_of(2, part_a, near_a, far_a)
    mlp_rows = gather_of(0, full)
    back_rows = gather_of(1, full)
    token_rows = gather_of(2, token_full)

    def load(k, source, target):
        return pltpu.make_async_copy(source, target, weight_sem.at[k])

    load_proj = load(1, weights_hbm.at[3], proj)
    load_query = load(2, w_query_hbm, w_query)
    load_out = load(3, w_out_hbm, w_out)
    load_units = [
        load(4, w_gate_hbm, w_gate),
        load(5, w_up_hbm, w_up),
        load(6, w_down_hbm, w_down),
    ]

    def grad_far(owner_chip, other):
        return net.to_peer(
            other,
            token_grad,
            grad_full.at[owner_chip * 2 + core],
            grad_far_send.at[other],
            grad_far_recv.at[owner_chip],
        )

    def grad_near_copy(owner_chip, owner_core):
        block = grad_full.at[owner_chip * 2 + owner_core]
        return net.to_sibling(
            block, block, grad_near.at[0, owner_chip], grad_near.at[1, owner_chip]
        )

    grad_local = pltpu.make_async_copy(token_grad, grad_full.at[me], local_sem)

    def grad_start():
        for other in net.others():
            grad_far(chip, other).start()

    def grad_middle():
        grad_local.wait()
        grad_near_copy(chip, core).start()
        for other in net.others():
            grad_far(other, other).wait_recv()
            grad_near_copy(other, core).start()

    def grad_chunk(i):
        return grad_full[i * owners : (i + 1) * owners].reshape(chunk_rows, width)

    def grad_finish(i):
        for owner in range(i * owners, (i + 1) * owners):

            @pl.when(core != owner % 2)
            def _():
                grad_near_copy(owner // 2, owner % 2).wait_recv()

    def embed(entries, pooled, embeds):
        load_entries = load(0, entries_hbm, entries)
        load_entries.start()
        for copy in (load_proj, load_query, load_out, *load_units):
            copy.start()
        grad_local.start()
        net.barrier()
        pl.when(core == 1)(grad_start)
        load_entries.wait()
        load_proj.wait()
        load_query.wait()

        @pl.loop(0, CHUNKS)
        def _(i):
            ids = entry_ids[i]
            owner = ids // entry_count
            owner_mp, owner_dp = lax.rem(owner, group), owner // group
            place = (lax.rem(owner_mp, 2) * chips + owner_mp // 2) * dp_count + owner_dp
            spots = column_of(
                (place * entry_count + lax.rem(ids, entry_count)).astype(F32)
            ).astype(jnp.int32)
            numbers = lax.broadcasted_iota(jnp.int32, (chunk_rows, entry_total), 1)
            chosen = jnp.where(numbers == spots, 1.0, 0.0).astype(BF16)
            pooled[...] = dot_nn(chosen, entries[...]).astype(BF16)
            pooled_own[i] = pooled[pl.ds(first_own, own_rows), :]
            for m, c, y in shards_of(chips):
                span = slice(m * columns, (m + 1) * columns)
                embeds[:, span] = (dot_nn(pooled[...], proj[c, y]) + bias_full[c, y]).astype(BF16)
            embeds_own[i] = embeds[pl.ds(first_own, own_rows), :]
            values = embeds[...].astype(F32)
            embeds[...] = (values * rms_scale(values) * gain_one[...]).astype(BF16)
            cosine, sine = cos_t[i], sin_t[i]

            def turned(block):
                low_half, high_half = block[: FHD // 2], block[FHD // 2 :]
                return jnp.concatenate(
                    [low_half * cosine - high_half * sine, high_half * cosine + low_half * sine],
                    axis=0,
                )

            queries = dot_nn(embeds[...], w_query[...]).T
            for h in range(head_count):
                span = slice(h * FHD, (h + 1) * FHD)
                q_t[i, span, :] = (
                    turned(queries[span]).astype(BF16).astype(F32) * FHD**-0.5
                ).astype(BF16)
            q_n[i] = q_t[i].T
            both = dot_nn(embeds[...], w_kv[...])
            keys_t = turned(both.T[:FHD]).astype(BF16)
            k_t[i] = keys_t
            k_n[i] = keys_t.T
            v_n[i] = both[:, FHD:].astype(BF16)
            v_t[i] = both.T[FHD:].astype(BF16)

        pl.when(core == 0)(grad_start)
        pl.when(core == 1)(grad_middle)

    pl.run_scoped(
        embed,
        pltpu.VMEM((entry_total, entry_width), BF16),
        pltpu.VMEM((chunk_rows, entry_width), BF16),
        pltpu.VMEM((chunk_rows, width), BF16),
    )

    def put_rows(part, slot, columns, values):
        half = chunk_rows // 2
        for k in range(2):
            for j in range(chips):
                first = k * half + j * own_rows
                part[slot, k, j, :, columns] = values[first : first + own_rows]

    def rows_of(ref, i):
        return ref[i].reshape(chunk_rows, width)

    def turned_back(sums_t):
        return sums_t.astype(BF16).T

    def make_bias(i):
        query_spots = i * chunk_rows + lax.broadcasted_iota(jnp.int32, (chunk_rows, chunk_rows), 1)
        query_segments = segments[i].astype(F32)
        for kb in range(i + 1):
            allowed = column_of(segments[kb].astype(F32)) == query_segments
            if kb == i:
                key_spots = kb * chunk_rows + lax.broadcasted_iota(
                    jnp.int32, (chunk_rows, chunk_rows), 0
                )
                allowed = allowed & (key_spots <= query_spots)
            bias[kb] = jnp.where(allowed, 0.0, FAR)

    def head_span(h):
        return pl.ds(pl.multiple_of(h * FHD, FHD), FHD)

    def layer(
        mixed,
        gate_grad,
        up_grad,
        out_stage,
        d_out_t,
        d_out_n,
        d_query_t,
        value_total,
        key_total,
    ):
        for ref in (value_total, key_total):
            ref[...] = jnp.zeros_like(ref)

        def stage_copy(i, tile):
            slot = lax.rem(tile, 2)
            columns = pl.ds(pl.multiple_of(tile * 512, 512), 512)
            return pltpu.make_async_copy(
                out_stage.at[slot], out_part.at[i, :, columns], stage_sem.at[slot]
            )

        def pair_t(ref, pair):
            return jnp.concatenate(
                [ref[head_span(pair * 2), :], ref[head_span(pair * 2 + 1), :]], axis=1
            )

        def pair_bias(kb):
            return jnp.concatenate([bias[kb], bias[kb]], axis=1)

        def attend(i):
            make_bias(i)

            @pl.loop(0, head_count // 2)
            def _(pair):
                query = pair_t(q_t.at[i], pair)
                scores = [dot_nn(k_n[kb], query) + pair_bias(kb) for kb in range(i + 1)]
                top = jnp.max(scores[0], axis=0, keepdims=True)
                for block in scores[1:]:
                    top = jnp.maximum(top, jnp.max(block, axis=0, keepdims=True))
                total = jnp.zeros_like(top)
                attended = jnp.zeros((FHD, 2 * chunk_rows), F32)
                for kb in range(i + 1):
                    weights_block = jnp.exp(scores[kb] - top)
                    total = total + jnp.sum(weights_block, axis=0, keepdims=True)
                    attended = attended + dot_nn(v_t[kb], weights_block.astype(BF16))
                logs[i, pair] = top + jnp.log(total)
                attended = (attended / total).astype(BF16)
                out_t[i, head_span(pair * 2), :] = attended[:, :chunk_rows]
                out_t[i, head_span(pair * 2 + 1), :] = attended[:, chunk_rows:]

        def attn_part(i):
            if i == CHUNKS - 1:
                load_out.wait()

            def tile(columns):
                put_rows(part_a, i, columns, turned_back(dot_nn(w_out[columns, :], out_t[i])))

            column_tiles(width, 512, tile)
            attn_sum.start(i)

        def norm(i):
            values = embeds_own[i].astype(F32) + attn_sum.finish(i)
            residual[i] = values
            full[i, core, chip] = (values * rms_scale(values) * gain_two[...]).astype(BF16)
            mlp_rows.start(i)

        def unit_tile(i, columns):
            rows = rows_of(full, i)
            gate_pre = dot_nn(rows, w_gate[:, columns])
            up_pre = dot_nn(rows, w_up[:, columns])
            act_grad = dot_nn(grad_chunk(i), w_down[:, columns])
            inverse = 1.0 / (1.0 + jnp.exp(-gate_pre))
            silu = gate_pre * inverse
            mixed[columns, :] = turned_back(silu * up_pre)
            up_grad[columns, :] = turned_back(act_grad * silu)
            slope = inverse * (1.0 + gate_pre * (1.0 - inverse))
            gate_grad[columns, :] = turned_back(act_grad * up_pre * slope)

        tile_width = 512 if units >= 1024 else 256
        tiles = units // tile_width
        middle_tile = (tiles + 1) // 2

        def unit_tiles(i, first, last):
            @pl.loop(first, last)
            def _(t):
                unit_tile(i, pl.ds(pl.multiple_of(t * tile_width, tile_width), tile_width))

        def units_low(i):
            if i == CHUNKS - 1:
                pl.when(core == 0)(grad_middle)
                for copy in load_units:
                    copy.wait()
            grad_finish(i)
            mlp_rows.finish(i)
            unit_tiles(i, 0, middle_tile)

        def units_high(i):
            unit_tiles(i, middle_tile, tiles)
            if units % tile_width:
                unit_tile(i, pl.ds(tiles * tile_width, units % tile_width))
            mlp_rows.sent(i)

        def unit_grads(i):
            if i + 2 < CHUNKS:
                mlp_sum.sent(i + 2)

            def tile(columns):
                put_rows(
                    part_b,
                    i % 2,
                    columns,
                    turned_back(
                        dot_nn(w_gate[columns, :], gate_grad[...])
                        + dot_nn(w_up[columns, :], up_grad[...])
                    ),
                )

            column_tiles(width, 512, tile)
            mlp_sum.start(i)

        def outputs(i):
            @pl.loop(0, width // 512)
            def _(t):
                columns = pl.ds(pl.multiple_of(t * 512, 512), 512)
                slot = lax.rem(t, 2)
                tile = turned_back(dot_nn(w_down[columns, :], mixed[...]))
                if i == CHUNKS - 1:
                    pl.when(t >= 2)(lambda: stage_copy(i, t).wait())
                else:
                    stage_copy(i, t).wait()
                out_stage[slot] = tile
                own = pl.ds(first_own, own_rows)
                out_stage[slot, own, :] = (
                    out_stage[slot, own, :].astype(F32) + residual[i, :, columns]
                ).astype(BF16)
                stage_copy(i, t).start()

        def residual_back(i):
            grad = mlp_sum.finish(i)
            block = i * owners + first_own // owned
            start = pl.multiple_of(lax.rem(first_own, owned), own_rows)
            own_grad = grad_full[block, pl.ds(start, own_rows), :].astype(F32)
            values = own_grad + rms_back(residual[i], grad, gain_two[...])
            full[i, core, chip] = values.astype(BF16)
            back_rows.start(i)

        def attend_back(i):
            back_rows.finish(i)
            attended_grad = dot_nn(rows_of(full, i), w_out[...]).astype(BF16)
            d_out_n[...] = attended_grad
            d_out_t[...] = attended_grad.T
            make_bias(i)
            cosine, sine = cos_t[i], sin_t[i]

            first_head = (
                lax.broadcasted_iota(jnp.int32, (chunk_rows, 2 * FHD), 1) < FHD
            )

            def stacked(rows):
                wide = rows.astype(F32)
                return jnp.concatenate(
                    [jnp.where(first_head, wide, 0.0), jnp.where(first_head, 0.0, wide)], axis=0
                ).astype(BF16)

            @pl.loop(0, head_count // 2)
            def _(pair):
                pair_span = pl.ds(pl.multiple_of(pair * 2 * FHD, 2 * FHD), 2 * FHD)
                query_rows = stacked(q_n[i, :, pair_span])
                grad_rows = stacked(d_out_n[:, pair_span])
                query = pair_t(q_t.at[i], pair)
                grad = pair_t(d_out_t, pair)
                log_row = logs[i, pair]
                centre = jnp.sum(
                    grad.astype(F32) * pair_t(out_t.at[i], pair).astype(F32),
                    axis=0,
                    keepdims=True,
                )
                query_grad = jnp.zeros((FHD, 2 * chunk_rows), F32)
                for kb in range(i + 1):
                    probs = jnp.exp(dot_nn(k_n[kb], query) + pair_bias(kb) - log_row)
                    value_total[kb] += dot_nn(probs.astype(BF16), grad_rows)
                    score_grad = (probs * (dot_nn(v_n[kb], grad) - centre)).astype(BF16)
                    key_total[kb] += dot_nn(score_grad, query_rows)
                    query_grad = query_grad + dot_nn(k_t[kb], score_grad)
                query_grad = query_grad * (FHD**-0.5)
                for odd in range(2):
                    lanes = slice(odd * chunk_rows, (odd + 1) * chunk_rows)
                    low_half = query_grad[: FHD // 2, lanes]
                    high_half = query_grad[FHD // 2 :, lanes]
                    d_query_t[head_span(pair * 2 + odd), :] = jnp.concatenate(
                        [
                            low_half * cosine + high_half * sine,
                            high_half * cosine - low_half * sine,
                        ],
                        axis=0,
                    ).astype(BF16)

        def normed_part(i):
            attn_sum.sent(i)
            key_grad = (key_total[i][:, :FHD] + key_total[i][:, FHD:]).T
            cosine, sine = cos_t[i], sin_t[i]
            low_half, high_half = key_grad[: FHD // 2], key_grad[FHD // 2 :]
            value_grad = (value_total[i][:, :FHD] + value_total[i][:, FHD:]).T
            both = jnp.concatenate(
                [
                    low_half * cosine + high_half * sine,
                    high_half * cosine - low_half * sine,
                    value_grad,
                ],
                axis=0,
            )
            both = both.astype(BF16)

            def tile(columns):
                put_rows(
                    part_a,
                    i,
                    columns,
                    turned_back(
                        dot_nn(w_query[columns, :], d_query_t[...])
                        + dot_nn(w_kv[columns, :], both)
                    ),
                )

            column_tiles(width, 512, tile)
            normed_sum.start(i)

        def embed_back(i):
            grad = normed_sum.finish(i)
            kept = full[i, core, chip].astype(F32)
            values = kept + rms_back(embeds_own[i].astype(F32), grad, gain_one[...])
            embed_grad[i] = values.astype(BF16)
            total = jnp.zeros((own_rows, entry_width), F32)
            for m, c, y in shards_of(chips):
                total = total + dot_nt(
                    embed_grad[i, :, m * columns : (m + 1) * columns], proj[c, y]
                )
            token_full[i, core, chip] = total.astype(BF16)
            token_rows.start(i)

        stages = {
            "attend": attend,
            "attn_part": attn_part,
            "attn_far": attn_sum.middle,
            "norm": norm,
            "rows_near": mlp_rows.middle,
            "units_low": units_low,
            "units_high": units_high,
            "unit_grads": unit_grads,
            "outputs": outputs,
            "units_far": mlp_sum.middle,
            "residual": residual_back,
            "back_near": back_rows.middle,
            "attend_back": attend_back,
            "normed_part": normed_part,
            "normed_far": normed_sum.middle,
            "embed_grad": embed_back,
            "token_near": token_rows.middle,
        }
        for name, turn in STEPS:
            stages[name](CHUNKS - 1 - turn)

        for tile in range(2):
            stage_copy(0, tile).wait()

    lines = (units, chunk_rows)
    keys = (CHUNKS, chunk_rows, 2 * FHD)
    pl.run_scoped(
        layer,
        pltpu.VMEM(lines, BF16),
        pltpu.VMEM(lines, BF16),
        pltpu.VMEM(lines, BF16),
        pltpu.VMEM((2, chunk_rows, 512), BF16),
        pltpu.VMEM((head_width, chunk_rows), BF16),
        pltpu.VMEM((chunk_rows, head_width), BF16),
        pltpu.VMEM((head_width, chunk_rows), BF16),
        pltpu.VMEM(keys, F32),
        pltpu.VMEM(keys, F32),
    )

    @pl.loop(0, CHUNKS)
    def _(i):
        token_rows.finish(i)
        token_rows.sent(i)
        normed_sum.sent(i)
        back_rows.sent(i)

    for i in range(2):
        mlp_sum.sent(i)
    for other in net.others():
        grad_far(chip, other).wait_send()
    for owner_chip in range(chips):
        grad_near_copy(owner_chip, core).wait_send()


def text_layer(
    group,
    dp_count,
    entry_count,
    entry_ids,
    segments,
    cos_t,
    sin_t,
    bias_full,
    gain_one,
    gain_two,
    w_kv,
    entries,
    weights,
    token_grad,
    w_query,
    w_out,
    w_gate,
    w_up,
    w_down,
):
    chips = group // 2
    chunks, _, chunk_rows = entry_ids.shape
    own_rows = chunk_rows // group
    owned, width = token_grad.shape
    head_width = w_query.shape[1]
    head_count = head_width // FHD
    entry_width = entries.shape[1]
    vmem = pl.BlockSpec(memory_space=pltpu.VMEM)
    hbm = pl.BlockSpec(memory_space=pl.ANY)
    dma = pltpu.SemaphoreType.DMA

    def low(*shape):
        return pltpu.VMEM(shape, BF16)

    return pl.pallas_call(
        partial(text_body, chips, dp_count, entry_count, head_count),
        out_shape=(
            jax.ShapeDtypeStruct((chunks, chunk_rows, width), BF16),
            jax.ShapeDtypeStruct((chunks, own_rows, width), BF16),
            jax.ShapeDtypeStruct((chunks, own_rows, entry_width), BF16),
            jax.ShapeDtypeStruct((chunks, 2, chips, own_rows, entry_width), BF16),
        ),
        in_specs=[vmem] * 8 + [hbm] * 8,
        out_specs=(hbm, vmem, vmem, vmem),
        scratch_shapes=[
            low(*weights.shape[1:]),
            low(*w_query.shape),
            low(*w_out.shape),
            low(*w_gate.shape),
            low(*w_up.shape),
            low(*w_down.shape),
            low(chunks, 2, chips, own_rows, width),
            low(chunks, chips, own_rows, width),
            low(chunks, chips - 1, own_rows, width),
            low(2, 2, chips, own_rows, width),
            low(chunks, chips, own_rows, width),
            low(chunks, chips - 1, own_rows, width),
            low(chunks, 2, chips, own_rows, width),
            low(group, owned, width),
            low(chunks, own_rows, width),
            low(chunks, head_width, chunk_rows),
            low(chunks, chunk_rows, head_width),
            low(chunks, chunk_rows, FHD),
            low(chunks, chunk_rows, FHD),
            low(chunks, FHD, chunk_rows),
            low(chunks, FHD, chunk_rows),
            low(chunks, head_width, chunk_rows),
            pltpu.VMEM((chunks, head_count // 2, 1, 2 * chunk_rows), F32),
            pltpu.VMEM((chunks, chunk_rows, chunk_rows), F32),
            pltpu.VMEM((chunks, own_rows, width), F32),
            dma((7,)),
            dma,
            dma((2,)),
            dma((3, 2, chunks)),
            dma((3, chunks, chips)),
            dma((3, chunks, chips)),
            dma((3, 2, chunks)),
            dma((3, chunks, chips)),
            dma((3, chunks, chips)),
            dma((2, chips)),
            dma((chips,)),
            dma((chips,)),
        ],
        compiler_params=pltpu.CompilerParams(
            collective_id=0, has_side_effects=True, vmem_limit_bytes=65280 * 1024
        ),
        cost_estimate=pl.CostEstimate(
            flops=90 * 10**9, bytes_accessed=40 * 10**6, transcendentals=20 * 10**6
        ),
    )(
        entry_ids,
        segments,
        cos_t,
        sin_t,
        bias_full,
        gain_one,
        gain_two,
        w_kv,
        entries,
        weights,
        token_grad,
        w_query,
        w_out,
        w_gate,
        w_up,
        w_down,
    )


def norm_parts(values):
    average = jnp.mean(values, axis=-1, keepdims=True)
    centred = values - average
    scale = lax.rsqrt(jnp.mean(centred * centred, axis=-1, keepdims=True) + 1e-05)
    return centred * scale, scale


def norm_back(values, grad, gain):
    unit, scale = norm_parts(values)
    scaled = grad * gain
    back = scale * (
        scaled
        - jnp.mean(scaled, axis=-1, keepdims=True)
        - unit * jnp.mean(scaled * unit, axis=-1, keepdims=True)
    )
    return (
        back,
        jnp.sum(grad * unit, axis=0, keepdims=True),
        jnp.sum(grad, axis=0, keepdims=True),
    )


def gelu_parts(values):
    root = math.sqrt(2.0 / math.pi)
    squared = values * values
    bent = jnp.tanh(root * values * (1.0 + 0.044715 * squared))
    half = 0.5 * (1.0 + bent)
    slope = half + 0.5 * values * (1.0 - bent * bent) * root * (1.0 + 3 * 0.044715 * squared)
    return values * half, slope


def pool_matrix(counts_col, entries, rows):
    entry = lax.broadcasted_iota(jnp.int32, (entries, rows), 0)
    row = lax.broadcasted_iota(jnp.int32, (entries, rows), 1)
    slots = rows // entries
    inside = (row // slots == entry) & (lax.rem(row, slots).astype(F32) < counts_col)
    return jnp.where(inside, 1.0, 0.0)


def spread_matrix(counts_row, entries, rows):
    row = lax.broadcasted_iota(jnp.int32, (rows, entries), 0)
    entry = lax.broadcasted_iota(jnp.int32, (rows, entries), 1)
    slots = rows // entries
    inside = (row // slots == entry) & (lax.rem(row, slots).astype(F32) < counts_row)
    return jnp.where(inside, 1.0, 0.0)


def slot_bias(valid_col, slots):
    rows = valid_col.shape[0]
    key = lax.broadcasted_iota(jnp.int32, (rows, rows), 0)
    query = lax.broadcasted_iota(jnp.int32, (rows, rows), 1)
    return jnp.where((key // slots == query // slots) & (valid_col > 0.5), 0.0, FAR)


ROW_BLOCK = 128


def fill_diagonal(ref, columns_t, heads):
    for h in range(heads):
        span = slice(h * HD, (h + 1) * HD)
        ref[span, h * ROW_BLOCK : (h + 1) * ROW_BLOCK] = columns_t[span, :]


def pair_blocks(both):
    return jnp.concatenate([both[:HD, :ROW_BLOCK], both[HD:, ROW_BLOCK:]], axis=0)


def tiled(block, count):
    return jnp.concatenate([block] * count, axis=1)


def shards_of(chips):
    return [(y * 2 + c, c, y) for y in range(chips) for c in range(2)]


def each_shard(chips, columns, body):
    @pl.loop(0, 2)
    def _(c):
        @pl.loop(0, chips)
        def _(y):
            first = pl.multiple_of((y * 2 + c) * columns, columns)
            body(c, y, pl.ds(first, columns))


def hyper_body(
    chips,
    dp_count,
    pieces,
    counts_all,
    gain_one,
    shift_one,
    gain_two,
    shift_two,
    w_query,
    w_key,
    w_value,
    w_out,
    bias_own,
    w_up_hbm,
    w_down_hbm,
    w_proj_hbm,
    text_key,
    text_value,
    entries,
    weights_out,
    attn_in,
    q_n,
    k_n,
    v_n,
    attended,
    logs,
    residual,
    ffn_in,
    counts_col,
    counts_row,
    bias_full,
    key_value,
    full,
    q_t,
    v_t,
    out_t,
    bias,
    diagonal,
    hidden,
    counts_scratch,
    local_sem,
    store_sem,
    far_send,
    far_recv,
    x_send,
    x_recv,
    near_send,
    near_recv,
    z_send,
    z_recv,
    mate_send,
    mate_recv,
    y_send,
    y_recv,
    last_send,
    last_recv,
    bias_far_send,
    bias_far_recv,
    bias_near,
    key_wide,
    value_wide,
    text_sem,
):
    me = lax.axis_index("mp")
    dp = lax.axis_index("dp")
    chip, core = me // 2, lax.rem(me, 2)
    net = Exchange(chips, chip, core, "mp")
    side = lax.rem(dp, 2)
    mate = dp + 1 - 2 * side
    spot, spots = dp // 2, dp_count // 2
    kinds, _, _, width, columns = full.shape
    sources = (None, w_up_hbm, w_down_hbm, w_proj_hbm)
    rows = pieces.shape[0]
    entry_count = counts_col.shape[0]
    slots = rows // entry_count
    head_columns = columns // 4
    half = width // 2
    heads = width // HD

    flag = pltpu.get_barrier_semaphore()
    pl.semaphore_signal(flag, inc=1, device_id=net.sibling(), device_id_type=MESH)
    for other in net.others():
        pl.semaphore_signal(flag, inc=1, device_id=net.peer(other), device_id_type=MESH)

    pl.semaphore_signal(flag, inc=1, device_id={"dp": mate}, device_id_type=MESH)

    @pl.loop(1, spots)
    def _(j):
        target = lax.rem(spot + j, spots) * 2 + side
        pl.semaphore_signal(flag, inc=1, device_id={"dp": target}, device_id_type=MESH)

    local = [
        pltpu.make_async_copy(sources[k], full.at[k, core, chip], local_sem.at[k - 1])
        for k in range(1, kinds)
    ]
    for copy in local:
        copy.start()
    for j, source in enumerate((w_query, w_key, w_value, w_out)):
        full[0, core, chip, :, j * head_columns : (j + 1) * head_columns] = source[...]
    bias_full[core, chip] = bias_own[...]
    pl.semaphore_wait(flag, chips + spots)

    def rows_half(which):
        return pl.ds(pl.multiple_of(which * half, half), half)

    def far_copy(k, other):
        return net.to_peer(
            other,
            sources[k].at[rows_half(side)] if k else full.at[0, core, chip, rows_half(side)],
            full.at[k, core, chip, rows_half(side)],
            far_send.at[k, other],
            far_recv.at[k, chip],
        )

    def far_landing(k, other):
        block = full.at[k, core, other, rows_half(side)]
        return net.to_peer(other, block, block, far_send.at[k, other], far_recv.at[k, other])

    def x_copy(k, other, which):
        block = full.at[k, core, other, rows_half(which)]
        return pltpu.make_async_remote_copy(
            src_ref=block,
            dst_ref=block,
            send_sem=x_send.at[k, other],
            recv_sem=x_recv.at[k, other],
            device_id={"dp": mate},
            device_id_type=MESH,
        )

    def near_copy(k, which):
        block = full.at[k, which]
        return net.to_sibling(block, block, near_send.at[k], near_recv.at[k])

    def far_middle(k):
        for other in net.others():
            far_landing(k, other).wait_recv()
            x_copy(k, other, side).start()

    def x_middle(k):
        for other in net.others():
            x_copy(k, other, 1 - side).wait_recv()
        if k:
            local[k - 1].wait()
        near_copy(k, core).start()

    def store(k):
        return pltpu.make_async_copy(full.at[k], weights_out.at[k], store_sem.at[k])

    def near_finish(k):
        near_copy(k, 1 - core).wait_recv()
        store(k).start()

    bias_rows = Gather(
        net, bias_full, (bias_far_send, bias_far_recv, bias_near.at[0], bias_near.at[1]), True
    )
    def far_start(k):
        for other in net.others():
            far_copy(k, other).start()

    far_start(0)
    bias_rows.start(0)
    text_copies = (
        pltpu.make_async_copy(text_key, key_wide, text_sem.at[0]),
        pltpu.make_async_copy(text_value, value_wide, text_sem.at[1]),
    )
    for copy in text_copies:
        copy.start()
    counts_scratch[...] = column_of(counts_all[...].astype(F32))
    own_counts = counts_scratch[pl.ds(pl.multiple_of(me * entry_count, entry_count), entry_count)]
    counts_col[...] = own_counts
    counts_row[...] = jnp.broadcast_to(own_counts, (entry_count, 128)).T[:1]

    values = pieces[...].astype(F32)
    attn_in[...] = (norm_parts(values)[0] * gain_one[...] + shift_one[...]).astype(BF16)
    blocks = rows // ROW_BLOCK
    valid = jnp.sum(spread_matrix(counts_row[...], entry_count, rows), axis=1, keepdims=True)
    for b in range(blocks):
        bias[b] = slot_bias(valid[b * ROW_BLOCK : (b + 1) * ROW_BLOCK], slots)

    for copy in text_copies:
        copy.wait()
    text_heads = QHEADS // (2 * chips)
    for j in range(KVHEADS):

        @pl.when(me * text_heads // (QHEADS // KVHEADS) == j)
        def _():
            key_value[:, :FHD] = key_wide[:, j * FHD : (j + 1) * FHD]
            key_value[:, FHD:] = value_wide[:, j * FHD : (j + 1) * FHD]

    far_middle(0)
    far_start(1)
    bias_rows.middle(0)
    far_middle(1)
    far_start(2)
    x_middle(0)
    near_finish(0)
    for m, c, y in shards_of(chips):
        span = slice(m * head_columns, (m + 1) * head_columns)
        projected = dot_nn(attn_in[...], full[0, c, y, :, : 3 * head_columns])
        q_n[:, span] = (projected[:, :head_columns].astype(BF16).astype(F32) * HD**-0.5).astype(
            BF16
        )
        k_n[:, span] = projected[:, head_columns : 2 * head_columns].astype(BF16)
        v_n[:, span] = projected[:, 2 * head_columns :].astype(BF16)
    far_middle(2)
    far_start(3)
    x_middle(1)
    for b in range(blocks):
        block_rows = slice(b * ROW_BLOCK, (b + 1) * ROW_BLOCK)
        q_t[b] = q_n[block_rows, :].T
        v_t[b] = v_n[block_rows, :].T

    diagonal[...] = jnp.zeros_like(diagonal)

    def attend_block(b):
        block_rows = pl.ds(pl.multiple_of(b * ROW_BLOCK, ROW_BLOCK), ROW_BLOCK)
        fill_diagonal(diagonal, q_t[b], heads)
        scores = dot_nn(k_n[block_rows, :], diagonal[...]) + tiled(bias[b], heads)
        top = jnp.max(scores, axis=0, keepdims=True)
        weights = jnp.exp(scores - top)
        total = jnp.sum(weights, axis=0, keepdims=True)
        logs[b] = top + jnp.log(total)
        weights = (weights / total).astype(BF16)
        for pair in range(heads // 2):
            span = slice(pair * 2 * HD, (pair + 1) * 2 * HD)
            lanes = slice(pair * 2 * ROW_BLOCK, (pair + 1) * 2 * ROW_BLOCK)
            both = dot_nn(v_t[b, span, :], weights[:, lanes])
            out_t[b, span, :] = pair_blocks(both).astype(BF16)

    pl.loop(0, blocks // 2)(attend_block)
    far_middle(3)
    x_middle(2)
    pl.loop(blocks // 2, blocks)(attend_block)
    for b in range(blocks):
        attended[b * ROW_BLOCK : (b + 1) * ROW_BLOCK, :] = out_t[b].T
    total = values
    for m, c, y in shards_of(chips):
        span = slice(m * head_columns, (m + 1) * head_columns)
        total = total + dot_nt(attended[:, span], full[0, c, y, :, 3 * head_columns :])
    residual[...] = total
    ffn_in[...] = (norm_parts(total)[0] * gain_two[...] + shift_two[...]).astype(BF16)
    near_finish(1)
    x_middle(3)
    pool = pool_matrix(counts_col[...], entry_count, rows).astype(BF16)

    def up_shard(c, y, span):
        act = gelu_parts(dot_nn(ffn_in[...], full[1, c, y]))[0]
        hidden[:, span] = dot_nn(pool, act.astype(BF16)).astype(BF16)

    each_shard(chips, columns, up_shard)
    near_finish(2)
    pooled = jnp.sum(
        (residual[...] * valid).reshape(entry_count, slots, width), axis=1
    )
    for m, c, y in shards_of(chips):
        pooled = pooled + dot_nt(hidden[:, m * columns : (m + 1) * columns], full[2, c, y])
    entries[core, chip, dp] = (pooled / counts_col[...]).astype(BF16)

    def z_copy(target, owner):
        piece = entries.at[core, chip, owner * 2 + side]
        return pltpu.make_async_remote_copy(
            src_ref=piece,
            dst_ref=piece,
            send_sem=z_send.at[target],
            recv_sem=z_recv.at[owner],
            device_id={"dp": target * 2 + side},
            device_id_type=MESH,
        )

    def mate_copy(owner, which):
        piece = entries.at[core, chip, owner * 2 + which]
        return pltpu.make_async_remote_copy(
            src_ref=piece,
            dst_ref=piece,
            send_sem=mate_send.at[owner],
            recv_sem=mate_recv.at[owner],
            device_id={"dp": mate},
            device_id_type=MESH,
        )

    def y_copy(other, owner, block):
        piece = entries.at[core, owner, block]
        return net.to_peer(
            other, piece, piece, y_send.at[other, block], y_recv.at[owner, block]
        )

    def y_start(block):
        for other in net.others():
            y_copy(other, chip, block).start()

    @pl.loop(1, spots)
    def _(j):
        z_copy(lax.rem(spot + j, spots), spot).start()

    mate_copy(spot, side).start()
    y_start(dp)
    near_finish(3)
    bias_rows.finish(0)

    @pl.loop(1, spots)
    def _(j):
        source = lax.rem(spot + spots - j, spots)
        z_copy(source, source).wait_recv()
        mate_copy(source, side).start()
        y_start(source * 2 + side)

    @pl.loop(0, spots)
    def _(j):
        source = lax.rem(spot + spots - j, spots)
        mate_copy(source, 1 - side).wait_recv()
        y_start(source * 2 + 1 - side)

    def last_copy(part, c, owner):
        piece = entries.at[c, owner]
        return net.to_sibling(piece, piece, last_send.at[part], last_recv.at[owner])

    last_copy(chip, core, chip).start()
    for other in net.others():

        @pl.loop(0, dp_count)
        def _(block):
            y_copy(other, other, block).wait_recv()

        last_copy(other, core, other).start()
    last_copy(chip, 1 - core, chip).wait_recv()
    for other in net.others():
        last_copy(other, 1 - core, other).wait_recv()

    bias_rows.sent(0)
    for k in range(kinds):
        store(k).wait()
        near_copy(k, core).wait_send()
        for other in net.others():
            far_copy(k, other).wait_send()
            x_copy(k, other, side).wait_send()

    @pl.loop(1, spots)
    def _(j):
        z_copy(lax.rem(spot + j, spots), spot).wait_send()

    @pl.loop(0, spots)
    def _(j):
        mate_copy(j, side).wait_send()

    last_copy(chip, core, chip).wait_send()
    for other in net.others():
        last_copy(other, core, other).wait_send()

        @pl.loop(0, dp_count)
        def _(block):
            y_copy(other, chip, block).wait_send()


def hyper_forward(
    group,
    dp_count,
    pieces,
    counts,
    gain_one,
    shift_one,
    gain_two,
    shift_two,
    head_weights,
    bias_own,
    unit_weights,
    text_key,
    text_value,
):
    chips = group // 2
    rows, width = pieces.shape
    columns = unit_weights[0].shape[1]
    kinds = 4
    entry_count = counts.shape[1] // group
    heads = width // HD
    blocks = rows // ROW_BLOCK
    vmem = pl.BlockSpec(memory_space=pltpu.VMEM)
    hbm = pl.BlockSpec(memory_space=pl.ANY)
    row_shape = jax.ShapeDtypeStruct((rows, width), BF16)
    dma = pltpu.SemaphoreType.DMA
    return pl.pallas_call(
        partial(hyper_body, chips, dp_count),
        out_shape=(
            jax.ShapeDtypeStruct((2, chips, dp_count, entry_count, width), BF16),
            jax.ShapeDtypeStruct((kinds, 2, chips, width, columns), BF16),
            row_shape,
            row_shape,
            row_shape,
            row_shape,
            row_shape,
            jax.ShapeDtypeStruct((blocks, 1, heads * ROW_BLOCK), F32),
            jax.ShapeDtypeStruct((rows, width), F32),
            row_shape,
            jax.ShapeDtypeStruct((entry_count, 1), F32),
            jax.ShapeDtypeStruct((1, entry_count), F32),
            jax.ShapeDtypeStruct((2, chips, 1, columns), F32),
            jax.ShapeDtypeStruct((text_key.shape[0], 2 * FHD), BF16),
        ),
        in_specs=[vmem] * 11 + [hbm] * 5,
        out_specs=(vmem, hbm) + (vmem,) * 12,
        scratch_shapes=[
            pltpu.VMEM((kinds, 2, chips, width, columns), BF16),
            pltpu.VMEM((blocks, width, ROW_BLOCK), BF16),
            pltpu.VMEM((blocks, width, ROW_BLOCK), BF16),
            pltpu.VMEM((blocks, width, ROW_BLOCK), BF16),
            pltpu.VMEM((blocks, ROW_BLOCK, ROW_BLOCK), F32),
            pltpu.VMEM((width, heads * ROW_BLOCK), BF16),
            pltpu.VMEM((entry_count, columns * group), BF16),
            pltpu.VMEM((counts.shape[1], 1), F32),
            dma((kinds - 1,)),
            dma((kinds,)),
            dma((kinds, chips)),
            dma((kinds, chips)),
            dma((kinds, chips)),
            dma((kinds, chips)),
            dma((kinds,)),
            dma((kinds,)),
            dma((dp_count // 2,)),
            dma((dp_count // 2,)),
            dma((dp_count // 2,)),
            dma((dp_count // 2,)),
            dma((chips, dp_count)),
            dma((chips, dp_count)),
            dma((chips,)),
            dma((chips,)),
            dma((1, chips)),
            dma((1, chips)),
            dma((2, 1)),
            pltpu.VMEM(text_key.shape, BF16),
            pltpu.VMEM(text_value.shape, BF16),
            dma((2,)),
        ],
        compiler_params=pltpu.CompilerParams(
            collective_id=1, has_side_effects=True, vmem_limit_bytes=60 * 1024 * 1024
        ),
        cost_estimate=pl.CostEstimate(
            flops=60 * 10**9, bytes_accessed=20 * 10**6, transcendentals=5 * 10**6
        ),
    )(
        pieces,
        counts,
        gain_one,
        shift_one,
        gain_two,
        shift_two,
        *head_weights,
        bias_own,
        *unit_weights,
        text_key,
        text_value,
    )


class Total:
    def __init__(self, net, dp, dp_count, scatter, mine, x_land, z_land, final, sems):
        self.net, self.scatter, self.mine = net, scatter, mine
        self.x_land, self.z_land, self.final = x_land, z_land, final
        self.x_send, self.x_recv, self.z_send, self.z_recv = sems[:4]
        self.g_send, self.g_recv, self.l_send, self.l_recv = sems[4:]
        self.side = lax.rem(dp, 2)
        self.spot = dp // 2
        self.mate = dp + 1 - 2 * self.side
        self.spots = dp_count // 2

    def remote(self, source, target, send, recv, device):
        return Pieces(source, target, send, recv, {"dp": device}, 1)

    def x_copy(self, k):
        return self.remote(
            self.mine.at[k, 1 - self.side],
            self.x_land.at[k],
            self.x_send.at[k],
            self.x_recv.at[k],
            self.mate,
        )

    def z_copy(self, k, spot, slot):
        return self.remote(
            self.mine.at[k, self.side, spot],
            self.z_land.at[k, slot],
            self.z_send.at[k, spot],
            self.z_recv.at[k, slot],
            spot * 2 + self.side,
        )

    def g_copy(self, k, spot, owner):
        block = self.final.at[k, self.side, owner]
        return self.remote(
            block, block, self.g_send.at[k, spot], self.g_recv.at[k, owner], spot * 2 + self.side
        )

    def l_copy(self, k, side):
        block = self.final.at[k, side]
        return self.remote(block, block, self.l_send.at[k], self.l_recv.at[k], self.mate)

    def each_spot(self, body):
        if self.spots > 1:

            @pl.loop(1, self.spots)
            def _(j):
                body(lax.rem(self.spot + j, self.spots))

    def start(self, k):
        self.scatter.start(k)

    def near_middle(self, k):
        self.scatter.middle(k)

    def far_middle(self, k):
        total = self.scatter.finish(k)
        self.mine[k] = total.astype(BF16).reshape(self.mine.shape[1:])
        self.x_copy(k).start()

    def x_middle(self, k):
        self.x_copy(k).wait_recv()
        block = self.mine[k, self.side].astype(F32) + self.x_land[k].astype(F32)
        self.mine[k, self.side] = block.astype(BF16)
        self.each_spot(lambda spot: self.z_copy(k, spot, self.spot).start())

    def z_middle(self, k):
        def add(spot):
            self.z_copy(k, spot, spot).wait_recv()

        self.each_spot(add)
        total = self.mine[k, self.side, self.spot].astype(F32)
        for j in range(1, self.spots):
            spot = lax.rem(self.spot + j, self.spots)
            total = total + self.z_land[k, spot].astype(F32)
        self.final[k, self.side, self.spot] = total.astype(BF16)
        self.each_spot(lambda spot: self.g_copy(k, spot, self.spot).start())

    def g_middle(self, k):
        self.each_spot(lambda spot: self.g_copy(k, spot, spot).wait_recv())
        self.l_copy(k, self.side).start()

    def finish(self, k):
        self.l_copy(k, 1 - self.side).wait_recv()

    def sent(self, k):
        self.scatter.sent(k)
        self.x_copy(k).wait_send()
        self.each_spot(lambda spot: self.z_copy(k, spot, self.spot).wait_send())
        self.each_spot(lambda spot: self.g_copy(k, spot, self.spot).wait_send())
        self.l_copy(k, self.side).wait_send()


PARTS = 8


def back_body(
    chips,
    dp_count,
    embed_rows,
    pooled_own,
    token_rows,
    token_row,
    pieces,
    counts_col,
    counts_row,
    gain_one,
    gain_two,
    attn_in,
    q_n,
    k_n,
    v_n,
    attended,
    logs,
    residual,
    ffn_in,
    weights_hbm,
    out_part,
    pieces_grad,
    final,
    small_total,
    text_out,
    weights,
    part,
    near,
    far,
    mine,
    x_land,
    z_land,
    entry_part,
    entry_land,
    hidden,
    slopes,
    ffn_t,
    row_total,
    d_out_n,
    d_query,
    d_key,
    d_value,
    q_t,
    out_t,
    d_out_t,
    k_t,
    d_query_t,
    bias,
    query_wide,
    grad_wide,
    small_near,
    small_far,
    small_dp,
    small_part,
    out_own,
    out_near,
    out_far,
    weight_sem,
    out_local,
    out_near_sem,
    out_far_send,
    out_far_recv,
    entry_send,
    entry_recv,
    scatter_near,
    scatter_far_send,
    scatter_far_recv,
    x_sem,
    z_send,
    z_recv,
    g_send,
    g_recv,
    l_sem,
    small_sem,
    small_far_send,
    small_far_recv,
    small_dp_send,
    small_dp_recv,
):
    me = lax.axis_index("mp")
    dp = lax.axis_index("dp")
    group = chips * 2
    chip, core = me // 2, lax.rem(me, 2)
    net = Exchange(chips, chip, core, "mp")
    rows, width = pieces.shape
    entry_count = counts_col.shape[0]
    slots = rows // entry_count
    columns = weights.shape[4]
    half_columns = columns // 2
    head_columns = columns // 4
    heads = width // HD
    blocks = rows // ROW_BLOCK
    total_sum = Total(
        net,
        dp,
        dp_count,
        Scatter(
            net,
            part,
            near,
            far,
            (scatter_near.at[0], scatter_near.at[1], scatter_far_send, scatter_far_recv),
        ),
        mine,
        x_land,
        z_land,
        final,
        (x_sem.at[0], x_sem.at[1], z_send, z_recv, g_send, g_recv, l_sem.at[0], l_sem.at[1]),
    )
    stages = (
        total_sum.near_middle,
        total_sum.far_middle,
        total_sum.x_middle,
        total_sum.z_middle,
        total_sum.g_middle,
        total_sum.finish,
    )

    def run(step):
        for offset, stage in enumerate(stages):
            if 0 <= step - offset < PARTS:
                stage(step - offset)

    flag = pltpu.get_barrier_semaphore()
    pl.semaphore_signal(flag, inc=1, device_id=net.sibling(), device_id_type=MESH)
    for other in net.others():
        pl.semaphore_signal(flag, inc=1, device_id=net.peer(other), device_id_type=MESH)

    def each_dp(body):
        @pl.loop(1, dp_count)
        def _(j):
            body(lax.rem(dp + j, dp_count))

    each_dp(
        lambda target: pl.semaphore_signal(
            flag, inc=1, device_id={"dp": target}, device_id_type=MESH
        )
    )
    loads = [
        pltpu.make_async_copy(weights_hbm.at[k], weights.at[k], weight_sem.at[k])
        for k in (1, 2, 0)
    ]
    for copy in loads:
        copy.start()
    out_copies = [
        pltpu.make_async_copy(out_part.at[y * 2 + core], out_own.at[y], out_local.at[y])
        for y in range(chips)
    ]
    for copy in out_copies:
        copy.start()
    pl.semaphore_wait(flag, chips + dp_count - 1)

    def out_near_copy(y):
        return net.to_sibling(
            out_part.at[y * 2 + 1 - core],
            out_near.at[y],
            out_near_sem.at[0, y],
            out_near_sem.at[1, y],
        )

    def out_far_copy(other, source):
        return net.to_peer(
            other,
            out_own.at[other],
            out_far.at[lax.rem(source - chip + chips - 1, chips)]
            if source is not chip
            else out_far.at[lax.rem(chip - other + chips - 1, chips)],
            out_far_send.at[other],
            out_far_recv.at[source],
        )

    for y in range(chips):
        out_near_copy(y).start()

    def put(k, c, y, values):
        part[k, c, y] = values[:, :half_columns].astype(BF16)
        part[k + 1, c, y] = values[:, half_columns:].astype(BF16)

    token_total = token_rows.shape[0]
    dp_step = max(1, 256 // entry_count)

    @pl.loop(0, dp_count // dp_step)
    def _(block):
        row = lax.broadcasted_iota(jnp.int32, (dp_step * entry_count, token_total), 0)
        owner = block * dp_step + row // entry_count
        number = (owner * group + me) * entry_count + lax.rem(row, entry_count)
        chosen = jnp.where(number == token_row[...], 1.0, 0.0).astype(BF16)
        sums = dot_nn(chosen, token_rows[...]).astype(BF16)
        for j in range(dp_step):
            entry_part[block * dp_step + j] = sums[j * entry_count : (j + 1) * entry_count]

    def entry_copy(target, slot):
        return pltpu.make_async_remote_copy(
            src_ref=entry_part.at[target],
            dst_ref=entry_land.at[slot],
            send_sem=entry_send.at[target],
            recv_sem=entry_recv.at[slot],
            device_id={"dp": target},
            device_id_type=MESH,
        )

    each_dp(lambda target: entry_copy(target, dp).start())
    pooled_t = pooled_own[...].T

    def proj_shard(c, y, span):
        put(0, c, y, dot_nn(pooled_t, embed_rows[:, span]))

    each_shard(chips, columns, proj_shard)
    total_sum.start(0)
    total_sum.start(1)
    bias_sums = jnp.sum(embed_rows[...].astype(F32), axis=0, keepdims=True)
    for j in range(4):
        small_part[4 + j : 5 + j, :] = bias_sums[:, j * width : (j + 1) * width]
    loads[0].wait()
    run(0)

    pool = pool_matrix(counts_col[...], entry_count, rows).astype(BF16)
    spread = spread_matrix(counts_row[...], entry_count, rows)
    valid = jnp.sum(spread, axis=1, keepdims=True)
    spread = spread.astype(BF16)
    for b in range(blocks):
        bias[b] = slot_bias(valid[b * ROW_BLOCK : (b + 1) * ROW_BLOCK], slots)
    ffn_t[...] = ffn_in[...].T

    def hidden_shard(c, y, span):
        act, slope = gelu_parts(dot_nn(ffn_in[...], weights[1, c, y]))
        slopes[:, span] = slope.astype(BF16)
        hidden[:, span] = dot_nn(pool, act.astype(BF16)).astype(BF16)

    each_shard(chips, columns, hidden_shard)
    run(1)
    each_dp(lambda source: entry_copy(source, source).wait_recv())
    pooled_grad = entry_part[dp].astype(F32)
    for j in range(1, dp_count):
        pooled_grad = pooled_grad + entry_land[lax.rem(dp + j, dp_count)].astype(F32)
    entry_low = (pooled_grad / counts_col[...]).astype(BF16)
    out_rows = dot_nn(spread, entry_low)
    entry_t = entry_low.T
    loads[1].wait()
    out_low = out_rows.astype(BF16)
    row_total[...] = jnp.zeros_like(row_total)

    def unit_shard(c, y, span):
        put(2, c, y, dot_nn(entry_t, hidden[:, span]))
        act_grad = dot_nn(out_low, weights[2, c, y])
        pre_grad = (act_grad * slopes[:, span].astype(F32)).astype(BF16)
        put(4, c, y, dot_nn(ffn_t[...], pre_grad))
        row_total[...] += dot_nt(pre_grad, weights[1, c, y])

    each_shard(chips, columns, unit_shard)
    for k in (2, 3, 4, 5):
        total_sum.start(k)
    run(2)
    back, gain_grad, shift_grad = norm_back(residual[...], row_total[...], gain_two[...])
    small_part[2:3, :] = gain_grad
    small_part[3:4, :] = shift_grad
    residual_grad = out_rows + back
    pieces_grad[...] = residual_grad
    attn_grad = residual_grad.astype(BF16)
    loads[2].wait()
    for m, c, y in shards_of(chips):
        span = slice(m * head_columns, (m + 1) * head_columns)
        d_out_n[:, span] = dot_nn(attn_grad, weights[0, c, y, :, 3 * head_columns :]).astype(BF16)
    out_grad = dot_nn(attn_grad.T, attended[...])
    for m, c, y in shards_of(chips):
        span = slice(m * head_columns, (m + 1) * head_columns)
        part[7, c, y, :, head_columns:] = out_grad[:, span].astype(BF16)
    for b in range(blocks):
        block_rows = slice(b * ROW_BLOCK, (b + 1) * ROW_BLOCK)
        q_t[b] = q_n[block_rows, :].T
        k_t[b] = k_n[block_rows, :].T
        out_t[b] = attended[block_rows, :].T
        d_out_t[b] = d_out_n[block_rows, :].T
    run(3)

    for ref in (query_wide, grad_wide):
        ref[...] = jnp.zeros_like(ref)

    @pl.loop(0, blocks)
    def _(b):
        block_rows = pl.ds(pl.multiple_of(b * ROW_BLOCK, ROW_BLOCK), ROW_BLOCK)
        fill_diagonal(query_wide, q_t[b], heads)
        fill_diagonal(grad_wide, d_out_t[b], heads)
        scores = dot_nn(k_n[block_rows, :], query_wide[...]) + tiled(bias[b], heads)
        probs = jnp.exp(scores - logs[b])
        d_value[block_rows, :] = dot_nt(probs.astype(BF16), grad_wide[...]).astype(BF16)
        moved = d_out_t[b].astype(F32) * out_t[b].astype(F32)
        centre = jnp.concatenate(
            [
                jnp.sum(moved[h * HD : (h + 1) * HD], axis=0, keepdims=True)
                for h in range(heads)
            ],
            axis=1,
        )
        score_grad = (probs * (dot_nn(v_n[block_rows, :], grad_wide[...]) - centre)).astype(BF16)
        d_key[block_rows, :] = dot_nt(score_grad, query_wide[...]).astype(BF16)
        for pair in range(heads // 2):
            span = slice(pair * 2 * HD, (pair + 1) * 2 * HD)
            lanes = slice(pair * 2 * ROW_BLOCK, (pair + 1) * 2 * ROW_BLOCK)
            both = dot_nn(k_t[b, span, :], score_grad[:, lanes]) * (HD**-0.5)
            d_query_t[b, span, :] = pair_blocks(both).astype(BF16)

    for b in range(blocks):
        d_query[b * ROW_BLOCK : (b + 1) * ROW_BLOCK, :] = d_query_t[b].T
    run(4)
    rows_t = attn_in[...].T
    for place, (k, lanes, source) in enumerate(
        ((6, 0, d_query), (6, 1, d_key), (7, 0, d_value))
    ):
        grads = dot_nn(rows_t, source[...])
        for m, c, y in shards_of(chips):
            span = slice(m * head_columns, (m + 1) * head_columns)
            part[k, c, y, :, lanes * head_columns : (lanes + 1) * head_columns] = grads[
                :, span
            ].astype(BF16)
    total_sum.start(6)
    total_sum.start(7)
    normed = jnp.zeros((rows, width), F32)
    for m, c, y in shards_of(chips):
        span = slice(m * head_columns, (m + 1) * head_columns)
        for j, source in enumerate((d_query, d_key, d_value)):
            normed = normed + dot_nt(
                source[:, span], weights[0, c, y, :, j * head_columns : (j + 1) * head_columns]
            )
    back, gain_grad, shift_grad = norm_back(pieces[...].astype(F32), normed, gain_one[...])
    small_part[0:1, :] = gain_grad
    small_part[1:2, :] = shift_grad
    pieces_grad[...] += back

    def out_middle():
        for y in range(chips):
            out_copies[y].wait()
            out_near_copy(y).wait_recv()
        for other in net.others():
            out_own[other] = (
                out_own[other].astype(F32) + out_near[other].astype(F32)
            ).astype(BF16)
            out_far_copy(other, chip).start()

    def out_finish():
        text_out[...] = out_own[chip].astype(F32) + out_near[chip].astype(F32)
        for other in net.others():
            out_far_copy(other, other).wait_recv()
            slot = lax.rem(other - chip + chips - 1, chips)
            text_out[...] += out_far[slot].astype(F32)

    small_copy = net.to_sibling(small_part, small_near, small_sem.at[0], small_sem.at[1])
    small_copy.start()

    def small_far_copy(other, owner):
        return net.to_peer(
            other,
            small_far.at[owner],
            small_far.at[owner],
            small_far_send.at[other],
            small_far_recv.at[owner],
        )

    def small_dp_copy(other, owner):
        return pltpu.make_async_remote_copy(
            src_ref=small_dp.at[owner],
            dst_ref=small_dp.at[owner],
            send_sem=small_dp_send.at[other],
            recv_sem=small_dp_recv.at[owner],
            device_id={"dp": other},
            device_id_type=MESH,
        )

    def small_near_done():
        small_copy.wait_recv()
        small_far[chip] = small_part[...] + small_near[...]
        for other in net.others():
            small_far_copy(other, chip).start()

    def small_far_done():
        for other in net.others():
            small_far_copy(other, other).wait_recv()
        total = small_far[0]
        for j in range(1, chips):
            total = total + small_far[j]
        small_dp[dp] = total
        each_dp(lambda other: small_dp_copy(other, dp).start())

    @pl.loop(5, PARTS + 5)
    def _(step):
        for offset, stage in enumerate(stages):
            k = step - offset

            @pl.when((k >= 0) & (k < PARTS))
            def _():
                stage(k)

        pl.when(step == 5)(small_near_done)
        pl.when(step == 7)(small_far_done)
        pl.when(step == PARTS)(out_middle)

    out_finish()
    each_dp(lambda other: small_dp_copy(other, other).wait_recv())
    total = small_dp[0]
    for j in range(1, dp_count):
        total = total + small_dp[j]
    small_total[...] = total

    for y in range(chips):
        out_near_copy(y).wait_send()
    for other in net.others():
        out_far_copy(other, chip).wait_send()
    small_copy.wait_send()
    for other in net.others():
        small_far_copy(other, chip).wait_send()
    each_dp(lambda other: small_dp_copy(other, dp).wait_send())
    each_dp(lambda other: entry_copy(other, dp).wait_send())

    @pl.loop(0, PARTS)
    def _(k):
        total_sum.sent(k)


def hyper_backward(
    group,
    dp_count,
    embed_rows,
    pooled_own,
    token_rows,
    token_row,
    pieces,
    counts_col,
    counts_row,
    gain_one,
    gain_two,
    saved,
    weights,
    out_part,
):
    chips = group // 2
    rows, width = pieces.shape
    entry_count = counts_col.shape[0]
    kinds, columns = weights.shape[0], weights.shape[4]
    half_columns = columns // 2
    heads = width // HD
    blocks = rows // ROW_BLOCK
    spots = dp_count // 2
    vmem = pl.BlockSpec(memory_space=pltpu.VMEM)
    hbm = pl.BlockSpec(memory_space=pl.ANY)
    dma = pltpu.SemaphoreType.DMA
    final = (PARTS, 2, spots, width // (2 * spots), half_columns)
    units = columns * group

    def low(*shape):
        return pltpu.VMEM(shape, BF16)

    def wide(*shape):
        return pltpu.VMEM(shape, F32)

    return pl.pallas_call(
        partial(back_body, chips, dp_count),
        out_shape=(
            jax.ShapeDtypeStruct((rows, width), F32),
            jax.ShapeDtypeStruct(final, BF16),
            jax.ShapeDtypeStruct((8, width), F32),
            jax.ShapeDtypeStruct(out_part.shape[1:], F32),
        ),
        in_specs=[vmem] * 17 + [hbm] * 2,
        out_specs=(vmem,) * 4,
        scratch_shapes=[
            low(kinds, 2, chips, width, columns),
            low(PARTS, 2, chips, width, half_columns),
            low(PARTS, chips, width, half_columns),
            low(PARTS, chips - 1, width, half_columns),
            low(*final),
            low(PARTS, spots, width // (2 * spots), half_columns),
            low(PARTS, spots, width // (2 * spots), half_columns),
            low(dp_count, entry_count, width),
            low(dp_count, entry_count, width),
            low(entry_count, units),
            low(rows, units),
            low(width, rows),
            wide(rows, width),
            low(rows, width),
            low(rows, width),
            low(rows, width),
            low(rows, width),
        ]
        + [low(blocks, width, ROW_BLOCK)] * 5
        + [
            wide(blocks, ROW_BLOCK, ROW_BLOCK),
            low(width, heads * ROW_BLOCK),
            low(width, heads * ROW_BLOCK),
            wide(8, width),
            wide(chips, 8, width),
            wide(dp_count, 8, width),
            wide(8, width),
            low(chips, *out_part.shape[1:]),
            low(chips, *out_part.shape[1:]),
            low(chips - 1, *out_part.shape[1:]),
            dma((kinds,)),
            dma((chips,)),
            dma((2, chips)),
            dma((chips,)),
            dma((chips,)),
            dma((dp_count,)),
            dma((dp_count,)),
            dma((2, PARTS)),
            dma((PARTS, chips)),
            dma((PARTS, chips)),
            dma((2, PARTS)),
            dma((PARTS, spots)),
            dma((PARTS, spots)),
            dma((PARTS, spots)),
            dma((PARTS, spots)),
            dma((2, PARTS)),
            dma((2,)),
            dma((chips,)),
            dma((chips,)),
            dma((dp_count,)),
            dma((dp_count,)),
        ],
        compiler_params=pltpu.CompilerParams(
            collective_id=2, has_side_effects=True, vmem_limit_bytes=62 * 1024 * 1024
        ),
        cost_estimate=pl.CostEstimate(
            flops=60 * 10**9, bytes_accessed=20 * 10**6, transcendentals=5 * 10**6
        ),
    )(
        embed_rows,
        pooled_own,
        token_rows,
        token_row,
        pieces,
        counts_col,
        counts_row,
        gain_one,
        gain_two,
        *saved,
        weights,
        out_part,
    )


def spread_body(
    group,
    sums,
    small,
    pieces_sum,
    out_sum,
    text_out,
    pieces_grad,
    gain_one,
    shift_one,
    query,
    key,
    value,
    out,
    gain_two,
    shift_two,
    up,
    down,
    proj,
    bias,
):
    me = lax.axis_index("mp")
    half_columns = sums.shape[2]
    head_columns = query.shape[1]
    width = small.shape[1]
    share = bias.shape[1]
    text_out[...] = out_sum[...]
    pieces_grad[...] = pieces_sum[...]
    for first, target in ((0, proj), (2, down), (4, up)):
        target[:, :half_columns] = sums[first].astype(F32)
        target[:, half_columns:] = sums[first + 1].astype(F32)
    for k, lanes, target in ((6, 0, query), (6, 1, key), (7, 0, value), (7, 1, out)):
        target[...] = sums[k, :, lanes * head_columns : (lanes + 1) * head_columns].astype(F32)
    for row, target in enumerate((gain_one, shift_one, gain_two, shift_two)):
        target[...] = small[row : row + 1, :]
    for m in range(group):
        first = m * share

        @pl.when(me == m)
        def _():
            row = 4 + first // width
            bias[...] = small[row : row + 1, first % width : first % width + share]


def spread_sums(group, sums, small, pieces_sum, out_sum, share):
    _, width, half_columns = sums.shape
    vmem = pl.BlockSpec(memory_space=pltpu.VMEM)

    def wide(*shape):
        return jax.ShapeDtypeStruct(shape, F32)

    heads = [wide(width, half_columns // 2)] * 4
    units = [wide(width, half_columns * 2)] * 3
    row = wide(1, width)
    return pl.pallas_call(
        partial(spread_body, group),
        out_shape=(
            wide(*out_sum.shape),
            wide(*pieces_sum.shape),
            row,
            row,
            *heads,
            row,
            row,
            *units,
            wide(1, share),
        ),
        in_specs=[vmem] * 4,
        out_specs=(vmem,) * 14,
        compiler_params=pltpu.CompilerParams(vmem_limit_bytes=40 * 1024 * 1024),
    )(sums, small, pieces_sum, out_sum)


def on_device(
    pieces,
    counts,
    entry_ids,
    segment_ids,
    norm1_gain,
    norm1_shift,
    query_weight,
    key_weight,
    value_weight,
    out_weight,
    norm2_gain,
    norm2_shift,
    up_weight,
    down_weight,
    proj_weight,
    proj_bias,
    text_norm1_gain,
    text_query,
    text_key,
    text_value,
    text_out_proj,
    text_norm2_gain,
    text_gate,
    text_up,
    text_down,
    token_grad,
):
    group, dp_count = lax.axis_size("mp"), lax.axis_size("dp")
    entry_count, slot_count, width = pieces.shape
    text_width = token_grad.shape[1]
    length = segment_ids.shape[1]
    chunk_rows = length // CHUNKS
    pieces_rows = pieces.reshape(entry_count * slot_count, width)
    entries, weights, *saved, counts_col, counts_row, bias_full, key_value = hyper_forward(
        group,
        dp_count,
        pieces_rows,
        counts[None, :],
        norm1_gain[None, :],
        norm1_shift[None, :],
        norm2_gain[None, :],
        norm2_shift[None, :],
        (query_weight, key_weight, value_weight, out_weight),
        proj_bias[None, :],
        (up_weight, down_weight, proj_weight),
        text_key,
        text_value,
    )
    cos_t, sin_t = rope_tables(length)
    out_part, embed_rows, pooled_own, token_rows = text_layer(
        group,
        dp_count,
        entry_count,
        entry_ids.reshape(CHUNKS, 1, chunk_rows),
        segment_ids.reshape(CHUNKS, 1, chunk_rows),
        cos_t,
        sin_t,
        bias_full,
        text_norm1_gain[None, :],
        text_norm2_gain[None, :],
        key_value,
        entries.reshape(-1, width),
        weights,
        token_grad,
        text_query,
        text_out_proj,
        text_gate,
        text_up,
        text_down,
    )
    pieces_grad, final, small, text_out = hyper_backward(
        group,
        dp_count,
        embed_rows.reshape(-1, text_width),
        pooled_own.reshape(-1, width),
        token_rows.reshape(length, width),
        entry_ids[None, :],
        pieces_rows,
        counts_col,
        counts_row,
        norm1_gain[None, :],
        norm2_gain[None, :],
        saved,
        weights,
        out_part.reshape(group, -1, text_width),
    )
    outputs = spread_sums(
        group, final.reshape(PARTS, width, -1), small, pieces_grad, text_out, proj_bias.shape[0]
    )
    shapes = ((-1, text_width), pieces.shape) + ((width,),) * 2 + (None,) * 4
    shapes = shapes + ((width,),) * 2 + (None,) * 3 + ((-1,),)
    return tuple(
        value if shape is None else value.reshape(shape)
        for value, shape in zip(outputs, shapes)
    )


def solution(mesh):
    return jax.shard_map(
        on_device,
        mesh=mesh,
        in_specs=(
            P(("dp", "mp"), None, None),
            P("dp"),
            P("dp"),
            P("dp", None),
            P(),
            P(),
            P(None, "mp"),
            P(None, "mp"),
            P(None, "mp"),
            P(None, "mp"),
            P(),
            P(),
            P(None, "mp"),
            P(None, "mp"),
            P(None, "mp"),
            P("mp"),
            P(),
            P(None, "mp"),
            P(),
            P(),
            P(None, "mp"),
            P(),
            P(None, "mp"),
            P(None, "mp"),
            P(None, "mp"),
            P(("dp", "mp"), None),
        ),
        out_specs=(
            P(("dp", "mp"), None),
            P(("dp", "mp"), None, None),
            P(),
            P(),
            P(None, "mp"),
            P(None, "mp"),
            P(None, "mp"),
            P(None, "mp"),
            P(),
            P(),
            P(None, "mp"),
            P(None, "mp"),
            P(None, "mp"),
            P("mp"),
        ),
        check_vma=False,
    )
```

```python
from functools import partial
import math

import jax
import jax.numpy as jnp
import numpy as np
from jax import lax
from jax.experimental import pallas as pl
from jax.experimental.pallas import tpu as pltpu
from jax.sharding import PartitionSpec as P

HD = 64
QHEADS = 32
KVHEADS = 4
FHD = 64


def rope_tables(length):
    positions = np.arange(length, dtype=np.float32)
    rates = np.exp(
        np.arange(FHD // 2, dtype=np.float32) * np.float32(-2.0 * math.log(10000.0) / FHD)
    ).astype(np.float32)
    angles = (positions[None, :] * rates[:, None]).reshape(FHD // 2, CHUNKS, length // CHUNKS)
    angles = angles.transpose(1, 0, 2)
    return jnp.asarray(np.cos(angles)), jnp.asarray(np.sin(angles))


MESH = pl.DeviceIdType.MESH
F32 = jnp.float32
BF16 = jnp.bfloat16
CHUNKS = 4
FAR = -1e30


def dot_nn(a, b):
    return lax.dot_general(a, b, (((1,), (0,)), ((), ())), preferred_element_type=F32)


def dot_nt(a, b):
    return lax.dot_general(a, b, (((1,), (1,)), ((), ())), preferred_element_type=F32)


def column_tiles(total, width, body):
    full = total // width
    if full > 0:

        @pl.loop(0, full)
        def _(t):
            body(pl.ds(pl.multiple_of(t * width, width), width))

    if total % width:
        body(pl.ds(full * width, total % width))


def rms_scale(values):
    return lax.rsqrt(jnp.mean(values * values, axis=-1, keepdims=True) + 1e-05)


def rms_back(values, grad, gain):
    scale = rms_scale(values)
    scaled = grad * gain
    return scale * (
        scaled - values * (scale * scale) * jnp.mean(scaled * values, axis=-1, keepdims=True)
    )


def piece_indices(shape, row_pieces):
    places = [()]
    for size in shape[:-2]:
        places = [place + (j,) for place in places for j in range(size)]
    rows = shape[-2]
    if rows % (16 * row_pieces):
        return places
    step = rows // row_pieces
    return [place + (pl.ds(j * step, step),) for place in places for j in range(row_pieces)]


class Pieces:
    def __init__(self, source, target, send, recv, device, row_pieces=2):
        self.parts = (source, target, send, recv, device)
        self.row_pieces = row_pieces

    def copy(self, source, target):
        _, _, send, recv, device = self.parts
        return pltpu.make_async_remote_copy(
            src_ref=source,
            dst_ref=target,
            send_sem=send,
            recv_sem=recv,
            device_id=device,
            device_id_type=MESH,
        )

    def start(self):
        source, target = self.parts[:2]
        for place in piece_indices(source.shape, self.row_pieces):
            if place:
                self.copy(source.at[place], target.at[place]).start()
            else:
                self.copy(source, target).start()

    def wait_send(self):
        self.copy(*self.parts[:2]).wait_send()

    def wait_recv(self):
        self.copy(*self.parts[:2]).wait_recv()


class Exchange:
    def __init__(self, chips, chip, core, group_axis):
        self.chips, self.chip, self.core = chips, chip, core
        self.axis = group_axis

    def sibling(self):
        return {self.axis: self.chip * 2 + 1 - self.core}

    def peer(self, other):
        return {self.axis: other * 2 + self.core}

    def others(self):
        return [lax.rem(self.chip + step, self.chips) for step in range(1, self.chips)]

    def barrier(self):
        flag = pltpu.get_barrier_semaphore()
        pl.semaphore_signal(flag, inc=1, device_id=self.sibling(), device_id_type=MESH)
        for other in self.others():
            pl.semaphore_signal(flag, inc=1, device_id=self.peer(other), device_id_type=MESH)
        pl.semaphore_wait(flag, self.chips)

    def to_sibling(self, source, target, send, recv):
        return Pieces(source, target, send, recv, self.sibling())

    def to_peer(self, other, source, target, send, recv):
        return Pieces(source, target, send, recv, self.peer(other))


class Scatter:
    def __init__(self, net, part, near, far, sems):
        self.net, self.part, self.near, self.far = net, part, near, far
        self.slots = None if part.shape[0] == near.shape[0] else part.shape[0]
        self.near_send, self.near_recv, self.far_send, self.far_recv = sems

    def slot(self, i):
        return i if self.slots is None else i % self.slots

    def landing(self, source, target):
        return lax.rem(source - target + self.net.chips - 1, self.net.chips)

    def near_copy(self, i):
        net = self.net
        return net.to_sibling(
            self.part.at[self.slot(i), 1 - net.core],
            self.near.at[i],
            self.near_send.at[i],
            self.near_recv.at[i],
        )

    def far_copy(self, i, other):
        net = self.net
        return net.to_peer(
            other,
            self.part.at[self.slot(i), net.core, other],
            self.far.at[i, self.landing(net.chip, other)],
            self.far_send.at[i, other],
            self.far_recv.at[i, net.chip],
        )

    def far_landing(self, i, other):
        net = self.net
        return net.to_peer(
            other,
            self.part.at[self.slot(i), net.core, other],
            self.far.at[i, self.landing(other, net.chip)],
            self.far_send.at[i, other],
            self.far_recv.at[i, other],
        )

    def start(self, i):
        self.near_copy(i).start()

    def middle(self, i):
        net = self.net
        self.near_copy(i).wait_recv()
        slot = self.slot(i)
        for other in net.others():
            total = self.part[slot, net.core, other].astype(F32) + self.near[
                i, other
            ].astype(F32)
            self.part[slot, net.core, other] = total.astype(BF16)
            self.far_copy(i, other).start()

    def finish(self, i):
        net = self.net
        slot = self.slot(i)
        total = self.part[slot, net.core, net.chip].astype(F32) + self.near[
            i, net.chip
        ].astype(F32)
        for other in net.others():
            self.far_landing(i, other).wait_recv()
            total = total + self.far[i, self.landing(other, net.chip)].astype(F32)
        return total

    def sent(self, i):
        self.near_copy(i).wait_send()
        for other in self.net.others():
            self.far_copy(i, other).wait_send()


class Gather:
    def __init__(self, net, full, sems, single=False):
        self.net, self.full, self.single = net, full, single
        self.far_send, self.far_recv, self.near_send, self.near_recv = sems

    def block(self, i, *place):
        return self.full.at[place] if self.single else self.full.at[(i, *place)]

    def far_copy(self, i, other):
        net = self.net
        block = self.block(i, net.core, net.chip)
        return net.to_peer(
            other, block, block, self.far_send.at[i, other], self.far_recv.at[i, net.chip]
        )

    def far_landing(self, i, other):
        net = self.net
        block = self.block(i, net.core, other)
        return net.to_peer(
            other, block, block, self.far_send.at[i, other], self.far_recv.at[i, other]
        )

    def near_copy(self, i):
        block = self.block(i, self.net.core)
        return self.net.to_sibling(block, block, self.near_send.at[i], self.near_recv.at[i])

    def near_landing(self, i):
        block = self.block(i, 1 - self.net.core)
        return self.net.to_sibling(block, block, self.near_send.at[i], self.near_recv.at[i])

    def start(self, i):
        for other in self.net.others():
            self.far_copy(i, other).start()

    def middle(self, i):
        for other in self.net.others():
            self.far_landing(i, other).wait_recv()
        self.near_copy(i).start()

    def finish(self, i):
        self.near_landing(i).wait_recv()

    def sent(self, i):
        for other in self.net.others():
            self.far_copy(i, other).wait_send()
        self.near_copy(i).wait_send()


STEPS = (
    ("attend", 0),
    ("attn_part", 0),
    ("attend", 2),
    ("attn_far", 0),
    ("attend", 1),
    ("attn_part", 2),
    ("norm", 0),
    ("attn_part", 1),
    ("attend", 3),
    ("attn_far", 1),
    ("attn_far", 2),
    ("attn_part", 3),
    ("rows_near", 0),
    ("units_low", 0),
    ("norm", 1),
    ("units_high", 0),
    ("unit_grads", 0),
    ("norm", 2),
    ("rows_near", 1),
    ("outputs", 0),
    ("attn_far", 3),
    ("units_far", 0),
    ("units_low", 1),
    ("units_high", 1),
    ("rows_near", 2),
    ("unit_grads", 1),
    ("norm", 3),
    ("outputs", 1),
    ("units_far", 1),
    ("residual", 0),
    ("units_low", 2),
    ("units_high", 2),
    ("rows_near", 3),
    ("unit_grads", 2),
    ("residual", 1),
    ("outputs", 2),
    ("units_low", 3),
    ("units_far", 2),
    ("back_near", 0),
    ("units_high", 3),
    ("back_near", 1),
    ("unit_grads", 3),
    ("residual", 2),
    ("attend_back", 0),
    ("units_far", 3),
    ("back_near", 2),
    ("normed_part", 0),
    ("attend_back", 1),
    ("residual", 3),
    ("normed_part", 1),
    ("normed_far", 0),
    ("attend_back", 2),
    ("normed_far", 1),
    ("back_near", 3),
    ("normed_part", 2),
    ("attend_back", 3),
    ("normed_far", 2),
    ("normed_part", 3),
    ("embed_grad", 0),
    ("outputs", 3),
    ("normed_far", 3),
    ("embed_grad", 1),
    ("token_near", 0),
    ("embed_grad", 2),
    ("token_near", 1),
    ("embed_grad", 3),
    ("token_near", 2),
    ("token_near", 3),
)


def column_of(row):
    return jnp.broadcast_to(row, (8, row.shape[1])).T[:, :1]


def text_body(
    chips,
    dp_count,
    entry_count,
    head_count,
    entry_ids,
    segments,
    cos_t,
    sin_t,
    bias_full,
    gain_one,
    gain_two,
    w_kv,
    entries_hbm,
    weights_hbm,
    token_grad,
    w_query_hbm,
    w_out_hbm,
    w_gate_hbm,
    w_up_hbm,
    w_down_hbm,
    out_part,
    embed_grad,
    pooled_own,
    token_full,
    proj,
    w_query,
    w_out,
    w_gate,
    w_up,
    w_down,
    part_a,
    near_a,
    far_a,
    part_b,
    near_b,
    far_b,
    full,
    grad_full,
    embeds_own,
    q_t,
    q_n,
    k_n,
    v_n,
    k_t,
    v_t,
    out_t,
    logs,
    bias,
    residual,
    weight_sem,
    local_sem,
    stage_sem,
    scatter_near,
    scatter_far_send,
    scatter_far_recv,
    gather_near,
    gather_far_send,
    gather_far_recv,
    grad_near,
    grad_far_send,
    grad_far_recv,
):
    me = lax.axis_index("mp")
    chip, core = me // 2, lax.rem(me, 2)
    net = Exchange(chips, chip, core, "mp")
    group = chips * 2
    chunk_rows = q_n.shape[1]
    width = embeds_own.shape[2]
    units = w_gate.shape[1]
    own_rows = embeds_own.shape[1]
    head_width = FHD * head_count
    columns = proj.shape[3]
    entry_total, entry_width = entries_hbm.shape
    owned = token_grad.shape[0]
    first_own = pl.multiple_of((core * chips + chip) * own_rows, own_rows)
    owners = group // CHUNKS if group > CHUNKS else 1

    def scatter_of(kind, part, near, far):
        return Scatter(
            net,
            part,
            near,
            far,
            (
                scatter_near.at[kind, 0],
                scatter_near.at[kind, 1],
                scatter_far_send.at[kind],
                scatter_far_recv.at[kind],
            ),
        )

    def gather_of(kind, ref):
        return Gather(
            net,
            ref,
            (
                gather_far_send.at[kind],
                gather_far_recv.at[kind],
                gather_near.at[kind, 0],
                gather_near.at[kind, 1],
            ),
        )

    attn_sum = scatter_of(0, part_a, near_a, far_a)
    mlp_sum = scatter_of(1, part_b, near_b, far_b)
    normed_sum = scatter_of(2, part_a, near_a, far_a)
    mlp_rows = gather_of(0, full)
    back_rows = gather_of(1, full)
    token_rows = gather_of(2, token_full)

    def load(k, source, target):
        return pltpu.make_async_copy(source, target, weight_sem.at[k])

    load_proj = load(1, weights_hbm.at[3], proj)
    load_query = load(2, w_query_hbm, w_query)
    load_out = load(3, w_out_hbm, w_out)
    load_units = [
        load(4, w_gate_hbm, w_gate),
        load(5, w_up_hbm, w_up),
        load(6, w_down_hbm, w_down),
    ]

    def grad_far(owner_chip, other):
        return net.to_peer(
            other,
            token_grad,
            grad_full.at[owner_chip * 2 + core],
            grad_far_send.at[other],
            grad_far_recv.at[owner_chip],
        )

    def grad_near_copy(owner_chip, owner_core):
        block = grad_full.at[owner_chip * 2 + owner_core]
        return net.to_sibling(
            block, block, grad_near.at[0, owner_chip], grad_near.at[1, owner_chip]
        )

    grad_local = pltpu.make_async_copy(token_grad, grad_full.at[me], local_sem)

    def grad_start():
        for other in net.others():
            grad_far(chip, other).start()

    def grad_middle():
        grad_local.wait()
        grad_near_copy(chip, core).start()
        for other in net.others():
            grad_far(other, other).wait_recv()
            grad_near_copy(other, core).start()

    def grad_chunk(i):
        return grad_full[i * owners : (i + 1) * owners].reshape(chunk_rows, width)

    def grad_finish(i):
        for owner in range(i * owners, (i + 1) * owners):

            @pl.when(core != owner % 2)
            def _():
                grad_near_copy(owner // 2, owner % 2).wait_recv()

    def embed(entries, pooled, embeds):
        load_entries = load(0, entries_hbm, entries)
        load_entries.start()
        for copy in (load_proj, load_query, load_out, *load_units):
            copy.start()
        grad_local.start()
        net.barrier()
        pl.when(core == 1)(grad_start)
        load_entries.wait()
        load_proj.wait()
        load_query.wait()

        @pl.loop(0, CHUNKS)
        def _(i):
            ids = entry_ids[i]
            owner = ids // entry_count
            owner_mp, owner_dp = lax.rem(owner, group), owner // group
            place = (lax.rem(owner_mp, 2) * chips + owner_mp // 2) * dp_count + owner_dp
            spots = column_of(
                (place * entry_count + lax.rem(ids, entry_count)).astype(F32)
            ).astype(jnp.int32)
            numbers = lax.broadcasted_iota(jnp.int32, (chunk_rows, entry_total), 1)
            chosen = jnp.where(numbers == spots, 1.0, 0.0).astype(BF16)
            pooled[...] = dot_nn(chosen, entries[...]).astype(BF16)
            pooled_own[i] = pooled[pl.ds(first_own, own_rows), :]
            for m, c, y in shards_of(chips):
                span = slice(m * columns, (m + 1) * columns)
                embeds[:, span] = (dot_nn(pooled[...], proj[c, y]) + bias_full[c, y]).astype(BF16)
            embeds_own[i] = embeds[pl.ds(first_own, own_rows), :]
            values = embeds[...].astype(F32)
            embeds[...] = (values * rms_scale(values) * gain_one[...]).astype(BF16)
            cosine, sine = cos_t[i], sin_t[i]

            def turned(block):
                low_half, high_half = block[: FHD // 2], block[FHD // 2 :]
                return jnp.concatenate(
                    [low_half * cosine - high_half * sine, high_half * cosine + low_half * sine],
                    axis=0,
                )

            queries = dot_nn(embeds[...], w_query[...]).T
            for h in range(head_count):
                span = slice(h * FHD, (h + 1) * FHD)
                q_t[i, span, :] = (
                    turned(queries[span]).astype(BF16).astype(F32) * FHD**-0.5
                ).astype(BF16)
            q_n[i] = q_t[i].T
            both = dot_nn(embeds[...], w_kv[...])
            keys_t = turned(both.T[:FHD]).astype(BF16)
            k_t[i] = keys_t
            k_n[i] = keys_t.T
            v_n[i] = both[:, FHD:].astype(BF16)
            v_t[i] = both.T[FHD:].astype(BF16)

        pl.when(core == 0)(grad_start)
        pl.when(core == 1)(grad_middle)

    pl.run_scoped(
        embed,
        pltpu.VMEM((entry_total, entry_width), BF16),
        pltpu.VMEM((chunk_rows, entry_width), BF16),
        pltpu.VMEM((chunk_rows, width), BF16),
    )

    def put_rows(part, slot, columns, values):
        half = chunk_rows // 2
        for k in range(2):
            for j in range(chips):
                first = k * half + j * own_rows
                part[slot, k, j, :, columns] = values[first : first + own_rows]

    def rows_of(ref, i):
        return ref[i].reshape(chunk_rows, width)

    def turned_back(sums_t):
        return sums_t.astype(BF16).T

    def make_bias(i):
        query_spots = i * chunk_rows + lax.broadcasted_iota(jnp.int32, (chunk_rows, chunk_rows), 1)
        query_segments = segments[i].astype(F32)
        for kb in range(i + 1):
            allowed = column_of(segments[kb].astype(F32)) == query_segments
            if kb == i:
                key_spots = kb * chunk_rows + lax.broadcasted_iota(
                    jnp.int32, (chunk_rows, chunk_rows), 0
                )
                allowed = allowed & (key_spots <= query_spots)
            bias[kb] = jnp.where(allowed, 0.0, FAR)

    def head_span(h):
        return pl.ds(pl.multiple_of(h * FHD, FHD), FHD)

    def layer(
        mixed,
        gate_grad,
        up_grad,
        out_stage,
        d_out_t,
        d_out_n,
        d_query_t,
        value_total,
        key_total,
    ):
        for ref in (value_total, key_total):
            ref[...] = jnp.zeros_like(ref)

        def stage_copy(i, tile):
            slot = lax.rem(tile, 2)
            columns = pl.ds(pl.multiple_of(tile * 512, 512), 512)
            return pltpu.make_async_copy(
                out_stage.at[slot], out_part.at[i, :, columns], stage_sem.at[slot]
            )

        def pair_t(ref, pair):
            return jnp.concatenate(
                [ref[head_span(pair * 2), :], ref[head_span(pair * 2 + 1), :]], axis=1
            )

        def pair_bias(kb):
            return jnp.concatenate([bias[kb], bias[kb]], axis=1)

        def attend(i):
            make_bias(i)

            @pl.loop(0, head_count // 2)
            def _(pair):
                query = pair_t(q_t.at[i], pair)
                scores = [dot_nn(k_n[kb], query) + pair_bias(kb) for kb in range(i + 1)]
                top = jnp.max(scores[0], axis=0, keepdims=True)
                for block in scores[1:]:
                    top = jnp.maximum(top, jnp.max(block, axis=0, keepdims=True))
                total = jnp.zeros_like(top)
                attended = jnp.zeros((FHD, 2 * chunk_rows), F32)
                for kb in range(i + 1):
                    weights_block = jnp.exp(scores[kb] - top)
                    total = total + jnp.sum(weights_block, axis=0, keepdims=True)
                    attended = attended + dot_nn(v_t[kb], weights_block.astype(BF16))
                logs[i, pair] = top + jnp.log(total)
                attended = (attended / total).astype(BF16)
                out_t[i, head_span(pair * 2), :] = attended[:, :chunk_rows]
                out_t[i, head_span(pair * 2 + 1), :] = attended[:, chunk_rows:]

        def attn_part(i):
            if i == CHUNKS - 1:
                load_out.wait()

            def tile(columns):
                put_rows(part_a, i, columns, turned_back(dot_nn(w_out[columns, :], out_t[i])))

            column_tiles(width, 512, tile)
            attn_sum.start(i)

        def norm(i):
            values = embeds_own[i].astype(F32) + attn_sum.finish(i)
            residual[i] = values
            full[i, core, chip] = (values * rms_scale(values) * gain_two[...]).astype(BF16)
            mlp_rows.start(i)

        def unit_tile(i, columns):
            rows = rows_of(full, i)
            gate_pre = dot_nn(rows, w_gate[:, columns])
            up_pre = dot_nn(rows, w_up[:, columns])
            act_grad = dot_nn(grad_chunk(i), w_down[:, columns])
            inverse = 1.0 / (1.0 + jnp.exp(-gate_pre))
            silu = gate_pre * inverse
            mixed[columns, :] = turned_back(silu * up_pre)
            up_grad[columns, :] = turned_back(act_grad * silu)
            slope = inverse * (1.0 + gate_pre * (1.0 - inverse))
            gate_grad[columns, :] = turned_back(act_grad * up_pre * slope)

        tile_width = 512 if units >= 1024 else 256
        tiles = units // tile_width
        middle_tile = (tiles + 1) // 2

        def unit_tiles(i, first, last):
            @pl.loop(first, last)
            def _(t):
                unit_tile(i, pl.ds(pl.multiple_of(t * tile_width, tile_width), tile_width))

        def units_low(i):
            if i == CHUNKS - 1:
                pl.when(core == 0)(grad_middle)
                for copy in load_units:
                    copy.wait()
            grad_finish(i)
            mlp_rows.finish(i)
            unit_tiles(i, 0, middle_tile)

        def units_high(i):
            unit_tiles(i, middle_tile, tiles)
            if units % tile_width:
                unit_tile(i, pl.ds(tiles * tile_width, units % tile_width))
            mlp_rows.sent(i)

        def unit_grads(i):
            if i + 2 < CHUNKS:
                mlp_sum.sent(i + 2)

            def tile(columns):
                put_rows(
                    part_b,
                    i % 2,
                    columns,
                    turned_back(
                        dot_nn(w_gate[columns, :], gate_grad[...])
                        + dot_nn(w_up[columns, :], up_grad[...])
                    ),
                )

            column_tiles(width, 512, tile)
            mlp_sum.start(i)

        def outputs(i):
            @pl.loop(0, width // 512)
            def _(t):
                columns = pl.ds(pl.multiple_of(t * 512, 512), 512)
                slot = lax.rem(t, 2)
                tile = turned_back(dot_nn(w_down[columns, :], mixed[...]))
                if i == CHUNKS - 1:
                    pl.when(t >= 2)(lambda: stage_copy(i, t).wait())
                else:
                    stage_copy(i, t).wait()
                out_stage[slot] = tile
                own = pl.ds(first_own, own_rows)
                out_stage[slot, own, :] = (
                    out_stage[slot, own, :].astype(F32) + residual[i, :, columns]
                ).astype(BF16)
                stage_copy(i, t).start()

        def residual_back(i):
            grad = mlp_sum.finish(i)
            block = i * owners + first_own // owned
            start = pl.multiple_of(lax.rem(first_own, owned), own_rows)
            own_grad = grad_full[block, pl.ds(start, own_rows), :].astype(F32)
            values = own_grad + rms_back(residual[i], grad, gain_two[...])
            full[i, core, chip] = values.astype(BF16)
            back_rows.start(i)

        def attend_back(i):
            back_rows.finish(i)
            attended_grad = dot_nn(rows_of(full, i), w_out[...]).astype(BF16)
            d_out_n[...] = attended_grad
            d_out_t[...] = attended_grad.T
            make_bias(i)
            cosine, sine = cos_t[i], sin_t[i]

            first_head = (
                lax.broadcasted_iota(jnp.int32, (chunk_rows, 2 * FHD), 1) < FHD
            )

            def stacked(rows):
                wide = rows.astype(F32)
                return jnp.concatenate(
                    [jnp.where(first_head, wide, 0.0), jnp.where(first_head, 0.0, wide)], axis=0
                ).astype(BF16)

            @pl.loop(0, head_count // 2)
            def _(pair):
                pair_span = pl.ds(pl.multiple_of(pair * 2 * FHD, 2 * FHD), 2 * FHD)
                query_rows = stacked(q_n[i, :, pair_span])
                grad_rows = stacked(d_out_n[:, pair_span])
                query = pair_t(q_t.at[i], pair)
                grad = pair_t(d_out_t, pair)
                log_row = logs[i, pair]
                centre = jnp.sum(
                    grad.astype(F32) * pair_t(out_t.at[i], pair).astype(F32),
                    axis=0,
                    keepdims=True,
                )
                query_grad = jnp.zeros((FHD, 2 * chunk_rows), F32)
                for kb in range(i + 1):
                    probs = jnp.exp(dot_nn(k_n[kb], query) + pair_bias(kb) - log_row)
                    value_total[kb] += dot_nn(probs.astype(BF16), grad_rows)
                    score_grad = (probs * (dot_nn(v_n[kb], grad) - centre)).astype(BF16)
                    key_total[kb] += dot_nn(score_grad, query_rows)
                    query_grad = query_grad + dot_nn(k_t[kb], score_grad)
                query_grad = query_grad * (FHD**-0.5)
                for odd in range(2):
                    lanes = slice(odd * chunk_rows, (odd + 1) * chunk_rows)
                    low_half = query_grad[: FHD // 2, lanes]
                    high_half = query_grad[FHD // 2 :, lanes]
                    d_query_t[head_span(pair * 2 + odd), :] = jnp.concatenate(
                        [
                            low_half * cosine + high_half * sine,
                            high_half * cosine - low_half * sine,
                        ],
                        axis=0,
                    ).astype(BF16)

        def normed_part(i):
            attn_sum.sent(i)
            key_grad = (key_total[i][:, :FHD] + key_total[i][:, FHD:]).T
            cosine, sine = cos_t[i], sin_t[i]
            low_half, high_half = key_grad[: FHD // 2], key_grad[FHD // 2 :]
            value_grad = (value_total[i][:, :FHD] + value_total[i][:, FHD:]).T
            both = jnp.concatenate(
                [
                    low_half * cosine + high_half * sine,
                    high_half * cosine - low_half * sine,
                    value_grad,
                ],
                axis=0,
            )
            both = both.astype(BF16)

            def tile(columns):
                put_rows(
                    part_a,
                    i,
                    columns,
                    turned_back(
                        dot_nn(w_query[columns, :], d_query_t[...])
                        + dot_nn(w_kv[columns, :], both)
                    ),
                )

            column_tiles(width, 512, tile)
            normed_sum.start(i)

        def embed_back(i):
            grad = normed_sum.finish(i)
            kept = full[i, core, chip].astype(F32)
            values = kept + rms_back(embeds_own[i].astype(F32), grad, gain_one[...])
            embed_grad[i] = values.astype(BF16)
            total = jnp.zeros((own_rows, entry_width), F32)
            for m, c, y in shards_of(chips):
                total = total + dot_nt(
                    embed_grad[i, :, m * columns : (m + 1) * columns], proj[c, y]
                )
            token_full[i, core, chip] = total.astype(BF16)
            token_rows.start(i)

        stages = {
            "attend": attend,
            "attn_part": attn_part,
            "attn_far": attn_sum.middle,
            "norm": norm,
            "rows_near": mlp_rows.middle,
            "units_low": units_low,
            "units_high": units_high,
            "unit_grads": unit_grads,
            "outputs": outputs,
            "units_far": mlp_sum.middle,
            "residual": residual_back,
            "back_near": back_rows.middle,
            "attend_back": attend_back,
            "normed_part": normed_part,
            "normed_far": normed_sum.middle,
            "embed_grad": embed_back,
            "token_near": token_rows.middle,
        }
        for name, turn in STEPS:
            stages[name](CHUNKS - 1 - turn)

        for tile in range(2):
            stage_copy(0, tile).wait()

    lines = (units, chunk_rows)
    keys = (CHUNKS, chunk_rows, 2 * FHD)
    pl.run_scoped(
        layer,
        pltpu.VMEM(lines, BF16),
        pltpu.VMEM(lines, BF16),
        pltpu.VMEM(lines, BF16),
        pltpu.VMEM((2, chunk_rows, 512), BF16),
        pltpu.VMEM((head_width, chunk_rows), BF16),
        pltpu.VMEM((chunk_rows, head_width), BF16),
        pltpu.VMEM((head_width, chunk_rows), BF16),
        pltpu.VMEM(keys, F32),
        pltpu.VMEM(keys, F32),
    )

    @pl.loop(0, CHUNKS)
    def _(i):
        token_rows.finish(i)
        token_rows.sent(i)
        normed_sum.sent(i)
        back_rows.sent(i)

    for i in range(2):
        mlp_sum.sent(i)
    for other in net.others():
        grad_far(chip, other).wait_send()
    for owner_chip in range(chips):
        grad_near_copy(owner_chip, core).wait_send()


def text_layer(
    group,
    dp_count,
    entry_count,
    entry_ids,
    segments,
    cos_t,
    sin_t,
    bias_full,
    gain_one,
    gain_two,
    w_kv,
    entries,
    weights,
    token_grad,
    w_query,
    w_out,
    w_gate,
    w_up,
    w_down,
):
    chips = group // 2
    chunks, _, chunk_rows = entry_ids.shape
    own_rows = chunk_rows // group
    owned, width = token_grad.shape
    head_width = w_query.shape[1]
    head_count = head_width // FHD
    entry_width = entries.shape[1]
    vmem = pl.BlockSpec(memory_space=pltpu.VMEM)
    hbm = pl.BlockSpec(memory_space=pl.ANY)
    dma = pltpu.SemaphoreType.DMA

    def low(*shape):
        return pltpu.VMEM(shape, BF16)

    return pl.pallas_call(
        partial(text_body, chips, dp_count, entry_count, head_count),
        out_shape=(
            jax.ShapeDtypeStruct((chunks, chunk_rows, width), BF16),
            jax.ShapeDtypeStruct((chunks, own_rows, width), BF16),
            jax.ShapeDtypeStruct((chunks, own_rows, entry_width), BF16),
            jax.ShapeDtypeStruct((chunks, 2, chips, own_rows, entry_width), BF16),
        ),
        in_specs=[vmem] * 8 + [hbm] * 8,
        out_specs=(hbm, vmem, vmem, vmem),
        scratch_shapes=[
            low(*weights.shape[1:]),
            low(*w_query.shape),
            low(*w_out.shape),
            low(*w_gate.shape),
            low(*w_up.shape),
            low(*w_down.shape),
            low(chunks, 2, chips, own_rows, width),
            low(chunks, chips, own_rows, width),
            low(chunks, chips - 1, own_rows, width),
            low(2, 2, chips, own_rows, width),
            low(chunks, chips, own_rows, width),
            low(chunks, chips - 1, own_rows, width),
            low(chunks, 2, chips, own_rows, width),
            low(group, owned, width),
            low(chunks, own_rows, width),
            low(chunks, head_width, chunk_rows),
            low(chunks, chunk_rows, head_width),
            low(chunks, chunk_rows, FHD),
            low(chunks, chunk_rows, FHD),
            low(chunks, FHD, chunk_rows),
            low(chunks, FHD, chunk_rows),
            low(chunks, head_width, chunk_rows),
            pltpu.VMEM((chunks, head_count // 2, 1, 2 * chunk_rows), F32),
            pltpu.VMEM((chunks, chunk_rows, chunk_rows), F32),
            pltpu.VMEM((chunks, own_rows, width), F32),
            dma((7,)),
            dma,
            dma((2,)),
            dma((3, 2, chunks)),
            dma((3, chunks, chips)),
            dma((3, chunks, chips)),
            dma((3, 2, chunks)),
            dma((3, chunks, chips)),
            dma((3, chunks, chips)),
            dma((2, chips)),
            dma((chips,)),
            dma((chips,)),
        ],
        compiler_params=pltpu.CompilerParams(
            collective_id=0, has_side_effects=True, vmem_limit_bytes=65280 * 1024
        ),
        cost_estimate=pl.CostEstimate(
            flops=90 * 10**9, bytes_accessed=40 * 10**6, transcendentals=20 * 10**6
        ),
    )(
        entry_ids,
        segments,
        cos_t,
        sin_t,
        bias_full,
        gain_one,
        gain_two,
        w_kv,
        entries,
        weights,
        token_grad,
        w_query,
        w_out,
        w_gate,
        w_up,
        w_down,
    )


def norm_parts(values):
    average = jnp.mean(values, axis=-1, keepdims=True)
    centred = values - average
    scale = lax.rsqrt(jnp.mean(centred * centred, axis=-1, keepdims=True) + 1e-05)
    return centred * scale, scale


def norm_back(values, grad, gain):
    unit, scale = norm_parts(values)
    scaled = grad * gain
    back = scale * (
        scaled
        - jnp.mean(scaled, axis=-1, keepdims=True)
        - unit * jnp.mean(scaled * unit, axis=-1, keepdims=True)
    )
    return (
        back,
        jnp.sum(grad * unit, axis=0, keepdims=True),
        jnp.sum(grad, axis=0, keepdims=True),
    )


def gelu_parts(values):
    root = math.sqrt(2.0 / math.pi)
    squared = values * values
    bent = jnp.tanh(root * values * (1.0 + 0.044715 * squared))
    half = 0.5 * (1.0 + bent)
    slope = half + 0.5 * values * (1.0 - bent * bent) * root * (1.0 + 3 * 0.044715 * squared)
    return values * half, slope


def pool_matrix(counts_col, entries, rows):
    entry = lax.broadcasted_iota(jnp.int32, (entries, rows), 0)
    row = lax.broadcasted_iota(jnp.int32, (entries, rows), 1)
    slots = rows // entries
    inside = (row // slots == entry) & (lax.rem(row, slots).astype(F32) < counts_col)
    return jnp.where(inside, 1.0, 0.0)


def spread_matrix(counts_row, entries, rows):
    row = lax.broadcasted_iota(jnp.int32, (rows, entries), 0)
    entry = lax.broadcasted_iota(jnp.int32, (rows, entries), 1)
    slots = rows // entries
    inside = (row // slots == entry) & (lax.rem(row, slots).astype(F32) < counts_row)
    return jnp.where(inside, 1.0, 0.0)


def slot_bias(valid_col, slots):
    rows = valid_col.shape[0]
    key = lax.broadcasted_iota(jnp.int32, (rows, rows), 0)
    query = lax.broadcasted_iota(jnp.int32, (rows, rows), 1)
    return jnp.where((key // slots == query // slots) & (valid_col > 0.5), 0.0, FAR)


ROW_BLOCK = 128


def fill_diagonal(ref, columns_t, heads):
    for h in range(heads):
        span = slice(h * HD, (h + 1) * HD)
        ref[span, h * ROW_BLOCK : (h + 1) * ROW_BLOCK] = columns_t[span, :]


def pair_blocks(both):
    return jnp.concatenate([both[:HD, :ROW_BLOCK], both[HD:, ROW_BLOCK:]], axis=0)


def tiled(block, count):
    return jnp.concatenate([block] * count, axis=1)


def shards_of(chips):
    return [(y * 2 + c, c, y) for y in range(chips) for c in range(2)]


def each_shard(chips, columns, body):
    @pl.loop(0, 2)
    def _(c):
        @pl.loop(0, chips)
        def _(y):
            first = pl.multiple_of((y * 2 + c) * columns, columns)
            body(c, y, pl.ds(first, columns))


def hyper_body(
    chips,
    dp_count,
    pieces,
    counts_all,
    gain_one,
    shift_one,
    gain_two,
    shift_two,
    w_query,
    w_key,
    w_value,
    w_out,
    bias_own,
    w_up_hbm,
    w_down_hbm,
    w_proj_hbm,
    text_key,
    text_value,
    entries,
    weights_out,
    attn_in,
    q_n,
    k_n,
    v_n,
    attended,
    logs,
    residual,
    ffn_in,
    counts_col,
    counts_row,
    bias_full,
    key_value,
    full,
    q_t,
    v_t,
    out_t,
    bias,
    diagonal,
    hidden,
    counts_scratch,
    local_sem,
    store_sem,
    far_send,
    far_recv,
    x_send,
    x_recv,
    near_send,
    near_recv,
    z_send,
    z_recv,
    mate_send,
    mate_recv,
    y_send,
    y_recv,
    last_send,
    last_recv,
    bias_far_send,
    bias_far_recv,
    bias_near,
    key_wide,
    value_wide,
    text_sem,
):
    me = lax.axis_index("mp")
    dp = lax.axis_index("dp")
    chip, core = me // 2, lax.rem(me, 2)
    net = Exchange(chips, chip, core, "mp")
    side = lax.rem(dp, 2)
    mate = dp + 1 - 2 * side
    spot, spots = dp // 2, dp_count // 2
    kinds, _, _, width, columns = full.shape
    sources = (None, w_up_hbm, w_down_hbm, w_proj_hbm)
    rows = pieces.shape[0]
    entry_count = counts_col.shape[0]
    slots = rows // entry_count
    head_columns = columns // 4
    half = width // 2
    heads = width // HD

    flag = pltpu.get_barrier_semaphore()
    pl.semaphore_signal(flag, inc=1, device_id=net.sibling(), device_id_type=MESH)
    for other in net.others():
        pl.semaphore_signal(flag, inc=1, device_id=net.peer(other), device_id_type=MESH)

    pl.semaphore_signal(flag, inc=1, device_id={"dp": mate}, device_id_type=MESH)

    @pl.loop(1, spots)
    def _(j):
        target = lax.rem(spot + j, spots) * 2 + side
        pl.semaphore_signal(flag, inc=1, device_id={"dp": target}, device_id_type=MESH)

    local = [
        pltpu.make_async_copy(sources[k], full.at[k, core, chip], local_sem.at[k - 1])
        for k in range(1, kinds)
    ]
    for copy in local:
        copy.start()
    for j, source in enumerate((w_query, w_key, w_value, w_out)):
        full[0, core, chip, :, j * head_columns : (j + 1) * head_columns] = source[...]
    bias_full[core, chip] = bias_own[...]
    pl.semaphore_wait(flag, chips + spots)

    def rows_half(which):
        return pl.ds(pl.multiple_of(which * half, half), half)

    def far_copy(k, other):
        return net.to_peer(
            other,
            sources[k].at[rows_half(side)] if k else full.at[0, core, chip, rows_half(side)],
            full.at[k, core, chip, rows_half(side)],
            far_send.at[k, other],
            far_recv.at[k, chip],
        )

    def far_landing(k, other):
        block = full.at[k, core, other, rows_half(side)]
        return net.to_peer(other, block, block, far_send.at[k, other], far_recv.at[k, other])

    def x_copy(k, other, which):
        block = full.at[k, core, other, rows_half(which)]
        return pltpu.make_async_remote_copy(
            src_ref=block,
            dst_ref=block,
            send_sem=x_send.at[k, other],
            recv_sem=x_recv.at[k, other],
            device_id={"dp": mate},
            device_id_type=MESH,
        )

    def near_copy(k, which):
        block = full.at[k, which]
        return net.to_sibling(block, block, near_send.at[k], near_recv.at[k])

    def far_middle(k):
        for other in net.others():
            far_landing(k, other).wait_recv()
            x_copy(k, other, side).start()

    def x_middle(k):
        for other in net.others():
            x_copy(k, other, 1 - side).wait_recv()
        if k:
            local[k - 1].wait()
        near_copy(k, core).start()

    def store(k):
        return pltpu.make_async_copy(full.at[k], weights_out.at[k], store_sem.at[k])

    def near_finish(k):
        near_copy(k, 1 - core).wait_recv()
        store(k).start()

    bias_rows = Gather(
        net, bias_full, (bias_far_send, bias_far_recv, bias_near.at[0], bias_near.at[1]), True
    )
    def far_start(k):
        for other in net.others():
            far_copy(k, other).start()

    far_start(0)
    bias_rows.start(0)
    text_copies = (
        pltpu.make_async_copy(text_key, key_wide, text_sem.at[0]),
        pltpu.make_async_copy(text_value, value_wide, text_sem.at[1]),
    )
    for copy in text_copies:
        copy.start()
    counts_scratch[...] = column_of(counts_all[...].astype(F32))
    own_counts = counts_scratch[pl.ds(pl.multiple_of(me * entry_count, entry_count), entry_count)]
    counts_col[...] = own_counts
    counts_row[...] = jnp.broadcast_to(own_counts, (entry_count, 128)).T[:1]

    values = pieces[...].astype(F32)
    attn_in[...] = (norm_parts(values)[0] * gain_one[...] + shift_one[...]).astype(BF16)
    blocks = rows // ROW_BLOCK
    valid = jnp.sum(spread_matrix(counts_row[...], entry_count, rows), axis=1, keepdims=True)
    for b in range(blocks):
        bias[b] = slot_bias(valid[b * ROW_BLOCK : (b + 1) * ROW_BLOCK], slots)

    for copy in text_copies:
        copy.wait()
    text_heads = QHEADS // (2 * chips)
    for j in range(KVHEADS):

        @pl.when(me * text_heads // (QHEADS // KVHEADS) == j)
        def _():
            key_value[:, :FHD] = key_wide[:, j * FHD : (j + 1) * FHD]
            key_value[:, FHD:] = value_wide[:, j * FHD : (j + 1) * FHD]

    far_middle(0)
    far_start(1)
    bias_rows.middle(0)
    far_middle(1)
    far_start(2)
    x_middle(0)
    near_finish(0)
    for m, c, y in shards_of(chips):
        span = slice(m * head_columns, (m + 1) * head_columns)
        projected = dot_nn(attn_in[...], full[0, c, y, :, : 3 * head_columns])
        q_n[:, span] = (projected[:, :head_columns].astype(BF16).astype(F32) * HD**-0.5).astype(
            BF16
        )
        k_n[:, span] = projected[:, head_columns : 2 * head_columns].astype(BF16)
        v_n[:, span] = projected[:, 2 * head_columns :].astype(BF16)
    far_middle(2)
    far_start(3)
    x_middle(1)
    for b in range(blocks):
        block_rows = slice(b * ROW_BLOCK, (b + 1) * ROW_BLOCK)
        q_t[b] = q_n[block_rows, :].T
        v_t[b] = v_n[block_rows, :].T

    diagonal[...] = jnp.zeros_like(diagonal)

    def attend_block(b):
        block_rows = pl.ds(pl.multiple_of(b * ROW_BLOCK, ROW_BLOCK), ROW_BLOCK)
        fill_diagonal(diagonal, q_t[b], heads)
        scores = dot_nn(k_n[block_rows, :], diagonal[...]) + tiled(bias[b], heads)
        top = jnp.max(scores, axis=0, keepdims=True)
        weights = jnp.exp(scores - top)
        total = jnp.sum(weights, axis=0, keepdims=True)
        logs[b] = top + jnp.log(total)
        weights = (weights / total).astype(BF16)
        for pair in range(heads // 2):
            span = slice(pair * 2 * HD, (pair + 1) * 2 * HD)
            lanes = slice(pair * 2 * ROW_BLOCK, (pair + 1) * 2 * ROW_BLOCK)
            both = dot_nn(v_t[b, span, :], weights[:, lanes])
            out_t[b, span, :] = pair_blocks(both).astype(BF16)

    pl.loop(0, blocks // 2)(attend_block)
    far_middle(3)
    x_middle(2)
    pl.loop(blocks // 2, blocks)(attend_block)
    for b in range(blocks):
        attended[b * ROW_BLOCK : (b + 1) * ROW_BLOCK, :] = out_t[b].T
    total = values
    for m, c, y in shards_of(chips):
        span = slice(m * head_columns, (m + 1) * head_columns)
        total = total + dot_nt(attended[:, span], full[0, c, y, :, 3 * head_columns :])
    residual[...] = total
    ffn_in[...] = (norm_parts(total)[0] * gain_two[...] + shift_two[...]).astype(BF16)
    near_finish(1)
    x_middle(3)
    pool = pool_matrix(counts_col[...], entry_count, rows).astype(BF16)

    def up_shard(c, y, span):
        act = gelu_parts(dot_nn(ffn_in[...], full[1, c, y]))[0]
        hidden[:, span] = dot_nn(pool, act.astype(BF16)).astype(BF16)

    each_shard(chips, columns, up_shard)
    near_finish(2)
    pooled = jnp.sum(
        (residual[...] * valid).reshape(entry_count, slots, width), axis=1
    )
    for m, c, y in shards_of(chips):
        pooled = pooled + dot_nt(hidden[:, m * columns : (m + 1) * columns], full[2, c, y])
    entries[core, chip, dp] = (pooled / counts_col[...]).astype(BF16)

    def z_copy(target, owner):
        piece = entries.at[core, chip, owner * 2 + side]
        return pltpu.make_async_remote_copy(
            src_ref=piece,
            dst_ref=piece,
            send_sem=z_send.at[target],
            recv_sem=z_recv.at[owner],
            device_id={"dp": target * 2 + side},
            device_id_type=MESH,
        )

    def mate_copy(owner, which):
        piece = entries.at[core, chip, owner * 2 + which]
        return pltpu.make_async_remote_copy(
            src_ref=piece,
            dst_ref=piece,
            send_sem=mate_send.at[owner],
            recv_sem=mate_recv.at[owner],
            device_id={"dp": mate},
            device_id_type=MESH,
        )

    def y_copy(other, owner, block):
        piece = entries.at[core, owner, block]
        return net.to_peer(
            other, piece, piece, y_send.at[other, block], y_recv.at[owner, block]
        )

    def y_start(block):
        for other in net.others():
            y_copy(other, chip, block).start()

    @pl.loop(1, spots)
    def _(j):
        z_copy(lax.rem(spot + j, spots), spot).start()

    mate_copy(spot, side).start()
    y_start(dp)
    near_finish(3)
    bias_rows.finish(0)

    @pl.loop(1, spots)
    def _(j):
        source = lax.rem(spot + spots - j, spots)
        z_copy(source, source).wait_recv()
        mate_copy(source, side).start()
        y_start(source * 2 + side)

    @pl.loop(0, spots)
    def _(j):
        source = lax.rem(spot + spots - j, spots)
        mate_copy(source, 1 - side).wait_recv()
        y_start(source * 2 + 1 - side)

    def last_copy(part, c, owner):
        piece = entries.at[c, owner]
        return net.to_sibling(piece, piece, last_send.at[part], last_recv.at[owner])

    last_copy(chip, core, chip).start()
    for other in net.others():

        @pl.loop(0, dp_count)
        def _(block):
            y_copy(other, other, block).wait_recv()

        last_copy(other, core, other).start()
    last_copy(chip, 1 - core, chip).wait_recv()
    for other in net.others():
        last_copy(other, 1 - core, other).wait_recv()

    bias_rows.sent(0)
    for k in range(kinds):
        store(k).wait()
        near_copy(k, core).wait_send()
        for other in net.others():
            far_copy(k, other).wait_send()
            x_copy(k, other, side).wait_send()

    @pl.loop(1, spots)
    def _(j):
        z_copy(lax.rem(spot + j, spots), spot).wait_send()

    @pl.loop(0, spots)
    def _(j):
        mate_copy(j, side).wait_send()

    last_copy(chip, core, chip).wait_send()
    for other in net.others():
        last_copy(other, core, other).wait_send()

        @pl.loop(0, dp_count)
        def _(block):
            y_copy(other, chip, block).wait_send()


def hyper_forward(
    group,
    dp_count,
    pieces,
    counts,
    gain_one,
    shift_one,
    gain_two,
    shift_two,
    head_weights,
    bias_own,
    unit_weights,
    text_key,
    text_value,
):
    chips = group // 2
    rows, width = pieces.shape
    columns = unit_weights[0].shape[1]
    kinds = 4
    entry_count = counts.shape[1] // group
    heads = width // HD
    blocks = rows // ROW_BLOCK
    vmem = pl.BlockSpec(memory_space=pltpu.VMEM)
    hbm = pl.BlockSpec(memory_space=pl.ANY)
    row_shape = jax.ShapeDtypeStruct((rows, width), BF16)
    dma = pltpu.SemaphoreType.DMA
    return pl.pallas_call(
        partial(hyper_body, chips, dp_count),
        out_shape=(
            jax.ShapeDtypeStruct((2, chips, dp_count, entry_count, width), BF16),
            jax.ShapeDtypeStruct((kinds, 2, chips, width, columns), BF16),
            row_shape,
            row_shape,
            row_shape,
            row_shape,
            row_shape,
            jax.ShapeDtypeStruct((blocks, 1, heads * ROW_BLOCK), F32),
            jax.ShapeDtypeStruct((rows, width), F32),
            row_shape,
            jax.ShapeDtypeStruct((entry_count, 1), F32),
            jax.ShapeDtypeStruct((1, entry_count), F32),
            jax.ShapeDtypeStruct((2, chips, 1, columns), F32),
            jax.ShapeDtypeStruct((text_key.shape[0], 2 * FHD), BF16),
        ),
        in_specs=[vmem] * 11 + [hbm] * 5,
        out_specs=(vmem, hbm) + (vmem,) * 12,
        scratch_shapes=[
            pltpu.VMEM((kinds, 2, chips, width, columns), BF16),
            pltpu.VMEM((blocks, width, ROW_BLOCK), BF16),
            pltpu.VMEM((blocks, width, ROW_BLOCK), BF16),
            pltpu.VMEM((blocks, width, ROW_BLOCK), BF16),
            pltpu.VMEM((blocks, ROW_BLOCK, ROW_BLOCK), F32),
            pltpu.VMEM((width, heads * ROW_BLOCK), BF16),
            pltpu.VMEM((entry_count, columns * group), BF16),
            pltpu.VMEM((counts.shape[1], 1), F32),
            dma((kinds - 1,)),
            dma((kinds,)),
            dma((kinds, chips)),
            dma((kinds, chips)),
            dma((kinds, chips)),
            dma((kinds, chips)),
            dma((kinds,)),
            dma((kinds,)),
            dma((dp_count // 2,)),
            dma((dp_count // 2,)),
            dma((dp_count // 2,)),
            dma((dp_count // 2,)),
            dma((chips, dp_count)),
            dma((chips, dp_count)),
            dma((chips,)),
            dma((chips,)),
            dma((1, chips)),
            dma((1, chips)),
            dma((2, 1)),
            pltpu.VMEM(text_key.shape, BF16),
            pltpu.VMEM(text_value.shape, BF16),
            dma((2,)),
        ],
        compiler_params=pltpu.CompilerParams(
            collective_id=1, has_side_effects=True, vmem_limit_bytes=60 * 1024 * 1024
        ),
        cost_estimate=pl.CostEstimate(
            flops=60 * 10**9, bytes_accessed=20 * 10**6, transcendentals=5 * 10**6
        ),
    )(
        pieces,
        counts,
        gain_one,
        shift_one,
        gain_two,
        shift_two,
        *head_weights,
        bias_own,
        *unit_weights,
        text_key,
        text_value,
    )


class Total:
    def __init__(self, net, dp, dp_count, scatter, mine, x_land, z_land, final, sems):
        self.net, self.scatter, self.mine = net, scatter, mine
        self.x_land, self.z_land, self.final = x_land, z_land, final
        self.x_send, self.x_recv, self.z_send, self.z_recv = sems[:4]
        self.g_send, self.g_recv, self.l_send, self.l_recv = sems[4:]
        self.side = lax.rem(dp, 2)
        self.spot = dp // 2
        self.mate = dp + 1 - 2 * self.side
        self.spots = dp_count // 2

    def remote(self, source, target, send, recv, device):
        return Pieces(source, target, send, recv, {"dp": device}, 1)

    def x_copy(self, k):
        return self.remote(
            self.mine.at[k, 1 - self.side],
            self.x_land.at[k],
            self.x_send.at[k],
            self.x_recv.at[k],
            self.mate,
        )

    def z_copy(self, k, spot, slot):
        return self.remote(
            self.mine.at[k, self.side, spot],
            self.z_land.at[k, slot],
            self.z_send.at[k, spot],
            self.z_recv.at[k, slot],
            spot * 2 + self.side,
        )

    def g_copy(self, k, spot, owner):
        block = self.final.at[k, self.side, owner]
        return self.remote(
            block, block, self.g_send.at[k, spot], self.g_recv.at[k, owner], spot * 2 + self.side
        )

    def l_copy(self, k, side):
        block = self.final.at[k, side]
        return self.remote(block, block, self.l_send.at[k], self.l_recv.at[k], self.mate)

    def each_spot(self, body):
        if self.spots > 1:

            @pl.loop(1, self.spots)
            def _(j):
                body(lax.rem(self.spot + j, self.spots))

    def start(self, k):
        self.scatter.start(k)

    def near_middle(self, k):
        self.scatter.middle(k)

    def far_middle(self, k):
        total = self.scatter.finish(k)
        self.mine[k] = total.astype(BF16).reshape(self.mine.shape[1:])
        self.x_copy(k).start()

    def x_middle(self, k):
        self.x_copy(k).wait_recv()
        block = self.mine[k, self.side].astype(F32) + self.x_land[k].astype(F32)
        self.mine[k, self.side] = block.astype(BF16)
        self.each_spot(lambda spot: self.z_copy(k, spot, self.spot).start())

    def z_middle(self, k):
        def add(spot):
            self.z_copy(k, spot, spot).wait_recv()

        self.each_spot(add)
        total = self.mine[k, self.side, self.spot].astype(F32)
        for j in range(1, self.spots):
            spot = lax.rem(self.spot + j, self.spots)
            total = total + self.z_land[k, spot].astype(F32)
        self.final[k, self.side, self.spot] = total.astype(BF16)
        self.each_spot(lambda spot: self.g_copy(k, spot, self.spot).start())

    def g_middle(self, k):
        self.each_spot(lambda spot: self.g_copy(k, spot, spot).wait_recv())
        self.l_copy(k, self.side).start()

    def finish(self, k):
        self.l_copy(k, 1 - self.side).wait_recv()

    def sent(self, k):
        self.scatter.sent(k)
        self.x_copy(k).wait_send()
        self.each_spot(lambda spot: self.z_copy(k, spot, self.spot).wait_send())
        self.each_spot(lambda spot: self.g_copy(k, spot, self.spot).wait_send())
        self.l_copy(k, self.side).wait_send()


PARTS = 8


def back_body(
    chips,
    dp_count,
    embed_rows,
    pooled_own,
    token_rows,
    token_row,
    pieces,
    counts_col,
    counts_row,
    gain_one,
    gain_two,
    attn_in,
    q_n,
    k_n,
    v_n,
    attended,
    logs,
    residual,
    ffn_in,
    weights_hbm,
    out_part,
    pieces_grad,
    final,
    small_total,
    text_out,
    weights,
    part,
    near,
    far,
    mine,
    x_land,
    z_land,
    entry_part,
    entry_land,
    hidden,
    slopes,
    ffn_t,
    row_total,
    d_out_n,
    d_query,
    d_key,
    d_value,
    q_t,
    out_t,
    d_out_t,
    k_t,
    d_query_t,
    bias,
    query_wide,
    grad_wide,
    small_near,
    small_far,
    small_dp,
    small_part,
    out_own,
    out_near,
    out_far,
    weight_sem,
    out_local,
    out_near_sem,
    out_far_send,
    out_far_recv,
    entry_send,
    entry_recv,
    scatter_near,
    scatter_far_send,
    scatter_far_recv,
    x_sem,
    z_send,
    z_recv,
    g_send,
    g_recv,
    l_sem,
    small_sem,
    small_far_send,
    small_far_recv,
    small_dp_send,
    small_dp_recv,
):
    me = lax.axis_index("mp")
    dp = lax.axis_index("dp")
    group = chips * 2
    chip, core = me // 2, lax.rem(me, 2)
    net = Exchange(chips, chip, core, "mp")
    rows, width = pieces.shape
    entry_count = counts_col.shape[0]
    slots = rows // entry_count
    columns = weights.shape[4]
    half_columns = columns // 2
    head_columns = columns // 4
    heads = width // HD
    blocks = rows // ROW_BLOCK
    total_sum = Total(
        net,
        dp,
        dp_count,
        Scatter(
            net,
            part,
            near,
            far,
            (scatter_near.at[0], scatter_near.at[1], scatter_far_send, scatter_far_recv),
        ),
        mine,
        x_land,
        z_land,
        final,
        (x_sem.at[0], x_sem.at[1], z_send, z_recv, g_send, g_recv, l_sem.at[0], l_sem.at[1]),
    )
    stages = (
        total_sum.near_middle,
        total_sum.far_middle,
        total_sum.x_middle,
        total_sum.z_middle,
        total_sum.g_middle,
        total_sum.finish,
    )

    def run(step):
        for offset, stage in enumerate(stages):
            if 0 <= step - offset < PARTS:
                stage(step - offset)

    flag = pltpu.get_barrier_semaphore()
    pl.semaphore_signal(flag, inc=1, device_id=net.sibling(), device_id_type=MESH)
    for other in net.others():
        pl.semaphore_signal(flag, inc=1, device_id=net.peer(other), device_id_type=MESH)

    def each_dp(body):
        @pl.loop(1, dp_count)
        def _(j):
            body(lax.rem(dp + j, dp_count))

    each_dp(
        lambda target: pl.semaphore_signal(
            flag, inc=1, device_id={"dp": target}, device_id_type=MESH
        )
    )
    loads = [
        pltpu.make_async_copy(weights_hbm.at[k], weights.at[k], weight_sem.at[k])
        for k in (1, 2, 0)
    ]
    for copy in loads:
        copy.start()
    out_copies = [
        pltpu.make_async_copy(out_part.at[y * 2 + core], out_own.at[y], out_local.at[y])
        for y in range(chips)
    ]
    for copy in out_copies:
        copy.start()
    pl.semaphore_wait(flag, chips + dp_count - 1)

    def out_near_copy(y):
        return net.to_sibling(
            out_part.at[y * 2 + 1 - core],
            out_near.at[y],
            out_near_sem.at[0, y],
            out_near_sem.at[1, y],
        )

    def out_far_copy(other, source):
        return net.to_peer(
            other,
            out_own.at[other],
            out_far.at[lax.rem(source - chip + chips - 1, chips)]
            if source is not chip
            else out_far.at[lax.rem(chip - other + chips - 1, chips)],
            out_far_send.at[other],
            out_far_recv.at[source],
        )

    for y in range(chips):
        out_near_copy(y).start()

    def put(k, c, y, values):
        part[k, c, y] = values[:, :half_columns].astype(BF16)
        part[k + 1, c, y] = values[:, half_columns:].astype(BF16)

    token_total = token_rows.shape[0]
    dp_step = max(1, 256 // entry_count)

    @pl.loop(0, dp_count // dp_step)
    def _(block):
        row = lax.broadcasted_iota(jnp.int32, (dp_step * entry_count, token_total), 0)
        owner = block * dp_step + row // entry_count
        number = (owner * group + me) * entry_count + lax.rem(row, entry_count)
        chosen = jnp.where(number == token_row[...], 1.0, 0.0).astype(BF16)
        sums = dot_nn(chosen, token_rows[...]).astype(BF16)
        for j in range(dp_step):
            entry_part[block * dp_step + j] = sums[j * entry_count : (j + 1) * entry_count]

    def entry_copy(target, slot):
        return pltpu.make_async_remote_copy(
            src_ref=entry_part.at[target],
            dst_ref=entry_land.at[slot],
            send_sem=entry_send.at[target],
            recv_sem=entry_recv.at[slot],
            device_id={"dp": target},
            device_id_type=MESH,
        )

    each_dp(lambda target: entry_copy(target, dp).start())
    pooled_t = pooled_own[...].T

    def proj_shard(c, y, span):
        put(0, c, y, dot_nn(pooled_t, embed_rows[:, span]))

    each_shard(chips, columns, proj_shard)
    total_sum.start(0)
    total_sum.start(1)
    bias_sums = jnp.sum(embed_rows[...].astype(F32), axis=0, keepdims=True)
    for j in range(4):
        small_part[4 + j : 5 + j, :] = bias_sums[:, j * width : (j + 1) * width]
    loads[0].wait()
    run(0)

    pool = pool_matrix(counts_col[...], entry_count, rows).astype(BF16)
    spread = spread_matrix(counts_row[...], entry_count, rows)
    valid = jnp.sum(spread, axis=1, keepdims=True)
    spread = spread.astype(BF16)
    for b in range(blocks):
        bias[b] = slot_bias(valid[b * ROW_BLOCK : (b + 1) * ROW_BLOCK], slots)
    ffn_t[...] = ffn_in[...].T

    def hidden_shard(c, y, span):
        act, slope = gelu_parts(dot_nn(ffn_in[...], weights[1, c, y]))
        slopes[:, span] = slope.astype(BF16)
        hidden[:, span] = dot_nn(pool, act.astype(BF16)).astype(BF16)

    each_shard(chips, columns, hidden_shard)
    run(1)
    each_dp(lambda source: entry_copy(source, source).wait_recv())
    pooled_grad = entry_part[dp].astype(F32)
    for j in range(1, dp_count):
        pooled_grad = pooled_grad + entry_land[lax.rem(dp + j, dp_count)].astype(F32)
    entry_low = (pooled_grad / counts_col[...]).astype(BF16)
    out_rows = dot_nn(spread, entry_low)
    entry_t = entry_low.T
    loads[1].wait()
    out_low = out_rows.astype(BF16)
    row_total[...] = jnp.zeros_like(row_total)

    def unit_shard(c, y, span):
        put(2, c, y, dot_nn(entry_t, hidden[:, span]))
        act_grad = dot_nn(out_low, weights[2, c, y])
        pre_grad = (act_grad * slopes[:, span].astype(F32)).astype(BF16)
        put(4, c, y, dot_nn(ffn_t[...], pre_grad))
        row_total[...] += dot_nt(pre_grad, weights[1, c, y])

    each_shard(chips, columns, unit_shard)
    for k in (2, 3, 4, 5):
        total_sum.start(k)
    run(2)
    back, gain_grad, shift_grad = norm_back(residual[...], row_total[...], gain_two[...])
    small_part[2:3, :] = gain_grad
    small_part[3:4, :] = shift_grad
    residual_grad = out_rows + back
    pieces_grad[...] = residual_grad
    attn_grad = residual_grad.astype(BF16)
    loads[2].wait()
    for m, c, y in shards_of(chips):
        span = slice(m * head_columns, (m + 1) * head_columns)
        d_out_n[:, span] = dot_nn(attn_grad, weights[0, c, y, :, 3 * head_columns :]).astype(BF16)
    out_grad = dot_nn(attn_grad.T, attended[...])
    for m, c, y in shards_of(chips):
        span = slice(m * head_columns, (m + 1) * head_columns)
        part[7, c, y, :, head_columns:] = out_grad[:, span].astype(BF16)
    for b in range(blocks):
        block_rows = slice(b * ROW_BLOCK, (b + 1) * ROW_BLOCK)
        q_t[b] = q_n[block_rows, :].T
        k_t[b] = k_n[block_rows, :].T
        out_t[b] = attended[block_rows, :].T
        d_out_t[b] = d_out_n[block_rows, :].T
    run(3)

    for ref in (query_wide, grad_wide):
        ref[...] = jnp.zeros_like(ref)

    @pl.loop(0, blocks)
    def _(b):
        block_rows = pl.ds(pl.multiple_of(b * ROW_BLOCK, ROW_BLOCK), ROW_BLOCK)
        fill_diagonal(query_wide, q_t[b], heads)
        fill_diagonal(grad_wide, d_out_t[b], heads)
        scores = dot_nn(k_n[block_rows, :], query_wide[...]) + tiled(bias[b], heads)
        probs = jnp.exp(scores - logs[b])
        d_value[block_rows, :] = dot_nt(probs.astype(BF16), grad_wide[...]).astype(BF16)
        moved = d_out_t[b].astype(F32) * out_t[b].astype(F32)
        centre = jnp.concatenate(
            [
                jnp.sum(moved[h * HD : (h + 1) * HD], axis=0, keepdims=True)
                for h in range(heads)
            ],
            axis=1,
        )
        score_grad = (probs * (dot_nn(v_n[block_rows, :], grad_wide[...]) - centre)).astype(BF16)
        d_key[block_rows, :] = dot_nt(score_grad, query_wide[...]).astype(BF16)
        for pair in range(heads // 2):
            span = slice(pair * 2 * HD, (pair + 1) * 2 * HD)
            lanes = slice(pair * 2 * ROW_BLOCK, (pair + 1) * 2 * ROW_BLOCK)
            both = dot_nn(k_t[b, span, :], score_grad[:, lanes]) * (HD**-0.5)
            d_query_t[b, span, :] = pair_blocks(both).astype(BF16)

    for b in range(blocks):
        d_query[b * ROW_BLOCK : (b + 1) * ROW_BLOCK, :] = d_query_t[b].T
    run(4)
    rows_t = attn_in[...].T
    for place, (k, lanes, source) in enumerate(
        ((6, 0, d_query), (6, 1, d_key), (7, 0, d_value))
    ):
        grads = dot_nn(rows_t, source[...])
        for m, c, y in shards_of(chips):
            span = slice(m * head_columns, (m + 1) * head_columns)
            part[k, c, y, :, lanes * head_columns : (lanes + 1) * head_columns] = grads[
                :, span
            ].astype(BF16)
    total_sum.start(6)
    total_sum.start(7)
    normed = jnp.zeros((rows, width), F32)
    for m, c, y in shards_of(chips):
        span = slice(m * head_columns, (m + 1) * head_columns)
        for j, source in enumerate((d_query, d_key, d_value)):
            normed = normed + dot_nt(
                source[:, span], weights[0, c, y, :, j * head_columns : (j + 1) * head_columns]
            )
    back, gain_grad, shift_grad = norm_back(pieces[...].astype(F32), normed, gain_one[...])
    small_part[0:1, :] = gain_grad
    small_part[1:2, :] = shift_grad
    pieces_grad[...] += back

    def out_middle():
        for y in range(chips):
            out_copies[y].wait()
            out_near_copy(y).wait_recv()
        for other in net.others():
            out_own[other] = (
                out_own[other].astype(F32) + out_near[other].astype(F32)
            ).astype(BF16)
            out_far_copy(other, chip).start()

    def out_finish():
        text_out[...] = out_own[chip].astype(F32) + out_near[chip].astype(F32)
        for other in net.others():
            out_far_copy(other, other).wait_recv()
            slot = lax.rem(other - chip + chips - 1, chips)
            text_out[...] += out_far[slot].astype(F32)

    small_copy = net.to_sibling(small_part, small_near, small_sem.at[0], small_sem.at[1])
    small_copy.start()

    def small_far_copy(other, owner):
        return net.to_peer(
            other,
            small_far.at[owner],
            small_far.at[owner],
            small_far_send.at[other],
            small_far_recv.at[owner],
        )

    def small_dp_copy(other, owner):
        return pltpu.make_async_remote_copy(
            src_ref=small_dp.at[owner],
            dst_ref=small_dp.at[owner],
            send_sem=small_dp_send.at[other],
            recv_sem=small_dp_recv.at[owner],
            device_id={"dp": other},
            device_id_type=MESH,
        )

    def small_near_done():
        small_copy.wait_recv()
        small_far[chip] = small_part[...] + small_near[...]
        for other in net.others():
            small_far_copy(other, chip).start()

    def small_far_done():
        for other in net.others():
            small_far_copy(other, other).wait_recv()
        total = small_far[0]
        for j in range(1, chips):
            total = total + small_far[j]
        small_dp[dp] = total
        each_dp(lambda other: small_dp_copy(other, dp).start())

    @pl.loop(5, PARTS + 5)
    def _(step):
        for offset, stage in enumerate(stages):
            k = step - offset

            @pl.when((k >= 0) & (k < PARTS))
            def _():
                stage(k)

        pl.when(step == 5)(small_near_done)
        pl.when(step == 7)(small_far_done)
        pl.when(step == PARTS)(out_middle)

    out_finish()
    each_dp(lambda other: small_dp_copy(other, other).wait_recv())
    total = small_dp[0]
    for j in range(1, dp_count):
        total = total + small_dp[j]
    small_total[...] = total

    for y in range(chips):
        out_near_copy(y).wait_send()
    for other in net.others():
        out_far_copy(other, chip).wait_send()
    small_copy.wait_send()
    for other in net.others():
        small_far_copy(other, chip).wait_send()
    each_dp(lambda other: small_dp_copy(other, dp).wait_send())
    each_dp(lambda other: entry_copy(other, dp).wait_send())

    @pl.loop(0, PARTS)
    def _(k):
        total_sum.sent(k)


def hyper_backward(
    group,
    dp_count,
    embed_rows,
    pooled_own,
    token_rows,
    token_row,
    pieces,
    counts_col,
    counts_row,
    gain_one,
    gain_two,
    saved,
    weights,
    out_part,
):
    chips = group // 2
    rows, width = pieces.shape
    entry_count = counts_col.shape[0]
    kinds, columns = weights.shape[0], weights.shape[4]
    half_columns = columns // 2
    heads = width // HD
    blocks = rows // ROW_BLOCK
    spots = dp_count // 2
    vmem = pl.BlockSpec(memory_space=pltpu.VMEM)
    hbm = pl.BlockSpec(memory_space=pl.ANY)
    dma = pltpu.SemaphoreType.DMA
    final = (PARTS, 2, spots, width // (2 * spots), half_columns)
    units = columns * group

    def low(*shape):
        return pltpu.VMEM(shape, BF16)

    def wide(*shape):
        return pltpu.VMEM(shape, F32)

    return pl.pallas_call(
        partial(back_body, chips, dp_count),
        out_shape=(
            jax.ShapeDtypeStruct((rows, width), F32),
            jax.ShapeDtypeStruct(final, BF16),
            jax.ShapeDtypeStruct((8, width), F32),
            jax.ShapeDtypeStruct(out_part.shape[1:], F32),
        ),
        in_specs=[vmem] * 17 + [hbm] * 2,
        out_specs=(vmem,) * 4,
        scratch_shapes=[
            low(kinds, 2, chips, width, columns),
            low(PARTS, 2, chips, width, half_columns),
            low(PARTS, chips, width, half_columns),
            low(PARTS, chips - 1, width, half_columns),
            low(*final),
            low(PARTS, spots, width // (2 * spots), half_columns),
            low(PARTS, spots, width // (2 * spots), half_columns),
            low(dp_count, entry_count, width),
            low(dp_count, entry_count, width),
            low(entry_count, units),
            low(rows, units),
            low(width, rows),
            wide(rows, width),
            low(rows, width),
            low(rows, width),
            low(rows, width),
            low(rows, width),
        ]
        + [low(blocks, width, ROW_BLOCK)] * 5
        + [
            wide(blocks, ROW_BLOCK, ROW_BLOCK),
            low(width, heads * ROW_BLOCK),
            low(width, heads * ROW_BLOCK),
            wide(8, width),
            wide(chips, 8, width),
            wide(dp_count, 8, width),
            wide(8, width),
            low(chips, *out_part.shape[1:]),
            low(chips, *out_part.shape[1:]),
            low(chips - 1, *out_part.shape[1:]),
            dma((kinds,)),
            dma((chips,)),
            dma((2, chips)),
            dma((chips,)),
            dma((chips,)),
            dma((dp_count,)),
            dma((dp_count,)),
            dma((2, PARTS)),
            dma((PARTS, chips)),
            dma((PARTS, chips)),
            dma((2, PARTS)),
            dma((PARTS, spots)),
            dma((PARTS, spots)),
            dma((PARTS, spots)),
            dma((PARTS, spots)),
            dma((2, PARTS)),
            dma((2,)),
            dma((chips,)),
            dma((chips,)),
            dma((dp_count,)),
            dma((dp_count,)),
        ],
        compiler_params=pltpu.CompilerParams(
            collective_id=2, has_side_effects=True, vmem_limit_bytes=62 * 1024 * 1024
        ),
        cost_estimate=pl.CostEstimate(
            flops=60 * 10**9, bytes_accessed=20 * 10**6, transcendentals=5 * 10**6
        ),
    )(
        embed_rows,
        pooled_own,
        token_rows,
        token_row,
        pieces,
        counts_col,
        counts_row,
        gain_one,
        gain_two,
        *saved,
        weights,
        out_part,
    )


SPREAD_STEPS = 4


def spread_body(
    group,
    sums,
    small,
    pieces_sum,
    out_sum,
    text_out,
    pieces_grad,
    gain_one,
    shift_one,
    query,
    key,
    value,
    out,
    gain_two,
    shift_two,
    up,
    down,
    proj,
    bias,
):
    me = lax.axis_index("mp")
    half_columns = sums.shape[2]
    head_columns = query.shape[1]
    width = small.shape[1]
    share = bias.shape[1]
    text_out[...] = out_sum[...]
    pieces_grad[...] = pieces_sum[...]
    for first, target in ((0, proj), (2, down), (4, up)):
        target[:, :half_columns] = sums[first].astype(F32)
        target[:, half_columns:] = sums[first + 1].astype(F32)
    for k, lanes, target in ((6, 0, query), (6, 1, key), (7, 0, value), (7, 1, out)):
        target[...] = sums[k, :, lanes * head_columns : (lanes + 1) * head_columns].astype(F32)
    for row, target in enumerate((gain_one, shift_one, gain_two, shift_two)):
        target[...] = small[row : row + 1, :]
    for m in range(group):
        first = m * share

        @pl.when(me == m)
        def _():
            row = 4 + first // width
            bias[...] = small[row : row + 1, first % width : first % width + share]


def spread_sums(group, sums, small, pieces_sum, out_sum, share):
    _, width, half_columns = sums.shape

    def wide(*shape):
        return jax.ShapeDtypeStruct(shape, F32)

    def split(shape):
        lead = (0,) * (len(shape) - 2)
        block = tuple(shape[:-2]) + (shape[-2] // SPREAD_STEPS, shape[-1])
        return pl.BlockSpec(block, lambda i: lead + (i, 0))

    def whole(shape):
        return pl.BlockSpec(shape, lambda i: (0, 0))

    heads = [wide(width, half_columns // 2)] * 4
    units = [wide(width, half_columns * 2)] * 3
    row = wide(1, width)
    return pl.pallas_call(
        partial(spread_body, group),
        out_shape=(
            wide(*out_sum.shape),
            wide(*pieces_sum.shape),
            row,
            row,
            *heads,
            row,
            row,
            *units,
            wide(1, share),
        ),
        grid=(SPREAD_STEPS,),
        in_specs=[split(sums.shape), whole(small.shape), split(pieces_sum.shape), split(out_sum.shape)],
        out_specs=(
            split(out_sum.shape),
            split(pieces_sum.shape),
            whole((1, width)),
            whole((1, width)),
            *[split(shape.shape) for shape in heads],
            whole((1, width)),
            whole((1, width)),
            *[split(shape.shape) for shape in units],
            whole((1, share)),
        ),
        compiler_params=pltpu.CompilerParams(vmem_limit_bytes=63 * 1024 * 1024),
    )(sums, small, pieces_sum, out_sum)


def on_device(
    pieces,
    counts,
    entry_ids,
    segment_ids,
    norm1_gain,
    norm1_shift,
    query_weight,
    key_weight,
    value_weight,
    out_weight,
    norm2_gain,
    norm2_shift,
    up_weight,
    down_weight,
    proj_weight,
    proj_bias,
    text_norm1_gain,
    text_query,
    text_key,
    text_value,
    text_out_proj,
    text_norm2_gain,
    text_gate,
    text_up,
    text_down,
    token_grad,
):
    group, dp_count = lax.axis_size("mp"), lax.axis_size("dp")
    entry_count, slot_count, width = pieces.shape
    text_width = token_grad.shape[1]
    length = segment_ids.shape[1]
    chunk_rows = length // CHUNKS
    pieces_rows = pieces.reshape(entry_count * slot_count, width)
    entries, weights, *saved, counts_col, counts_row, bias_full, key_value = hyper_forward(
        group,
        dp_count,
        pieces_rows,
        counts[None, :],
        norm1_gain[None, :],
        norm1_shift[None, :],
        norm2_gain[None, :],
        norm2_shift[None, :],
        (query_weight, key_weight, value_weight, out_weight),
        proj_bias[None, :],
        (up_weight, down_weight, proj_weight),
        text_key,
        text_value,
    )
    cos_t, sin_t = rope_tables(length)
    out_part, embed_rows, pooled_own, token_rows = text_layer(
        group,
        dp_count,
        entry_count,
        entry_ids.reshape(CHUNKS, 1, chunk_rows),
        segment_ids.reshape(CHUNKS, 1, chunk_rows),
        cos_t,
        sin_t,
        bias_full,
        text_norm1_gain[None, :],
        text_norm2_gain[None, :],
        key_value,
        entries.reshape(-1, width),
        weights,
        token_grad,
        text_query,
        text_out_proj,
        text_gate,
        text_up,
        text_down,
    )
    pieces_grad, final, small, text_out = hyper_backward(
        group,
        dp_count,
        embed_rows.reshape(-1, text_width),
        pooled_own.reshape(-1, width),
        token_rows.reshape(length, width),
        entry_ids[None, :],
        pieces_rows,
        counts_col,
        counts_row,
        norm1_gain[None, :],
        norm2_gain[None, :],
        saved,
        weights,
        out_part.reshape(group, -1, text_width),
    )
    outputs = spread_sums(
        group, final.reshape(PARTS, width, -1), small, pieces_grad, text_out, proj_bias.shape[0]
    )
    shapes = ((-1, text_width), pieces.shape) + ((width,),) * 2 + (None,) * 4
    shapes = shapes + ((width,),) * 2 + (None,) * 3 + ((-1,),)
    return tuple(
        value if shape is None else value.reshape(shape)
        for value, shape in zip(outputs, shapes)
    )


def solution(mesh):
    return jax.shard_map(
        on_device,
        mesh=mesh,
        in_specs=(
            P(("dp", "mp"), None, None),
            P("dp"),
            P("dp"),
            P("dp", None),
            P(),
            P(),
            P(None, "mp"),
            P(None, "mp"),
            P(None, "mp"),
            P(None, "mp"),
            P(),
            P(),
            P(None, "mp"),
            P(None, "mp"),
            P(None, "mp"),
            P("mp"),
            P(),
            P(None, "mp"),
            P(),
            P(),
            P(None, "mp"),
            P(),
            P(None, "mp"),
            P(None, "mp"),
            P(None, "mp"),
            P(("dp", "mp"), None),
        ),
        out_specs=(
            P(("dp", "mp"), None),
            P(("dp", "mp"), None, None),
            P(),
            P(),
            P(None, "mp"),
            P(None, "mp"),
            P(None, "mp"),
            P(None, "mp"),
            P(),
            P(),
            P(None, "mp"),
            P(None, "mp"),
            P(None, "mp"),
            P("mp"),
        ),
        check_vma=False,
    )
```
